32 devices in a mesh: dp: 4 (over y, x), expert: 8 (over z, core).
Axes of the slice: x: 2, y: 2, z: 4, core: 2. Of those that a mesh axis runs over, the one named last changes fastest.
Arguments:
- tokens: bfloat16 [8, 1024, 1024], P('expert', 'dp'), may hold values from -6 to 6
- cotangent: bfloat16 [8, 1024, 1024], P('expert', 'dp'), may hold values from -6 to 6
- lengths: int32 [8], P('expert'), may hold values from 128 to 1024, as said below
- picks: int32 [8, 1024, 8, 2], P('expert', 'dp'), may hold values from 0 to 4, all different within a row
- routes: int32 [8, 1024, 16], P('expert', 'dp'), may hold values from 0 to 95, all different within a row; in each aligned block of 256 rows (0 to 255, 256 to 511, ..., all dimensions but the last counted through in order) at most 77 rows name the same one
- qk_weight: float32 [1024, 1024], P(('dp', 'expert')), may hold values from -0.25 to 0.25
- qk_first: float32 [1024, 1024], P(('dp', 'expert')), may hold values from -192 to 192
- qk_second: float32 [1024, 1024], P(('dp', 'expert')), may hold values from 1884.16 to 31129.6
- value_weight: float32 [1024, 2560], P(('dp', 'expert')), may hold values from -0.1875 to 0.1875
- value_first: float32 [1024, 2560], P(('dp', 'expert')), may hold values from -64 to 64
- value_second: float32 [1024, 2560], P(('dp', 'expert')), may hold values from 212.992 to 3440.64
- output_weight: float32 [1024, 2560], P(('dp', 'expert')), may hold values from -10 to 10
- output_first: float32 [1024, 2560], P(('dp', 'expert')), may hold values from -0.75 to 0.75
- output_second: float32 [1024, 2560], P(('dp', 'expert')), may hold values from 0.0303104 to 0.49152
- select_weight: float32 [1024, 40], P(('dp', 'expert')), may hold values from -0.1875 to 0.1875
- select_first: float32 [1024, 40], P(('dp', 'expert')), may hold values from -320 to 320
- select_second: float32 [1024, 40], P(('dp', 'expert')), may hold values from 5324.8 to 86016
- router_weight: float32 [1024, 96], P(('dp', 'expert')), may hold values from -0.09375 to 0.09375
- router_first: float32 [1024, 96], P(('dp', 'expert')), may hold values from -64 to 64
- router_second: float32 [1024, 96], P(('dp', 'expert')), may hold values from 313.95 to 5187
- gain_weight: float32 [1024], P(('dp', 'expert')), may hold values from 0.4 to 1.6
- gain_first: float32 [1024], P(('dp', 'expert')), may hold values from -768 to 768
- gain_second: float32 [1024], P(('dp', 'expert')), may hold values from 15099.494 to 964689.92
- expert_weight: float32 [96, 1024, 256], P('expert', 'dp'), may hold values from -0.3125 to 0.3125
- expert_first: float32 [96, 1024, 256], P('expert', 'dp'), may hold values from -12 to 12
- expert_second: float32 [96, 1024, 256], P('expert', 'dp'), may hold values from 8.8725 to 143.325
Outputs:
- layer_out: bfloat16 [8, 1024, 1024], P('expert', 'dp')
- input_grad: float32 [8, 1024, 1024], P('expert', 'dp')
- qk_new: float32 [1024, 1024], P(('dp', 'expert'))
- qk_first_new: float32 [1024, 1024], P(('dp', 'expert'))
- qk_second_new: float32 [1024, 1024], P(('dp', 'expert'))
- value_new: float32 [1024, 2560], P(('dp', 'expert'))
- value_first_new: float32 [1024, 2560], P(('dp', 'expert'))
- value_second_new: float32 [1024, 2560], P(('dp', 'expert'))
- output_new: float32 [1024, 2560], P(('dp', 'expert'))
- output_first_new: float32 [1024, 2560], P(('dp', 'expert'))
- output_second_new: float32 [1024, 2560], P(('dp', 'expert'))
- select_new: float32 [1024, 40], P(('dp', 'expert'))
- select_first_new: float32 [1024, 40], P(('dp', 'expert'))
- select_second_new: float32 [1024, 40], P(('dp', 'expert'))
- router_new: float32 [1024, 96], P(('dp', 'expert'))
- router_first_new: float32 [1024, 96], P(('dp', 'expert'))
- router_second_new: float32 [1024, 96], P(('dp', 'expert'))
- gain_new: float32 [1024], P(('dp', 'expert'))
- gain_first_new: float32 [1024], P(('dp', 'expert'))
- gain_second_new: float32 [1024], P(('dp', 'expert'))
- expert_new: float32 [96, 1024, 256], P('expert', 'dp')
- expert_first_new: float32 [96, 1024, 256], P('expert', 'dp')
- expert_second_new: float32 [96, 1024, 256], P('expert', 'dp')
- expert_counts: int32 [96], replicated
The draws below stay inside these ranges and needn't reach their ends.
Inputs may be any that keep to these rules, and one draw needn't show every extreme that they name: `lengths`: A sequence has 128 to 1024 valid positions at its start; some sequence has all 1024. `picks`: two different experts for each head's value projection and for its output projection. `routes`: each token names 16 different experts; the 256 rows of one device name no expert more than 77 times, a bound that some block reaches.
All inputs are finite; a program needn't handle non-finite values.
Results may differ from the reference program's by a relative error of at most 0.02.
The reference program's roundings to bfloat16 on the way count: a program that leaves them out, or rounds other values in their place, can miss the bound.
Values may be sent and summed in bfloat16 or wider, within the bound.
No kernel may reach another device: no remote copies, remote signals or barrier semaphores. Data moves between devices by JAX's collectives and lax.ppermute only.
A program may use at most 320 MiB of HBM per device.

```python
import math
import jax
import jax.numpy as jnp
import numpy as np
from jax import lax

D = 1024
HEADS = 4
HEAD_DIM = 128
ATT_EXPERTS = 5
EXPERT_H = 128
TOPK = 16
TOK_DEV = 256
LEN_MIN = 128
STEP = 10
EXPERTS = 96
CAP = 77
BUCKET = 1024
SEQS = 8
N_DP = 4
DEVICES = 32


def draw_lengths(key, part):
    key = jax.random.fold_in(key, 7)
    length_key, pick_key = jax.random.split(key)
    drawn = jax.random.randint(length_key, (SEQS,), LEN_MIN, BUCKET + 1)
    longest = jax.random.randint(pick_key, (), 0, SEQS)
    return jnp.where(jnp.arange(SEQS) == longest, BUCKET, drawn).astype(jnp.int32)


def draw_gain_second(key, part):
    key = jax.random.fold_in(key, 11)
    fraction = jax.random.uniform(key, (D,), jnp.float32)
    total = float(BUCKET * SEQS * BUCKET)
    lower = 0.0036
    upper = 0.058
    return (total * lower * jnp.exp(fraction * jnp.log(upper / lower))).astype(jnp.float32)


def levels(rng, shape, pieces, smallest, top_value):
    factor_of = 1.0
    for position, shards_of in pieces:
        heights = jax.random.uniform(jax.random.fold_in(jax.random.fold_in(rng, 6), position), (shards_of,), jnp.float32, smallest / len(pieces), top_value / len(pieces))
        factor_of = factor_of * jnp.repeat(jnp.exp(heights), shape[position] // shards_of).reshape((-1,) + (1,) * (len(shape) - 1 - position))
    return factor_of


def choose_distinct(rng, rows, amount, top, lift):
    order = jax.random.permutation(jax.random.fold_in(rng, 1), amount)
    pull = order
    for power in range(3):
        pull = pull * pull // amount
    pull = pull * lift // amount
    lots = jax.random.randint(jax.random.fold_in(rng, 2), (rows, amount), 0, 4096) + pull
    fixed_rows = jax.random.permutation(jax.random.fold_in(rng, 3), rows)[jnp.arange(amount) % rows]
    lots = jnp.where(jnp.arange(rows)[:, None] == fixed_rows[None, :], 1 << 14, lots)
    score = lots * amount + jnp.arange(amount)
    return lax.top_k(score.astype(jnp.int32), top)[1].astype(jnp.int32)


def deal_out(key, own, number, rows, number_of, top, limit, lean):
    ranking = jax.random.permutation(key, number_of)
    crowded, common = portions_of(number_of, rows * top, limit, lean, True), portions_of(number_of, rows * top, limit, lean, False)
    places = jnp.arange(number_of)

    def named(sizes, turn):
        used = int((sizes > 0).sum())
        fixed = max(1, used // 4)
        passed = fixed + (places - fixed + turn * (used - fixed)) % max(1, number_of - fixed)
        return jnp.zeros((number_of,), jnp.int32).at[ranking[jnp.where(places < fixed, places, passed)]].set(jnp.asarray(sizes, jnp.int32))

    sizes = jnp.where(number % 4 == 0, named(crowded, number // 4), named(common, number - number // 4 - 1))
    mixed = jax.random.permutation(jax.random.fold_in(own, 3), number_of)
    donor, taker = mixed[0:number_of // 2 * 2:2], mixed[1:number_of // 2 * 2:2]
    slack = jnp.minimum(sizes[donor] - 1, limit - sizes[taker]) // 2
    slack = jnp.where((donor == ranking[0]) | (taker == ranking[0]) | (sizes[taker] == 0), 0, jnp.maximum(slack, 0))
    passed = jax.random.randint(jax.random.fold_in(own, 4), (number_of // 2,), 0, 1 << 20) % (slack + 1)
    sizes = sizes.at[donor].add(-passed).at[taker].add(passed)
    members = jnp.searchsorted(jnp.cumsum(sizes), jnp.arange(rows * top), side="right").astype(jnp.int32)
    listing = members.reshape(top, rows).T
    listing = listing[jax.random.permutation(jax.random.fold_in(own, 1), rows)]
    turn = jax.random.randint(jax.random.fold_in(own, 2), (rows, 1), 0, top)
    return jnp.take_along_axis(listing, (jnp.arange(top)[None, :] + turn) % top, axis=1)


def portions_of(number_of, total, bound, lean, full):
    portions = [(1 << 20) // math.isqrt(standing ** lean) + 1 for standing in range(1, number_of + 1)]
    largest = bound if full else min(bound, max(-(-total // number_of), total * portions[0] // sum(portions)))
    least = 1 if total - largest >= number_of - 1 else 0
    holding, surplus = [largest] + [least] * (number_of - 1), total - largest - least * (number_of - 1)
    while surplus > 0:
        free = [i for i in range(1, number_of) if holding[i] < largest] or [i for i in range(1, number_of) if holding[i] < bound]
        whole, left = sum([portions[i] for i in free]), surplus
        for i in free:
            extra = min(bound - holding[i], max(1, left * portions[i] // whole), surplus)
            holding[i] = holding[i] + extra
            surplus = surplus - extra
    return np.array(holding)


def normal_values(rng, dims, scale, most, cuts=(), dtype=jnp.bfloat16):
    factor_of = levels(rng, dims, cuts, -0.22, 0.18) if cuts else 1.0
    values = jax.random.normal(rng, dims, jnp.float32) * scale * factor_of
    return jnp.minimum(jnp.maximum(values, -most), most).astype(dtype)


def setup_inputs(seed: int = 0) -> dict:
    key_of = jax.random.split(jax.random.key(seed), 27)
    tokens = normal_values(key_of[0], (SEQS, BUCKET, D), 1.0, 6.0, ((0, 8), (1, 4)))
    cotangent = normal_values(key_of[1], (SEQS, BUCKET, D), 1.0, 6.0, ((0, 8), (1, 4)))
    lengths = draw_lengths(jax.random.fold_in(key_of[26], 71), 0)
    picks = choose_distinct(key_of[3], SEQS * BUCKET * (2 * HEADS), ATT_EXPERTS, 2, 0).reshape((SEQS, BUCKET, 2 * HEADS, 2))
    routes_keys = jax.random.split(jax.random.fold_in(key_of[4], 1), SEQS * BUCKET // TOK_DEV)
    routes_turns = jax.random.permutation(jax.random.fold_in(key_of[4], 3), SEQS * BUCKET // TOK_DEV)
    routes = jax.vmap(lambda own, number: deal_out(jax.random.fold_in(key_of[4], 2), own, number, TOK_DEV, EXPERTS, TOPK, CAP, 1))(routes_keys, routes_turns).reshape((SEQS, BUCKET, TOPK))
    qk_weight = normal_values(key_of[5], (D, 2 * HEADS * HEAD_DIM), (1.4 * D ** -0.5), 0.25, ((0, 32),), jnp.float32)
    qk_first = normal_values(key_of[6], (D, 2 * HEADS * HEAD_DIM), (0.33 * (TOK_DEV * DEVICES) ** 0.5), 192.0, ((0, 32),), jnp.float32)
    qk_second = jnp.clip(jnp.exp(math.log(31129.6) - 2.804677 * jax.random.uniform(key_of[7], (D, 2 * HEADS * HEAD_DIM), jnp.float32) ** levels(key_of[7], (D, 2 * HEADS * HEAD_DIM), ((0, 32),), -0.2, 0.2)), 1884.16, 31129.6)
    value_weight = normal_values(key_of[8], (D, HEADS * ATT_EXPERTS * HEAD_DIM), D ** -0.5, 0.1875, ((0, 32),), jnp.float32)
    value_first = normal_values(key_of[9], (D, HEADS * ATT_EXPERTS * HEAD_DIM), (0.11 * (TOK_DEV * DEVICES) ** 0.5), 64.0, ((0, 32),), jnp.float32)
    value_second = jnp.clip(jnp.exp(math.log(3440.64) - 2.7821581 * jax.random.uniform(key_of[10], (D, HEADS * ATT_EXPERTS * HEAD_DIM), jnp.float32) ** levels(key_of[10], (D, HEADS * ATT_EXPERTS * HEAD_DIM), ((0, 32),), -0.2, 0.2)), 212.992, 3440.64)
    output_weight = normal_values(key_of[11], (D, HEADS * ATT_EXPERTS * HEAD_DIM), (1.2 * (BUCKET / (HEADS * HEAD_DIM)) ** 0.5), 10.0, ((0, 32),), jnp.float32)
    output_first = normal_values(key_of[12], (D, HEADS * ATT_EXPERTS * HEAD_DIM), (0.0013 * (TOK_DEV * DEVICES) ** 0.5), 0.75, ((0, 32),), jnp.float32)
    output_second = jnp.clip(jnp.exp(math.log(0.49152) - 2.7860117 * jax.random.uniform(key_of[13], (D, HEADS * ATT_EXPERTS * HEAD_DIM), jnp.float32) ** levels(key_of[13], (D, HEADS * ATT_EXPERTS * HEAD_DIM), ((0, 32),), -0.2, 0.2)), 0.0303104, 0.49152)
    select_weight = normal_values(key_of[14], (D, 2 * HEADS * ATT_EXPERTS), (D ** -0.5), 0.1875, ((0, 32),), jnp.float32)
    select_first = normal_values(key_of[15], (D, 2 * HEADS * ATT_EXPERTS), (0.55 * (TOK_DEV * DEVICES) ** 0.5), 320.0, ((0, 32),), jnp.float32)
    select_second = jnp.clip(jnp.exp(math.log(86016.0) - 2.7821582 * jax.random.uniform(key_of[16], (D, 2 * HEADS * ATT_EXPERTS), jnp.float32) ** levels(key_of[16], (D, 2 * HEADS * ATT_EXPERTS), ((0, 32),), -0.2, 0.2)), 5324.8, 86016.0)
    router_weight = normal_values(key_of[17], (D, EXPERTS), (0.5 * D ** -0.5), 0.09375, ((0, 32),), jnp.float32)
    router_first = normal_values(key_of[18], (D, EXPERTS), (0.33 * (TOK_DEV * DEVICES * TOPK // EXPERTS) ** 0.5), 64.0, ((0, 32),), jnp.float32)
    router_second = jnp.clip(jnp.exp(math.log(5187.0) - 2.804677 * jax.random.uniform(key_of[19], (D, EXPERTS), jnp.float32) ** levels(key_of[19], (D, EXPERTS), ((0, 32),), -0.2, 0.2)), 313.95, 5187.0)
    gain_weight = jnp.clip(0.4 + 1.2 * jax.random.uniform(key_of[20], (D,), jnp.float32) ** levels(key_of[20], (D,), ((0, 32),), -0.2, 0.2), 0.4, 1.6)
    gain_first = normal_values(key_of[21], (D,), (0.041 * (BUCKET * TOK_DEV * DEVICES) ** 0.5), 768.0, ((0, 32),), jnp.float32)
    gain_second = draw_gain_second(jax.random.fold_in(key_of[26], 71), 0)
    expert_weight = normal_values(key_of[23], (EXPERTS, D, 2 * EXPERT_H), ((D * EXPERT_H) ** -0.25), 0.3125, ((0, 8), (1, 4)), jnp.float32)
    expert_first = normal_values(key_of[24], (EXPERTS, D, 2 * EXPERT_H), (0.055 * (TOK_DEV * DEVICES * TOPK // EXPERTS) ** 0.5), 12.0, ((0, 8), (1, 4)), jnp.float32)
    expert_second = jnp.clip(jnp.exp(math.log(143.325) - 2.7821581 * jax.random.uniform(key_of[25], (EXPERTS, D, 2 * EXPERT_H), jnp.float32) ** levels(key_of[25], (EXPERTS, D, 2 * EXPERT_H), ((0, 8), (1, 4)), -0.2, 0.2)), 8.8725, 143.325)
    return dict(tokens=tokens, cotangent=cotangent, lengths=lengths, picks=picks, routes=routes, qk_weight=qk_weight, qk_first=qk_first, qk_second=qk_second, value_weight=value_weight, value_first=value_first, value_second=value_second, output_weight=output_weight, output_first=output_first, output_second=output_second, select_weight=select_weight, select_first=select_first, select_second=select_second, router_weight=router_weight, router_first=router_first, router_second=router_second, gain_weight=gain_weight, gain_first=gain_first, gain_second=gain_second, expert_weight=expert_weight, expert_first=expert_first, expert_second=expert_second)


@jax.custom_vjp
def low(v):
    return lax.optimization_barrier(v.astype(jnp.bfloat16)).astype(jnp.float32)

@jax.custom_vjp
def low_back(v):
    return v

def low_keep(v):
    return (low(v), None)

def low_pass(kept, grad):
    return (grad,)

def back_keep(v):
    return (v, None)

def back_low(kept, grad):
    return (low(grad),)
low.defvjp(low_keep, low_pass)
low_back.defvjp(back_keep, back_low)
norm_eps = 1e-05
beta_first = 0.9
beta_second = 0.95
adam_eps = 1e-08
weight_decay = 0.1
masked_score = -1e+30
rope_base = 10000.0
rate_query_key = 0.04
rate_value = 0.03
rate_output = 2.0
rate_select = 0.03
rate_router = 0.015
rate_gain = 1.2
rate_expert = 0.05

def matmul(former, latter):
    return jnp.dot(former, latter, precision=lax.Precision.HIGHEST, preferred_element_type=jnp.float32)

def einsum_high(formula, former, latter):
    return jnp.einsum(formula, former, latter, precision=lax.Precision.HIGHEST, preferred_element_type=jnp.float32)

def layer_norm(values, gain_row):
    center = values - lax.optimization_barrier(jnp.mean(values, axis=-1, keepdims=True))
    spread = lax.optimization_barrier(jnp.mean(center * center, axis=-1, keepdims=True))
    return center * lax.rsqrt(spread + norm_eps) * gain_row

def rope_tables(positions, head_size):
    half_size = head_size // 2
    frequency = jnp.exp(-jnp.log(rope_base) * jnp.arange(half_size).astype(jnp.float32) / half_size)
    angles = positions[:, None] * frequency[None, :]
    return (jnp.cos(angles)[:, None, :], jnp.sin(angles)[:, None, :])

def rotate(head_rows, cosine, sine_table):
    half_size = head_rows.shape[-1] // 2
    leading = head_rows[..., :half_size]
    trailing = head_rows[..., half_size:]
    return jnp.concatenate([leading * cosine - trailing * sine_table, leading * sine_table + trailing * cosine], axis=-1)

def slot_numbers(route_block):
    hot_table = (route_block[:, :, None] == jnp.arange(EXPERTS).astype(jnp.int32)[None, None, :]).astype(jnp.int32)
    per_token = lax.optimization_barrier(jnp.sum(hot_table, axis=1))
    earlier = jnp.cumsum(per_token, axis=0) - per_token
    return jnp.take_along_axis(earlier, route_block, axis=1).astype(jnp.int32)

def sequence_forward(weights, sequence, seq_len, pick_rows, route_rows):
    qk_full, value_full, output_full, select_full, router_full, gain_full, expert_full = weights
    positions = jnp.arange(BUCKET).astype(jnp.float32)
    cosine, sine_table = rope_tables(positions, HEAD_DIM)
    normed_low = low(layer_norm(sequence, gain_full))
    query_key = low_back(matmul(normed_low, qk_full)).reshape(BUCKET, 2, HEADS, HEAD_DIM)
    queries = low(rotate(query_key[:, 0], cosine, sine_table))
    key_rows = low(rotate(query_key[:, 1], cosine, sine_table))
    chosen = lax.optimization_barrier(jnp.sum((pick_rows[..., None] == jnp.arange(ATT_EXPERTS).astype(jnp.int32)).astype(jnp.float32), axis=-2))
    chosen = chosen.reshape(BUCKET, 2, HEADS, ATT_EXPERTS)
    selection = low_back(matmul(normed_low, select_full)).reshape(BUCKET, 2, HEADS, ATT_EXPERTS)
    weighting = jax.nn.sigmoid(selection) * chosen
    projected = low_back(matmul(sequence, value_full)).reshape(BUCKET, HEADS, ATT_EXPERTS, HEAD_DIM)
    values = low(lax.optimization_barrier(jnp.sum(weighting[:, 0, :, :, None] * projected, axis=2)))
    scores = low_back(einsum_high('qhd,khd->hqk', queries, key_rows) * HEAD_DIM ** (-0.5))
    place = jnp.arange(BUCKET).astype(jnp.int32)
    allowed = (place[None, :] <= place[:, None]) & (place[None, :] < seq_len)
    scores = jnp.where(allowed[None], scores, masked_score)
    highest = lax.optimization_barrier(jnp.max(scores, axis=-1, keepdims=True))
    raised = jnp.exp(scores - highest)
    attention_probs = raised / lax.optimization_barrier(jnp.sum(raised, axis=-1, keepdims=True))
    attended = low_back(einsum_high('hqk,khd->qhd', low(attention_probs), values))
    mixed_heads = low(weighting[:, 1, :, :, None] * attended[:, :, None, :]).reshape(BUCKET, HEADS * ATT_EXPERTS * HEAD_DIM)
    branch_out = low_back(matmul(mixed_heads, output_full.T))
    hidden = sequence + branch_out
    normed_two = low(layer_norm(hidden, 1.0))
    logits = low_back(matmul(normed_two, router_full))
    route_gates = jax.nn.sigmoid(jnp.take_along_axis(logits, route_rows, axis=1))
    block_routes = route_rows.reshape(N_DP, TOK_DEV, TOPK)
    slots = jax.vmap(slot_numbers)(block_routes)
    block_ids = jnp.broadcast_to(jnp.arange(N_DP).astype(jnp.int32)[:, None, None], block_routes.shape)
    sources = jnp.broadcast_to(low(hidden).reshape(N_DP, TOK_DEV, 1, D), (N_DP, TOK_DEV, TOPK, D))
    buffer = jnp.zeros((EXPERTS, N_DP, CAP, D), jnp.float32).at[block_routes, block_ids, slots].set(sources)
    buffer = low_back(buffer)
    inner = low_back(einsum_high('ebcd,edh->ebch', buffer, expert_full[:, :, :EXPERT_H]))
    active = low(jax.nn.silu(inner))
    produced = low_back(low(einsum_high('ebch,edh->ebcd', active, expert_full[:, :, EXPERT_H:])))
    picked = produced[block_routes, block_ids, slots].reshape(BUCKET, TOPK, D)
    return hidden + lax.optimization_barrier(jnp.sum(route_gates[:, :, None] * picked, axis=1))

def adamw_update(weight, first_moment, second_moment, gradient, rate):
    first_new = beta_first * first_moment + (1.0 - beta_first) * gradient
    second_new = beta_second * second_moment + (1.0 - beta_second) * gradient * gradient
    first_hat = first_new / (1.0 - beta_first ** STEP)
    second_hat = second_new / (1.0 - beta_second ** STEP)
    weight_new = weight - rate * (first_hat / (jnp.sqrt(second_hat) + adam_eps) + weight_decay * weight)
    return (weight_new, first_new, second_new)

def reference(tokens, cotangent, lengths, picks, routes, qk_weight, qk_first, qk_second, value_weight, value_first, value_second, output_weight, output_first, output_second, select_weight, select_first, select_second, router_weight, router_first, router_second, gain_weight, gain_first, gain_second, expert_weight, expert_first, expert_second):

    def forward(inputs_all, qk_master, value_master, output_master, select_master, router_master, gain_master, expert_master):
        lowered = (low(qk_master), low(value_master), low(output_master), low(select_master), low(router_master), low(gain_master), low(expert_master))

        def step(running, inputs):
            sequence, seq_len, pick_rows, route_rows = inputs
            return (running, sequence_forward(lowered, sequence, seq_len, pick_rows, route_rows))
        _, outputs = lax.scan(jax.checkpoint(step), jnp.zeros((), jnp.float32), (inputs_all, lengths, picks, routes))
        return outputs
    valid = jnp.arange(BUCKET).astype(jnp.int32)[None, :] < lengths[:, None]
    outputs, backward = jax.vjp(forward, tokens.astype(jnp.float32), qk_weight, value_weight, output_weight, select_weight, router_weight, gain_weight, expert_weight)
    gradients = backward(cotangent.astype(jnp.float32) * valid[..., None].astype(jnp.float32))
    qk_new, qk_first_new, qk_second_new = adamw_update(qk_weight, qk_first, qk_second, gradients[1], rate_query_key)
    value_new, value_first_new, value_second_new = adamw_update(value_weight, value_first, value_second, gradients[2], rate_value)
    output_new, output_first_new, output_second_new = adamw_update(output_weight, output_first, output_second, gradients[3], rate_output)
    select_new, select_first_new, select_second_new = adamw_update(select_weight, select_first, select_second, gradients[4], rate_select)
    router_new, router_first_new, router_second_new = adamw_update(router_weight, router_first, router_second, gradients[5], rate_router)
    gain_new, gain_first_new, gain_second_new = adamw_update(gain_weight, gain_first, gain_second, gradients[6], rate_gain)
    expert_new, expert_first_new, expert_second_new = adamw_update(expert_weight, expert_first, expert_second, gradients[7], rate_expert)
    valid_routes = jnp.broadcast_to(valid[..., None], routes.shape).astype(jnp.int32)
    expert_counts = jnp.zeros((EXPERTS,), jnp.int32).at[routes.reshape(-1)].add(valid_routes.reshape(-1))
    return (outputs.astype(jnp.bfloat16), gradients[0], qk_new, qk_first_new, qk_second_new, value_new, value_first_new, value_second_new, output_new, output_first_new, output_second_new, select_new, select_first_new, select_second_new, router_new, router_first_new, router_second_new, gain_new, gain_first_new, gain_second_new, expert_new, expert_first_new, expert_second_new, expert_counts)
```

```python
import jax
import jax.numpy as jnp
from jax import lax
from jax.sharding import PartitionSpec as P

HEADS = 4
HEAD_DIM = 128
ATT_EXPERTS = 5
EXPERT_H = 128
TOPK = 16
STEP = 10


norm_eps = 1e-05
beta_first = 0.9
beta_second = 0.95
adam_eps = 1e-08
weight_decay = 0.1
masked_score = -1e30
rope_base = 10000.0
rate_query_key = 0.04
rate_value = 0.03
rate_output = 2.0
rate_select = 0.03
rate_router = 0.015
rate_gain = 1.2
rate_expert = 0.05


def product(former, latter):
    return jnp.dot(former, latter, preferred_element_type=jnp.float32)


def product_rows(former, latter):
    return lax.dot_general(
        former, latter, (((0,), (0,)), ((), ())), preferred_element_type=jnp.float32
    )


def product_last(former, latter):
    return lax.dot_general(
        former, latter, (((1,), (1,)), ((), ())), preferred_element_type=jnp.float32
    )


def layer_norm(values, gain_row):
    center = values - jnp.mean(values, axis=-1, keepdims=True)
    spread = jnp.mean(center * center, axis=-1, keepdims=True)
    return center * lax.rsqrt(spread + norm_eps) * gain_row


def norm_backward(values, gain_row, upstream):
    center = values - jnp.mean(values, axis=-1, keepdims=True)
    inverse = lax.rsqrt(jnp.mean(center * center, axis=-1, keepdims=True) + norm_eps)
    scaled = center * inverse
    gain_grad = jnp.sum(upstream * scaled, axis=0)
    through = upstream * gain_row
    input_grad = inverse * (
        through
        - jnp.mean(through, axis=-1, keepdims=True)
        - scaled * jnp.mean(through * scaled, axis=-1, keepdims=True)
    )
    return (input_grad, gain_grad)


def rope_tables(positions, head_size):
    half_size = head_size // 2
    frequency = jnp.exp(-jnp.log(rope_base) * jnp.arange(half_size).astype(jnp.float32) / half_size)
    angles = positions[:, None] * frequency[None, :]
    return (jnp.cos(angles)[:, None, :], jnp.sin(angles)[:, None, :])


def rotate(head_rows, cosine, sine_table, direction):
    half_size = head_rows.shape[-1] // 2
    leading = head_rows[..., :half_size]
    trailing = head_rows[..., half_size:]
    return jnp.concatenate(
        [
            leading * cosine - direction * trailing * sine_table,
            direction * leading * sine_table + trailing * cosine,
        ],
        axis=-1,
    )


def silu_slope(inner):
    sigma = jax.nn.sigmoid(inner)
    return sigma * (1.0 + inner * (1.0 - sigma))


def adamw_update(weight, first_moment, second_moment, gradient, rate):
    first_new = beta_first * first_moment + (1.0 - beta_first) * gradient
    second_new = beta_second * second_moment + (1.0 - beta_second) * gradient * gradient
    first_hat = first_new / (1.0 - beta_first**STEP)
    second_hat = second_new / (1.0 - beta_second**STEP)
    weight_new = weight - rate * (
        first_hat / (jnp.sqrt(second_hat) + adam_eps) + weight_decay * weight
    )
    return (weight_new, first_new, second_new)


def lower(values):
    return values.astype(jnp.bfloat16)


def swap_dp(values, relative):
    count = lax.axis_size("dp")
    return lax.ppermute(values, "dp", [(place, place ^ relative) for place in range(count)])


def gather_dp(values):
    half = values.shape[0] // 2
    first = swap_dp(values, 1)
    second = swap_dp(values, 2)
    upper = swap_dp(first[:half], 2)
    under = swap_dp(second[half:], 1)
    return [values, first, second, jnp.concatenate([upper, under], axis=0)]


def scatter_dp(parts):
    half = parts[0].shape[0] // 2
    low_parts = [lower(part) for part in parts]
    upper = swap_dp(low_parts[3][:half], 2)
    under = swap_dp(low_parts[3][half:], 1)
    first = lower(
        jnp.concatenate([parts[1][:half] + upper.astype(jnp.float32), parts[1][half:]], axis=0)
    )
    second = lower(
        jnp.concatenate([parts[2][:half], parts[2][half:] + under.astype(jnp.float32)], axis=0)
    )
    return (
        parts[0]
        + swap_dp(first, 1).astype(jnp.float32)
        + swap_dp(second, 2).astype(jnp.float32)
    )


def split_heads(weights, pieces):
    part = weights.shape[0]
    return lower(weights).reshape(part, pieces, HEADS, -1).transpose(2, 0, 1, 3).reshape(HEADS, part, -1)


def local(
    tokens,
    cotangent,
    lengths,
    picks,
    routes,
    qk_weight,
    qk_first,
    qk_second,
    value_weight,
    value_first,
    value_second,
    output_weight,
    output_first,
    output_second,
    select_weight,
    select_first,
    select_second,
    router_weight,
    router_first,
    router_second,
    gain_weight,
    gain_first,
    gain_second,
    expert_weight,
    expert_first,
    expert_second,
):
    row_count = tokens.shape[1]
    model_width = tokens.shape[2]
    group_count = lax.axis_size("dp")
    owner_count = lax.axis_size("expert")
    local_count = expert_weight.shape[0]
    expert_total = local_count * owner_count
    bucket_rows = row_count * group_count
    score_scale = HEAD_DIM ** (-0.5)
    hidden_width = local_count * EXPERT_H
    value_width = ATT_EXPERTS * HEAD_DIM
    part = qk_weight.shape[0]
    select_count = 2 * ATT_EXPERTS
    place = lax.axis_index("dp")
    seq_len = lengths[0]
    sequence = tokens[0]
    route_rows = routes[0]
    own_place = place * row_count + jnp.arange(row_count, dtype=jnp.int32)
    valid = own_place < seq_len

    hot = jnp.max(
        (route_rows[:, :, None] == jnp.arange(expert_total, dtype=jnp.int32)[None, None, :]).astype(
            jnp.float32
        ),
        axis=1,
    )
    counts_local = jnp.sum(hot * valid[:, None].astype(jnp.float32), axis=0)
    count_columns = -(-expert_total // part)
    counts_block = lower(
        jnp.pad(counts_local, (0, count_columns * part - expert_total)).reshape(part, count_columns)
    )

    small_width = select_count + expert_total + 1 + count_columns
    small_pad = -small_width % 128
    shared = jnp.concatenate(
        [
            lower(router_weight),
            lower(gain_weight)[:, None],
            counts_block,
            jnp.zeros((part, small_pad), jnp.bfloat16),
        ],
        axis=1,
    )
    payload = jnp.concatenate(
        [
            split_heads(qk_weight, 2),
            split_heads(value_weight, 1),
            split_heads(output_weight, 1),
            split_heads(select_weight, 2),
            jnp.broadcast_to(shared[None], (HEADS,) + shared.shape),
        ],
        axis=2,
    )
    mine = lax.all_to_all(payload, "dp", split_axis=0, concat_axis=0, tiled=True)
    dense = lax.all_gather(mine, "expert", axis=1, tiled=True).reshape(model_width, -1)
    edge = 2 * HEAD_DIM
    qk_head = dense[:, :edge]
    value_head = dense[:, edge : edge + value_width]
    output_head = dense[:, edge + value_width : edge + 2 * value_width]
    edge = edge + 2 * value_width
    select_head = dense[:, edge : edge + select_count]
    edge = edge + select_count
    router_full = dense[:, edge : edge + expert_total]
    edge = edge + expert_total
    gain_one = dense[:, edge].astype(jnp.float32)
    edge = edge + 1
    expert_counts = jnp.sum(
        dense[:, edge : edge + count_columns]
        .reshape(group_count * owner_count, part * count_columns)[:, :expert_total]
        .astype(jnp.float32),
        axis=0,
    ).astype(jnp.int32)

    expert_low = lower(expert_weight)
    expert_rows = jnp.concatenate(
        [
            expert_low[:, :, :EXPERT_H].transpose(1, 0, 2).reshape(row_count, hidden_width),
            expert_low[:, :, EXPERT_H:].transpose(1, 0, 2).reshape(row_count, hidden_width),
        ],
        axis=1,
    )
    expert_full = lax.all_gather(expert_rows, "dp", axis=0, tiled=True)
    expert_in = expert_full[:, :hidden_width]
    expert_out = expert_full[:, hidden_width:]

    chosen_own = jnp.sum(
        (picks[0][..., None] == jnp.arange(ATT_EXPERTS, dtype=jnp.int32)).astype(jnp.float32),
        axis=-2,
    )
    chosen_own = (
        chosen_own.reshape(row_count, 2, HEADS, ATT_EXPERTS)
        .transpose(0, 2, 1, 3)
        .reshape(row_count, HEADS * select_count)
    )
    chosen_own = jnp.pad(lower(chosen_own), ((0, 0), (0, -(HEADS * select_count) % 128)))
    token_blocks = gather_dp(jnp.concatenate([sequence, chosen_own], axis=1))
    token_rows = jnp.concatenate(token_blocks, axis=0)
    inputs_low = token_rows[:, :model_width]
    inputs_f = inputs_low.astype(jnp.float32)
    chosen = lax.dynamic_slice_in_dim(
        token_rows[:, model_width:], place * select_count, select_count, axis=1
    ).astype(jnp.float32)
    positions = jnp.concatenate(
        [
            (place ^ relative) * row_count + jnp.arange(row_count, dtype=jnp.int32)
            for relative in range(group_count)
        ]
    )
    cosine, sine_table = rope_tables(positions.astype(jnp.float32), HEAD_DIM)
    cosine, sine_table = cosine[:, 0], sine_table[:, 0]

    normed_low = lower(layer_norm(inputs_f, gain_one))
    query_key = product(normed_low, qk_head)
    queries = lower(rotate(query_key[:, :HEAD_DIM], cosine, sine_table, 1.0))
    key_rows = lower(rotate(query_key[:, HEAD_DIM:], cosine, sine_table, 1.0))
    sigma_sel = jax.nn.sigmoid(product(normed_low, select_head))
    weighting = sigma_sel * chosen
    projected = product(inputs_low, value_head).reshape(bucket_rows, ATT_EXPERTS, HEAD_DIM)
    weight_in = weighting[:, :ATT_EXPERTS, None]
    weight_out = weighting[:, ATT_EXPERTS:, None]
    values = lower(jnp.sum(weight_in * projected, axis=1))
    allowed = (positions[None, :] <= positions[:, None]) & (positions[None, :] < seq_len)
    scores = jnp.where(allowed, product_last(queries, key_rows) * score_scale, masked_score)
    highest = jnp.max(scores, axis=-1, keepdims=True)
    raised = jnp.exp(scores - highest)
    attention_probs = raised / jnp.sum(raised, axis=-1, keepdims=True)
    probs_low = lower(attention_probs)
    attended = product(probs_low, values)
    mixed = lower(weight_out * attended[:, None, :]).reshape(bucket_rows, value_width)
    branch = product_last(mixed, output_head).reshape(group_count, row_count, model_width)
    hidden = sequence.astype(jnp.float32) + scatter_dp([branch[r] for r in range(group_count)])

    normed_two = lower(layer_norm(hidden, 1.0))
    gate_table = jax.nn.sigmoid(product(normed_two, router_full)) * hot
    gates = lax.all_to_all(
        gate_table.T.reshape(owner_count, local_count, row_count),
        "expert",
        split_axis=0,
        concat_axis=0,
        tiled=True,
    )
    gates = gates.transpose(0, 2, 1).reshape(owner_count * row_count, local_count)
    wide = (owner_count * row_count, local_count, EXPERT_H)
    gates_wide = jnp.broadcast_to(gates[:, :, None], wide).reshape(-1, hidden_width)
    expert_rows_in = lax.all_gather(lower(hidden), "expert", axis=0, tiled=True)
    upstream_low = jnp.where(valid[:, None], cotangent[0], jnp.zeros((), jnp.bfloat16))
    upstream = upstream_low.astype(jnp.float32)
    expert_up = lax.all_gather(upstream_low, "expert", axis=0, tiled=True)

    inner = product(expert_rows_in, expert_in)
    sigma = jax.nn.sigmoid(inner)
    active = lower(inner * sigma).astype(jnp.float32)
    gated = lower(gates_wide * active)
    produced = product_last(gated, expert_out)
    moe_out = lax.psum_scatter(
        lower(produced), "expert", scatter_dimension=0, tiled=True
    ).astype(jnp.float32)
    layer_out = lower(hidden + moe_out)
    out_terms = product(expert_up, expert_out)
    gate_terms = jnp.sum((out_terms * active).reshape(wide), axis=-1)
    inner_grad = lower(gates_wide * out_terms * sigma * (1.0 + inner * (1.0 - sigma)))
    back = product_last(inner_grad, expert_in)
    moe_input_grad = lax.psum_scatter(
        lower(back), "expert", scatter_dimension=0, tiled=True
    ).astype(jnp.float32)
    gate_grad = lax.all_to_all(
        gate_terms.reshape(owner_count, row_count, local_count).transpose(0, 2, 1),
        "expert",
        split_axis=0,
        concat_axis=0,
        tiled=True,
    )
    gate_grad = gate_grad.reshape(expert_total, row_count).T
    expert_grad = jnp.concatenate(
        [product_rows(expert_rows_in, inner_grad), product_rows(expert_up, gated)], axis=1
    )
    expert_sum = lax.psum_scatter(
        lower(expert_grad), "dp", scatter_dimension=0, tiled=True
    ).astype(jnp.float32)
    expert_sum = (
        expert_sum.reshape(row_count, 2, local_count, EXPERT_H)
        .transpose(2, 0, 1, 3)
        .reshape(local_count, row_count, 2 * EXPERT_H)
    )

    logit_grad = lower(gate_grad * gate_table * (1.0 - gate_table))
    router_grad = product_rows(normed_two, logit_grad)
    normed_two_grad = product_last(logit_grad, router_full)
    hidden_norm_grad = norm_backward(hidden, 1.0, normed_two_grad)[0]
    hidden_grad = upstream + moe_input_grad + hidden_norm_grad
    hidden_grad_low = jnp.concatenate(gather_dp(lower(hidden_grad)), axis=0)

    output_grad = product_rows(hidden_grad_low, mixed)
    mixed_grad = product(hidden_grad_low, output_head).reshape(bucket_rows, ATT_EXPERTS, HEAD_DIM)
    attended_low = lower(jnp.sum(weight_out * mixed_grad, axis=1))
    out_weighting_grad = jnp.sum(mixed_grad * attended[:, None, :], axis=-1)
    value_terms = product_rows(probs_low, attended_low)
    prob_grad = product_last(attended_low, values)
    delta = jnp.sum(attention_probs * prob_grad, axis=-1, keepdims=True)
    score_grad = lower(attention_probs * (prob_grad - delta))
    query_grad = product(score_grad, key_rows) * score_scale
    key_grad = product_rows(score_grad, queries) * score_scale
    projected_grad = lower(weight_in * value_terms[:, None, :]).reshape(bucket_rows, value_width)
    in_weighting_grad = jnp.sum(value_terms[:, None, :] * projected, axis=-1)
    value_grad = product_rows(inputs_low, projected_grad)
    query_key_grad = lower(
        jnp.concatenate(
            [
                rotate(query_grad, cosine, sine_table, -1.0),
                rotate(key_grad, cosine, sine_table, -1.0),
            ],
            axis=1,
        )
    )
    qk_grad = product_rows(normed_low, query_key_grad)
    weighting_grad = jnp.concatenate([in_weighting_grad, out_weighting_grad], axis=1)
    selection_grad = lower(weighting_grad * chosen * sigma_sel * (1.0 - sigma_sel))
    select_grad = product_rows(normed_low, selection_grad)
    normed_grad = product_last(query_key_grad, qk_head) + product_last(selection_grad, select_head)
    input_norm_grad, gain_grad = norm_backward(inputs_f, gain_one, normed_grad)
    input_terms = (product_last(projected_grad, value_head) + input_norm_grad).reshape(
        group_count, row_count, model_width
    )
    input_grad = hidden_grad + scatter_dp([input_terms[r] for r in range(group_count)])

    dense_grad = lower(
        jnp.concatenate(
            [
                qk_grad,
                value_grad,
                output_grad,
                select_grad,
                router_grad,
                gain_grad[:, None],
                jnp.zeros((model_width, small_pad + count_columns), jnp.float32),
            ],
            axis=1,
        )
    )
    dense_grad = dense_grad.reshape(group_count, owner_count, part, -1).transpose(1, 0, 2, 3)
    dense_sum = lax.psum_scatter(dense_grad, "expert", scatter_dimension=0, tiled=True)[0]
    dense_sum = lax.all_to_all(dense_sum, "dp", split_axis=0, concat_axis=0, tiled=True).astype(
        jnp.float32
    )

    def join_heads(columns, pieces):
        return columns.reshape(HEADS, part, pieces, -1).transpose(1, 2, 0, 3).reshape(part, -1)

    edge = 2 * HEAD_DIM
    qk_sum = join_heads(dense_sum[:, :, :edge], 2)
    value_sum = join_heads(dense_sum[:, :, edge : edge + value_width], 1)
    output_sum = join_heads(dense_sum[:, :, edge + value_width : edge + 2 * value_width], 1)
    edge = edge + 2 * value_width
    select_sum = join_heads(dense_sum[:, :, edge : edge + select_count], 2)
    edge = edge + select_count
    shared_sum = jnp.sum(dense_sum[:, :, edge : edge + expert_total + 1], axis=0)
    router_sum = shared_sum[:, :expert_total]
    gain_sum = shared_sum[:, expert_total]
    qk_new, qk_first_new, qk_second_new = adamw_update(
        qk_weight, qk_first, qk_second, qk_sum, rate_query_key
    )
    value_new, value_first_new, value_second_new = adamw_update(
        value_weight, value_first, value_second, value_sum, rate_value
    )
    output_new, output_first_new, output_second_new = adamw_update(
        output_weight, output_first, output_second, output_sum, rate_output
    )
    select_new, select_first_new, select_second_new = adamw_update(
        select_weight, select_first, select_second, select_sum, rate_select
    )
    router_new, router_first_new, router_second_new = adamw_update(
        router_weight, router_first, router_second, router_sum, rate_router
    )
    gain_new, gain_first_new, gain_second_new = adamw_update(
        gain_weight, gain_first, gain_second, gain_sum, rate_gain
    )
    expert_new, expert_first_new, expert_second_new = adamw_update(
        expert_weight, expert_first, expert_second, expert_sum, rate_expert
    )
    return (
        layer_out[None],
        input_grad[None],
        qk_new,
        qk_first_new,
        qk_second_new,
        value_new,
        value_first_new,
        value_second_new,
        output_new,
        output_first_new,
        output_second_new,
        select_new,
        select_first_new,
        select_second_new,
        router_new,
        router_first_new,
        router_second_new,
        gain_new,
        gain_first_new,
        gain_second_new,
        expert_new,
        expert_first_new,
        expert_second_new,
        expert_counts,
    )


def solution(mesh):
    placed = (
        P("expert", "dp", None),
        P("expert", "dp", None),
        P("expert"),
        P("expert", "dp", None, None),
        P("expert", "dp", None),
        P(("dp", "expert"), None),
        P(("dp", "expert"), None),
        P(("dp", "expert"), None),
        P(("dp", "expert"), None),
        P(("dp", "expert"), None),
        P(("dp", "expert"), None),
        P(("dp", "expert"), None),
        P(("dp", "expert"), None),
        P(("dp", "expert"), None),
        P(("dp", "expert"), None),
        P(("dp", "expert"), None),
        P(("dp", "expert"), None),
        P(("dp", "expert"), None),
        P(("dp", "expert"), None),
        P(("dp", "expert"), None),
        P(("dp", "expert")),
        P(("dp", "expert")),
        P(("dp", "expert")),
        P("expert", "dp", None),
        P("expert", "dp", None),
        P("expert", "dp", None),
    )
    return jax.shard_map(
        local,
        mesh=mesh,
        in_specs=placed,
        out_specs=(
            P("expert", "dp", None),
            P("expert", "dp", None),
            P(("dp", "expert"), None),
            P(("dp", "expert"), None),
            P(("dp", "expert"), None),
            P(("dp", "expert"), None),
            P(("dp", "expert"), None),
            P(("dp", "expert"), None),
            P(("dp", "expert"), None),
            P(("dp", "expert"), None),
            P(("dp", "expert"), None),
            P(("dp", "expert"), None),
            P(("dp", "expert"), None),
            P(("dp", "expert"), None),
            P(("dp", "expert"), None),
            P(("dp", "expert"), None),
            P(("dp", "expert"), None),
            P(("dp", "expert")),
            P(("dp", "expert")),
            P(("dp", "expert")),
            P("expert", "dp", None),
            P("expert", "dp", None),
            P("expert", "dp", None),
            P(),
        ),
        check_vma=False,
    )
```

```python
import functools

import numpy as np
import jax
import jax.numpy as jnp
from jax import lax
from jax.experimental import pallas as pl
from jax.experimental.pallas import tpu as pltpu
from jax.sharding import PartitionSpec as P

HEADS = 4
HEAD_DIM = 128
ATT_EXPERTS = 5
EXPERT_H = 128
TOPK = 16
STEP = 10


norm_eps = 1e-05
beta_first = 0.9
beta_second = 0.95
adam_eps = 1e-08
weight_decay = 0.1
masked_score = -1e30
rope_base = 10000.0
rate_query_key = 0.04
rate_value = 0.03
rate_output = 2.0
rate_select = 0.03
rate_router = 0.015
rate_gain = 1.2
rate_expert = 0.05


def product(former, latter):
    return jnp.dot(former, latter, preferred_element_type=jnp.float32)


def product_rows(former, latter):
    return lax.dot_general(
        former, latter, (((0,), (0,)), ((), ())), preferred_element_type=jnp.float32
    )


def product_last(former, latter):
    return lax.dot_general(
        former, latter, (((1,), (1,)), ((), ())), preferred_element_type=jnp.float32
    )


def rope_tables(rows):
    half = HEAD_DIM // 2
    frequency = np.exp(-np.log(rope_base) * np.arange(half) / half)
    angles = np.arange(rows)[:, None] * frequency[None, :]
    cosine, sine = np.cos(angles), np.sin(angles)
    return (
        jnp.asarray(np.concatenate([cosine, cosine], axis=1), jnp.float32),
        jnp.asarray(np.concatenate([-sine, sine], axis=1), jnp.float32),
    )


def adamw_update(weight, first_moment, second_moment, gradient, rate):
    first_new = beta_first * first_moment + (1.0 - beta_first) * gradient
    second_new = beta_second * second_moment + (1.0 - beta_second) * gradient * gradient
    first_hat = first_new / (1.0 - beta_first**STEP)
    second_hat = second_new / (1.0 - beta_second**STEP)
    weight_new = weight - rate * (
        first_hat / (jnp.sqrt(second_hat) + adam_eps) + weight_decay * weight
    )
    return (weight_new, first_new, second_new)


LIGHT = pl.CostEstimate(flops=1000, bytes_accessed=1000, transcendentals=0)


def swap(values, axis, relative):
    count = lax.axis_size(axis)
    return lax.ppermute(values, axis, [(place, place ^ relative) for place in range(count)])


def lower(values):
    return values.astype(jnp.bfloat16)


def raise_(values):
    return values.astype(jnp.float32)


def after(values, *others):
    return lax.optimization_barrier((values,) + others)[0]


def dp_copies(values):
    return jnp.broadcast_to(values[None], (lax.axis_size("dp"),) + values.shape)


def exchange_rows(copies):
    blocks = lax.all_to_all(copies, "dp", split_axis=0, concat_axis=0, tiled=True)
    return blocks.reshape((-1,) + copies.shape[2:])


def scatter_rows(values):
    count = lax.axis_size("dp")
    blocks = values.reshape((count, values.shape[0] // count) + values.shape[1:])
    return lax.all_to_all(blocks, "dp", split_axis=0, concat_axis=0, tiled=True)


def add_blocks(values, blocks):
    for index in range(blocks.shape[0]):
        values = values + raise_(blocks[index])
    return values


def join(own, other):
    return lower(raise_(own) + raise_(other))


def forwarded(relative):
    return relative & 2 and relative > 2


def gather_chips(values):
    return [values] + [
        swap(values, "expert", relative) for relative in range(2, lax.axis_size("expert"), 2)
    ]


def send_expert(joined):
    return [joined[0]] + [
        swap(term, "expert", 2 * index) for index, term in enumerate(joined) if index
    ]


def full(shape):
    return pl.BlockSpec(shape, lambda *_: (0,) * len(shape))


def wide_call(kernel, inputs, outputs, scratch=()):
    specs = [pl.BlockSpec(memory_space=pltpu.SMEM)] + [full(value.shape) for value in inputs[1:]]
    return pl.pallas_call(
        kernel,
        grid=(1,),
        in_specs=specs,
        out_specs=[full(value.shape) for value in outputs],
        out_shape=outputs,
        scratch_shapes=list(scratch),
        compiler_params=pltpu.CompilerParams(vmem_limit_bytes=56 * 2**20),
        cost_estimate=LIGHT,
    )(*inputs)


def shift_table(rows, columns, offset, count):
    source = lax.broadcasted_iota(jnp.int32, (rows, columns), 0)
    target = lax.broadcasted_iota(jnp.int32, (rows, columns), 1)
    return lower(jnp.where((source == target + offset) & (target < count), 1.0, 0.0))


def moments(values):
    center = values - jnp.mean(values, axis=-1, keepdims=True)
    inverse = lax.rsqrt(jnp.mean(center * center, axis=-1, keepdims=True) + norm_eps)
    return center * inverse, inverse


def turn(rows, cosine, signed_sine, direction):
    return rows * cosine + direction * pltpu.roll(rows, HEAD_DIM // 2, 1) * signed_sine


def masked_scores(queries, key_rows, seq_len, start):
    scores = product_last(queries, key_rows) * HEAD_DIM ** (-0.5)
    query_place = start + lax.broadcasted_iota(jnp.int32, scores.shape, 0)
    key_place = lax.broadcasted_iota(jnp.int32, scores.shape, 1)
    return jnp.where((key_place <= query_place) & (key_place < seq_len), scores, masked_score)


VALUE_WIDTH = ATT_EXPERTS * HEAD_DIM
QK_EDGE = 2 * HEAD_DIM
VALUE_EDGE = QK_EDGE + VALUE_WIDTH
OUTPUT_EDGE = VALUE_EDGE + VALUE_WIDTH
SELECT_COUNT = 2 * ATT_EXPERTS


def attention_kernel(block, gain_column, chips, scalars, tokens, cosine, sine, *refs):
    if chips:
        evens, odds, dense = refs[:chips], refs[chips], refs[chips + 1]
        refs = refs[chips + 2 :]
        groups, part = odds.shape[1:3]
        for group in range(groups):
            for chip in range(chips):
                for other, rows in ((0, evens[chip][group]), (1, odds[chip, group])):
                    spot = group * 2 * chips + (scalars[2] ^ (2 * chip + other))
                    dense[pl.ds(pl.multiple_of(spot * part, part), part), :] = rows
    else:
        dense, refs = refs[0], refs[1:]
    (normed, queries, key_rows, values, sigma, weighting, projected, attended, mixed) = refs[:9]
    log_total, branch = refs[9:]
    place, seq_len = scalars[0], scalars[1]
    width = dense.shape[0]
    gain = raise_(dense[:, OUTPUT_EDGE:]).T[gain_column : gain_column + 1, :]
    head_table = shift_table(
        tokens.shape[1] - width, dense.shape[1] - OUTPUT_EDGE, place * SELECT_COUNT, SELECT_COUNT
    )
    for start in range(0, tokens.shape[0], block):
        span = pl.ds(start, block)
        rows = tokens[span, :width]
        scaled, _ = moments(raise_(rows))
        normed_rows = lower(scaled * gain)
        normed[span, :] = normed_rows
        both = product(normed_rows, dense[:, :QK_EDGE])
        queries[span, :] = lower(turn(both[:, :HEAD_DIM], cosine[span, :], sine[span, :], 1.0))
        key_rows[span, :] = lower(turn(both[:, HEAD_DIM:], cosine[span, :], sine[span, :], 1.0))
        chosen = product(tokens[span, width:], head_table)
        sigma_rows = jax.nn.sigmoid(product(normed_rows, dense[:, OUTPUT_EDGE:]))
        sigma[span, :] = sigma_rows
        weights = sigma_rows * chosen
        weighting[span, :] = weights
        columns = product(rows, dense[:, QK_EDGE:VALUE_EDGE])
        projected[span, :] = columns
        total = weights[:, 0:1] * columns[:, :HEAD_DIM]
        for expert in range(1, ATT_EXPERTS):
            total += (
                weights[:, expert : expert + 1]
                * columns[:, expert * HEAD_DIM : (expert + 1) * HEAD_DIM]
            )
        values[span, :] = lower(total)
    for start in range(0, tokens.shape[0], block):
        span = pl.ds(start, block)
        scores = masked_scores(queries[span, :], key_rows[...], seq_len, start)
        highest = jnp.max(scores, axis=-1, keepdims=True)
        raised = jnp.exp(scores - highest)
        row_total = jnp.sum(raised, axis=-1, keepdims=True)
        log_total[span, :] = highest + jnp.log(row_total)
        rows = product(lower(raised / row_total), values[...])
        attended[span, :] = rows
        weights = weighting[span, :]
        for expert in range(ATT_EXPERTS):
            mixed[span, pl.ds(expert * HEAD_DIM, HEAD_DIM)] = lower(
                weights[:, ATT_EXPERTS + expert : ATT_EXPERTS + expert + 1] * rows
            )
        branch[span, :] = lower(product_last(mixed[span, :], dense[:, VALUE_EDGE:OUTPUT_EDGE]))


def attention_back_kernel(block, gain_column, chips, scalars, upstream, tokens, *refs):
    if chips:
        evens, odds, terms, grads = refs[14:17] + refs[-1:]
        refs = refs[:14] + refs[17:-1]
    else:
        grads, terms = refs[14:16]
        refs = refs[:14] + refs[16:]
    (normed, queries, key_rows, values, sigma, weighting, projected, attended, mixed) = refs[:9]
    log_total, cosine, sine, dense, router_grad = refs[9:14]
    (attended_grad, weight_grad, key_grad, value_grad, query_grad) = refs[14:19]
    projected_grad, pair_grad, select_grad = refs[19:]
    seq_len = scalars[1]
    width = dense.shape[0]
    small = dense.shape[1] - OUTPUT_EDGE
    lane = lax.broadcasted_iota(jnp.int32, (block, small), 1)
    scale = HEAD_DIM ** (-0.5)
    gain = raise_(dense[:, OUTPUT_EDGE:]).T[gain_column : gain_column + 1, :]
    for start in range(0, tokens.shape[0], block):
        span = pl.ds(start, block)
        mixed_grad = product(upstream[span, :], dense[:, VALUE_EDGE:OUTPUT_EDGE])
        weights = weighting[span, :]
        heads = attended[span, :]
        total = jnp.zeros((block, HEAD_DIM), jnp.float32)
        found = jnp.zeros((block, small), jnp.float32)
        for expert in range(ATT_EXPERTS):
            piece = mixed_grad[:, expert * HEAD_DIM : (expert + 1) * HEAD_DIM]
            column = ATT_EXPERTS + expert
            total += weights[:, column : column + 1] * piece
            found = jnp.where(lane == column, jnp.sum(piece * heads, axis=1, keepdims=True), found)
        attended_grad[span, :] = lower(total)
        weight_grad[span, :] = found
    grads[:, VALUE_EDGE:OUTPUT_EDGE] = lower(product_rows(upstream[...], mixed[...]))
    for start in range(0, tokens.shape[0], block):
        span = pl.ds(start, block)
        scores = masked_scores(queries[span, :], key_rows[...], seq_len, start)
        probs = jnp.exp(scores - log_total[span, :])
        prob_grad = product_last(attended_grad[span, :], values[...])
        delta = jnp.sum(probs * prob_grad, axis=-1, keepdims=True)
        score_grad = lower(probs * (prob_grad - delta))
        query_grad[span, :] = product(score_grad, key_rows[...]) * scale
        key_terms = product_rows(score_grad, queries[span, :])
        value_terms = product_rows(lower(probs), attended_grad[span, :])
        if start:
            key_grad[...] += key_terms
            value_grad[...] += value_terms
        else:
            key_grad[...] = key_terms
            value_grad[...] = value_terms
    gain_grad = jnp.zeros((1, width), jnp.float32)
    for start in range(0, tokens.shape[0], block):
        span = pl.ds(start, block)
        rows = value_grad[span, :]
        weights = weighting[span, :]
        found = weight_grad[span, :]
        for expert in range(ATT_EXPERTS):
            piece = pl.ds(expert * HEAD_DIM, HEAD_DIM)
            projected_grad[span, piece] = lower(weights[:, expert : expert + 1] * rows)
            found = jnp.where(
                lane == expert,
                jnp.sum(rows * projected[span, piece], axis=1, keepdims=True),
                found,
            )
        pair_grad[span, :HEAD_DIM] = lower(
            turn(query_grad[span, :], cosine[span, :], sine[span, :], -1.0)
        )
        pair_grad[span, HEAD_DIM:] = lower(
            turn(key_grad[span, :] * scale, cosine[span, :], sine[span, :], -1.0)
        )
        select_rows = lower(found * weights * (1.0 - sigma[span, :]))
        select_grad[span, :] = select_rows
        normed_grad = product_last(pair_grad[span, :], dense[:, :QK_EDGE]) + product_last(
            select_rows, dense[:, OUTPUT_EDGE:]
        )
        scaled, inverse = moments(raise_(tokens[span, :width]))
        gain_grad += jnp.sum(normed_grad * scaled, axis=0, keepdims=True)
        through = normed_grad * gain
        norm_grad = inverse * (
            through
            - jnp.mean(through, axis=-1, keepdims=True)
            - scaled * jnp.mean(through * scaled, axis=-1, keepdims=True)
        )
        terms[span, :] = lower(
            product_last(projected_grad[span, :], dense[:, QK_EDGE:VALUE_EDGE]) + norm_grad
        )
    grads[:, QK_EDGE:VALUE_EDGE] = lower(product_rows(tokens[:, :width], projected_grad[...]))
    grads[:, :QK_EDGE] = lower(product_rows(normed[...], pair_grad[...]))
    row = lax.broadcasted_iota(jnp.int32, (small, width), 0)
    gain_part = jnp.where(row == gain_column, gain_grad, 0.0).T
    grads[:, OUTPUT_EDGE:] = lower(
        product_rows(normed[...], select_grad[...]) + gain_part + router_grad[...]
    )
    if chips:
        groups, part = evens.shape[1:3]
        for group in range(groups):
            for relative in range(2 * chips):
                spot = group * 2 * chips + (scalars[2] ^ relative)
                rows = grads[pl.ds(pl.multiple_of(spot * part, part), part), :]
                (odds if relative % 2 else evens)[relative // 2, group] = rows


def piece_spans(place, pieces):
    part, last = pieces[0].shape[0], len(pieces) - 2
    spans = [pl.ds(pl.multiple_of((place ^ index) * part, part), part) for index in range(last)]
    half = part // 2
    for index in range(2):
        start = pl.multiple_of((place ^ last) * part + index * half, half)
        spans.append(pl.ds(start, half))
    return spans


def expert_kernel(pieces, scalars, rows, up, router, *refs):
    weights = refs[: 2 * pieces]
    back, slope, gated = refs[2 * pieces :]
    block, width = rows.shape
    hidden = slope.shape[1] // 2
    count = hidden // EXPERT_H
    small = up.shape[1] - width
    lanes = router.shape[1]
    spans = piece_spans(scalars[0], weights[:pieces])
    offsets = [SELECT_COUNT + (scalars[1] ^ index) * count for index in range(2)]

    def column_of(entry):
        return jnp.where(entry < count, offsets[0] + entry, offsets[1] + entry - count)

    source = lax.broadcasted_iota(jnp.int32, (small, lanes), 0)
    entry = lax.broadcasted_iota(jnp.int32, (small, lanes), 1)
    pick_table = lower(jnp.where((source == column_of(entry)) & (entry < 2 * count), 1.0, 0.0))
    entry = lax.broadcasted_iota(jnp.int32, (lanes, small), 0)
    target = lax.broadcasted_iota(jnp.int32, (lanes, small), 1)
    place_table = lower(jnp.where((target == column_of(entry)) & (entry < 2 * count), 1.0, 0.0))
    lane = lax.broadcasted_iota(jnp.int32, (block, lanes), 1)
    scaled, _ = moments(raise_(rows[...]))
    sigma_gate = jax.nn.sigmoid(product(lower(scaled), router[...]))
    gates = sigma_gate * product(up[:, width:], pick_table)
    found = jnp.zeros((block, lanes), jnp.float32)
    for first in range(0, 2 * count, 2):
        own = weights[first // count * pieces : (first // count + 1) * pieces]
        local = pl.ds(first % count * EXPERT_H, 2 * EXPERT_H)
        outer = pl.ds(hidden + first % count * EXPERT_H, 2 * EXPERT_H)
        columns = pl.ds(first * EXPERT_H, 2 * EXPERT_H)
        inner = product(rows[:, spans[0]], own[0][:, local])
        terms = product(up[:, spans[0]], own[0][:, outer])
        for span, piece in zip(spans[1:], own[1:]):
            inner += product(rows[:, span], piece[:, local])
            terms += product(up[:, span], piece[:, outer])
        sigma = jax.nn.sigmoid(inner)
        active = raise_(lower(inner * sigma))
        wide = jnp.concatenate(
            [
                jnp.broadcast_to(gates[:, first + k : first + k + 1], (block, EXPERT_H))
                for k in range(2)
            ],
            axis=1,
        )
        gated[:, columns] = lower(wide * active)
        both = terms * active
        for k in range(2):
            summed = jnp.sum(both[:, k * EXPERT_H : (k + 1) * EXPERT_H], axis=1, keepdims=True)
            found = jnp.where(lane == first + k, summed, found)
        slope[:, columns] = lower(wide * terms * (sigma * (1.0 + inner * (1.0 - sigma))))
    for index, span in enumerate(spans):
        total = product_last(slope[:, :hidden], weights[index][:, :hidden])
        total += product_last(slope[:, hidden:], weights[pieces + index][:, :hidden])
        back[:, span] = lower(total)
    back[:, width:] = lower(product(lower(found * gates * (1.0 - sigma_gate)), place_table))


def expert_call(scalars, rows, up, router, weights):
    block, width = rows.shape
    hidden = weights[0].shape[1] // 2
    return wide_call(
        functools.partial(expert_kernel, len(weights) // 2),
        [scalars, rows, up, router] + weights,
        [
            jax.ShapeDtypeStruct(up.shape, jnp.bfloat16),
            jax.ShapeDtypeStruct((block, 2 * hidden), jnp.bfloat16),
            jax.ShapeDtypeStruct((block, 2 * hidden), jnp.bfloat16),
        ],
    )


def expert_grad_kernel(chips, indices, scalars, *refs):
    rows = refs[:chips]
    ups = refs[chips : 2 * chips]
    slopes = refs[2 * chips : 3 * chips]
    gateds = refs[3 * chips : 4 * chips]
    grads = refs[4 * chips]
    part = grads.shape[0] // len(indices)
    half = pl.num_programs(0) // 2

    def total(lefts, rights):
        for place, index in enumerate(indices):
            columns = pl.ds(pl.multiple_of((scalars[0] ^ index) * part, part), part)
            result = product_rows(lefts[0][:, columns], rights[0][...])
            for left, right in zip(lefts[1:], rights[1:]):
                result += product_rows(left[:, columns], right[...])
            grads[pl.ds(place * part, part), :] = lower(result)

    @pl.when(pl.program_id(0) < half)
    def _():
        total(rows, slopes)

    @pl.when(pl.program_id(0) >= half)
    def _():
        total(ups, gateds)


def expert_grads(scalars, rows, ups, slopes, gateds, side, blocks, indices):
    chips = len(slopes)
    block, width = rows[0].shape
    hidden = slopes[0].shape[1] // 2
    tile = min(512, hidden)
    half = hidden // tile
    once = pl.Buffered(buffer_count=1)
    first = side * half
    rows_out = width // blocks * len(indices)
    return pl.pallas_call(
        functools.partial(expert_grad_kernel, chips, indices),
        grid=(2 * half,),
        in_specs=[pl.BlockSpec(memory_space=pltpu.SMEM)]
        + [pl.BlockSpec(v.shape, lambda j: (0, 0), pipeline_mode=once) for v in rows + ups]
        + [pl.BlockSpec((block, tile), lambda j: (0, first + jnp.minimum(j, half - 1)))] * chips
        + [pl.BlockSpec((block, tile), lambda j: (0, first + jnp.maximum(j - half, 0)))] * chips,
        out_specs=pl.BlockSpec((rows_out, tile), lambda j: (0, j)),
        out_shape=jax.ShapeDtypeStruct((rows_out, 2 * hidden), jnp.bfloat16),
        compiler_params=pltpu.CompilerParams(vmem_limit_bytes=56 * 2**20),
        cost_estimate=LIGHT,
    )(scalars, *rows, *ups, *slopes, *gateds)


def expert_out_kernel(pieces, scalars, *refs):
    weights = refs[: 2 * pieces]
    count = (len(refs) - 2 * pieces) // 2
    gateds, results = refs[2 * pieces : 2 * pieces + count], refs[2 * pieces + count :]
    hidden = weights[0].shape[1]
    spans = piece_spans(scalars[0], weights[:pieces])
    for gated, result in zip(gateds, results):
        for index, span in enumerate(spans):
            total = product_last(gated[:, :hidden], weights[index][...])
            total += product_last(gated[:, hidden:], weights[pieces + index][...])
            result[:, span] = lower(total)


def expert_out_call(scalars, weights, gateds):
    pieces = len(weights) // 2
    columns = weights[0].shape[1]
    width = sum(weight.shape[0] for weight in weights[:pieces])
    shape = (gateds[0].shape[0], width)
    return pl.pallas_call(
        functools.partial(expert_out_kernel, pieces),
        grid=(1,),
        in_specs=[pl.BlockSpec(memory_space=pltpu.SMEM)]
        + [pl.BlockSpec((weight.shape[0], columns // 2), lambda i: (0, 1)) for weight in weights]
        + [full(gated.shape) for gated in gateds],
        out_specs=[full(shape)] * len(gateds),
        out_shape=[jax.ShapeDtypeStruct(shape, jnp.bfloat16)] * len(gateds),
        compiler_params=pltpu.CompilerParams(vmem_limit_bytes=56 * 2**20),
        cost_estimate=LIGHT,
    )(scalars, *weights, *gateds)


def hidden_back_kernel(count, scalars, *refs):
    terms = refs[:count]
    hidden, upstream, small, hidden_grad, hidden_grad_low, router_grad = refs[count:]
    width = hidden.shape[1]
    total = raise_(terms[0][...])
    for term in terms[1:]:
        total += raise_(term[...])
    logit_grad = lower(total[:, width:])
    scaled, inverse = moments(hidden[...])
    router_grad[...] = product_rows(lower(scaled), logit_grad)
    through = product_last(logit_grad, small[...])
    norm_grad = inverse * (
        through
        - jnp.mean(through, axis=-1, keepdims=True)
        - scaled * jnp.mean(through * scaled, axis=-1, keepdims=True)
    )
    result = raise_(upstream[:, :width]) + total[:, :width] + norm_grad
    hidden_grad[...] = result
    hidden_grad_low[...] = lower(result)


def expert_update_kernel(terms, *refs):
    grads = refs[: 2 * terms]
    weight, first, second, new, first_new, second_new = refs[2 * terms :]
    for half in range(2):
        for expert in range(weight.shape[0]):
            source = pl.ds(expert * EXPERT_H, EXPERT_H)
            columns = pl.ds(half * EXPERT_H, EXPERT_H)
            total = raise_(grads[half * terms][:, source])
            for grad in grads[half * terms + 1 : (half + 1) * terms]:
                total += raise_(grad[:, source])
            results = adamw_update(
                weight[expert, :, columns],
                first[expert, :, columns],
                second[expert, :, columns],
                total,
                rate_expert,
            )
            for target, result in zip((new, first_new, second_new), results):
                target[expert, :, columns] = result


def expert_update(grads, weight, first, second):
    count, rows, columns = weight.shape
    some = 2 if count % 2 == 0 else 1
    steps = count // some
    whole = pl.BlockSpec((some, rows, columns), lambda e: (e, 0, 0))
    shape = jax.ShapeDtypeStruct(weight.shape, jnp.float32)
    specs = [
        pl.BlockSpec((rows, some * EXPERT_H), lambda e, row=row, half=half: (row, half * steps + e))
        for half in range(2)
        for _, row in grads
    ]
    return pl.pallas_call(
        functools.partial(expert_update_kernel, len(grads)),
        grid=(steps,),
        in_specs=specs + [whole] * 3,
        out_specs=[whole] * 3,
        out_shape=[shape] * 3,
        compiler_params=pltpu.CompilerParams(vmem_limit_bytes=56 * 2**20),
        cost_estimate=LIGHT,
    )(*[grad for grad, _ in grads] * 2, weight, first, second)


def sum_kernel(half, scalars, *refs):
    *terms, target = refs
    more = terms.pop() if half is not None else None
    total = raise_(terms[0][...])
    for term in terms[1:]:
        total += raise_(term[...])
    if half is None:
        target[...] = lower(total)
        return
    rows = target.shape[0] // 2
    for index in range(2):
        span = slice(index * rows, (index + 1) * rows)
        part = total[span]
        target[span, :] = lower(part + raise_(more[...]) if index == half else part)


def sum_rows(scalars, terms, half=None, more=None):
    count = terms[0][0].shape[1]
    rows = more.shape[0] * 2 if more is not None else terms[0][2]
    specs = [pl.BlockSpec((rows, count), lambda i, row=term[1]: (row, 0)) for term in terms]
    inputs = [term[0] for term in terms]
    if more is not None:
        specs.append(full(more.shape))
        inputs.append(more)
    return pl.pallas_call(
        functools.partial(sum_kernel, half),
        grid=(1,),
        in_specs=[pl.BlockSpec(memory_space=pltpu.SMEM)] + specs,
        out_specs=full((rows, count)),
        out_shape=jax.ShapeDtypeStruct((rows, count), jnp.bfloat16),
        compiler_params=pltpu.CompilerParams(vmem_limit_bytes=56 * 2**20),
        cost_estimate=LIGHT,
    )(scalars, *inputs)


def dense_update_kernel(scalars, sums, *refs):
    inputs = [refs[3 * index : 3 * index + 3] for index in range(6)]
    outputs = [refs[3 * index : 3 * index + 3] for index in range(6, 12)]

    def update(index, gradient, columns, rate):
        results = adamw_update(*[ref[:, columns] for ref in inputs[index]], gradient, rate)
        for target, result in zip(outputs[index], results):
            target[:, columns] = result

    part, small = sums.shape[1], sums.shape[2] - OUTPUT_EDGE
    shared = jnp.zeros((part, small), jnp.float32)
    chosen = jnp.zeros((part, inputs[3][0].shape[1]), jnp.float32)
    for head in range(HEADS):
        for side in range(2):
            span = pl.ds((side * HEADS + head) * HEAD_DIM, HEAD_DIM)
            source = pl.ds(side * HEAD_DIM, HEAD_DIM)
            update(0, raise_(sums[head, :, source]), span, rate_query_key)
        span = pl.ds(head * VALUE_WIDTH, VALUE_WIDTH)
        update(1, raise_(sums[head, :, QK_EDGE:VALUE_EDGE]), span, rate_value)
        update(2, raise_(sums[head, :, VALUE_EDGE:OUTPUT_EDGE]), span, rate_output)
        rows = sums[head, :, OUTPUT_EDGE:]
        source = lax.broadcasted_iota(jnp.int32, (small, chosen.shape[1]), 0)
        target = lax.broadcasted_iota(jnp.int32, (small, chosen.shape[1]), 1)
        side, entry = lax.div(source, ATT_EXPERTS), lax.rem(source, ATT_EXPERTS)
        table = (target == (side * HEADS + head) * ATT_EXPERTS + entry) & (source < SELECT_COUNT)
        chosen += product(rows, lower(jnp.where(table, 1.0, 0.0)))
        shared += raise_(rows)
    every = slice(None)
    update(3, chosen, every, rate_select)
    expert_total = inputs[4][0].shape[1]
    update(4, pltpu.roll(shared, small - SELECT_COUNT, 1)[:, :expert_total], every, rate_router)
    gain_column = SELECT_COUNT + expert_total
    diagonal = lax.broadcasted_iota(jnp.int32, (part, part), 0) == lax.broadcasted_iota(
        jnp.int32, (part, part), 1
    )
    gain = jnp.where(diagonal, shared[:, gain_column : gain_column + 1], 0.0)
    update(5, jnp.sum(gain, axis=0, keepdims=True), every, rate_gain)


def expert_rows_kernel(weight, rows):
    count = weight.shape[0]
    for expert in range(count):
        rows[:, pl.ds(expert * EXPERT_H, EXPERT_H)] = lower(weight[expert, :, :EXPERT_H])
        rows[:, pl.ds((count + expert) * EXPERT_H, EXPERT_H)] = lower(weight[expert, :, EXPERT_H:])


def expert_rows_of(weight):
    count, rows, columns = weight.shape
    return pl.pallas_call(
        expert_rows_kernel,
        out_shape=jax.ShapeDtypeStruct((rows, count * columns), jnp.bfloat16),
        compiler_params=pltpu.CompilerParams(vmem_limit_bytes=56 * 2**20),
        cost_estimate=LIGHT,
    )(weight)


def front_kernel(
    scalars, cotangent, routes, qk, value, output, select, router, gain, *outs
):
    payload, upstream = outs
    rows, width = cotangent.shape
    part = qk.shape[0]
    small = upstream.shape[1] - width
    expert_total = router.shape[1]
    position = scalars[0] * rows + lax.broadcasted_iota(jnp.int32, (rows, 1), 0)
    valid = position < scalars[1]
    upstream[:, :width] = lower(jnp.where(valid, raise_(cotangent[...]), 0.0))
    lane = lax.broadcasted_iota(jnp.int32, (rows, small), 1)
    hot = jnp.zeros(lane.shape, jnp.float32)
    for column in range(routes.shape[1]):
        hot = jnp.where(lane == SELECT_COUNT + routes[:, column : column + 1], 1.0, hot)
    upstream[:, width:] = lower(hot)
    counts = jnp.sum(jnp.where(valid, hot, 0.0), axis=0, keepdims=True)
    gain_column = SELECT_COUNT + expert_total
    count_columns = -(-expert_total // part)
    row = lax.broadcasted_iota(jnp.int32, (part, small), 0)
    lane = lax.broadcasted_iota(jnp.int32, (part, small), 1)
    shared = product(lower(router[...]), shift_back(expert_total, small, SELECT_COUNT))
    diagonal = lax.broadcasted_iota(jnp.int32, (part, part), 0) == lax.broadcasted_iota(
        jnp.int32, (part, part), 1
    )
    gain_rows = jnp.sum(jnp.where(diagonal, gain[...], 0.0), axis=1, keepdims=True)
    shared = jnp.where(lane == gain_column, gain_rows, shared)
    for column in range(count_columns):
        mine = lane - SELECT_COUNT == row * count_columns + column
        found = jnp.sum(jnp.where(mine, counts, 0.0), axis=1, keepdims=True)
        shared = jnp.where(lane == gain_column + 1 + column, found, shared)
    picked = lower(select[...])
    for head in range(HEADS):
        span = pl.ds(head * HEAD_DIM, HEAD_DIM)
        payload[head, :, :HEAD_DIM] = lower(qk[:, span])
        span = pl.ds((HEADS + head) * HEAD_DIM, HEAD_DIM)
        payload[head, :, HEAD_DIM:QK_EDGE] = lower(qk[:, span])
        span = pl.ds(head * VALUE_WIDTH, VALUE_WIDTH)
        payload[head, :, QK_EDGE:VALUE_EDGE] = lower(value[:, span])
        payload[head, :, VALUE_EDGE:OUTPUT_EDGE] = lower(output[:, span])
        source = lax.broadcasted_iota(jnp.int32, (picked.shape[1], small), 0)
        target = lax.broadcasted_iota(jnp.int32, (picked.shape[1], small), 1)
        side, entry = lax.div(target, ATT_EXPERTS), lax.rem(target, ATT_EXPERTS)
        table = (source == (side * HEADS + head) * ATT_EXPERTS + entry) & (target < SELECT_COUNT)
        chosen = product(picked, lower(jnp.where(table, 1.0, 0.0)))
        payload[head, :, OUTPUT_EDGE:] = lower(shared + chosen)


def token_kernel(tokens, picks, token_rows):
    rows, width = tokens.shape
    token_rows[:, :width] = tokens[...]
    lane = lax.broadcasted_iota(jnp.int32, (rows, token_rows.shape[1] - width), 1)
    chosen = jnp.zeros(lane.shape, jnp.float32)
    for column in range(picks.shape[1]):
        side, head = column // (2 * HEADS), column // 2 % HEADS
        target = head * SELECT_COUNT + side * ATT_EXPERTS + picks[:, column : column + 1]
        chosen = jnp.where(lane == target, 1.0, chosen)
    token_rows[:, width:] = lower(chosen)


def shift_back(rows, columns, offset):
    source = lax.broadcasted_iota(jnp.int32, (rows, columns), 0)
    target = lax.broadcasted_iota(jnp.int32, (rows, columns), 1)
    return lower(jnp.where(target == source + offset, 1.0, 0.0))


def local(
    tokens,
    cotangent,
    lengths,
    picks,
    routes,
    qk_weight,
    qk_first,
    qk_second,
    value_weight,
    value_first,
    value_second,
    output_weight,
    output_first,
    output_second,
    select_weight,
    select_first,
    select_second,
    router_weight,
    router_first,
    router_second,
    gain_weight,
    gain_first,
    gain_second,
    expert_weight,
    expert_first,
    expert_second,
):
    row_count = tokens.shape[1]
    model_width = tokens.shape[2]
    group_count = lax.axis_size("dp")
    owner_count = lax.axis_size("expert")
    local_count = expert_weight.shape[0]
    expert_total = local_count * owner_count
    bucket_rows = row_count * group_count
    part = qk_weight.shape[0]
    place = lax.axis_index("dp")
    owner = lax.axis_index("expert")
    seq_len = lengths[0]
    sequence = tokens[0]
    scalars = jnp.stack(
        [place.astype(jnp.int32), seq_len.astype(jnp.int32), owner.astype(jnp.int32)]
    )
    spots = jnp.stack([place.astype(jnp.int32), owner.astype(jnp.int32)])
    low, high = jnp.bfloat16, jnp.float32

    def shaped(columns, kind, rows=bucket_rows):
        return jax.ShapeDtypeStruct((rows, columns), kind)

    gain_column = SELECT_COUNT + expert_total
    count_columns = -(-expert_total // part)
    small_used = gain_column + 1 + count_columns
    small_width = small_used + -small_used % 128
    token_width = model_width + HEADS * SELECT_COUNT + -(HEADS * SELECT_COUNT) % 128

    token_own = pl.pallas_call(
        token_kernel, out_shape=shaped(token_width, low, row_count), cost_estimate=LIGHT
    )(sequence, picks[0].reshape(row_count, -1))
    token_blocks = [token_own] + [
        swap(token_own, "dp", relative) for relative in range(1, group_count)
    ]

    payload, upstream = wide_call(
        front_kernel,
        [
            after(scalars, token_own),
            cotangent[0],
            routes[0],
            qk_weight,
            value_weight,
            output_weight,
            select_weight,
            router_weight,
            gain_weight[None],
        ],
        [
            jax.ShapeDtypeStruct((HEADS, part, OUTPUT_EDGE + small_width), low),
            shaped(model_width + small_width, low, row_count),
        ],
    )
    mine = lax.all_to_all(payload, "dp", split_axis=0, concat_axis=0, tiled=True)

    mine = after(mine, *token_blocks[1:])
    token_rows = jnp.zeros((group_count,) + token_own.shape, low)
    for relative, block in enumerate(token_blocks):
        token_rows = lax.dynamic_update_index_in_dim(token_rows, block, place ^ relative, axis=0)
    token_rows = token_rows.reshape(bucket_rows, -1)
    half = row_count // 2
    expert_own = after(expert_rows_of(expert_weight), mine)
    expert_pieces = [expert_own, swap(expert_own, "dp", 1), swap(expert_own, "dp", 2)]
    dense_blocks = gather_chips(mine)
    dense_others = swap(
        after(jnp.stack(dense_blocks), *expert_pieces[1:]), "expert", 1
    )

    upstream_late = after(upstream, *dense_blocks[1:])
    expert_up = {0: upstream}
    for relative in range(2, owner_count, 2):
        if forwarded(relative):
            expert_up[relative] = swap(expert_up[relative ^ 2], "expert", 2)
        else:
            expert_up[relative] = swap(upstream_late, "expert", relative)
    expert_up = [expert_up[relative] for relative in range(0, owner_count, 2)]

    cosine, sine = rope_tables(bucket_rows)
    if part % 16 == 0:
        chips, made = owner_count // 2, [shaped(payload.shape[2], low, model_width)]
        given = dense_blocks + [dense_others]
    else:
        dense = jnp.zeros((group_count, owner_count) + mine.shape[1:], jnp.bfloat16)
        for chip, block in enumerate(dense_blocks):
            for other, rows in enumerate((block, dense_others[chip])):
                spot = owner ^ (2 * chip + other)
                dense = lax.dynamic_update_slice_in_dim(dense, rows[:, None], spot, axis=1)
        dense = dense.reshape(model_width, -1)
        chips, made, given = 0, [], [dense]
    kept = wide_call(
        functools.partial(attention_kernel, row_count, gain_column, chips),
        [scalars, token_rows, cosine, sine] + given,
        made
        + [
            shaped(model_width, low),
            shaped(HEAD_DIM, low),
            shaped(HEAD_DIM, low),
            shaped(HEAD_DIM, low),
            shaped(small_width, high),
            shaped(small_width, high),
            shaped(VALUE_WIDTH, high),
            shaped(HEAD_DIM, high),
            shaped(VALUE_WIDTH, low),
            shaped(1, high),
            shaped(model_width, low),
        ],
    )
    if made:
        dense, kept = kept[0], kept[1:]
    saved, branch = list(kept[:10]), kept[10]
    direct = [up for chip, up in enumerate(expert_up) if chip and not forwarded(2 * chip)]
    near = [after(piece, branch, *direct[:1]) for piece in expert_pieces]
    expert_others = [swap(piece, "expert", 1) for piece in near]
    far = [
        swap(expert_pieces[1][:half], "dp", 2),
        swap(expert_pieces[2][half:], "dp", 1),
    ]
    expert_others += [swap(after(piece, branch), "expert", 1) for piece in far]
    branch = scatter_rows(branch)
    hidden = add_blocks(raise_(sequence), after(branch, expert_up[-1], *expert_others))
    small = dense[:, OUTPUT_EDGE:]
    router_local = jnp.concatenate(
        [
            lax.dynamic_slice_in_dim(
                small, SELECT_COUNT + (owner ^ other) * local_count, local_count, axis=1
            )
            for other in range(2)
        ]
        + [jnp.zeros((model_width, -2 * local_count % 128), jnp.bfloat16)],
        axis=1,
    )
    expert_counts = jnp.sum(
        small[:, gain_column + 1 : small_used]
        .reshape(group_count * owner_count, part * count_columns)[:, :expert_total]
        .astype(jnp.float32),
        axis=0,
    ).astype(jnp.int32)

    hidden_low = lower(hidden)
    expert_both = expert_pieces + far + expert_others
    expert_rows, back, slopes, gateds = [hidden_low], [], [], []
    arriving = {}
    for relative in range(2, owner_count, 2):
        if not forwarded(relative):
            arriving[relative] = swap(hidden_low, "expert", relative)
    for chip, up in enumerate(expert_up):
        if chip:
            block = after(arriving[2 * chip], slopes[-1])
            if chip % 2 == 0 and chip + 1 < len(expert_up):
                arriving[2 * chip + 2] = swap(block, "expert", 2)
            expert_rows.append(block)
        term, slope, gated = expert_call(
            spots, expert_rows[chip], up, router_local, expert_both
        )
        back.append(term)
        slopes.append(slope)
        gateds.append(gated)
    back_terms = send_expert(back)

    def side_grads(after_spots, side):
        return expert_grads(
            after_spots,
            expert_rows,
            expert_up,
            slopes,
            gateds,
            side,
            group_count,
            tuple(range(group_count)),
        )

    other_grads = side_grads(spots, 1)
    own_grads = side_grads(after(spots, other_grads), 0)
    back_terms[1:] = [after(term, own_grads) for term in back_terms[1:]]

    hidden_grad, hidden_grad_low, router_grad = wide_call(
        functools.partial(hidden_back_kernel, len(back_terms)),
        [scalars] + back_terms + [hidden, upstream, small],
        [
            shaped(model_width, high, row_count),
            shaped(model_width, low, row_count),
            shaped(small_width, high, model_width),
        ],
    )
    hidden_grad_rows = exchange_rows(dp_copies(hidden_grad_low))
    produced = expert_out_call(after(spots, hidden_grad_low), expert_both, gateds)
    moe_terms = send_expert(produced)
    other_grads = swap(after(other_grads, hidden_grad_low), "expert", 1)

    far_grad = sum_rows(
        after(spots, *produced), [(own_grads, 3, row_count), (other_grads, 3, row_count)]
    )
    upper, under = swap(far_grad[:half], "dp", 2), swap(far_grad[half:], "dp", 1)
    layer_out = hidden
    for term in moe_terms:
        layer_out = layer_out + raise_(term)
    layer_out = lower(layer_out)

    scratch = [
        pltpu.VMEM((bucket_rows, HEAD_DIM), low),
        pltpu.VMEM((bucket_rows, small_width), high),
        pltpu.VMEM((bucket_rows, HEAD_DIM), high),
        pltpu.VMEM((bucket_rows, HEAD_DIM), high),
        pltpu.VMEM((bucket_rows, HEAD_DIM), high),
        pltpu.VMEM((bucket_rows, VALUE_WIDTH), low),
        pltpu.VMEM((bucket_rows, QK_EDGE), low),
        pltpu.VMEM((bucket_rows, small_width), low),
    ]
    if chips:
        kind = jax.ShapeDtypeStruct((chips, group_count, part, dense.shape[1]), low)
        made = [kind, kind]
        scratch.append(pltpu.VMEM((model_width, dense.shape[1]), low))
    else:
        made = [shaped(dense.shape[1], low, model_width)]
    *dense_parts, input_terms = wide_call(
        functools.partial(attention_back_kernel, row_count, gain_column, chips),
        [scalars, hidden_grad_rows, token_rows] + saved + [cosine, sine, dense, router_grad],
        made + [shaped(model_width, low)],
        scratch,
    )

    if not chips:
        dense_grad = dense_parts[0].reshape(group_count, owner_count, part, -1)
        dense_parts = [
            jnp.stack(
                [
                    lax.dynamic_index_in_dim(dense_grad, owner ^ relative, 1, keepdims=False)
                    for relative in range(side, owner_count, 2)
                ]
            )
            for side in range(2)
        ]
    late = after(spots, input_terms)
    first = sum_rows(late, [(own_grads, 1), (other_grads, 1)], 0, upper)
    second = sum_rows(late, [(own_grads, 2), (other_grads, 2)], 1, under)
    dense_parts[1] = after(dense_parts[1], first, second, *moe_terms)
    dense_parts = join(dense_parts[0], swap(dense_parts[1], "expert", 1))
    first, second = swap(first, "dp", 1), swap(second, "dp", 2)
    input_grad = add_blocks(hidden_grad, scatter_rows(after(input_terms, dense_parts)))
    dense_terms = send_expert([dense_parts[chip] for chip in range(owner_count // 2)])
    dense_terms[1:] = [after(term, input_grad) for term in dense_terms[1:]]
    dense_sum = raise_(dense_terms[0])
    for term in dense_terms[1:]:
        dense_sum = dense_sum + raise_(term)
    dense_sum = lower(dense_sum)
    dense_sum = lax.all_to_all(dense_sum, "dp", split_axis=0, concat_axis=0, tiled=True)
    masters = [
        (qk_weight, qk_first, qk_second),
        (value_weight, value_first, value_second),
        (output_weight, output_first, output_second),
        (select_weight, select_first, select_second),
        (router_weight, router_first, router_second),
        (gain_weight[None], gain_first[None], gain_second[None]),
    ]
    masters = [array for group in masters for array in group]
    updated = wide_call(
        dense_update_kernel,
        [scalars, dense_sum] + masters,
        [jax.ShapeDtypeStruct(array.shape, high) for array in masters],
    )
    updated = list(updated[:15]) + [array[0] for array in updated[15:]]
    expert_results = expert_update(
        [(after(own_grads, updated[0]), 0), (other_grads, 0), (first, 0), (second, 0)],
        expert_weight,
        expert_first,
        expert_second,
    )
    return (layer_out[None], input_grad[None], *updated, *expert_results, expert_counts)


def solution(mesh):
    placed = (
        P("expert", "dp", None),
        P("expert", "dp", None),
        P("expert"),
        P("expert", "dp", None, None),
        P("expert", "dp", None),
        P(("dp", "expert"), None),
        P(("dp", "expert"), None),
        P(("dp", "expert"), None),
        P(("dp", "expert"), None),
        P(("dp", "expert"), None),
        P(("dp", "expert"), None),
        P(("dp", "expert"), None),
        P(("dp", "expert"), None),
        P(("dp", "expert"), None),
        P(("dp", "expert"), None),
        P(("dp", "expert"), None),
        P(("dp", "expert"), None),
        P(("dp", "expert"), None),
        P(("dp", "expert"), None),
        P(("dp", "expert"), None),
        P(("dp", "expert")),
        P(("dp", "expert")),
        P(("dp", "expert")),
        P("expert", "dp", None),
        P("expert", "dp", None),
        P("expert", "dp", None),
    )
    return jax.shard_map(
        local,
        mesh=mesh,
        in_specs=placed,
        out_specs=(
            P("expert", "dp", None),
            P("expert", "dp", None),
            P(("dp", "expert"), None),
            P(("dp", "expert"), None),
            P(("dp", "expert"), None),
            P(("dp", "expert"), None),
            P(("dp", "expert"), None),
            P(("dp", "expert"), None),
            P(("dp", "expert"), None),
            P(("dp", "expert"), None),
            P(("dp", "expert"), None),
            P(("dp", "expert"), None),
            P(("dp", "expert"), None),
            P(("dp", "expert"), None),
            P(("dp", "expert"), None),
            P(("dp", "expert"), None),
            P(("dp", "expert"), None),
            P(("dp", "expert")),
            P(("dp", "expert")),
            P(("dp", "expert")),
            P("expert", "dp", None),
            P("expert", "dp", None),
            P("expert", "dp", None),
            P(),
        ),
        check_vma=False,
    )
```

```python
import functools

import numpy as np
import jax
import jax.numpy as jnp
from jax import lax
from jax.experimental import pallas as pl
from jax.experimental.pallas import tpu as pltpu
from jax.sharding import PartitionSpec as P

HEADS = 4
HEAD_DIM = 128
ATT_EXPERTS = 5
EXPERT_H = 128
TOPK = 16
STEP = 10


norm_eps = 1e-05
beta_first = 0.9
beta_second = 0.95
adam_eps = 1e-08
weight_decay = 0.1
masked_score = -1e30
rope_base = 10000.0
rate_query_key = 0.04
rate_value = 0.03
rate_output = 2.0
rate_select = 0.03
rate_router = 0.015
rate_gain = 1.2
rate_expert = 0.05


def product(former, latter):
    return jnp.dot(former, latter, preferred_element_type=jnp.float32)


def product_rows(former, latter):
    return lax.dot_general(
        former, latter, (((0,), (0,)), ((), ())), preferred_element_type=jnp.float32
    )


def product_last(former, latter):
    return lax.dot_general(
        former, latter, (((1,), (1,)), ((), ())), preferred_element_type=jnp.float32
    )


def rope_tables(rows):
    half = HEAD_DIM // 2
    frequency = np.exp(-np.log(rope_base) * np.arange(half) / half)
    angles = np.arange(rows)[:, None] * frequency[None, :]
    cosine, sine = np.cos(angles), np.sin(angles)
    return (
        jnp.asarray(np.concatenate([cosine, cosine], axis=1), jnp.float32),
        jnp.asarray(np.concatenate([-sine, sine], axis=1), jnp.float32),
    )


def adamw_update(weight, first_moment, second_moment, gradient, rate):
    first_new = beta_first * first_moment + (1.0 - beta_first) * gradient
    second_new = beta_second * second_moment + (1.0 - beta_second) * gradient * gradient
    first_hat = first_new / (1.0 - beta_first**STEP)
    second_hat = second_new / (1.0 - beta_second**STEP)
    weight_new = weight - rate * (
        first_hat / (jnp.sqrt(second_hat) + adam_eps) + weight_decay * weight
    )
    return (weight_new, first_new, second_new)


LIGHT = pl.CostEstimate(flops=1000, bytes_accessed=1000, transcendentals=0)


def swap(values, axis, relative):
    count = lax.axis_size(axis)
    return lax.ppermute(values, axis, [(place, place ^ relative) for place in range(count)])


def lower(values):
    return values.astype(jnp.bfloat16)


def raise_(values):
    return values.astype(jnp.float32)


def after(values, *others):
    return lax.optimization_barrier((values,) + others)[0]


def dp_copies(values):
    return jnp.broadcast_to(values[None], (lax.axis_size("dp"),) + values.shape)


def exchange_rows(copies):
    blocks = lax.all_to_all(copies, "dp", split_axis=0, concat_axis=0, tiled=True)
    return blocks.reshape((-1,) + copies.shape[2:])


def scatter_rows(values):
    count = lax.axis_size("dp")
    blocks = values.reshape((count, values.shape[0] // count) + values.shape[1:])
    return lax.all_to_all(blocks, "dp", split_axis=0, concat_axis=0, tiled=True)


def add_blocks(values, blocks):
    for index in range(blocks.shape[0]):
        values = values + raise_(blocks[index])
    return values


def join(own, other):
    return lower(raise_(own) + raise_(other))


def forwarded(relative):
    return relative & 2 and relative > 2


def gather_chips(values):
    return [values] + [
        swap(values, "expert", relative) for relative in range(2, lax.axis_size("expert"), 2)
    ]


def send_expert(joined):
    return [joined[0]] + [
        swap(term, "expert", 2 * index) for index, term in enumerate(joined) if index
    ]


def full(shape):
    return pl.BlockSpec(shape, lambda *_: (0,) * len(shape))


def wide_call(kernel, inputs, outputs, scratch=()):
    specs = [pl.BlockSpec(memory_space=pltpu.SMEM)] + [full(value.shape) for value in inputs[1:]]
    return pl.pallas_call(
        kernel,
        grid=(1,),
        in_specs=specs,
        out_specs=[full(value.shape) for value in outputs],
        out_shape=outputs,
        scratch_shapes=list(scratch),
        compiler_params=pltpu.CompilerParams(vmem_limit_bytes=56 * 2**20),
        cost_estimate=LIGHT,
    )(*inputs)


def shift_table(rows, columns, offset, count):
    source = lax.broadcasted_iota(jnp.int32, (rows, columns), 0)
    target = lax.broadcasted_iota(jnp.int32, (rows, columns), 1)
    return lower(jnp.where((source == target + offset) & (target < count), 1.0, 0.0))


def moments(values):
    center = values - jnp.mean(values, axis=-1, keepdims=True)
    inverse = lax.rsqrt(jnp.mean(center * center, axis=-1, keepdims=True) + norm_eps)
    return center * inverse, inverse


def turn(rows, cosine, signed_sine, direction):
    return rows * cosine + direction * pltpu.roll(rows, HEAD_DIM // 2, 1) * signed_sine


def masked_scores(queries, key_rows, seq_len, start):
    scores = product_last(queries, key_rows) * HEAD_DIM ** (-0.5)
    query_place = start + lax.broadcasted_iota(jnp.int32, scores.shape, 0)
    key_place = lax.broadcasted_iota(jnp.int32, scores.shape, 1)
    return jnp.where((key_place <= query_place) & (key_place < seq_len), scores, masked_score)


VALUE_WIDTH = ATT_EXPERTS * HEAD_DIM
QK_EDGE = 2 * HEAD_DIM
VALUE_EDGE = QK_EDGE + VALUE_WIDTH
OUTPUT_EDGE = VALUE_EDGE + VALUE_WIDTH
SELECT_COUNT = 2 * ATT_EXPERTS


def attention_kernel(blocks, gain_column, chips, local_count, scalars, *refs):
    tokens, (cosine, sine), refs = refs[:blocks], refs[blocks : blocks + 2], refs[blocks + 2 :]
    block = tokens[0].shape[0]
    if chips:
        evens, odds, dense = refs[:chips], refs[chips], refs[chips + 1]
        refs = refs[chips + 2 :]
        groups, part = odds.shape[1:3]
        for group in range(groups):
            for chip in range(chips):
                for other, rows in ((0, evens[chip][group]), (1, odds[chip, group])):
                    spot = group * 2 * chips + (scalars[2] ^ (2 * chip + other))
                    dense[pl.ds(pl.multiple_of(spot * part, part), part), :] = rows
    else:
        dense, refs = refs[0], refs[1:]
    (normed, queries, key_rows, values, sigma, weighting, projected, attended, mixed) = refs[:9]
    log_total, branch, router_local, counts = refs[9:]
    place, seq_len = scalars[0], scalars[1]
    width = dense.shape[0]
    small_rows = dense[:, OUTPUT_EDGE:]
    count = local_count
    source = lax.broadcasted_iota(jnp.int32, (small_rows.shape[1], router_local.shape[1]), 0)
    entry = lax.broadcasted_iota(jnp.int32, source.shape, 1)
    first = SELECT_COUNT + scalars[2] * count + entry
    second = SELECT_COUNT + (scalars[2] ^ 1) * count + entry - count
    table = (source == jnp.where(entry < count, first, second)) & (entry < 2 * count)
    router_local[...] = lower(product(small_rows, lower(jnp.where(table, 1.0, 0.0))))
    part = counts.shape[0]
    total = raise_(small_rows[:part])
    for start in range(part, width, part):
        total += raise_(small_rows[start : start + part])
    counts[...] = total
    gain = raise_(small_rows).T[gain_column : gain_column + 1, :]
    head_table = shift_table(
        tokens[0].shape[1] - width, dense.shape[1] - OUTPUT_EDGE, place * SELECT_COUNT, SELECT_COUNT
    )
    for index in range(blocks):
        span = pl.ds(pl.multiple_of((place ^ index) * block, block), block)
        rows = tokens[index][:, :width]
        scaled, _ = moments(raise_(rows))
        normed_rows = lower(scaled * gain)
        normed[span, :] = normed_rows
        both = product(normed_rows, dense[:, :QK_EDGE])
        queries[span, :] = lower(turn(both[:, :HEAD_DIM], cosine[span, :], sine[span, :], 1.0))
        key_rows[span, :] = lower(turn(both[:, HEAD_DIM:], cosine[span, :], sine[span, :], 1.0))
        chosen = product(tokens[index][:, width:], head_table)
        sigma_rows = jax.nn.sigmoid(product(normed_rows, dense[:, OUTPUT_EDGE:]))
        sigma[span, :] = sigma_rows
        weights = sigma_rows * chosen
        weighting[span, :] = weights
        columns = product(rows, dense[:, QK_EDGE:VALUE_EDGE])
        projected[span, :] = columns
        total = weights[:, 0:1] * columns[:, :HEAD_DIM]
        for expert in range(1, ATT_EXPERTS):
            total += (
                weights[:, expert : expert + 1]
                * columns[:, expert * HEAD_DIM : (expert + 1) * HEAD_DIM]
            )
        values[span, :] = lower(total)
    for start in range(0, blocks * block, block):
        span = pl.ds(start, block)
        scores = masked_scores(queries[span, :], key_rows[...], seq_len, start)
        highest = jnp.max(scores, axis=-1, keepdims=True)
        raised = jnp.exp(scores - highest)
        row_total = jnp.sum(raised, axis=-1, keepdims=True)
        log_total[span, :] = highest + jnp.log(row_total)
        rows = product(lower(raised / row_total), values[...])
        attended[span, :] = rows
        weights = weighting[span, :]
        for expert in range(ATT_EXPERTS):
            mixed[span, pl.ds(expert * HEAD_DIM, HEAD_DIM)] = lower(
                weights[:, ATT_EXPERTS + expert : ATT_EXPERTS + expert + 1] * rows
            )
        branch[span, :] = lower(product_last(mixed[span, :], dense[:, VALUE_EDGE:OUTPUT_EDGE]))


def attention_back_kernel(blocks, gain_column, chips, scalars, upstream, *refs):
    token_blocks, refs, tokens = refs[:blocks], refs[blocks:-1], refs[-1]
    block = token_blocks[0].shape[0]
    if chips:
        evens, odds, terms, grads = refs[14:17] + refs[-1:]
        refs = refs[:14] + refs[17:-1]
    else:
        grads, terms = refs[14:16]
        refs = refs[:14] + refs[16:]
    (normed, queries, key_rows, values, sigma, weighting, projected, attended, mixed) = refs[:9]
    log_total, cosine, sine, dense, router_grad = refs[9:14]
    (attended_grad, weight_grad, key_grad, value_grad, query_grad) = refs[14:19]
    projected_grad, pair_grad, select_grad = refs[19:]
    seq_len = scalars[1]
    width = dense.shape[0]
    small = dense.shape[1] - OUTPUT_EDGE
    lane = lax.broadcasted_iota(jnp.int32, (block, small), 1)
    scale = HEAD_DIM ** (-0.5)
    gain = raise_(dense[:, OUTPUT_EDGE:]).T[gain_column : gain_column + 1, :]
    for index, rows in enumerate(token_blocks):
        span = pl.ds(pl.multiple_of((scalars[0] ^ index) * block, block), block)
        tokens[span, :] = rows[:, :width]
    for start in range(0, tokens.shape[0], block):
        span = pl.ds(start, block)
        mixed_grad = product(upstream[span, :], dense[:, VALUE_EDGE:OUTPUT_EDGE])
        weights = weighting[span, :]
        heads = attended[span, :]
        total = jnp.zeros((block, HEAD_DIM), jnp.float32)
        found = jnp.zeros((block, small), jnp.float32)
        for expert in range(ATT_EXPERTS):
            piece = mixed_grad[:, expert * HEAD_DIM : (expert + 1) * HEAD_DIM]
            column = ATT_EXPERTS + expert
            total += weights[:, column : column + 1] * piece
            found = jnp.where(lane == column, jnp.sum(piece * heads, axis=1, keepdims=True), found)
        attended_grad[span, :] = lower(total)
        weight_grad[span, :] = found
    grads[:, VALUE_EDGE:OUTPUT_EDGE] = lower(product_rows(upstream[...], mixed[...]))
    for start in range(0, tokens.shape[0], block):
        span = pl.ds(start, block)
        scores = masked_scores(queries[span, :], key_rows[...], seq_len, start)
        probs = jnp.exp(scores - log_total[span, :])
        prob_grad = product_last(attended_grad[span, :], values[...])
        delta = jnp.sum(probs * prob_grad, axis=-1, keepdims=True)
        score_grad = lower(probs * (prob_grad - delta))
        query_grad[span, :] = product(score_grad, key_rows[...]) * scale
        key_terms = product_rows(score_grad, queries[span, :])
        value_terms = product_rows(lower(probs), attended_grad[span, :])
        if start:
            key_grad[...] += key_terms
            value_grad[...] += value_terms
        else:
            key_grad[...] = key_terms
            value_grad[...] = value_terms
    gain_grad = jnp.zeros((1, width), jnp.float32)
    for start in range(0, tokens.shape[0], block):
        span = pl.ds(start, block)
        rows = value_grad[span, :]
        weights = weighting[span, :]
        found = weight_grad[span, :]
        for expert in range(ATT_EXPERTS):
            piece = pl.ds(expert * HEAD_DIM, HEAD_DIM)
            projected_grad[span, piece] = lower(weights[:, expert : expert + 1] * rows)
            found = jnp.where(
                lane == expert,
                jnp.sum(rows * projected[span, piece], axis=1, keepdims=True),
                found,
            )
        pair_grad[span, :HEAD_DIM] = lower(
            turn(query_grad[span, :], cosine[span, :], sine[span, :], -1.0)
        )
        pair_grad[span, HEAD_DIM:] = lower(
            turn(key_grad[span, :] * scale, cosine[span, :], sine[span, :], -1.0)
        )
        select_rows = lower(found * weights * (1.0 - sigma[span, :]))
        select_grad[span, :] = select_rows
        normed_grad = product_last(pair_grad[span, :], dense[:, :QK_EDGE]) + product_last(
            select_rows, dense[:, OUTPUT_EDGE:]
        )
        scaled, inverse = moments(raise_(tokens[span, :]))
        gain_grad += jnp.sum(normed_grad * scaled, axis=0, keepdims=True)
        through = normed_grad * gain
        norm_grad = inverse * (
            through
            - jnp.mean(through, axis=-1, keepdims=True)
            - scaled * jnp.mean(through * scaled, axis=-1, keepdims=True)
        )
        terms[span, :] = lower(
            product_last(projected_grad[span, :], dense[:, QK_EDGE:VALUE_EDGE]) + norm_grad
        )
    grads[:, QK_EDGE:VALUE_EDGE] = lower(product_rows(tokens[...], projected_grad[...]))
    grads[:, :QK_EDGE] = lower(product_rows(normed[...], pair_grad[...]))
    row = lax.broadcasted_iota(jnp.int32, (small, width), 0)
    gain_part = jnp.where(row == gain_column, gain_grad, 0.0).T
    grads[:, OUTPUT_EDGE:] = lower(
        product_rows(normed[...], select_grad[...]) + gain_part + router_grad[...]
    )
    if chips:
        groups, part = evens.shape[1:3]
        for group in range(groups):
            for relative in range(2 * chips):
                spot = group * 2 * chips + (scalars[2] ^ relative)
                rows = grads[pl.ds(pl.multiple_of(spot * part, part), part), :]
                (odds if relative % 2 else evens)[relative // 2, group] = rows


def piece_spans(place, pieces):
    part, last = pieces[0].shape[0], len(pieces) - 2
    spans = [pl.ds(pl.multiple_of((place ^ index) * part, part), part) for index in range(last)]
    half = part // 2
    for index in range(2):
        start = pl.multiple_of((place ^ last) * part + index * half, half)
        spans.append(pl.ds(start, half))
    return spans


def piece_copies(place, pieces, target, columns, sems):
    part, last = pieces[0].shape[0], len(pieces) - 2
    half = part // 2
    copies = []
    for index, piece in enumerate(pieces):
        start = (place ^ min(index, last)) * part + (half if index > last else 0)
        rows = pl.ds(pl.multiple_of(start, half), piece.shape[0])
        source = piece.at[:, columns]
        copies.append(pltpu.make_async_copy(source, target.at[rows, :], sems.at[index]))
    return copies


def expert_kernel(pieces, scalars, rows, up, router, *refs):
    weights = refs[: 2 * pieces]
    back, slope, gated, insides, outsides, sems = refs[2 * pieces :]
    block, width = rows.shape
    hidden = slope.shape[1] // 2
    count = hidden // EXPERT_H
    copies = []
    for side in range(2):
        own = weights[side * pieces : (side + 1) * pieces]
        copies.append(
            piece_copies(scalars[0], own, insides.at[side], pl.ds(0, hidden), sems.at[side, 0])
            + piece_copies(
                scalars[0], own, outsides.at[side], pl.ds(hidden, hidden), sems.at[side, 1]
            )
        )
        for copy in copies[side]:
            copy.start()
    small = up.shape[1] - width
    lanes = router.shape[1]
    offsets = [SELECT_COUNT + (scalars[1] ^ index) * count for index in range(2)]

    def column_of(entry):
        return jnp.where(entry < count, offsets[0] + entry, offsets[1] + entry - count)

    source = lax.broadcasted_iota(jnp.int32, (small, lanes), 0)
    entry = lax.broadcasted_iota(jnp.int32, (small, lanes), 1)
    pick_table = lower(jnp.where((source == column_of(entry)) & (entry < 2 * count), 1.0, 0.0))
    entry = lax.broadcasted_iota(jnp.int32, (lanes, small), 0)
    target = lax.broadcasted_iota(jnp.int32, (lanes, small), 1)
    place_table = lower(jnp.where((target == column_of(entry)) & (entry < 2 * count), 1.0, 0.0))
    lane = lax.broadcasted_iota(jnp.int32, (block, lanes), 1)
    scaled, _ = moments(raise_(rows[...]))
    sigma_gate = jax.nn.sigmoid(product(lower(scaled), router[...]))
    gates = sigma_gate * product(up[:, width:], pick_table)
    found = jnp.zeros((block, lanes), jnp.float32)
    for first in range(0, 2 * count, 2):
        side = first // count
        if first % count == 0:
            for copy in copies[side]:
                copy.wait()
        local = pl.ds(first % count * EXPERT_H, 2 * EXPERT_H)
        inner = product(rows[...], insides[side, :, local])
        terms = product(up[:, :width], outsides[side, :, local])
        sigma = jax.nn.sigmoid(inner)
        silu = inner * sigma
        active = raise_(lower(silu))
        both = terms * active
        tilt = sigma + silu * (1.0 - sigma)
        for k in range(2):
            part = slice(k * EXPERT_H, (k + 1) * EXPERT_H)
            columns = pl.ds((first + k) * EXPERT_H, EXPERT_H)
            gate = gates[:, first + k : first + k + 1]
            gated[:, columns] = lower(gate * active[:, part])
            slope[:, columns] = lower(gate * terms[:, part] * tilt[:, part])
            summed = jnp.sum(both[:, part], axis=1, keepdims=True)
            found = jnp.where(lane == first + k, summed, found)
    back[:, :width] = lower(
        product_last(slope[:, :hidden], insides[0]) + product_last(slope[:, hidden:], insides[1])
    )
    back[:, width:] = lower(product(lower(found * gates * (1.0 - sigma_gate)), place_table))


def expert_call(scalars, rows, up, router, weights):
    block, width = rows.shape
    hidden = weights[0].shape[1] // 2
    pieces = len(weights) // 2
    outputs = [
        jax.ShapeDtypeStruct(up.shape, jnp.bfloat16),
        jax.ShapeDtypeStruct((block, 2 * hidden), jnp.bfloat16),
        jax.ShapeDtypeStruct((block, 2 * hidden), jnp.bfloat16),
    ]
    return pl.pallas_call(
        functools.partial(expert_kernel, pieces),
        grid=(1,),
        in_specs=[pl.BlockSpec(memory_space=pltpu.SMEM)]
        + [full(value.shape) for value in (rows, up, router)]
        + [pl.BlockSpec(memory_space=pl.ANY)] * len(weights),
        out_specs=[full(value.shape) for value in outputs],
        out_shape=outputs,
        scratch_shapes=[
            pltpu.VMEM((2, width, hidden), jnp.bfloat16),
            pltpu.VMEM((2, width, hidden), jnp.bfloat16),
            pltpu.SemaphoreType.DMA((2, 2, pieces)),
        ],
        compiler_params=pltpu.CompilerParams(vmem_limit_bytes=56 * 2**20),
        cost_estimate=LIGHT,
    )(scalars, rows, up, router, *weights)


def expert_grad_kernel(chips, indices, scalars, *refs):
    rows = refs[:chips]
    ups = refs[chips : 2 * chips]
    slopes = refs[2 * chips : 3 * chips]
    gateds = refs[3 * chips : 4 * chips]
    grads = refs[4 * chips]
    part = grads.shape[0] // len(indices)
    half = pl.num_programs(0) // 2

    def total(lefts, rights):
        for place, index in enumerate(indices):
            columns = pl.ds(pl.multiple_of((scalars[0] ^ index) * part, part), part)
            result = product_rows(lefts[0][:, columns], rights[0][...])
            for left, right in zip(lefts[1:], rights[1:]):
                result += product_rows(left[:, columns], right[...])
            grads[pl.ds(place * part, part), :] = lower(result)

    @pl.when(pl.program_id(0) < half)
    def _():
        total(rows, slopes)

    @pl.when(pl.program_id(0) >= half)
    def _():
        total(ups, gateds)


def expert_grads(scalars, rows, ups, slopes, gateds, side, blocks, indices):
    chips = len(slopes)
    block, width = rows[0].shape
    hidden = slopes[0].shape[1] // 2
    tile = min(512, hidden)
    half = hidden // tile
    once = pl.Buffered(buffer_count=1)
    first = side * half
    rows_out = width // blocks * len(indices)
    return pl.pallas_call(
        functools.partial(expert_grad_kernel, chips, indices),
        grid=(2 * half,),
        in_specs=[pl.BlockSpec(memory_space=pltpu.SMEM)]
        + [pl.BlockSpec(v.shape, lambda j: (0, 0), pipeline_mode=once) for v in rows + ups]
        + [pl.BlockSpec((block, tile), lambda j: (0, first + jnp.minimum(j, half - 1)))] * chips
        + [pl.BlockSpec((block, tile), lambda j: (0, first + jnp.maximum(j - half, 0)))] * chips,
        out_specs=pl.BlockSpec((rows_out, tile), lambda j: (0, j)),
        out_shape=jax.ShapeDtypeStruct((rows_out, 2 * hidden), jnp.bfloat16),
        compiler_params=pltpu.CompilerParams(vmem_limit_bytes=56 * 2**20),
        cost_estimate=LIGHT,
    )(scalars, *rows, *ups, *slopes, *gateds)


def expert_out_kernel(pieces, scalars, *refs):
    weights = refs[: 2 * pieces]
    count = (len(refs) - 2 * pieces) // 2
    gateds, results = refs[2 * pieces : 2 * pieces + count], refs[2 * pieces + count :]
    hidden = weights[0].shape[1]
    spans = piece_spans(scalars[0], weights[:pieces])
    for gated, result in zip(gateds, results):
        for index, span in enumerate(spans):
            total = product_last(gated[:, :hidden], weights[index][...])
            total += product_last(gated[:, hidden:], weights[pieces + index][...])
            result[:, span] = lower(total)


def expert_out_call(scalars, weights, gateds):
    pieces = len(weights) // 2
    columns = weights[0].shape[1]
    width = sum(weight.shape[0] for weight in weights[:pieces])
    shape = (gateds[0].shape[0], width)
    return pl.pallas_call(
        functools.partial(expert_out_kernel, pieces),
        grid=(1,),
        in_specs=[pl.BlockSpec(memory_space=pltpu.SMEM)]
        + [pl.BlockSpec((weight.shape[0], columns // 2), lambda i: (0, 1)) for weight in weights]
        + [full(gated.shape) for gated in gateds],
        out_specs=[full(shape)] * len(gateds),
        out_shape=[jax.ShapeDtypeStruct(shape, jnp.bfloat16)] * len(gateds),
        compiler_params=pltpu.CompilerParams(vmem_limit_bytes=56 * 2**20),
        cost_estimate=LIGHT,
    )(scalars, *weights, *gateds)


def hidden_back_kernel(count, scalars, *refs):
    terms = refs[:count]
    hidden, upstream, small, hidden_grad, hidden_grad_low, router_grad = refs[count:]
    width = hidden.shape[1]
    total = raise_(terms[0][...])
    for term in terms[1:]:
        total += raise_(term[...])
    logit_grad = lower(total[:, width:])
    scaled, inverse = moments(hidden[...])
    router_grad[...] = product_rows(lower(scaled), logit_grad)
    through = product_last(logit_grad, small[...])
    norm_grad = inverse * (
        through
        - jnp.mean(through, axis=-1, keepdims=True)
        - scaled * jnp.mean(through * scaled, axis=-1, keepdims=True)
    )
    result = raise_(upstream[:, :width]) + total[:, :width] + norm_grad
    hidden_grad[...] = result
    hidden_grad_low[...] = lower(result)


def expert_update_kernel(terms, *refs):
    grads = refs[: 2 * terms]
    weight, first, second, new, first_new, second_new = refs[2 * terms :]
    for half in range(2):
        for expert in range(weight.shape[0]):
            source = pl.ds(expert * EXPERT_H, EXPERT_H)
            columns = pl.ds(half * EXPERT_H, EXPERT_H)
            total = raise_(grads[half * terms][:, source])
            for grad in grads[half * terms + 1 : (half + 1) * terms]:
                total += raise_(grad[:, source])
            results = adamw_update(
                weight[expert, :, columns],
                first[expert, :, columns],
                second[expert, :, columns],
                total,
                rate_expert,
            )
            for target, result in zip((new, first_new, second_new), results):
                target[expert, :, columns] = result


def expert_update(grads, weight, first, second):
    count, rows, columns = weight.shape
    some = 2 if count % 2 == 0 else 1
    steps = count // some
    whole = pl.BlockSpec((some, rows, columns), lambda e: (e, 0, 0))
    shape = jax.ShapeDtypeStruct(weight.shape, jnp.float32)
    specs = [
        pl.BlockSpec(
            (rows, some * EXPERT_H), lambda e, start=half * steps * both: (0, start + e)
        )
        for half in range(2)
        for _, both in grads[half]
    ]
    return pl.pallas_call(
        functools.partial(expert_update_kernel, len(grads[0])),
        grid=(steps,),
        in_specs=specs + [whole] * 3,
        out_specs=[whole] * 3,
        out_shape=[shape] * 3,
        compiler_params=pltpu.CompilerParams(vmem_limit_bytes=56 * 2**20),
        cost_estimate=LIGHT,
    )(*[grad for half in grads for grad, _ in half], weight, first, second)


def halving_kernel(scalars, own, other, across, along):
    rows = across.shape[0] // 2
    columns = across.shape[1]
    for side, target in enumerate((across, along)):
        span = pl.ds(side * columns, columns)
        for index, source in enumerate((side + 1, 3)):
            block = pl.ds(source * rows, rows)
            total = raise_(own[block, span]) + raise_(other[block, span])
            target[pl.ds(index * rows, rows), :] = lower(total)


def halved_kernel(scalars, own_two, other_two, own_one, other_one, across, along, first, second):
    first[...] = lower(raise_(own_two[...]) + raise_(other_two[...]) + raise_(across[...]))
    second[...] = lower(raise_(own_one[...]) + raise_(other_one[...]) + raise_(along[...]))


def halved(scalars, own, other, across, along):
    rows, columns = across.shape[0] // 2, across.shape[1]

    def block(row, column):
        return pl.BlockSpec((rows, columns), lambda i: (row, column))

    return pl.pallas_call(
        halved_kernel,
        grid=(1,),
        in_specs=[pl.BlockSpec(memory_space=pltpu.SMEM)]
        + [block(2, 0), block(2, 0), block(1, 1), block(1, 1), block(1, 0), block(1, 0)],
        out_specs=[block(0, 0)] * 2,
        out_shape=[jax.ShapeDtypeStruct((rows, columns), jnp.bfloat16)] * 2,
        compiler_params=pltpu.CompilerParams(vmem_limit_bytes=56 * 2**20),
        cost_estimate=LIGHT,
    )(scalars, own, other, own, other, across, along)


def dense_update_kernel(scalars, sums, *refs):
    inputs = [refs[3 * index : 3 * index + 3] for index in range(6)]
    outputs = [refs[3 * index : 3 * index + 3] for index in range(6, 12)]

    def update(index, gradient, columns, rate):
        results = adamw_update(*[ref[:, columns] for ref in inputs[index]], gradient, rate)
        for target, result in zip(outputs[index], results):
            target[:, columns] = result

    part, small = sums.shape[1], sums.shape[2] - OUTPUT_EDGE
    shared = jnp.zeros((part, small), jnp.float32)
    chosen = jnp.zeros((part, inputs[3][0].shape[1]), jnp.float32)
    for head in range(HEADS):
        for side in range(2):
            span = pl.ds((side * HEADS + head) * HEAD_DIM, HEAD_DIM)
            source = pl.ds(side * HEAD_DIM, HEAD_DIM)
            update(0, raise_(sums[head, :, source]), span, rate_query_key)
        span = pl.ds(head * VALUE_WIDTH, VALUE_WIDTH)
        update(1, raise_(sums[head, :, QK_EDGE:VALUE_EDGE]), span, rate_value)
        update(2, raise_(sums[head, :, VALUE_EDGE:OUTPUT_EDGE]), span, rate_output)
        rows = sums[head, :, OUTPUT_EDGE:]
        source = lax.broadcasted_iota(jnp.int32, (small, chosen.shape[1]), 0)
        target = lax.broadcasted_iota(jnp.int32, (small, chosen.shape[1]), 1)
        side, entry = lax.div(source, ATT_EXPERTS), lax.rem(source, ATT_EXPERTS)
        table = (target == (side * HEADS + head) * ATT_EXPERTS + entry) & (source < SELECT_COUNT)
        chosen += product(rows, lower(jnp.where(table, 1.0, 0.0)))
        shared += raise_(rows)
    every = slice(None)
    update(3, chosen, every, rate_select)
    expert_total = inputs[4][0].shape[1]
    update(4, pltpu.roll(shared, small - SELECT_COUNT, 1)[:, :expert_total], every, rate_router)
    gain_column = SELECT_COUNT + expert_total
    diagonal = lax.broadcasted_iota(jnp.int32, (part, part), 0) == lax.broadcasted_iota(
        jnp.int32, (part, part), 1
    )
    gain = jnp.where(diagonal, shared[:, gain_column : gain_column + 1], 0.0)
    update(5, jnp.sum(gain, axis=0, keepdims=True), every, rate_gain)


def expert_rows_kernel(weight, rows):
    count = weight.shape[0]
    for expert in range(count):
        rows[:, pl.ds(expert * EXPERT_H, EXPERT_H)] = lower(weight[expert, :, :EXPERT_H])
        rows[:, pl.ds((count + expert) * EXPERT_H, EXPERT_H)] = lower(weight[expert, :, EXPERT_H:])


def expert_rows_of(weight):
    count, rows, columns = weight.shape
    return pl.pallas_call(
        expert_rows_kernel,
        out_shape=jax.ShapeDtypeStruct((rows, count * columns), jnp.bfloat16),
        compiler_params=pltpu.CompilerParams(vmem_limit_bytes=56 * 2**20),
        cost_estimate=LIGHT,
    )(weight)


def front_kernel(scalars, tokens, picks, cotangent, routes, token_rows, upstream):
    rows, width = tokens.shape
    token_rows[:, :width] = tokens[...]
    lane = lax.broadcasted_iota(jnp.int32, (rows, token_rows.shape[1] - width), 1)
    chosen = jnp.zeros(lane.shape, jnp.float32)
    for column in range(picks.shape[1]):
        side, head = column // (2 * HEADS), column // 2 % HEADS
        target = head * SELECT_COUNT + side * ATT_EXPERTS + picks[:, column : column + 1]
        chosen = jnp.where(lane == target, 1.0, chosen)
    token_rows[:, width:] = lower(chosen)
    position = scalars[0] * rows + lax.broadcasted_iota(jnp.int32, (rows, 1), 0)
    upstream[:, :width] = lower(jnp.where(position < scalars[1], raise_(cotangent[...]), 0.0))
    lane = lax.broadcasted_iota(jnp.int32, (rows, upstream.shape[1] - width), 1)
    hot = jnp.zeros(lane.shape, jnp.float32)
    for column in range(routes.shape[1]):
        hot = jnp.where(lane == SELECT_COUNT + routes[:, column : column + 1], 1.0, hot)
    upstream[:, width:] = lower(hot)


def payload_kernel(scalars, upstream, qk, value, output, select, router, gain, payload):
    part = qk.shape[0]
    small = payload.shape[2] - OUTPUT_EDGE
    rows, width = upstream.shape[0], upstream.shape[1] - small
    expert_total = router.shape[1]
    position = scalars[0] * rows + lax.broadcasted_iota(jnp.int32, (rows, 1), 0)
    valid = position < scalars[1]
    hot = raise_(upstream[:, width:])
    counts = jnp.sum(jnp.where(valid, hot, 0.0), axis=0, keepdims=True)
    gain_column = SELECT_COUNT + expert_total
    count_columns = -(-expert_total // part)
    row = lax.broadcasted_iota(jnp.int32, (part, small), 0)
    lane = lax.broadcasted_iota(jnp.int32, (part, small), 1)
    shared = product(lower(router[...]), shift_back(expert_total, small, SELECT_COUNT))
    diagonal = lax.broadcasted_iota(jnp.int32, (part, part), 0) == lax.broadcasted_iota(
        jnp.int32, (part, part), 1
    )
    gain_rows = jnp.sum(jnp.where(diagonal, gain[...], 0.0), axis=1, keepdims=True)
    shared = jnp.where(lane == gain_column, gain_rows, shared)
    for column in range(count_columns):
        mine = lane - SELECT_COUNT == row * count_columns + column
        found = jnp.sum(jnp.where(mine, counts, 0.0), axis=1, keepdims=True)
        shared = jnp.where(lane == gain_column + 1 + column, found, shared)
    picked = lower(select[...])
    for head in range(HEADS):
        span = pl.ds(head * HEAD_DIM, HEAD_DIM)
        payload[head, :, :HEAD_DIM] = lower(qk[:, span])
        span = pl.ds((HEADS + head) * HEAD_DIM, HEAD_DIM)
        payload[head, :, HEAD_DIM:QK_EDGE] = lower(qk[:, span])
        span = pl.ds(head * VALUE_WIDTH, VALUE_WIDTH)
        payload[head, :, QK_EDGE:VALUE_EDGE] = lower(value[:, span])
        payload[head, :, VALUE_EDGE:OUTPUT_EDGE] = lower(output[:, span])
        source = lax.broadcasted_iota(jnp.int32, (picked.shape[1], small), 0)
        target = lax.broadcasted_iota(jnp.int32, (picked.shape[1], small), 1)
        side, entry = lax.div(target, ATT_EXPERTS), lax.rem(target, ATT_EXPERTS)
        table = (source == (side * HEADS + head) * ATT_EXPERTS + entry) & (target < SELECT_COUNT)
        chosen = product(picked, lower(jnp.where(table, 1.0, 0.0)))
        payload[head, :, OUTPUT_EDGE:] = lower(shared + chosen)


def shift_back(rows, columns, offset):
    source = lax.broadcasted_iota(jnp.int32, (rows, columns), 0)
    target = lax.broadcasted_iota(jnp.int32, (rows, columns), 1)
    return lower(jnp.where(target == source + offset, 1.0, 0.0))


def local(
    tokens,
    cotangent,
    lengths,
    picks,
    routes,
    qk_weight,
    qk_first,
    qk_second,
    value_weight,
    value_first,
    value_second,
    output_weight,
    output_first,
    output_second,
    select_weight,
    select_first,
    select_second,
    router_weight,
    router_first,
    router_second,
    gain_weight,
    gain_first,
    gain_second,
    expert_weight,
    expert_first,
    expert_second,
):
    row_count = tokens.shape[1]
    model_width = tokens.shape[2]
    group_count = lax.axis_size("dp")
    owner_count = lax.axis_size("expert")
    local_count = expert_weight.shape[0]
    expert_total = local_count * owner_count
    bucket_rows = row_count * group_count
    part = qk_weight.shape[0]
    place = lax.axis_index("dp")
    owner = lax.axis_index("expert")
    seq_len = lengths[0]
    sequence = tokens[0]
    scalars = jnp.stack(
        [place.astype(jnp.int32), seq_len.astype(jnp.int32), owner.astype(jnp.int32)]
    )
    spots = jnp.stack([place.astype(jnp.int32), owner.astype(jnp.int32)])
    low, high = jnp.bfloat16, jnp.float32

    def shaped(columns, kind, rows=bucket_rows):
        return jax.ShapeDtypeStruct((rows, columns), kind)

    gain_column = SELECT_COUNT + expert_total
    count_columns = -(-expert_total // part)
    small_used = gain_column + 1 + count_columns
    small_width = small_used + -small_used % 128
    token_width = model_width + HEADS * SELECT_COUNT + -(HEADS * SELECT_COUNT) % 128

    token_own, upstream = wide_call(
        front_kernel,
        [scalars, sequence, picks[0].reshape(row_count, -1), cotangent[0], routes[0]],
        [
            shaped(token_width, low, row_count),
            shaped(model_width + small_width, low, row_count),
        ],
    )
    expert_up = {0: upstream}
    for relative in range(2, owner_count, 2):
        if not forwarded(relative):
            expert_up[relative] = swap(upstream, "expert", relative)
    token_blocks = [token_own] + [
        swap(token_own, "dp", relative) for relative in range(1, group_count)
    ]

    (payload,) = wide_call(
        payload_kernel,
        [
            scalars,
            upstream,
            qk_weight,
            value_weight,
            output_weight,
            select_weight,
            router_weight,
            gain_weight[None],
        ],
        [jax.ShapeDtypeStruct((HEADS, part, OUTPUT_EDGE + small_width), low)],
    )
    mine = lax.all_to_all(payload, "dp", split_axis=0, concat_axis=0, tiled=True)
    mine = after(
        mine, *token_blocks[1:], *[up for relative, up in expert_up.items() if relative]
    )

    half = row_count // 2
    expert_own = after(expert_rows_of(expert_weight), mine)
    expert_pieces = [expert_own, swap(expert_own, "dp", 1), swap(expert_own, "dp", 2)]
    dense_blocks = gather_chips(mine)
    dense_others = swap(
        after(jnp.stack(dense_blocks), *expert_pieces[1:]), "expert", 1
    )

    cosine, sine = rope_tables(bucket_rows)
    if part % 16 == 0:
        chips, made = owner_count // 2, [shaped(payload.shape[2], low, model_width)]
        given = dense_blocks + [dense_others]
    else:
        dense = jnp.zeros((group_count, owner_count) + mine.shape[1:], jnp.bfloat16)
        for chip, block in enumerate(dense_blocks):
            for other, rows in enumerate((block, dense_others[chip])):
                spot = owner ^ (2 * chip + other)
                dense = lax.dynamic_update_slice_in_dim(dense, rows[:, None], spot, axis=1)
        dense = dense.reshape(model_width, -1)
        chips, made, given = 0, [], [dense]
    kept = wide_call(
        functools.partial(attention_kernel, group_count, gain_column, chips, local_count),
        [scalars] + token_blocks + [cosine, sine] + given,
        made
        + [
            shaped(model_width, low),
            shaped(HEAD_DIM, low),
            shaped(HEAD_DIM, low),
            shaped(HEAD_DIM, low),
            shaped(small_width, high),
            shaped(small_width, high),
            shaped(VALUE_WIDTH, high),
            shaped(HEAD_DIM, high),
            shaped(VALUE_WIDTH, low),
            shaped(1, high),
            shaped(model_width, low),
            shaped(2 * local_count + -2 * local_count % 128, low, model_width),
            shaped(small_width, high, part),
        ],
    )
    if made:
        dense, kept = kept[0], kept[1:]
    saved, (branch, router_local, counts) = list(kept[:10]), kept[10:]
    for relative in range(2, owner_count, 2):
        if forwarded(relative):
            block = after(expert_up[relative ^ 2], branch)
            expert_up[relative] = swap(block, "expert", 2)
    expert_up = [expert_up[relative] for relative in range(0, owner_count, 2)]
    near = [after(piece, branch) for piece in expert_pieces]
    expert_others = [swap(piece, "expert", 1) for piece in near]
    far = [
        swap(expert_pieces[1][:half], "dp", 2),
        swap(expert_pieces[2][half:], "dp", 1),
    ]
    expert_others += [swap(after(piece, branch), "expert", 1) for piece in far]
    branch = scatter_rows(branch)
    hidden = add_blocks(raise_(sequence), after(branch, expert_up[-1], *expert_others))
    small = dense[:, OUTPUT_EDGE:]
    expert_counts = counts[:, gain_column + 1 : small_used].reshape(-1)[:expert_total]
    expert_counts = expert_counts.astype(jnp.int32)

    hidden_low = lower(hidden)
    expert_both = expert_pieces + far + expert_others
    expert_rows, back, slopes, gateds = [hidden_low], [], [], []
    arriving = {}
    for relative in range(2, owner_count, 2):
        if not forwarded(relative):
            arriving[relative] = swap(hidden_low, "expert", relative)
    for chip, up in enumerate(expert_up):
        if chip:
            block = after(arriving[2 * chip], slopes[-1])
            if chip % 2 == 0 and chip + 1 < len(expert_up):
                arriving[2 * chip + 2] = swap(block, "expert", 2)
            expert_rows.append(block)
        term, slope, gated = expert_call(
            spots, expert_rows[chip], up, router_local, expert_both
        )
        back.append(term)
        slopes.append(slope)
        gateds.append(gated)
    back_terms = send_expert(back)

    def side_grads(after_spots, side):
        return expert_grads(
            after_spots,
            expert_rows,
            expert_up,
            slopes,
            gateds,
            side,
            group_count,
            tuple(range(group_count)),
        )

    other_grads = side_grads(spots, 1)
    own_grads = side_grads(after(spots, other_grads), 0)
    back_terms[1:] = [after(term, own_grads) for term in back_terms[1:]]

    hidden_grad, hidden_grad_low, router_grad = wide_call(
        functools.partial(hidden_back_kernel, len(back_terms)),
        [scalars] + back_terms + [hidden, upstream, small],
        [
            shaped(model_width, high, row_count),
            shaped(model_width, low, row_count),
            shaped(small_width, high, model_width),
        ],
    )
    hidden_grad_rows = exchange_rows(dp_copies(hidden_grad_low))
    produced = expert_out_call(after(spots, hidden_grad_low), expert_both, gateds)
    moe_terms = send_expert(produced)
    other_grads = swap(after(other_grads, hidden_grad_low), "expert", 1)

    columns = own_grads.shape[1] // 2
    across, along = wide_call(
        halving_kernel,
        [after(spots, *produced), own_grads, other_grads],
        [shaped(columns, low, 2 * row_count)] * 2,
    )
    across, along = swap(across, "dp", 1), swap(along, "dp", 2)
    layer_out = hidden
    for term in moe_terms:
        layer_out = layer_out + raise_(term)
    layer_out = lower(layer_out)

    scratch = [
        pltpu.VMEM((bucket_rows, HEAD_DIM), low),
        pltpu.VMEM((bucket_rows, small_width), high),
        pltpu.VMEM((bucket_rows, HEAD_DIM), high),
        pltpu.VMEM((bucket_rows, HEAD_DIM), high),
        pltpu.VMEM((bucket_rows, HEAD_DIM), high),
        pltpu.VMEM((bucket_rows, VALUE_WIDTH), low),
        pltpu.VMEM((bucket_rows, QK_EDGE), low),
        pltpu.VMEM((bucket_rows, small_width), low),
    ]
    if chips:
        kind = jax.ShapeDtypeStruct((chips, group_count, part, dense.shape[1]), low)
        made = [kind, kind]
        scratch.append(pltpu.VMEM((model_width, dense.shape[1]), low))
    else:
        made = [shaped(dense.shape[1], low, model_width)]
    *dense_parts, input_terms = wide_call(
        functools.partial(attention_back_kernel, group_count, gain_column, chips),
        [scalars, hidden_grad_rows] + token_blocks + saved + [cosine, sine, dense, router_grad],
        made + [shaped(model_width, low)],
        scratch + [pltpu.VMEM((bucket_rows, model_width), low)],
    )

    if not chips:
        dense_grad = dense_parts[0].reshape(group_count, owner_count, part, -1)
        dense_parts = [
            jnp.stack(
                [
                    lax.dynamic_index_in_dim(dense_grad, owner ^ relative, 1, keepdims=False)
                    for relative in range(side, owner_count, 2)
                ]
            )
            for side in range(2)
        ]
    late = after(spots, input_terms)
    first, second = halved(late, own_grads, other_grads, across, along)
    dense_parts[1] = after(dense_parts[1], first, second, *moe_terms)
    dense_parts = join(dense_parts[0], swap(dense_parts[1], "expert", 1))
    first, second = swap(first, "dp", 2), swap(second, "dp", 1)
    input_grad = add_blocks(hidden_grad, scatter_rows(after(input_terms, dense_parts)))
    dense_terms = send_expert([dense_parts[chip] for chip in range(owner_count // 2)])
    dense_terms[1:] = [after(term, input_grad) for term in dense_terms[1:]]
    dense_sum = raise_(dense_terms[0])
    for term in dense_terms[1:]:
        dense_sum = dense_sum + raise_(term)
    dense_sum = lower(dense_sum)
    dense_sum = lax.all_to_all(dense_sum, "dp", split_axis=0, concat_axis=0, tiled=True)
    masters = [
        (qk_weight, qk_first, qk_second),
        (value_weight, value_first, value_second),
        (output_weight, output_first, output_second),
        (select_weight, select_first, select_second),
        (router_weight, router_first, router_second),
        (gain_weight[None], gain_first[None], gain_second[None]),
    ]
    masters = [array for group in masters for array in group]
    updated = wide_call(
        dense_update_kernel,
        [scalars, dense_sum] + masters,
        [jax.ShapeDtypeStruct(array.shape, high) for array in masters],
    )
    updated = list(updated[:15]) + [array[0] for array in updated[15:]]
    expert_results = expert_update(
        [
            [(own_grads, 1), (other_grads, 1), (across, 0), (first, 0)],
            [(own_grads, 1), (other_grads, 1), (along, 0), (second, 0)],
        ],
        expert_weight,
        expert_first,
        expert_second,
    )
    return (layer_out[None], input_grad[None], *updated, *expert_results, expert_counts)


def solution(mesh):
    placed = (
        P("expert", "dp", None),
        P("expert", "dp", None),
        P("expert"),
        P("expert", "dp", None, None),
        P("expert", "dp", None),
        P(("dp", "expert"), None),
        P(("dp", "expert"), None),
        P(("dp", "expert"), None),
        P(("dp", "expert"), None),
        P(("dp", "expert"), None),
        P(("dp", "expert"), None),
        P(("dp", "expert"), None),
        P(("dp", "expert"), None),
        P(("dp", "expert"), None),
        P(("dp", "expert"), None),
        P(("dp", "expert"), None),
        P(("dp", "expert"), None),
        P(("dp", "expert"), None),
        P(("dp", "expert"), None),
        P(("dp", "expert"), None),
        P(("dp", "expert")),
        P(("dp", "expert")),
        P(("dp", "expert")),
        P("expert", "dp", None),
        P("expert", "dp", None),
        P("expert", "dp", None),
    )
    return jax.shard_map(
        local,
        mesh=mesh,
        in_specs=placed,
        out_specs=(
            P("expert", "dp", None),
            P("expert", "dp", None),
            P(("dp", "expert"), None),
            P(("dp", "expert"), None),
            P(("dp", "expert"), None),
            P(("dp", "expert"), None),
            P(("dp", "expert"), None),
            P(("dp", "expert"), None),
            P(("dp", "expert"), None),
            P(("dp", "expert"), None),
            P(("dp", "expert"), None),
            P(("dp", "expert"), None),
            P(("dp", "expert"), None),
            P(("dp", "expert"), None),
            P(("dp", "expert"), None),
            P(("dp", "expert"), None),
            P(("dp", "expert"), None),
            P(("dp", "expert")),
            P(("dp", "expert")),
            P(("dp", "expert")),
            P("expert", "dp", None),
            P("expert", "dp", None),
            P("expert", "dp", None),
            P(),
        ),
        check_vma=False,
    )
```

```python
import functools

import numpy as np
import jax
import jax.numpy as jnp
from jax import lax
from jax.experimental import pallas as pl
from jax.experimental.pallas import tpu as pltpu
from jax.sharding import PartitionSpec as P

HEADS = 4
HEAD_DIM = 128
ATT_EXPERTS = 5
EXPERT_H = 128
TOPK = 16
STEP = 10


norm_eps = 1e-05
beta_first = 0.9
beta_second = 0.95
adam_eps = 1e-08
weight_decay = 0.1
masked_score = -1e30
rope_base = 10000.0
rate_query_key = 0.04
rate_value = 0.03
rate_output = 2.0
rate_select = 0.03
rate_router = 0.015
rate_gain = 1.2
rate_expert = 0.05


def product(former, latter):
    return jnp.dot(former, latter, preferred_element_type=jnp.float32)


def product_rows(former, latter):
    return lax.dot_general(
        former, latter, (((0,), (0,)), ((), ())), preferred_element_type=jnp.float32
    )


def product_last(former, latter):
    return lax.dot_general(
        former, latter, (((1,), (1,)), ((), ())), preferred_element_type=jnp.float32
    )


def rope_tables(rows):
    half = HEAD_DIM // 2
    frequency = np.exp(-np.log(rope_base) * np.arange(half) / half)
    angles = np.arange(rows)[:, None] * frequency[None, :]
    cosine, sine = np.cos(angles), np.sin(angles)
    return (
        jnp.asarray(np.concatenate([cosine, cosine], axis=1), jnp.float32),
        jnp.asarray(np.concatenate([-sine, sine], axis=1), jnp.float32),
    )


def adamw_update(weight, first_moment, second_moment, gradient, rate):
    first_new = beta_first * first_moment + (1.0 - beta_first) * gradient
    second_new = beta_second * second_moment + (1.0 - beta_second) * gradient * gradient
    first_hat = first_new / (1.0 - beta_first**STEP)
    second_hat = second_new / (1.0 - beta_second**STEP)
    weight_new = weight - rate * (
        first_hat / (jnp.sqrt(second_hat) + adam_eps) + weight_decay * weight
    )
    return (weight_new, first_new, second_new)


LIGHT = pl.CostEstimate(flops=1000, bytes_accessed=1000, transcendentals=0)


def swap(values, axis, relative):
    count = lax.axis_size(axis)
    return lax.ppermute(values, axis, [(place, place ^ relative) for place in range(count)])


def lower(values):
    return values.astype(jnp.bfloat16)


def raise_(values):
    return values.astype(jnp.float32)


def after(values, *others):
    return lax.optimization_barrier((values,) + others)[0]


def dp_copies(values):
    return jnp.broadcast_to(values[None], (lax.axis_size("dp"),) + values.shape)


def exchange_rows(copies):
    blocks = lax.all_to_all(copies, "dp", split_axis=0, concat_axis=0, tiled=True)
    return blocks.reshape((-1,) + copies.shape[2:])


def scatter_rows(values):
    count = lax.axis_size("dp")
    blocks = values.reshape((count, values.shape[0] // count) + values.shape[1:])
    return lax.all_to_all(blocks, "dp", split_axis=0, concat_axis=0, tiled=True)


def add_blocks(values, blocks):
    for index in range(blocks.shape[0]):
        values = values + raise_(blocks[index])
    return values


def join_kernel(scalars, evens, odds, *results):
    for chip, result in enumerate(results):
        result[...] = lower(raise_(evens[chip]) + raise_(odds[chip]))


def join(scalars, evens, odds):
    shape = jax.ShapeDtypeStruct(evens.shape[1:], jnp.bfloat16)
    return list(wide_call(join_kernel, [scalars, evens, odds], [shape] * evens.shape[0]))


def forwarded(relative):
    return relative & 2 and relative > 2


def gather_chips(values):
    return [values] + [
        swap(values, "expert", relative) for relative in range(2, lax.axis_size("expert"), 2)
    ]


def send_expert(joined):
    return [joined[0]] + [
        swap(term, "expert", 2 * index) for index, term in enumerate(joined) if index
    ]


def full(shape):
    return pl.BlockSpec(shape, lambda *_: (0,) * len(shape))


def wide_call(kernel, inputs, outputs, scratch=()):
    specs = [pl.BlockSpec(memory_space=pltpu.SMEM)] + [full(value.shape) for value in inputs[1:]]
    return pl.pallas_call(
        kernel,
        grid=(1,),
        in_specs=specs,
        out_specs=[full(value.shape) for value in outputs],
        out_shape=outputs,
        scratch_shapes=list(scratch),
        compiler_params=pltpu.CompilerParams(vmem_limit_bytes=56 * 2**20),
        cost_estimate=LIGHT,
    )(*inputs)


class Copies:
    def __init__(self, sems):
        self.sems, self.count, self.waiting = sems, 0, {}

    def start(self, name, source, target):
        copy = pltpu.make_async_copy(source, target, self.sems.at[self.count])
        copy.start()
        self.count += 1
        self.waiting.setdefault(name, []).append(copy)

    def wait(self, *names):
        for name in names:
            for copy in self.waiting.pop(name, []):
                copy.wait()


def staged_call(kernel, inputs, outputs, held, scratch, copies):
    somewhere = pl.BlockSpec(memory_space=pl.ANY)
    return pl.pallas_call(
        kernel,
        grid=(1,),
        in_specs=[pl.BlockSpec(memory_space=pltpu.SMEM)] + [somewhere] * (len(inputs) - 1),
        out_specs=[somewhere] * len(outputs),
        out_shape=outputs,
        scratch_shapes=[pltpu.VMEM(value.shape, value.dtype) for value in held]
        + list(scratch)
        + [pltpu.SemaphoreType.DMA((copies,))],
        compiler_params=pltpu.CompilerParams(vmem_limit_bytes=56 * 2**20),
        cost_estimate=LIGHT,
    )(*inputs)


def shift_table(rows, columns, offset, count):
    source = lax.broadcasted_iota(jnp.int32, (rows, columns), 0)
    target = lax.broadcasted_iota(jnp.int32, (rows, columns), 1)
    return lower(jnp.where((source == target + offset) & (target < count), 1.0, 0.0))


def moments(values):
    center = values - jnp.mean(values, axis=-1, keepdims=True)
    inverse = lax.rsqrt(jnp.mean(center * center, axis=-1, keepdims=True) + norm_eps)
    return center * inverse, inverse


def turn(rows, cosine, signed_sine, direction):
    return rows * cosine + direction * pltpu.roll(rows, HEAD_DIM // 2, 1) * signed_sine


def masked_scores(queries, key_rows, seq_len, start):
    scores = product_last(queries, key_rows) * HEAD_DIM ** (-0.5)
    query_place = start + lax.broadcasted_iota(jnp.int32, scores.shape, 0)
    key_place = lax.broadcasted_iota(jnp.int32, scores.shape, 1)
    return jnp.where((key_place <= query_place) & (key_place < seq_len), scores, masked_score)


VALUE_WIDTH = ATT_EXPERTS * HEAD_DIM
QK_EDGE = 2 * HEAD_DIM
VALUE_EDGE = QK_EDGE + VALUE_WIDTH
OUTPUT_EDGE = VALUE_EDGE + VALUE_WIDTH
SELECT_COUNT = 2 * ATT_EXPERTS


KEPT = ("queries", "key_rows", "values", "weighting", "projected", "attended", "mixed", "log_total")


def attention_kernel(blocks, gain_column, chips, local_count, scalars, *refs):
    given = blocks + 2 + (chips + 1 if chips else 1)
    outs = (["dense"] if chips else []) + list(KEPT) + ["branch", "router_local", "counts"]
    count = len(outs)
    sources, targets = refs[:given], dict(zip(outs, refs[given : given + count]))
    tokens, (cosine, sine, dense), refs = (
        refs[given + count : given + count + blocks],
        refs[given + count + blocks : given + count + blocks + 3],
        refs[given + count + blocks + 3 : -1] + refs[-1:],
    )
    *kept, branch, router_local, counts, sems = refs
    (queries, key_rows, values, weighting, projected, attended, mixed, log_total) = kept
    copies = Copies(sems)
    for index in range(blocks):
        copies.start("in", sources[index], tokens[index])
    copies.start("in", sources[blocks], cosine)
    copies.start("in", sources[blocks + 1], sine)
    if chips:
        evens, odds = sources[blocks + 2 : blocks + 2 + chips], sources[blocks + 2 + chips]
        part = odds.shape[2]
        for chip in range(chips):
            for other, rows in ((0, evens[chip]), (1, odds.at[chip])):
                start = (scalars[2] ^ (2 * chip + other)) * part
                copies.start("in", rows, dense.at[:, pl.ds(pl.multiple_of(start, part), part), :])
    else:
        copies.start("in", sources[blocks + 2], dense)
    copies.wait("in")
    if chips:
        copies.start("out", dense, targets["dense"])
    place, seq_len = scalars[0], scalars[1]
    width = dense.shape[0] * dense.shape[1]
    block = tokens[0].shape[0]

    def weight(start, end):
        return dense[:, :, start:end].reshape(width, end - start)

    small_rows = weight(OUTPUT_EDGE, dense.shape[2])
    count = local_count
    source = lax.broadcasted_iota(jnp.int32, (small_rows.shape[1], router_local.shape[1]), 0)
    entry = lax.broadcasted_iota(jnp.int32, source.shape, 1)
    first = SELECT_COUNT + scalars[2] * count + entry
    second = SELECT_COUNT + (scalars[2] ^ 1) * count + entry - count
    table = (source == jnp.where(entry < count, first, second)) & (entry < 2 * count)
    router_local[...] = lower(product(small_rows, lower(jnp.where(table, 1.0, 0.0))))
    part = counts.shape[0]
    total = raise_(small_rows[:part])
    for start in range(part, width, part):
        total += raise_(small_rows[start : start + part])
    counts[...] = total
    copies.start("out", counts, targets["counts"])
    copies.start("out", router_local, targets["router_local"])
    gain = raise_(small_rows).T[gain_column : gain_column + 1, :]
    head_table = shift_table(
        tokens[0].shape[1] - width, dense.shape[2] - OUTPUT_EDGE, place * SELECT_COUNT, SELECT_COUNT
    )
    for index in range(blocks):
        span = pl.ds(pl.multiple_of((place ^ index) * block, block), block)
        rows = tokens[index][:, :width]
        scaled, _ = moments(raise_(rows))
        normed_rows = lower(scaled * gain)
        both = product(normed_rows, weight(0, QK_EDGE))
        queries[span, :] = lower(turn(both[:, :HEAD_DIM], cosine[span, :], sine[span, :], 1.0))
        key_rows[span, :] = lower(turn(both[:, HEAD_DIM:], cosine[span, :], sine[span, :], 1.0))
        chosen = product(tokens[index][:, width:], head_table)
        sigma_rows = jax.nn.sigmoid(product(normed_rows, small_rows))
        weights = sigma_rows * chosen
        weighting[span, :] = weights
        columns = product(rows, weight(QK_EDGE, VALUE_EDGE))
        projected[span, :] = columns
        total = weights[:, 0:1] * columns[:, :HEAD_DIM]
        for expert in range(1, ATT_EXPERTS):
            total += (
                weights[:, expert : expert + 1]
                * columns[:, expert * HEAD_DIM : (expert + 1) * HEAD_DIM]
            )
        values[span, :] = lower(total)
    for name, ref in zip(KEPT[:5], kept):
        copies.start("out", ref, targets[name])
    for start in range(0, blocks * block, block):
        span = pl.ds(start, block)
        scores = masked_scores(queries[span, :], key_rows[...], seq_len, start)
        highest = jnp.max(scores, axis=-1, keepdims=True)
        raised = jnp.exp(scores - highest)
        row_total = jnp.sum(raised, axis=-1, keepdims=True)
        log_total[span, :] = jnp.broadcast_to(highest + jnp.log(row_total), (block, HEAD_DIM))
        rows = product(lower(raised / row_total), values[...])
        attended[span, :] = rows
        weights = weighting[span, :]
        for expert in range(ATT_EXPERTS):
            mixed[span, pl.ds(expert * HEAD_DIM, HEAD_DIM)] = lower(
                weights[:, ATT_EXPERTS + expert : ATT_EXPERTS + expert + 1] * rows
            )
        branch[span, :] = lower(product_last(mixed[span, :], weight(VALUE_EDGE, OUTPUT_EDGE)))
        for name, ref in (("mixed", mixed), ("branch", branch)):
            copies.start("out", ref.at[span, :], targets[name].at[span, :])
    copies.start("out", attended, targets["attended"])
    copies.start("out", log_total, targets["log_total"])
    copies.wait("out")


BACK = ("upstream", "dense", "weighting", "attended", "mixed", "queries", "key_rows", "values") + (
    "log_total",
    "projected",
    "cosine",
    "sine",
    "router_grad",
)


def attention_back_kernel(blocks, gain_column, chips, scalars, *refs):
    count = len(BACK)
    sources, token_blocks, refs = refs[:count], refs[count : count + blocks], refs[count + blocks :]
    results, out_terms, refs = refs[: 2 if chips else 1], refs[2 if chips else 1], refs[3 if chips else 2 :]
    held, (grads, terms, tokens), refs = refs[:count], refs[count : count + 3], refs[count + 3 :]
    (upstream, dense, weighting, attended, mixed, queries, key_rows, values, log_total) = held[:9]
    projected, cosine, sine, router_grad = held[9:]
    (attended_grad, weight_grad, key_grad, value_grad, query_grad) = refs[:5]
    projected_grad, pair_grad, select_grad, normed, sems = refs[5:]
    copies = Copies(sems)
    for name, source, target in zip(BACK, sources, held):
        copies.start(name, source, target)
    block = token_blocks[0].shape[0]
    for index, rows in enumerate(token_blocks):
        span = pl.ds(pl.multiple_of((scalars[0] ^ index) * block, block), block)
        copies.start("tokens", rows.at[:, pl.ds(0, tokens.shape[1])], tokens.at[span, :])

    def weight(start, end):
        return dense[:, :, start:end].reshape(tokens.shape[1], end - start)

    def leave(columns):
        if not chips:
            copies.start("out", grads.at[:, :, columns], results[0].at[:, :, columns])
            return
        part = results[0].shape[2]
        for relative in range(2 * chips):
            start = pl.multiple_of((scalars[2] ^ relative) * part, part)
            target = results[relative % 2].at[relative // 2, :, :, columns]
            copies.start("out", grads.at[:, pl.ds(start, part), columns], target)

    def keep(start, values):
        columns = pl.ds(start, values.shape[1])
        grads[:, :, columns] = values.reshape(grads.shape[:2] + values.shape[1:])

    copies.wait("upstream", "dense", "weighting", "attended")
    seq_len = scalars[1]
    width = tokens.shape[1]
    small = dense.shape[2] - OUTPUT_EDGE
    lane = lax.broadcasted_iota(jnp.int32, (block, small), 1)
    scale = HEAD_DIM ** (-0.5)
    gain = raise_(weight(OUTPUT_EDGE, dense.shape[2])).T[gain_column : gain_column + 1, :]
    for start in range(0, tokens.shape[0], block):
        span = pl.ds(start, block)
        mixed_grad = product(upstream[span, :], weight(VALUE_EDGE, OUTPUT_EDGE))
        weights = weighting[span, :]
        heads = attended[span, :]
        total = jnp.zeros((block, HEAD_DIM), jnp.float32)
        found = jnp.zeros((block, small), jnp.float32)
        for expert in range(ATT_EXPERTS):
            piece = mixed_grad[:, expert * HEAD_DIM : (expert + 1) * HEAD_DIM]
            column = ATT_EXPERTS + expert
            total += weights[:, column : column + 1] * piece
            found = jnp.where(lane == column, jnp.sum(piece * heads, axis=1, keepdims=True), found)
        attended_grad[span, :] = lower(total)
        weight_grad[span, :] = found
    copies.wait("mixed")
    keep(VALUE_EDGE, lower(product_rows(upstream[...], mixed[...])))
    leave(pl.ds(VALUE_EDGE, OUTPUT_EDGE - VALUE_EDGE))
    copies.wait("queries", "key_rows", "values", "log_total")
    for start in range(0, tokens.shape[0], block):
        span = pl.ds(start, block)
        scores = masked_scores(queries[span, :], key_rows[...], seq_len, start)
        probs = jnp.exp(scores - log_total[span, :1])
        prob_grad = product_last(attended_grad[span, :], values[...])
        delta = jnp.sum(probs * prob_grad, axis=-1, keepdims=True)
        score_grad = lower(probs * (prob_grad - delta))
        query_grad[span, :] = product(score_grad, key_rows[...]) * scale
        key_terms = product_rows(score_grad, queries[span, :])
        value_terms = product_rows(lower(probs), attended_grad[span, :])
        if start:
            key_grad[...] += key_terms
            value_grad[...] += value_terms
        else:
            key_grad[...] = key_terms
            value_grad[...] = value_terms
    copies.wait("projected", "cosine", "sine", "router_grad", "tokens")
    gain_grad = jnp.zeros((1, width), jnp.float32)
    for start in range(0, tokens.shape[0], block):
        span = pl.ds(start, block)
        rows = value_grad[span, :]
        weights = weighting[span, :]
        found = weight_grad[span, :]
        for expert in range(ATT_EXPERTS):
            piece = pl.ds(expert * HEAD_DIM, HEAD_DIM)
            projected_grad[span, piece] = lower(weights[:, expert : expert + 1] * rows)
            found = jnp.where(
                lane == expert,
                jnp.sum(rows * projected[span, piece], axis=1, keepdims=True),
                found,
            )
        pair_grad[span, :HEAD_DIM] = lower(
            turn(query_grad[span, :], cosine[span, :], sine[span, :], -1.0)
        )
        pair_grad[span, HEAD_DIM:] = lower(
            turn(key_grad[span, :] * scale, cosine[span, :], sine[span, :], -1.0)
        )
        select_rows = lower(found * weights * (1.0 - weights))
        select_grad[span, :] = select_rows
        normed_grad = product_last(pair_grad[span, :], weight(0, QK_EDGE)) + product_last(
            select_rows, weight(OUTPUT_EDGE, dense.shape[2])
        )
        scaled, inverse = moments(raise_(tokens[span, :]))
        normed[span, :] = lower(scaled * gain)
        gain_grad += jnp.sum(normed_grad * scaled, axis=0, keepdims=True)
        through = normed_grad * gain
        norm_grad = inverse * (
            through
            - jnp.mean(through, axis=-1, keepdims=True)
            - scaled * jnp.mean(through * scaled, axis=-1, keepdims=True)
        )
        terms[span, :] = lower(
            product_last(projected_grad[span, :], weight(QK_EDGE, VALUE_EDGE)) + norm_grad
        )
        copies.start("out", terms.at[span, :], out_terms.at[span, :])
    keep(QK_EDGE, lower(product_rows(tokens[...], projected_grad[...])))
    keep(0, lower(product_rows(normed[...], pair_grad[...])))
    row = lax.broadcasted_iota(jnp.int32, (small, width), 0)
    gain_part = jnp.where(row == gain_column, gain_grad, 0.0).T
    rest = product_rows(normed[...], select_grad[...]) + gain_part + router_grad[...]
    keep(OUTPUT_EDGE, lower(rest))
    leave(pl.ds(0, VALUE_EDGE))
    leave(pl.ds(OUTPUT_EDGE, small))
    copies.wait("out")


def piece_copies(place, pieces, target, columns, sems):
    part, last = pieces[0].shape[0], len(pieces) - 2
    half = part // 2
    copies = []
    for index, piece in enumerate(pieces):
        start = (place ^ min(index, last)) * part + (half if index > last else 0)
        rows = pl.ds(pl.multiple_of(start, half), piece.shape[0])
        source = piece.at[:, columns]
        copies.append(pltpu.make_async_copy(source, target.at[rows, :], sems.at[index]))
    return copies


def expert_kernel(pieces, scalars, rows, up, router, *refs):
    weights = refs[: 2 * pieces]
    back, slope, gated, insides, outsides, sems = refs[2 * pieces :]
    block, width = rows.shape
    hidden = slope.shape[1] // 2
    count = hidden // EXPERT_H
    copies = []
    for side in range(2):
        own = weights[side * pieces : (side + 1) * pieces]
        copies.append(
            piece_copies(scalars[0], own, insides.at[side], pl.ds(0, hidden), sems.at[side, 0])
            + piece_copies(
                scalars[0], own, outsides.at[side], pl.ds(hidden, hidden), sems.at[side, 1]
            )
        )
        for copy in copies[side]:
            copy.start()
    small = up.shape[1] - width
    lanes = router.shape[1]
    offsets = [SELECT_COUNT + (scalars[1] ^ index) * count for index in range(2)]

    def column_of(entry):
        return jnp.where(entry < count, offsets[0] + entry, offsets[1] + entry - count)

    source = lax.broadcasted_iota(jnp.int32, (small, lanes), 0)
    entry = lax.broadcasted_iota(jnp.int32, (small, lanes), 1)
    pick_table = lower(jnp.where((source == column_of(entry)) & (entry < 2 * count), 1.0, 0.0))
    entry = lax.broadcasted_iota(jnp.int32, (lanes, small), 0)
    target = lax.broadcasted_iota(jnp.int32, (lanes, small), 1)
    place_table = lower(jnp.where((target == column_of(entry)) & (entry < 2 * count), 1.0, 0.0))
    lane = lax.broadcasted_iota(jnp.int32, (block, lanes), 1)
    scaled, _ = moments(raise_(rows[...]))
    sigma_gate = jax.nn.sigmoid(product(lower(scaled), router[...]))
    gates = sigma_gate * product(up[:, width:], pick_table)
    found = jnp.zeros((block, lanes), jnp.float32)
    for first in range(0, 2 * count, 2):
        side = first // count
        if first % count == 0:
            for copy in copies[side]:
                copy.wait()
        local = pl.ds(first % count * EXPERT_H, 2 * EXPERT_H)
        inner = product(rows[...], insides[side, :, local])
        terms = product(up[:, :width], outsides[side, :, local])
        sigma = jax.nn.sigmoid(inner)
        silu = inner * sigma
        active = raise_(lower(silu))
        both = terms * active
        tilt = sigma + silu * (1.0 - sigma)
        for k in range(2):
            part = slice(k * EXPERT_H, (k + 1) * EXPERT_H)
            columns = pl.ds((first + k) * EXPERT_H, EXPERT_H)
            gate = gates[:, first + k : first + k + 1]
            gated[:, columns] = lower(gate * active[:, part])
            slope[:, columns] = lower(gate * terms[:, part] * tilt[:, part])
            summed = jnp.sum(both[:, part], axis=1, keepdims=True)
            found = jnp.where(lane == first + k, summed, found)
    back[:, :width] = lower(
        product_last(slope[:, :hidden], insides[0]) + product_last(slope[:, hidden:], insides[1])
    )
    back[:, width:] = lower(product(lower(found * gates * (1.0 - sigma_gate)), place_table))


def expert_call(scalars, rows, up, router, weights):
    block, width = rows.shape
    hidden = weights[0].shape[1] // 2
    pieces = len(weights) // 2
    outputs = [
        jax.ShapeDtypeStruct(up.shape, jnp.bfloat16),
        jax.ShapeDtypeStruct((block, 2 * hidden), jnp.bfloat16),
        jax.ShapeDtypeStruct((block, 2 * hidden), jnp.bfloat16),
    ]
    return pl.pallas_call(
        functools.partial(expert_kernel, pieces),
        grid=(1,),
        in_specs=[pl.BlockSpec(memory_space=pltpu.SMEM)]
        + [full(value.shape) for value in (rows, up, router)]
        + [pl.BlockSpec(memory_space=pl.ANY)] * len(weights),
        out_specs=[full(value.shape) for value in outputs],
        out_shape=outputs,
        scratch_shapes=[
            pltpu.VMEM((2, width, hidden), jnp.bfloat16),
            pltpu.VMEM((2, width, hidden), jnp.bfloat16),
            pltpu.SemaphoreType.DMA((2, 2, pieces)),
        ],
        compiler_params=pltpu.CompilerParams(vmem_limit_bytes=56 * 2**20),
        cost_estimate=LIGHT,
    )(scalars, rows, up, router, *weights)


def expert_grad_kernel(chips, indices, scalars, *refs):
    rows = refs[:chips]
    ups = refs[chips : 2 * chips]
    slopes = refs[2 * chips : 3 * chips]
    gateds = refs[3 * chips : 4 * chips]
    grads = refs[4 * chips]
    part = grads.shape[0] // len(indices)
    half = pl.num_programs(0) // 2

    def total(lefts, rights):
        for place, index in enumerate(indices):
            columns = pl.ds(pl.multiple_of((scalars[0] ^ index) * part, part), part)
            result = product_rows(lefts[0][:, columns], rights[0][...])
            for left, right in zip(lefts[1:], rights[1:]):
                result += product_rows(left[:, columns], right[...])
            grads[pl.ds(place * part, part), :] = lower(result)

    @pl.when(pl.program_id(0) < half)
    def _():
        total(rows, slopes)

    @pl.when(pl.program_id(0) >= half)
    def _():
        total(ups, gateds)


def expert_grads(scalars, rows, ups, slopes, gateds, side, blocks, indices):
    chips = len(slopes)
    block, width = rows[0].shape
    hidden = slopes[0].shape[1] // 2
    tile = min(512, hidden)
    half = hidden // tile
    once = pl.Buffered(buffer_count=1)
    first = side * half
    rows_out = width // blocks * len(indices)
    return pl.pallas_call(
        functools.partial(expert_grad_kernel, chips, indices),
        grid=(2 * half,),
        in_specs=[pl.BlockSpec(memory_space=pltpu.SMEM)]
        + [pl.BlockSpec(v.shape, lambda j: (0, 0), pipeline_mode=once) for v in rows + ups]
        + [pl.BlockSpec((block, tile), lambda j: (0, first + jnp.minimum(j, half - 1)))] * chips
        + [pl.BlockSpec((block, tile), lambda j: (0, first + jnp.maximum(j - half, 0)))] * chips,
        out_specs=pl.BlockSpec((rows_out, tile), lambda j: (0, j)),
        out_shape=jax.ShapeDtypeStruct((rows_out, 2 * hidden), jnp.bfloat16),
        compiler_params=pltpu.CompilerParams(vmem_limit_bytes=56 * 2**20),
        cost_estimate=LIGHT,
    )(scalars, *rows, *ups, *slopes, *gateds)


def expert_out_kernel(pieces, scalars, *refs):
    weights, refs = refs[: 2 * pieces], refs[2 * pieces :]
    count = (len(refs) - 5) // 2
    gateds, results = refs[:count], refs[count : 2 * count]
    outsides, lefts, held, sems, gated_sems = refs[2 * count :]
    hidden = outsides.shape[2]
    block, width = results[0].shape
    tile = min(256, width)
    copies = []
    for side in range(2):
        own = weights[side * pieces : (side + 1) * pieces]
        columns = pl.ds(hidden, hidden)
        started = piece_copies(scalars[0], own, outsides.at[side], columns, sems.at[side])
        for index, gated in enumerate(gateds):
            source = gated.at[:, pl.ds(side * hidden, hidden)]
            target = lefts.at[side, pl.ds(index * block, block), :]
            started.append(pltpu.make_async_copy(source, target, gated_sems.at[side, index]))
        for copy in started:
            copy.start()
        copies.append(started)
    for side in range(2):
        for copy in copies[side]:
            copy.wait()
        for start in range(0, width, tile):
            columns = pl.ds(start, tile)
            total = product_last(lefts[side], outsides[side, columns, :])
            if side == 0:
                held[:, columns] = total
            else:
                total += held[:, columns]
                for index, result in enumerate(results):
                    result[:, columns] = lower(total[index * block : (index + 1) * block])


def expert_out_call(scalars, weights, gateds):
    pieces, count = len(weights) // 2, len(gateds)
    hidden = weights[0].shape[1] // 2
    width = sum(weight.shape[0] for weight in weights[:pieces])
    block = gateds[0].shape[0]
    return pl.pallas_call(
        functools.partial(expert_out_kernel, pieces),
        grid=(1,),
        in_specs=[pl.BlockSpec(memory_space=pltpu.SMEM)]
        + [pl.BlockSpec(memory_space=pl.ANY)] * (len(weights) + count),
        out_specs=[full((block, width))] * count,
        out_shape=[jax.ShapeDtypeStruct((block, width), jnp.bfloat16)] * count,
        scratch_shapes=[
            pltpu.VMEM((2, width, hidden), jnp.bfloat16),
            pltpu.VMEM((2, count * block, hidden), jnp.bfloat16),
            pltpu.VMEM((count * block, width), jnp.float32),
            pltpu.SemaphoreType.DMA((2, pieces)),
            pltpu.SemaphoreType.DMA((2, count)),
        ],
        compiler_params=pltpu.CompilerParams(vmem_limit_bytes=56 * 2**20),
        cost_estimate=LIGHT,
    )(scalars, *weights, *gateds)


def hidden_back_kernel(count, scalars, *refs):
    terms = refs[:count]
    hidden, upstream, small, hidden_grad, hidden_grad_low, router_grad = refs[count:]
    width = hidden.shape[1]
    total = raise_(terms[0][...])
    for term in terms[1:]:
        total += raise_(term[...])
    logit_grad = lower(total[:, width:])
    scaled, inverse = moments(hidden[...])
    router_grad[...] = product_rows(lower(scaled), logit_grad)
    through = product_last(logit_grad, small[...])
    norm_grad = inverse * (
        through
        - jnp.mean(through, axis=-1, keepdims=True)
        - scaled * jnp.mean(through * scaled, axis=-1, keepdims=True)
    )
    result = raise_(upstream[:, :width]) + total[:, :width] + norm_grad
    hidden_grad[...] = result
    hidden_grad_low[...] = lower(result)


def expert_update_kernel(terms, *refs):
    grads = refs[: 2 * terms]
    weight, first, second, new, first_new, second_new = refs[2 * terms :]
    for half in range(2):
        for expert in range(weight.shape[0]):
            source = pl.ds(expert * EXPERT_H, EXPERT_H)
            columns = pl.ds(half * EXPERT_H, EXPERT_H)
            total = raise_(grads[half * terms][:, source])
            for grad in grads[half * terms + 1 : (half + 1) * terms]:
                total += raise_(grad[:, source])
            results = adamw_update(
                weight[expert, :, columns],
                first[expert, :, columns],
                second[expert, :, columns],
                total,
                rate_expert,
            )
            for target, result in zip((new, first_new, second_new), results):
                target[expert, :, columns] = result


def expert_update(grads, weight, first, second):
    count, rows, columns = weight.shape
    some = 2 if count % 2 == 0 else 1
    steps = count // some
    whole = pl.BlockSpec((some, rows, columns), lambda e: (e, 0, 0))
    shape = jax.ShapeDtypeStruct(weight.shape, jnp.float32)
    specs = [
        pl.BlockSpec(
            (rows, some * EXPERT_H), lambda e, start=half * steps * both: (0, start + e)
        )
        for half in range(2)
        for _, both in grads[half]
    ]
    return pl.pallas_call(
        functools.partial(expert_update_kernel, len(grads[0])),
        grid=(steps,),
        in_specs=specs + [whole] * 3,
        out_specs=[whole] * 3,
        out_shape=[shape] * 3,
        compiler_params=pltpu.CompilerParams(vmem_limit_bytes=56 * 2**20),
        cost_estimate=LIGHT,
    )(*[grad for half in grads for grad, _ in half], weight, first, second)


def halving_kernel(scalars, *refs):
    across, along = refs[8:]
    rows = across.shape[0] // 2
    for index in range(4):
        target, half = (across, along)[index // 2], pl.ds(index % 2 * rows, rows)
        target[half, :] = lower(raise_(refs[2 * index][...]) + raise_(refs[2 * index + 1][...]))


def halving(scalars, own, other, rows):
    columns = own.shape[1] // 2
    specs = []
    for row, column in ((1, 0), (3, 0), (2, 1), (3, 1)):
        specs += [pl.BlockSpec((rows, columns), lambda i, row=row, column=column: (row, column))] * 2
    shape = jax.ShapeDtypeStruct((2 * rows, columns), jnp.bfloat16)
    return pl.pallas_call(
        halving_kernel,
        grid=(1,),
        in_specs=[pl.BlockSpec(memory_space=pltpu.SMEM)] + specs,
        out_specs=[full(shape.shape)] * 2,
        out_shape=[shape] * 2,
        compiler_params=pltpu.CompilerParams(vmem_limit_bytes=56 * 2**20),
        cost_estimate=LIGHT,
    )(scalars, *[own, other] * 4)


def halved_kernel(scalars, own_two, other_two, own_one, other_one, across, along, first, second):
    first[...] = lower(raise_(own_two[...]) + raise_(other_two[...]) + raise_(across[...]))
    second[...] = lower(raise_(own_one[...]) + raise_(other_one[...]) + raise_(along[...]))


def halved(scalars, own, other, across, along):
    rows, columns = across.shape[0] // 2, across.shape[1]

    def block(row, column):
        return pl.BlockSpec((rows, columns), lambda i: (row, column))

    return pl.pallas_call(
        halved_kernel,
        grid=(1,),
        in_specs=[pl.BlockSpec(memory_space=pltpu.SMEM)]
        + [block(2, 0), block(2, 0), block(1, 1), block(1, 1), block(1, 0), block(1, 0)],
        out_specs=[block(0, 0)] * 2,
        out_shape=[jax.ShapeDtypeStruct((rows, columns), jnp.bfloat16)] * 2,
        compiler_params=pltpu.CompilerParams(vmem_limit_bytes=56 * 2**20),
        cost_estimate=LIGHT,
    )(scalars, own, other, own, other, across, along)


def dense_sum_kernel(scalars, *refs):
    count = refs[0].shape[0]
    terms, results = refs[:-count], refs[-count:]
    for index, result in enumerate(results):
        spot = scalars[0] ^ index
        total = raise_(terms[0][spot])
        for term in terms[1:]:
            total += raise_(term[spot])
        result[...] = lower(total)


def dense_update_kernel(scalars, *refs):
    sums, refs = refs[:HEADS], refs[HEADS:]
    inputs = [refs[3 * index : 3 * index + 3] for index in range(6)]
    outputs = [refs[3 * index : 3 * index + 3] for index in range(6, 12)]

    def update(index, gradient, columns, rate):
        results = adamw_update(*[ref[:, columns] for ref in inputs[index]], gradient, rate)
        for target, result in zip(outputs[index], results):
            target[:, columns] = result

    part, small = sums[0].shape[0], sums[0].shape[1] - OUTPUT_EDGE
    shared = jnp.zeros((part, small), jnp.float32)
    chosen = jnp.zeros((part, inputs[3][0].shape[1]), jnp.float32)
    for index, rows in enumerate(sums):
        head = scalars[0] ^ index
        for side in range(2):
            span = pl.ds(pl.multiple_of((side * HEADS + head) * HEAD_DIM, HEAD_DIM), HEAD_DIM)
            source = pl.ds(side * HEAD_DIM, HEAD_DIM)
            update(0, raise_(rows[:, source]), span, rate_query_key)
        span = pl.ds(pl.multiple_of(head * VALUE_WIDTH, HEAD_DIM), VALUE_WIDTH)
        update(1, raise_(rows[:, QK_EDGE:VALUE_EDGE]), span, rate_value)
        update(2, raise_(rows[:, VALUE_EDGE:OUTPUT_EDGE]), span, rate_output)
        last = rows[:, OUTPUT_EDGE:]
        source = lax.broadcasted_iota(jnp.int32, (small, chosen.shape[1]), 0)
        target = lax.broadcasted_iota(jnp.int32, (small, chosen.shape[1]), 1)
        side, entry = lax.div(source, ATT_EXPERTS), lax.rem(source, ATT_EXPERTS)
        table = (target == (side * HEADS + head) * ATT_EXPERTS + entry) & (source < SELECT_COUNT)
        chosen += product(last, lower(jnp.where(table, 1.0, 0.0)))
        shared += raise_(last)
    every = slice(None)
    update(3, chosen, every, rate_select)
    expert_total = inputs[4][0].shape[1]
    update(4, pltpu.roll(shared, small - SELECT_COUNT, 1)[:, :expert_total], every, rate_router)
    gain_column = SELECT_COUNT + expert_total
    diagonal = lax.broadcasted_iota(jnp.int32, (part, part), 0) == lax.broadcasted_iota(
        jnp.int32, (part, part), 1
    )
    gain = jnp.where(diagonal, shared[:, gain_column : gain_column + 1], 0.0)
    update(5, jnp.sum(gain, axis=0, keepdims=True), every, rate_gain)


def expert_rows_kernel(weight, rows):
    count = weight.shape[0]
    for expert in range(count):
        rows[:, pl.ds(expert * EXPERT_H, EXPERT_H)] = lower(weight[expert, :, :EXPERT_H])
        rows[:, pl.ds((count + expert) * EXPERT_H, EXPERT_H)] = lower(weight[expert, :, EXPERT_H:])


def expert_rows_of(weight):
    count, rows, columns = weight.shape
    return pl.pallas_call(
        expert_rows_kernel,
        out_shape=jax.ShapeDtypeStruct((rows, count * columns), jnp.bfloat16),
        compiler_params=pltpu.CompilerParams(vmem_limit_bytes=56 * 2**20),
        cost_estimate=LIGHT,
    )(weight)


def front_kernel(scalars, tokens, picks, cotangent, routes, token_rows, upstream):
    rows, width = tokens.shape
    token_rows[:, :width] = tokens[...]
    lane = lax.broadcasted_iota(jnp.int32, (rows, token_rows.shape[1] - width), 1)
    chosen = jnp.zeros(lane.shape, jnp.float32)
    for column in range(picks.shape[1]):
        side, head = column // (2 * HEADS), column // 2 % HEADS
        target = head * SELECT_COUNT + side * ATT_EXPERTS + picks[:, column : column + 1]
        chosen = jnp.where(lane == target, 1.0, chosen)
    token_rows[:, width:] = lower(chosen)
    position = scalars[0] * rows + lax.broadcasted_iota(jnp.int32, (rows, 1), 0)
    upstream[:, :width] = lower(jnp.where(position < scalars[1], raise_(cotangent[...]), 0.0))
    lane = lax.broadcasted_iota(jnp.int32, (rows, upstream.shape[1] - width), 1)
    hot = jnp.zeros(lane.shape, jnp.float32)
    for column in range(routes.shape[1]):
        hot = jnp.where(lane == SELECT_COUNT + routes[:, column : column + 1], 1.0, hot)
    upstream[:, width:] = lower(hot)


def payload_kernel(scalars, upstream, qk, value, output, select, router, gain, payload):
    part = qk.shape[0]
    small = payload.shape[2] - OUTPUT_EDGE
    rows, width = upstream.shape[0], upstream.shape[1] - small
    expert_total = router.shape[1]
    position = scalars[0] * rows + lax.broadcasted_iota(jnp.int32, (rows, 1), 0)
    valid = position < scalars[1]
    hot = raise_(upstream[:, width:])
    counts = jnp.sum(jnp.where(valid, hot, 0.0), axis=0, keepdims=True)
    gain_column = SELECT_COUNT + expert_total
    count_columns = -(-expert_total // part)
    row = lax.broadcasted_iota(jnp.int32, (part, small), 0)
    lane = lax.broadcasted_iota(jnp.int32, (part, small), 1)
    shared = product(lower(router[...]), shift_back(expert_total, small, SELECT_COUNT))
    diagonal = lax.broadcasted_iota(jnp.int32, (part, part), 0) == lax.broadcasted_iota(
        jnp.int32, (part, part), 1
    )
    gain_rows = jnp.sum(jnp.where(diagonal, gain[...], 0.0), axis=1, keepdims=True)
    shared = jnp.where(lane == gain_column, gain_rows, shared)
    for column in range(count_columns):
        mine = lane - SELECT_COUNT == row * count_columns + column
        found = jnp.sum(jnp.where(mine, counts, 0.0), axis=1, keepdims=True)
        shared = jnp.where(lane == gain_column + 1 + column, found, shared)
    picked = lower(select[...])
    for head in range(HEADS):
        span = pl.ds(head * HEAD_DIM, HEAD_DIM)
        payload[head, :, :HEAD_DIM] = lower(qk[:, span])
        span = pl.ds((HEADS + head) * HEAD_DIM, HEAD_DIM)
        payload[head, :, HEAD_DIM:QK_EDGE] = lower(qk[:, span])
        span = pl.ds(head * VALUE_WIDTH, VALUE_WIDTH)
        payload[head, :, QK_EDGE:VALUE_EDGE] = lower(value[:, span])
        payload[head, :, VALUE_EDGE:OUTPUT_EDGE] = lower(output[:, span])
        source = lax.broadcasted_iota(jnp.int32, (picked.shape[1], small), 0)
        target = lax.broadcasted_iota(jnp.int32, (picked.shape[1], small), 1)
        side, entry = lax.div(target, ATT_EXPERTS), lax.rem(target, ATT_EXPERTS)
        table = (source == (side * HEADS + head) * ATT_EXPERTS + entry) & (target < SELECT_COUNT)
        chosen = product(picked, lower(jnp.where(table, 1.0, 0.0)))
        payload[head, :, OUTPUT_EDGE:] = lower(shared + chosen)


def shift_back(rows, columns, offset):
    source = lax.broadcasted_iota(jnp.int32, (rows, columns), 0)
    target = lax.broadcasted_iota(jnp.int32, (rows, columns), 1)
    return lower(jnp.where(target == source + offset, 1.0, 0.0))


def local(
    tokens,
    cotangent,
    lengths,
    picks,
    routes,
    qk_weight,
    qk_first,
    qk_second,
    value_weight,
    value_first,
    value_second,
    output_weight,
    output_first,
    output_second,
    select_weight,
    select_first,
    select_second,
    router_weight,
    router_first,
    router_second,
    gain_weight,
    gain_first,
    gain_second,
    expert_weight,
    expert_first,
    expert_second,
):
    row_count = tokens.shape[1]
    model_width = tokens.shape[2]
    group_count = lax.axis_size("dp")
    owner_count = lax.axis_size("expert")
    local_count = expert_weight.shape[0]
    expert_total = local_count * owner_count
    bucket_rows = row_count * group_count
    part = qk_weight.shape[0]
    place = lax.axis_index("dp")
    owner = lax.axis_index("expert")
    seq_len = lengths[0]
    sequence = tokens[0]
    scalars = jnp.stack(
        [place.astype(jnp.int32), seq_len.astype(jnp.int32), owner.astype(jnp.int32)]
    )
    spots = jnp.stack([place.astype(jnp.int32), owner.astype(jnp.int32)])
    low, high = jnp.bfloat16, jnp.float32

    def shaped(columns, kind, rows=bucket_rows):
        return jax.ShapeDtypeStruct((rows, columns), kind)

    gain_column = SELECT_COUNT + expert_total
    count_columns = -(-expert_total // part)
    small_used = gain_column + 1 + count_columns
    small_width = small_used + -small_used % 128
    token_width = model_width + HEADS * SELECT_COUNT + -(HEADS * SELECT_COUNT) % 128

    token_own, upstream = wide_call(
        front_kernel,
        [scalars, sequence, picks[0].reshape(row_count, -1), cotangent[0], routes[0]],
        [
            shaped(token_width, low, row_count),
            shaped(model_width + small_width, low, row_count),
        ],
    )
    expert_up = {0: upstream}
    for relative in range(2, owner_count, 2):
        if not forwarded(relative):
            expert_up[relative] = swap(upstream, "expert", relative)
    token_blocks = [token_own] + [
        swap(token_own, "dp", relative) for relative in range(1, group_count)
    ]

    (payload,) = wide_call(
        payload_kernel,
        [
            scalars,
            upstream,
            qk_weight,
            value_weight,
            output_weight,
            select_weight,
            router_weight,
            gain_weight[None],
        ],
        [jax.ShapeDtypeStruct((HEADS, part, OUTPUT_EDGE + small_width), low)],
    )
    mine = lax.all_to_all(payload, "dp", split_axis=0, concat_axis=0, tiled=True)
    mine = after(
        mine, *token_blocks[1:], *[up for relative, up in expert_up.items() if relative]
    )

    half = row_count // 2
    expert_own = after(expert_rows_of(expert_weight), mine)
    expert_pieces = [expert_own, swap(expert_own, "dp", 1), swap(expert_own, "dp", 2)]
    dense_blocks = gather_chips(mine)
    dense_others = swap(
        after(jnp.stack(dense_blocks), *expert_pieces[1:]), "expert", 1
    )

    cosine, sine = rope_tables(bucket_rows)
    if part % 16 == 0:
        chips, made = owner_count // 2, []
        given = dense_blocks + [dense_others]
    else:
        dense = jnp.zeros((group_count, owner_count) + mine.shape[1:], jnp.bfloat16)
        for chip, block in enumerate(dense_blocks):
            for other, rows in enumerate((block, dense_others[chip])):
                spot = owner ^ (2 * chip + other)
                dense = lax.dynamic_update_slice_in_dim(dense, rows[:, None], spot, axis=1)
        dense = dense.reshape(group_count, row_count, -1)
        chips, made, given = 0, [], [dense]
    dense_shape = jax.ShapeDtypeStruct((group_count, row_count, payload.shape[2]), low)
    if chips:
        made = [dense_shape]
    outputs = made + [
        shaped(HEAD_DIM, low),
        shaped(HEAD_DIM, low),
        shaped(HEAD_DIM, low),
        shaped(small_width, high),
        shaped(VALUE_WIDTH, high),
        shaped(HEAD_DIM, high),
        shaped(VALUE_WIDTH, low),
        shaped(HEAD_DIM, high),
        shaped(model_width, low),
        shaped(2 * local_count + -2 * local_count % 128, low, model_width),
        shaped(small_width, high, part),
    ]
    kept = staged_call(
        functools.partial(attention_kernel, group_count, gain_column, chips, local_count),
        [scalars] + token_blocks + [cosine, sine] + given,
        outputs,
        token_blocks + [cosine, sine, dense_shape] + outputs[len(made) :],
        [],
        group_count + 2 + owner_count + len(outputs) + 2 * group_count,
    )
    if chips:
        dense, kept = kept[0], kept[1:]
    saved, (branch, router_local, counts) = dict(zip(KEPT, kept)), kept[len(KEPT) :]
    for relative in range(2, owner_count, 2):
        if forwarded(relative):
            block = after(expert_up[relative ^ 2], branch)
            expert_up[relative] = swap(block, "expert", 2)
    expert_up = [expert_up[relative] for relative in range(0, owner_count, 2)]
    near = [after(piece, branch) for piece in expert_pieces]
    expert_others = [swap(piece, "expert", 1) for piece in near]
    far = [
        swap(expert_pieces[1][:half], "dp", 2),
        swap(expert_pieces[2][half:], "dp", 1),
    ]
    expert_others += [swap(after(piece, branch), "expert", 1) for piece in far]
    branch = scatter_rows(branch)
    hidden = add_blocks(raise_(sequence), after(branch, expert_up[-1], *expert_others))
    small = dense[:, :, OUTPUT_EDGE:].reshape(model_width, -1)
    expert_counts = counts[:, gain_column + 1 : small_used].reshape(-1)[:expert_total]
    expert_counts = expert_counts.astype(jnp.int32)

    hidden_low = lower(hidden)
    expert_both = expert_pieces + far + expert_others
    order = [0] + list(range(2, len(expert_up))) + [1]
    expert_rows, back, slopes, gateds = {0: hidden_low}, {}, {}, {}
    arriving = {}
    for relative in range(2, owner_count, 2):
        if not forwarded(relative):
            arriving[relative] = swap(hidden_low, "expert", relative)
    before = None
    for chip in order:
        if chip:
            others = [arriving[2]] if chip == order[1] else []
            block = after(arriving[2 * chip], before, *others)
            if chip % 2 == 0 and chip + 1 < len(expert_up):
                arriving[2 * chip + 2] = swap(block, "expert", 2)
            expert_rows[chip] = block
        back[chip], slopes[chip], gateds[chip] = expert_call(
            spots, expert_rows[chip], expert_up[chip], router_local, expert_both
        )
        before = slopes[chip]
    back_terms = send_expert([back[chip] for chip in range(len(order))])
    back_terms = [back_terms[chip] for chip in order]
    expert_rows, slopes, gateds = [
        [found[chip] for chip in range(len(order))] for found in (expert_rows, slopes, gateds)
    ]

    def side_grads(after_spots, side):
        return expert_grads(
            after_spots,
            expert_rows,
            expert_up,
            slopes,
            gateds,
            side,
            group_count,
            tuple(range(group_count)),
        )

    other_grads = side_grads(spots, 1)
    own_grads = side_grads(after(spots, other_grads), 0)
    back_terms[1:] = [after(term, own_grads) for term in back_terms[1:]]

    hidden_grad, hidden_grad_low, router_grad = wide_call(
        functools.partial(hidden_back_kernel, len(back_terms)),
        [scalars] + back_terms + [hidden, upstream, small],
        [
            shaped(model_width, high, row_count),
            shaped(model_width, low, row_count),
            shaped(small_width, high, model_width),
        ],
    )
    hidden_grad_rows = exchange_rows(dp_copies(hidden_grad_low))
    produced = []
    for start in range(0, len(gateds), 4):
        produced += expert_out_call(
            after(spots, hidden_grad_low), expert_both, gateds[start : start + 4]
        )
    moe_terms = send_expert(produced)
    other_grads = swap(after(other_grads, hidden_grad_low), "expert", 1)

    across, along = halving(after(spots, *produced), own_grads, other_grads, row_count)
    across, along = swap(across, "dp", 1), swap(along, "dp", 2)
    layer_out = hidden
    for term in moe_terms:
        layer_out = layer_out + raise_(term)
    layer_out = lower(layer_out)

    scratch = [
        pltpu.VMEM((bucket_rows, HEAD_DIM), low),
        pltpu.VMEM((bucket_rows, small_width), high),
        pltpu.VMEM((bucket_rows, HEAD_DIM), high),
        pltpu.VMEM((bucket_rows, HEAD_DIM), high),
        pltpu.VMEM((bucket_rows, HEAD_DIM), high),
        pltpu.VMEM((bucket_rows, VALUE_WIDTH), low),
        pltpu.VMEM((bucket_rows, QK_EDGE), low),
        pltpu.VMEM((bucket_rows, small_width), low),
        pltpu.VMEM((bucket_rows, model_width), low),
    ]
    made = [dense_shape]
    if chips:
        made = [jax.ShapeDtypeStruct((chips, group_count, part, dense.shape[2]), low)] * 2
    saved.update(
        upstream=hidden_grad_rows, dense=dense, cosine=cosine, sine=sine, router_grad=router_grad
    )
    inputs = [saved[name] for name in BACK]
    terms_shape = shaped(model_width, low)
    *dense_parts, input_terms = staged_call(
        functools.partial(attention_back_kernel, group_count, gain_column, chips),
        [scalars] + inputs + token_blocks,
        made + [terms_shape],
        inputs + [dense_shape, terms_shape, terms_shape],
        scratch,
        len(inputs) + 2 * group_count + 3 * owner_count,
    )

    if not chips:
        dense_grad = dense_parts[0].reshape(group_count, owner_count, part, -1)
        dense_parts = [
            jnp.stack(
                [
                    lax.dynamic_index_in_dim(dense_grad, owner ^ relative, 1, keepdims=False)
                    for relative in range(side, owner_count, 2)
                ]
            )
            for side in range(2)
        ]
    late = after(spots, input_terms)
    first, second = halved(late, own_grads, other_grads, across, along)
    dense_parts[1] = after(dense_parts[1], first, second, *moe_terms)
    dense_parts = join(spots, dense_parts[0], swap(dense_parts[1], "expert", 1))
    first, second = swap(first, "dp", 2), swap(second, "dp", 1)
    input_grad = add_blocks(hidden_grad, scatter_rows(input_terms))
    dense_terms = send_expert(dense_parts)
    dense_terms[1:] = [after(term, input_grad, first, second) for term in dense_terms[1:]]
    dense_sums = wide_call(
        dense_sum_kernel,
        [scalars] + dense_terms,
        [jax.ShapeDtypeStruct(dense_terms[0].shape[1:], low)] * group_count,
    )
    dense_sums = [dense_sums[0]] + [
        swap(dense_sums[relative], "dp", relative) for relative in range(1, group_count)
    ]
    masters = [
        (qk_weight, qk_first, qk_second),
        (value_weight, value_first, value_second),
        (output_weight, output_first, output_second),
        (select_weight, select_first, select_second),
        (router_weight, router_first, router_second),
        (gain_weight[None], gain_first[None], gain_second[None]),
    ]
    masters = [array for group in masters for array in group]
    updated = wide_call(
        dense_update_kernel,
        [scalars] + dense_sums + masters,
        [jax.ShapeDtypeStruct(array.shape, high) for array in masters],
    )
    updated = list(updated[:15]) + [array[0] for array in updated[15:]]
    expert_results = expert_update(
        [
            [(own_grads, 1), (other_grads, 1), (across, 0), (first, 0)],
            [(own_grads, 1), (other_grads, 1), (along, 0), (second, 0)],
        ],
        expert_weight,
        expert_first,
        expert_second,
    )
    return (layer_out[None], input_grad[None], *updated, *expert_results, expert_counts)


def solution(mesh):
    placed = (
        P("expert", "dp", None),
        P("expert", "dp", None),
        P("expert"),
        P("expert", "dp", None, None),
        P("expert", "dp", None),
        P(("dp", "expert"), None),
        P(("dp", "expert"), None),
        P(("dp", "expert"), None),
        P(("dp", "expert"), None),
        P(("dp", "expert"), None),
        P(("dp", "expert"), None),
        P(("dp", "expert"), None),
        P(("dp", "expert"), None),
        P(("dp", "expert"), None),
        P(("dp", "expert"), None),
        P(("dp", "expert"), None),
        P(("dp", "expert"), None),
        P(("dp", "expert"), None),
        P(("dp", "expert"), None),
        P(("dp", "expert"), None),
        P(("dp", "expert")),
        P(("dp", "expert")),
        P(("dp", "expert")),
        P("expert", "dp", None),
        P("expert", "dp", None),
        P("expert", "dp", None),
    )
    return jax.shard_map(
        local,
        mesh=mesh,
        in_specs=placed,
        out_specs=(
            P("expert", "dp", None),
            P("expert", "dp", None),
            P(("dp", "expert"), None),
            P(("dp", "expert"), None),
            P(("dp", "expert"), None),
            P(("dp", "expert"), None),
            P(("dp", "expert"), None),
            P(("dp", "expert"), None),
            P(("dp", "expert"), None),
            P(("dp", "expert"), None),
            P(("dp", "expert"), None),
            P(("dp", "expert"), None),
            P(("dp", "expert"), None),
            P(("dp", "expert"), None),
            P(("dp", "expert"), None),
            P(("dp", "expert"), None),
            P(("dp", "expert"), None),
            P(("dp", "expert")),
            P(("dp", "expert")),
            P(("dp", "expert")),
            P("expert", "dp", None),
            P("expert", "dp", None),
            P("expert", "dp", None),
            P(),
        ),
        check_vma=False,
    )
```

```python
import functools

import numpy as np
import jax
import jax.numpy as jnp
from jax import lax
from jax.experimental import pallas as pl
from jax.experimental.pallas import tpu as pltpu
from jax.sharding import PartitionSpec as P

HEADS = 4
HEAD_DIM = 128
ATT_EXPERTS = 5
EXPERT_H = 128
TOPK = 16
STEP = 10


norm_eps = 1e-05
beta_first = 0.9
beta_second = 0.95
adam_eps = 1e-08
weight_decay = 0.1
masked_score = -1e30
rope_base = 10000.0
rate_query_key = 0.04
rate_value = 0.03
rate_output = 2.0
rate_select = 0.03
rate_router = 0.015
rate_gain = 1.2
rate_expert = 0.05


def product(former, latter):
    return jnp.dot(former, latter, preferred_element_type=jnp.float32)


def product_rows(former, latter):
    return lax.dot_general(
        former, latter, (((0,), (0,)), ((), ())), preferred_element_type=jnp.float32
    )


def product_last(former, latter):
    return lax.dot_general(
        former, latter, (((1,), (1,)), ((), ())), preferred_element_type=jnp.float32
    )


def rope_tables(rows):
    half = HEAD_DIM // 2
    frequency = np.exp(-np.log(rope_base) * np.arange(half) / half)
    angles = np.arange(rows)[:, None] * frequency[None, :]
    cosine, sine = np.cos(angles), np.sin(angles)
    return (
        jnp.asarray(np.concatenate([cosine, cosine], axis=1), jnp.float32),
        jnp.asarray(np.concatenate([-sine, sine], axis=1), jnp.float32),
    )


def adamw_update(weight, first_moment, second_moment, gradient, rate):
    first_new = beta_first * first_moment + (1.0 - beta_first) * gradient
    second_new = beta_second * second_moment + (1.0 - beta_second) * gradient * gradient
    first_hat = first_new / (1.0 - beta_first**STEP)
    second_hat = second_new / (1.0 - beta_second**STEP)
    weight_new = weight - rate * (
        first_hat / (jnp.sqrt(second_hat) + adam_eps) + weight_decay * weight
    )
    return (weight_new, first_new, second_new)


LIGHT = pl.CostEstimate(flops=1000, bytes_accessed=1000, transcendentals=0)


def swap(values, axis, relative):
    count = lax.axis_size(axis)
    return lax.ppermute(values, axis, [(place, place ^ relative) for place in range(count)])


def lower(values):
    return values.astype(jnp.bfloat16)


def raise_(values):
    return values.astype(jnp.float32)


def after(values, *others):
    return lax.optimization_barrier((values,) + others)[0]


def exchange_rows(copies):
    blocks = lax.all_to_all(copies, "dp", split_axis=0, concat_axis=0, tiled=True)
    return blocks.reshape((-1,) + copies.shape[2:])


def scatter_rows(values):
    count = lax.axis_size("dp")
    blocks = values.reshape((count, values.shape[0] // count) + values.shape[1:])
    return lax.all_to_all(blocks, "dp", split_axis=0, concat_axis=0, tiled=True)


def add_blocks(values, blocks):
    for index in range(blocks.shape[0]):
        values = values + raise_(blocks[index])
    return values


def join_kernel(scalars, evens, odds, *results):
    for chip, result in enumerate(results):
        result[...] = lower(raise_(evens[chip]) + raise_(odds[chip]))


def join(scalars, evens, odds):
    shape = jax.ShapeDtypeStruct(evens.shape[1:], jnp.bfloat16)
    return list(wide_call(join_kernel, [scalars, evens, odds], [shape] * evens.shape[0]))


def forwarded(relative):
    return relative & 2 and relative > 2


def gather_chips(values):
    return [values] + [
        swap(values, "expert", relative) for relative in range(2, lax.axis_size("expert"), 2)
    ]


def send_expert(joined):
    return [joined[0]] + [
        swap(term, "expert", 2 * index) for index, term in enumerate(joined) if index
    ]


def full(shape):
    return pl.BlockSpec(shape, lambda *_: (0,) * len(shape))


def wide_call(kernel, inputs, outputs, limit=56):
    specs = [pl.BlockSpec(memory_space=pltpu.SMEM)] + [full(value.shape) for value in inputs[1:]]
    return pl.pallas_call(
        kernel,
        grid=(1,),
        in_specs=specs,
        out_specs=[full(value.shape) for value in outputs],
        out_shape=outputs,
        compiler_params=pltpu.CompilerParams(vmem_limit_bytes=limit * 2**20),
        cost_estimate=LIGHT,
    )(*inputs)


class Copies:
    def __init__(self, sems):
        self.sems, self.count, self.waiting = sems, 0, {}

    def start(self, name, source, target):
        copy = pltpu.make_async_copy(source, target, self.sems.at[self.count])
        copy.start()
        self.count += 1
        self.waiting.setdefault(name, []).append(copy)

    def wait(self, *names):
        for name in names:
            for copy in self.waiting.pop(name, []):
                copy.wait()


def staged_call(kernel, inputs, outputs, held, scratch, copies):
    somewhere = pl.BlockSpec(memory_space=pl.ANY)
    return pl.pallas_call(
        kernel,
        grid=(1,),
        in_specs=[pl.BlockSpec(memory_space=pltpu.SMEM)] + [somewhere] * (len(inputs) - 1),
        out_specs=[somewhere] * len(outputs),
        out_shape=outputs,
        scratch_shapes=[pltpu.VMEM(value.shape, value.dtype) for value in held]
        + list(scratch)
        + [pltpu.SemaphoreType.DMA((copies,))],
        compiler_params=pltpu.CompilerParams(vmem_limit_bytes=56 * 2**20),
        cost_estimate=LIGHT,
    )(*inputs)


def shift_table(rows, columns, offset, count):
    source = lax.broadcasted_iota(jnp.int32, (rows, columns), 0)
    target = lax.broadcasted_iota(jnp.int32, (rows, columns), 1)
    return lower(jnp.where((source == target + offset) & (target < count), 1.0, 0.0))


def moments(values):
    center = values - jnp.mean(values, axis=-1, keepdims=True)
    inverse = lax.rsqrt(jnp.mean(center * center, axis=-1, keepdims=True) + norm_eps)
    return center * inverse, inverse


def turn(rows, cosine, signed_sine, direction):
    return rows * cosine + direction * pltpu.roll(rows, HEAD_DIM // 2, 1) * signed_sine


def masked_scores(queries, key_rows, seq_len, start):
    scores = product_last(queries, key_rows) * HEAD_DIM ** (-0.5)
    query_place = start + lax.broadcasted_iota(jnp.int32, scores.shape, 0)
    key_place = lax.broadcasted_iota(jnp.int32, scores.shape, 1)
    return jnp.where((key_place <= query_place) & (key_place < seq_len), scores, masked_score)


VALUE_WIDTH = ATT_EXPERTS * HEAD_DIM
QK_EDGE = 2 * HEAD_DIM
VALUE_EDGE = QK_EDGE + VALUE_WIDTH
OUTPUT_EDGE = VALUE_EDGE + VALUE_WIDTH
SELECT_COUNT = 2 * ATT_EXPERTS


KEPT = ("queries", "key_rows", "values", "weighting", "projected", "attended", "mixed", "log_total")


def attention_kernel(blocks, gain_column, chips, local_count, scalars, *refs):
    given = blocks + 2 + (chips + 1 if chips else 1)
    outs = (["dense"] if chips else []) + list(KEPT) + ["branch", "router_local", "counts"]
    count = len(outs)
    sources, targets = refs[:given], dict(zip(outs, refs[given : given + count]))
    tokens, (cosine, sine, dense), refs = (
        refs[given + count : given + count + blocks],
        refs[given + count + blocks : given + count + blocks + 3],
        refs[given + count + blocks + 3 : -1] + refs[-1:],
    )
    *kept, branch, router_local, counts, sems = refs
    (queries, key_rows, values, weighting, projected, attended, mixed, log_total) = kept
    copies = Copies(sems)
    for index in range(blocks):
        copies.start("in", sources[index], tokens[index])
    copies.start("in", sources[blocks], cosine)
    copies.start("in", sources[blocks + 1], sine)
    if chips:
        evens, odds = sources[blocks + 2 : blocks + 2 + chips], sources[blocks + 2 + chips]
        part = odds.shape[2]
        for chip in range(chips):
            for other, rows in ((0, evens[chip]), (1, odds.at[chip])):
                start = (scalars[2] ^ (2 * chip + other)) * part
                copies.start("in", rows, dense.at[:, pl.ds(pl.multiple_of(start, part), part), :])
    else:
        copies.start("in", sources[blocks + 2], dense)
    copies.wait("in")
    if chips:
        copies.start("out", dense, targets["dense"])
    place, seq_len = scalars[0], scalars[1]
    width = dense.shape[0] * dense.shape[1]
    block = tokens[0].shape[0]

    def weight(start, end):
        return dense[:, :, start:end].reshape(width, end - start)

    small_rows = weight(OUTPUT_EDGE, dense.shape[2])
    count = local_count
    source = lax.broadcasted_iota(jnp.int32, (small_rows.shape[1], router_local.shape[1]), 0)
    entry = lax.broadcasted_iota(jnp.int32, source.shape, 1)
    first = SELECT_COUNT + scalars[2] * count + entry
    second = SELECT_COUNT + (scalars[2] ^ 1) * count + entry - count
    table = (source == jnp.where(entry < count, first, second)) & (entry < 2 * count)
    router_local[...] = lower(product(small_rows, lower(jnp.where(table, 1.0, 0.0))))
    part = counts.shape[0]
    total = raise_(small_rows[:part])
    for start in range(part, width, part):
        total += raise_(small_rows[start : start + part])
    counts[...] = total
    copies.start("out", counts, targets["counts"])
    copies.start("out", router_local, targets["router_local"])
    gain = raise_(small_rows).T[gain_column : gain_column + 1, :]
    head_table = shift_table(
        tokens[0].shape[1] - width, dense.shape[2] - OUTPUT_EDGE, place * SELECT_COUNT, SELECT_COUNT
    )
    for index in range(blocks):
        span = pl.ds(pl.multiple_of((place ^ index) * block, block), block)
        rows = tokens[index][:, :width]
        scaled, _ = moments(raise_(rows))
        normed_rows = lower(scaled * gain)
        both = product(normed_rows, weight(0, QK_EDGE))
        queries[span, :] = lower(turn(both[:, :HEAD_DIM], cosine[span, :], sine[span, :], 1.0))
        key_rows[span, :] = lower(turn(both[:, HEAD_DIM:], cosine[span, :], sine[span, :], 1.0))
        chosen = product(tokens[index][:, width:], head_table)
        sigma_rows = jax.nn.sigmoid(product(normed_rows, small_rows))
        weights = sigma_rows * chosen
        weighting[span, :] = weights
        columns = product(rows, weight(QK_EDGE, VALUE_EDGE))
        projected[span, :] = columns
        total = weights[:, 0:1] * columns[:, :HEAD_DIM]
        for expert in range(1, ATT_EXPERTS):
            total += (
                weights[:, expert : expert + 1]
                * columns[:, expert * HEAD_DIM : (expert + 1) * HEAD_DIM]
            )
        values[span, :] = lower(total)
    for name, ref in zip(KEPT[:5], kept):
        copies.start("out", ref, targets[name])
    for start in range(0, blocks * block, block):
        span = pl.ds(start, block)
        scores = masked_scores(queries[span, :], key_rows[...], seq_len, start)
        highest = jnp.max(scores, axis=-1, keepdims=True)
        raised = jnp.exp(scores - highest)
        row_total = jnp.sum(raised, axis=-1, keepdims=True)
        log_total[span, :] = jnp.broadcast_to(highest + jnp.log(row_total), (block, HEAD_DIM))
        rows = product(lower(raised / row_total), values[...])
        attended[span, :] = rows
        weights = weighting[span, :]
        for expert in range(ATT_EXPERTS):
            mixed[span, pl.ds(expert * HEAD_DIM, HEAD_DIM)] = lower(
                weights[:, ATT_EXPERTS + expert : ATT_EXPERTS + expert + 1] * rows
            )
        branch[span, :] = lower(product_last(mixed[span, :], weight(VALUE_EDGE, OUTPUT_EDGE)))
        for name, ref in (("mixed", mixed), ("branch", branch)):
            copies.start("out", ref.at[span, :], targets[name].at[span, :])
    copies.start("out", attended, targets["attended"])
    copies.start("out", log_total, targets["log_total"])
    copies.wait("out")


BACK = ("upstream", "dense", "weighting", "attended", "mixed", "queries", "key_rows", "values") + (
    "log_total",
    "projected",
    "cosine",
    "sine",
    "router_grad",
)


def attention_back_kernel(blocks, gain_column, chips, scalars, *refs):
    count = len(BACK)
    sources, token_blocks, refs = refs[:count], refs[count : count + blocks], refs[count + blocks :]
    results, out_terms, refs = refs[: 2 if chips else 1], refs[2 if chips else 1], refs[3 if chips else 2 :]
    held, (grads, terms, tokens), refs = refs[:count], refs[count : count + 3], refs[count + 3 :]
    (upstream, dense, weighting, attended, mixed, queries, key_rows, values, log_total) = held[:9]
    projected, cosine, sine, router_grad = held[9:]
    (attended_grad, weight_grad, key_grad, value_grad, query_grad) = refs[:5]
    projected_grad, pair_grad, select_grad, normed, sems = refs[5:]
    copies = Copies(sems)
    for name, source, target in zip(BACK, sources, held):
        copies.start(name, source, target)
    block = token_blocks[0].shape[0]
    for index, rows in enumerate(token_blocks):
        span = pl.ds(pl.multiple_of((scalars[0] ^ index) * block, block), block)
        copies.start("tokens", rows.at[:, pl.ds(0, tokens.shape[1])], tokens.at[span, :])

    def weight(start, end):
        return dense[:, :, start:end].reshape(tokens.shape[1], end - start)

    def leave(columns):
        if not chips:
            copies.start("out", grads.at[:, :, columns], results[0].at[:, :, columns])
            return
        part = results[0].shape[2]
        for relative in range(2 * chips):
            start = pl.multiple_of((scalars[2] ^ relative) * part, part)
            target = results[relative % 2].at[relative // 2, :, :, columns]
            copies.start("out", grads.at[:, pl.ds(start, part), columns], target)

    def keep(start, values):
        columns = pl.ds(start, values.shape[1])
        grads[:, :, columns] = values.reshape(grads.shape[:2] + values.shape[1:])

    copies.wait("upstream", "dense", "weighting", "attended")
    seq_len = scalars[1]
    width = tokens.shape[1]
    small = dense.shape[2] - OUTPUT_EDGE
    lane = lax.broadcasted_iota(jnp.int32, (block, small), 1)
    scale = HEAD_DIM ** (-0.5)
    gain = raise_(weight(OUTPUT_EDGE, dense.shape[2])).T[gain_column : gain_column + 1, :]
    for start in range(0, tokens.shape[0], block):
        span = pl.ds(start, block)
        mixed_grad = product(upstream[span, :], weight(VALUE_EDGE, OUTPUT_EDGE))
        weights = weighting[span, :]
        heads = attended[span, :]
        total = jnp.zeros((block, HEAD_DIM), jnp.float32)
        found = jnp.zeros((block, small), jnp.float32)
        for expert in range(ATT_EXPERTS):
            piece = mixed_grad[:, expert * HEAD_DIM : (expert + 1) * HEAD_DIM]
            column = ATT_EXPERTS + expert
            total += weights[:, column : column + 1] * piece
            found = jnp.where(lane == column, jnp.sum(piece * heads, axis=1, keepdims=True), found)
        attended_grad[span, :] = lower(total)
        weight_grad[span, :] = found
    copies.wait("mixed")
    keep(VALUE_EDGE, lower(product_rows(upstream[...], mixed[...])))
    leave(pl.ds(VALUE_EDGE, OUTPUT_EDGE - VALUE_EDGE))
    copies.wait("queries", "key_rows", "values", "log_total")
    for start in range(0, tokens.shape[0], block):
        span = pl.ds(start, block)
        scores = masked_scores(queries[span, :], key_rows[...], seq_len, start)
        probs = jnp.exp(scores - log_total[span, :1])
        prob_grad = product_last(attended_grad[span, :], values[...])
        delta = jnp.sum(probs * prob_grad, axis=-1, keepdims=True)
        score_grad = lower(probs * (prob_grad - delta))
        query_grad[span, :] = product(score_grad, key_rows[...]) * scale
        key_terms = product_rows(score_grad, queries[span, :])
        value_terms = product_rows(lower(probs), attended_grad[span, :])
        if start:
            key_grad[...] += key_terms
            value_grad[...] += value_terms
        else:
            key_grad[...] = key_terms
            value_grad[...] = value_terms
    copies.wait("projected", "cosine", "sine", "router_grad", "tokens")
    gain_grad = jnp.zeros((1, width), jnp.float32)
    for start in range(0, tokens.shape[0], block):
        span = pl.ds(start, block)
        rows = value_grad[span, :]
        weights = weighting[span, :]
        found = weight_grad[span, :]
        for expert in range(ATT_EXPERTS):
            piece = pl.ds(expert * HEAD_DIM, HEAD_DIM)
            projected_grad[span, piece] = lower(weights[:, expert : expert + 1] * rows)
            found = jnp.where(
                lane == expert,
                jnp.sum(rows * projected[span, piece], axis=1, keepdims=True),
                found,
            )
        pair_grad[span, :HEAD_DIM] = lower(
            turn(query_grad[span, :], cosine[span, :], sine[span, :], -1.0)
        )
        pair_grad[span, HEAD_DIM:] = lower(
            turn(key_grad[span, :] * scale, cosine[span, :], sine[span, :], -1.0)
        )
        select_rows = lower(found * weights * (1.0 - weights))
        select_grad[span, :] = select_rows
        normed_grad = product_last(pair_grad[span, :], weight(0, QK_EDGE)) + product_last(
            select_rows, weight(OUTPUT_EDGE, dense.shape[2])
        )
        scaled, inverse = moments(raise_(tokens[span, :]))
        normed[span, :] = lower(scaled * gain)
        gain_grad += jnp.sum(normed_grad * scaled, axis=0, keepdims=True)
        through = normed_grad * gain
        norm_grad = inverse * (
            through
            - jnp.mean(through, axis=-1, keepdims=True)
            - scaled * jnp.mean(through * scaled, axis=-1, keepdims=True)
        )
        terms[span, :] = lower(
            product_last(projected_grad[span, :], weight(QK_EDGE, VALUE_EDGE)) + norm_grad
        )
        copies.start("out", terms.at[span, :], out_terms.at[span, :])
    keep(QK_EDGE, lower(product_rows(tokens[...], projected_grad[...])))
    keep(0, lower(product_rows(normed[...], pair_grad[...])))
    row = lax.broadcasted_iota(jnp.int32, (small, width), 0)
    gain_part = jnp.where(row == gain_column, gain_grad, 0.0).T
    rest = product_rows(normed[...], select_grad[...]) + gain_part + router_grad[...]
    keep(OUTPUT_EDGE, lower(rest))
    leave(pl.ds(0, VALUE_EDGE))
    leave(pl.ds(OUTPUT_EDGE, small))
    copies.wait("out")


def piece_copies(place, pieces, target, columns, sems):
    part, last = pieces[0].shape[0], len(pieces) - 2
    half = part // 2
    copies = []
    for index, piece in enumerate(pieces):
        start = (place ^ min(index, last)) * part + (half if index > last else 0)
        rows = pl.ds(pl.multiple_of(start, half), piece.shape[0])
        source = piece.at[:, columns]
        copies.append(pltpu.make_async_copy(source, target.at[rows, :], sems.at[index]))
    return copies


def expert_kernel(pieces, scalars, rows, up, router, *refs):
    weights = refs[: 2 * pieces]
    back, slope, gated, insides, outsides, sems = refs[2 * pieces :]
    block, width = rows.shape
    hidden = slope.shape[1] // 2
    count = hidden // EXPERT_H
    copies = []
    for side in range(2):
        own = weights[side * pieces : (side + 1) * pieces]
        copies.append(
            piece_copies(scalars[0], own, insides.at[side], pl.ds(0, hidden), sems.at[side, 0])
            + piece_copies(
                scalars[0], own, outsides.at[side], pl.ds(hidden, hidden), sems.at[side, 1]
            )
        )
        for copy in copies[side]:
            copy.start()
    small = up.shape[1] - width
    lanes = router.shape[1]
    offsets = [SELECT_COUNT + (scalars[1] ^ index) * count for index in range(2)]

    def column_of(entry):
        return jnp.where(entry < count, offsets[0] + entry, offsets[1] + entry - count)

    source = lax.broadcasted_iota(jnp.int32, (small, lanes), 0)
    entry = lax.broadcasted_iota(jnp.int32, (small, lanes), 1)
    pick_table = lower(jnp.where((source == column_of(entry)) & (entry < 2 * count), 1.0, 0.0))
    entry = lax.broadcasted_iota(jnp.int32, (lanes, small), 0)
    target = lax.broadcasted_iota(jnp.int32, (lanes, small), 1)
    place_table = lower(jnp.where((target == column_of(entry)) & (entry < 2 * count), 1.0, 0.0))
    lane = lax.broadcasted_iota(jnp.int32, (block, lanes), 1)
    scaled, _ = moments(raise_(rows[...]))
    sigma_gate = jax.nn.sigmoid(product(lower(scaled), router[...]))
    gates = sigma_gate * product(up[:, width:], pick_table)
    found = jnp.zeros((block, lanes), jnp.float32)
    for first in range(0, 2 * count, 2):
        side = first // count
        if first % count == 0:
            for copy in copies[side]:
                copy.wait()
        local = pl.ds(first % count * EXPERT_H, 2 * EXPERT_H)
        inner = product(rows[...], insides[side, :, local])
        terms = product(up[:, :width], outsides[side, :, local])
        sigma = jax.nn.sigmoid(inner)
        silu = inner * sigma
        active = raise_(lower(silu))
        both = terms * active
        tilt = sigma + silu * (1.0 - sigma)
        for k in range(2):
            part = slice(k * EXPERT_H, (k + 1) * EXPERT_H)
            columns = pl.ds((first + k) * EXPERT_H, EXPERT_H)
            gate = gates[:, first + k : first + k + 1]
            gated[:, columns] = lower(gate * active[:, part])
            slope[:, columns] = lower(gate * terms[:, part] * tilt[:, part])
            summed = jnp.sum(both[:, part], axis=1, keepdims=True)
            found = jnp.where(lane == first + k, summed, found)
    back[:, :width] = lower(
        product_last(slope[:, :hidden], insides[0]) + product_last(slope[:, hidden:], insides[1])
    )
    back[:, width:] = lower(product(lower(found * gates * (1.0 - sigma_gate)), place_table))


def expert_call(scalars, rows, up, router, weights):
    block, width = rows.shape
    hidden = weights[0].shape[1] // 2
    pieces = len(weights) // 2
    outputs = [
        jax.ShapeDtypeStruct(up.shape, jnp.bfloat16),
        jax.ShapeDtypeStruct((block, 2 * hidden), jnp.bfloat16),
        jax.ShapeDtypeStruct((block, 2 * hidden), jnp.bfloat16),
    ]
    return pl.pallas_call(
        functools.partial(expert_kernel, pieces),
        grid=(1,),
        in_specs=[pl.BlockSpec(memory_space=pltpu.SMEM)]
        + [full(value.shape) for value in (rows, up, router)]
        + [pl.BlockSpec(memory_space=pl.ANY)] * len(weights),
        out_specs=[full(value.shape) for value in outputs],
        out_shape=outputs,
        scratch_shapes=[
            pltpu.VMEM((2, width, hidden), jnp.bfloat16),
            pltpu.VMEM((2, width, hidden), jnp.bfloat16),
            pltpu.SemaphoreType.DMA((2, 2, pieces)),
        ],
        compiler_params=pltpu.CompilerParams(vmem_limit_bytes=56 * 2**20),
        cost_estimate=LIGHT,
    )(scalars, rows, up, router, *weights)


def expert_grad_kernel(chips, indices, scalars, *refs):
    rows = refs[:chips]
    ups = refs[chips : 2 * chips]
    slopes = refs[2 * chips : 3 * chips]
    gateds = refs[3 * chips : 4 * chips]
    grads = refs[4 * chips]
    part = grads.shape[0] // len(indices)
    half = pl.num_programs(0) // 2

    def total(lefts, rights):
        for place, index in enumerate(indices):
            columns = pl.ds(pl.multiple_of((scalars[0] ^ index) * part, part), part)
            result = product_rows(lefts[0][:, columns], rights[0][...])
            for left, right in zip(lefts[1:], rights[1:]):
                result += product_rows(left[:, columns], right[...])
            grads[pl.ds(place * part, part), :] = lower(result)

    @pl.when(pl.program_id(0) < half)
    def _():
        total(rows, slopes)

    @pl.when(pl.program_id(0) >= half)
    def _():
        total(ups, gateds)


def expert_grads(scalars, rows, ups, slopes, gateds, side, blocks, indices):
    chips = len(slopes)
    block, width = rows[0].shape
    hidden = slopes[0].shape[1] // 2
    tile = min(512, hidden)
    half = hidden // tile
    once = pl.Buffered(buffer_count=1)
    first = side * half
    rows_out = width // blocks * len(indices)
    return pl.pallas_call(
        functools.partial(expert_grad_kernel, chips, indices),
        grid=(2 * half,),
        in_specs=[pl.BlockSpec(memory_space=pltpu.SMEM)]
        + [pl.BlockSpec(v.shape, lambda j: (0, 0), pipeline_mode=once) for v in rows + ups]
        + [pl.BlockSpec((block, tile), lambda j: (0, first + jnp.minimum(j, half - 1)))] * chips
        + [pl.BlockSpec((block, tile), lambda j: (0, first + jnp.maximum(j - half, 0)))] * chips,
        out_specs=pl.BlockSpec((rows_out, tile), lambda j: (0, j)),
        out_shape=jax.ShapeDtypeStruct((rows_out, 2 * hidden), jnp.bfloat16),
        compiler_params=pltpu.CompilerParams(vmem_limit_bytes=56 * 2**20),
        cost_estimate=LIGHT,
    )(scalars, *rows, *ups, *slopes, *gateds)


def expert_out_kernel(pieces, scalars, *refs):
    weights, refs = refs[: 2 * pieces], refs[2 * pieces :]
    count = (len(refs) - 5) // 2
    gateds, results = refs[:count], refs[count : 2 * count]
    outsides, lefts, held, sems, gated_sems = refs[2 * count :]
    hidden = outsides.shape[2]
    block, width = results[0].shape
    tile = min(256, width)
    copies = []
    for side in range(2):
        own = weights[side * pieces : (side + 1) * pieces]
        columns = pl.ds(hidden, hidden)
        started = piece_copies(scalars[0], own, outsides.at[side], columns, sems.at[side])
        for index, gated in enumerate(gateds):
            source = gated.at[:, pl.ds(side * hidden, hidden)]
            target = lefts.at[side, pl.ds(index * block, block), :]
            started.append(pltpu.make_async_copy(source, target, gated_sems.at[side, index]))
        for copy in started:
            copy.start()
        copies.append(started)
    for side in range(2):
        for copy in copies[side]:
            copy.wait()
        for start in range(0, width, tile):
            columns = pl.ds(start, tile)
            total = product_last(lefts[side], outsides[side, columns, :])
            if side == 0:
                held[:, columns] = total
            else:
                total += held[:, columns]
                for index, result in enumerate(results):
                    result[:, columns] = lower(total[index * block : (index + 1) * block])


def expert_out_call(scalars, weights, gateds):
    pieces, count = len(weights) // 2, len(gateds)
    hidden = weights[0].shape[1] // 2
    width = sum(weight.shape[0] for weight in weights[:pieces])
    block = gateds[0].shape[0]
    return pl.pallas_call(
        functools.partial(expert_out_kernel, pieces),
        grid=(1,),
        in_specs=[pl.BlockSpec(memory_space=pltpu.SMEM)]
        + [pl.BlockSpec(memory_space=pl.ANY)] * (len(weights) + count),
        out_specs=[full((block, width))] * count,
        out_shape=[jax.ShapeDtypeStruct((block, width), jnp.bfloat16)] * count,
        scratch_shapes=[
            pltpu.VMEM((2, width, hidden), jnp.bfloat16),
            pltpu.VMEM((2, count * block, hidden), jnp.bfloat16),
            pltpu.VMEM((count * block, width), jnp.float32),
            pltpu.SemaphoreType.DMA((2, pieces)),
            pltpu.SemaphoreType.DMA((2, count)),
        ],
        compiler_params=pltpu.CompilerParams(vmem_limit_bytes=56 * 2**20),
        cost_estimate=LIGHT,
    )(scalars, *weights, *gateds)


def hidden_back_kernel(count, scalars, *refs):
    terms = refs[:count]
    hidden, upstream, small, hidden_grad, hidden_grad_low, router_grad = refs[count:]
    width = hidden.shape[1]
    total = raise_(terms[0][...])
    for term in terms[1:]:
        total += raise_(term[...])
    logit_grad = lower(total[:, width:])
    scaled, inverse = moments(hidden[...])
    router_grad[...] = product_rows(lower(scaled), logit_grad)
    through = product_last(logit_grad, small[...])
    norm_grad = inverse * (
        through
        - jnp.mean(through, axis=-1, keepdims=True)
        - scaled * jnp.mean(through * scaled, axis=-1, keepdims=True)
    )
    result = raise_(upstream[:, :width]) + total[:, :width] + norm_grad
    hidden_grad[...] = result
    for index in range(hidden_grad_low.shape[0]):
        hidden_grad_low[index] = lower(result)


def expert_update_kernel(terms, *refs):
    grads = refs[: 2 * terms]
    weight, first, second, new, first_new, second_new = refs[2 * terms :]
    for half in range(2):
        for expert in range(weight.shape[0]):
            source = pl.ds(expert * EXPERT_H, EXPERT_H)
            columns = pl.ds(half * EXPERT_H, EXPERT_H)
            total = raise_(grads[half * terms][:, source])
            for grad in grads[half * terms + 1 : (half + 1) * terms]:
                total += raise_(grad[:, source])
            results = adamw_update(
                weight[expert, :, columns],
                first[expert, :, columns],
                second[expert, :, columns],
                total,
                rate_expert,
            )
            for target, result in zip((new, first_new, second_new), results):
                target[expert, :, columns] = result


def expert_update(grads, weight, first, second):
    count, rows, columns = weight.shape
    some = 3 if count % 3 == 0 else 1
    steps = count // some
    whole = pl.BlockSpec((some, rows, columns), lambda e: (e, 0, 0))
    shape = jax.ShapeDtypeStruct(weight.shape, jnp.float32)
    specs = [
        pl.BlockSpec(
            (rows, some * EXPERT_H), lambda e, start=half * steps * both: (0, start + e)
        )
        for half in range(2)
        for _, both in grads[half]
    ]
    return pl.pallas_call(
        functools.partial(expert_update_kernel, len(grads[0])),
        grid=(steps,),
        in_specs=specs + [whole] * 3,
        out_specs=[whole] * 3,
        out_shape=[shape] * 3,
        compiler_params=pltpu.CompilerParams(vmem_limit_bytes=56 * 2**20),
        cost_estimate=LIGHT,
    )(*[grad for half in grads for grad, _ in half], weight, first, second)


def halving_kernel(scalars, *refs):
    across, along = refs[8:]
    rows = across.shape[0] // 2
    for index in range(4):
        target, half = (across, along)[index // 2], pl.ds(index % 2 * rows, rows)
        target[half, :] = lower(raise_(refs[2 * index][...]) + raise_(refs[2 * index + 1][...]))


def halving(scalars, own, other, rows):
    columns = own.shape[1] // 2
    specs = []
    for row, column in ((1, 0), (3, 0), (2, 1), (3, 1)):
        specs += [pl.BlockSpec((rows, columns), lambda i, row=row, column=column: (row, column))] * 2
    shape = jax.ShapeDtypeStruct((2 * rows, columns), jnp.bfloat16)
    return pl.pallas_call(
        halving_kernel,
        grid=(1,),
        in_specs=[pl.BlockSpec(memory_space=pltpu.SMEM)] + specs,
        out_specs=[full(shape.shape)] * 2,
        out_shape=[shape] * 2,
        compiler_params=pltpu.CompilerParams(vmem_limit_bytes=56 * 2**20),
        cost_estimate=LIGHT,
    )(scalars, *[own, other] * 4)


def halved_kernel(scalars, own_two, other_two, own_one, other_one, across, along, first, second):
    first[...] = lower(raise_(own_two[...]) + raise_(other_two[...]) + raise_(across[...]))
    second[...] = lower(raise_(own_one[...]) + raise_(other_one[...]) + raise_(along[...]))


def halved(scalars, own, other, across, along):
    rows, columns = across.shape[0] // 2, across.shape[1]

    def block(row, column):
        return pl.BlockSpec((rows, columns), lambda i: (row, column))

    return pl.pallas_call(
        halved_kernel,
        grid=(1,),
        in_specs=[pl.BlockSpec(memory_space=pltpu.SMEM)]
        + [block(2, 0), block(2, 0), block(1, 1), block(1, 1), block(1, 0), block(1, 0)],
        out_specs=[block(0, 0)] * 2,
        out_shape=[jax.ShapeDtypeStruct((rows, columns), jnp.bfloat16)] * 2,
        compiler_params=pltpu.CompilerParams(vmem_limit_bytes=56 * 2**20),
        cost_estimate=LIGHT,
    )(scalars, own, other, own, other, across, along)


def dense_sum_kernel(scalars, *refs):
    count = refs[0].shape[0]
    terms, results = refs[:-count], refs[-count:]
    for index, result in enumerate(results):
        spot = scalars[0] ^ index
        total = raise_(terms[0][spot])
        for term in terms[1:]:
            total += raise_(term[spot])
        result[...] = lower(total)


def dense_update_kernel(scalars, *refs):
    sums, refs = refs[:HEADS], refs[HEADS:]
    inputs = [refs[3 * index : 3 * index + 3] for index in range(6)]
    outputs = [refs[3 * index : 3 * index + 3] for index in range(6, 12)]

    def update(index, gradient, columns, rate):
        results = adamw_update(*[ref[:, columns] for ref in inputs[index]], gradient, rate)
        for target, result in zip(outputs[index], results):
            target[:, columns] = result

    part, small = sums[0].shape[0], sums[0].shape[1] - OUTPUT_EDGE
    shared = jnp.zeros((part, small), jnp.float32)
    chosen = jnp.zeros((part, inputs[3][0].shape[1]), jnp.float32)
    for index, rows in enumerate(sums):
        head = scalars[0] ^ index
        for side in range(2):
            span = pl.ds(pl.multiple_of((side * HEADS + head) * HEAD_DIM, HEAD_DIM), HEAD_DIM)
            source = pl.ds(side * HEAD_DIM, HEAD_DIM)
            update(0, raise_(rows[:, source]), span, rate_query_key)
        span = pl.ds(pl.multiple_of(head * VALUE_WIDTH, HEAD_DIM), VALUE_WIDTH)
        update(1, raise_(rows[:, QK_EDGE:VALUE_EDGE]), span, rate_value)
        update(2, raise_(rows[:, VALUE_EDGE:OUTPUT_EDGE]), span, rate_output)
        last = rows[:, OUTPUT_EDGE:]
        source = lax.broadcasted_iota(jnp.int32, (small, chosen.shape[1]), 0)
        target = lax.broadcasted_iota(jnp.int32, (small, chosen.shape[1]), 1)
        side, entry = lax.div(source, ATT_EXPERTS), lax.rem(source, ATT_EXPERTS)
        table = (target == (side * HEADS + head) * ATT_EXPERTS + entry) & (source < SELECT_COUNT)
        chosen += product(last, lower(jnp.where(table, 1.0, 0.0)))
        shared += raise_(last)
    every = slice(None)
    update(3, chosen, every, rate_select)
    expert_total = inputs[4][0].shape[1]
    update(4, pltpu.roll(shared, small - SELECT_COUNT, 1)[:, :expert_total], every, rate_router)
    gain_column = SELECT_COUNT + expert_total
    diagonal = lax.broadcasted_iota(jnp.int32, (part, part), 0) == lax.broadcasted_iota(
        jnp.int32, (part, part), 1
    )
    gain = jnp.where(diagonal, shared[:, gain_column : gain_column + 1], 0.0)
    update(5, jnp.sum(gain, axis=0, keepdims=True), every, rate_gain)


def expert_rows_kernel(weight, rows):
    count = weight.shape[0]
    for expert in range(count):
        rows[:, pl.ds(expert * EXPERT_H, EXPERT_H)] = lower(weight[expert, :, :EXPERT_H])
        rows[:, pl.ds((count + expert) * EXPERT_H, EXPERT_H)] = lower(weight[expert, :, EXPERT_H:])


def expert_rows_of(weight):
    count, rows, columns = weight.shape
    return pl.pallas_call(
        expert_rows_kernel,
        out_shape=jax.ShapeDtypeStruct((rows, count * columns), jnp.bfloat16),
        compiler_params=pltpu.CompilerParams(vmem_limit_bytes=56 * 2**20),
        cost_estimate=LIGHT,
    )(weight)


def front_kernel(scalars, tokens, picks, cotangent, routes, token_rows, upstream):
    rows, width = tokens.shape
    token_rows[:, :width] = tokens[...]
    row = lax.broadcasted_iota(jnp.int32, (token_rows.shape[1] - width, rows), 0)
    chosen = jnp.zeros(row.shape, jnp.float32)
    for head in range(picks.shape[0]):
        start = head % HEADS * SELECT_COUNT + head // HEADS * ATT_EXPERTS
        for pick in range(picks.shape[1]):
            chosen = jnp.where(row == start + picks[head, pick : pick + 1, :], 1.0, chosen)
    token_rows[:, width:] = lower(chosen.T)
    position = scalars[0] * rows + lax.broadcasted_iota(jnp.int32, (rows, 1), 0)
    upstream[:, :width] = lower(jnp.where(position < scalars[1], raise_(cotangent[...]), 0.0))
    row = lax.broadcasted_iota(jnp.int32, (upstream.shape[1] - width, rows), 0)
    hot = jnp.zeros(row.shape, jnp.float32)
    for index in range(routes.shape[0]):
        hot = jnp.where(row == SELECT_COUNT + routes[index : index + 1, :], 1.0, hot)
    upstream[:, width:] = lower(hot.T)


def payload_kernel(scalars, upstream, qk, value, output, select, router, gain, payload):
    part = qk.shape[0]
    small = payload.shape[2] - OUTPUT_EDGE
    rows, width = upstream.shape[0], upstream.shape[1] - small
    expert_total = router.shape[1]
    position = scalars[0] * rows + lax.broadcasted_iota(jnp.int32, (rows, 1), 0)
    valid = position < scalars[1]
    hot = raise_(upstream[:, width:])
    counts = jnp.sum(jnp.where(valid, hot, 0.0), axis=0, keepdims=True)
    gain_column = SELECT_COUNT + expert_total
    count_columns = -(-expert_total // part)
    row = lax.broadcasted_iota(jnp.int32, (part, small), 0)
    lane = lax.broadcasted_iota(jnp.int32, (part, small), 1)
    shared = product(lower(router[...]), shift_back(expert_total, small, SELECT_COUNT))
    diagonal = lax.broadcasted_iota(jnp.int32, (part, part), 0) == lax.broadcasted_iota(
        jnp.int32, (part, part), 1
    )
    gain_rows = jnp.sum(jnp.where(diagonal, gain[...], 0.0), axis=1, keepdims=True)
    shared = jnp.where(lane == gain_column, gain_rows, shared)
    for column in range(count_columns):
        mine = lane - SELECT_COUNT == row * count_columns + column
        found = jnp.sum(jnp.where(mine, counts, 0.0), axis=1, keepdims=True)
        shared = jnp.where(lane == gain_column + 1 + column, found, shared)
    picked = lower(select[...])
    for head in range(HEADS):
        span = pl.ds(head * HEAD_DIM, HEAD_DIM)
        payload[head, :, :HEAD_DIM] = lower(qk[:, span])
        span = pl.ds((HEADS + head) * HEAD_DIM, HEAD_DIM)
        payload[head, :, HEAD_DIM:QK_EDGE] = lower(qk[:, span])
        span = pl.ds(head * VALUE_WIDTH, VALUE_WIDTH)
        payload[head, :, QK_EDGE:VALUE_EDGE] = lower(value[:, span])
        payload[head, :, VALUE_EDGE:OUTPUT_EDGE] = lower(output[:, span])
        source = lax.broadcasted_iota(jnp.int32, (picked.shape[1], small), 0)
        target = lax.broadcasted_iota(jnp.int32, (picked.shape[1], small), 1)
        side, entry = lax.div(target, ATT_EXPERTS), lax.rem(target, ATT_EXPERTS)
        table = (source == (side * HEADS + head) * ATT_EXPERTS + entry) & (target < SELECT_COUNT)
        chosen = product(picked, lower(jnp.where(table, 1.0, 0.0)))
        payload[head, :, OUTPUT_EDGE:] = lower(shared + chosen)


def shift_back(rows, columns, offset):
    source = lax.broadcasted_iota(jnp.int32, (rows, columns), 0)
    target = lax.broadcasted_iota(jnp.int32, (rows, columns), 1)
    return lower(jnp.where(target == source + offset, 1.0, 0.0))


def local(
    tokens,
    cotangent,
    lengths,
    picks,
    routes,
    qk_weight,
    qk_first,
    qk_second,
    value_weight,
    value_first,
    value_second,
    output_weight,
    output_first,
    output_second,
    select_weight,
    select_first,
    select_second,
    router_weight,
    router_first,
    router_second,
    gain_weight,
    gain_first,
    gain_second,
    expert_weight,
    expert_first,
    expert_second,
):
    row_count = tokens.shape[1]
    model_width = tokens.shape[2]
    group_count = lax.axis_size("dp")
    owner_count = lax.axis_size("expert")
    local_count = expert_weight.shape[0]
    expert_total = local_count * owner_count
    bucket_rows = row_count * group_count
    part = qk_weight.shape[0]
    place = lax.axis_index("dp")
    owner = lax.axis_index("expert")
    seq_len = lengths[0]
    sequence = tokens[0]
    scalars = jnp.stack(
        [place.astype(jnp.int32), seq_len.astype(jnp.int32), owner.astype(jnp.int32)]
    )
    spots = jnp.stack([place.astype(jnp.int32), owner.astype(jnp.int32)])
    low, high = jnp.bfloat16, jnp.float32

    def shaped(columns, kind, rows=bucket_rows):
        return jax.ShapeDtypeStruct((rows, columns), kind)

    gain_column = SELECT_COUNT + expert_total
    count_columns = -(-expert_total // part)
    small_used = gain_column + 1 + count_columns
    small_width = small_used + -small_used % 128
    token_width = model_width + HEADS * SELECT_COUNT + -(HEADS * SELECT_COUNT) % 128

    token_own, upstream = wide_call(
        front_kernel,
        [scalars, sequence, picks[0].transpose(1, 2, 0), cotangent[0], routes[0].T],
        [
            shaped(token_width, low, row_count),
            shaped(model_width + small_width, low, row_count),
        ],
    )
    expert_up = {0: upstream}
    for relative in range(2, owner_count, 2):
        if not forwarded(relative):
            expert_up[relative] = swap(upstream, "expert", relative)
    token_blocks = [token_own] + [
        swap(token_own, "dp", relative) for relative in range(1, group_count)
    ]

    (payload,) = wide_call(
        payload_kernel,
        [
            scalars,
            upstream,
            qk_weight,
            value_weight,
            output_weight,
            select_weight,
            router_weight,
            gain_weight[None],
        ],
        [jax.ShapeDtypeStruct((HEADS, part, OUTPUT_EDGE + small_width), low)],
    )
    mine = lax.all_to_all(payload, "dp", split_axis=0, concat_axis=0, tiled=True)
    mine = after(
        mine, *token_blocks[1:], *[up for relative, up in expert_up.items() if relative]
    )

    half = row_count // 2
    expert_own = after(expert_rows_of(expert_weight), mine)
    expert_pieces = [expert_own, swap(expert_own, "dp", 1), swap(expert_own, "dp", 2)]
    dense_blocks = gather_chips(mine)
    dense_others = swap(
        after(jnp.stack(dense_blocks), *expert_pieces[1:]), "expert", 1
    )

    cosine, sine = rope_tables(bucket_rows)
    if part % 16 == 0:
        chips, made = owner_count // 2, []
        given = dense_blocks + [dense_others]
    else:
        dense = jnp.zeros((group_count, owner_count) + mine.shape[1:], jnp.bfloat16)
        for chip, block in enumerate(dense_blocks):
            for other, rows in enumerate((block, dense_others[chip])):
                spot = owner ^ (2 * chip + other)
                dense = lax.dynamic_update_slice_in_dim(dense, rows[:, None], spot, axis=1)
        dense = dense.reshape(group_count, row_count, -1)
        chips, made, given = 0, [], [dense]
    dense_shape = jax.ShapeDtypeStruct((group_count, row_count, payload.shape[2]), low)
    if chips:
        made = [dense_shape]
    outputs = made + [
        shaped(HEAD_DIM, low),
        shaped(HEAD_DIM, low),
        shaped(HEAD_DIM, low),
        shaped(small_width, high),
        shaped(VALUE_WIDTH, high),
        shaped(HEAD_DIM, high),
        shaped(VALUE_WIDTH, low),
        shaped(HEAD_DIM, high),
        shaped(model_width, low),
        shaped(2 * local_count + -2 * local_count % 128, low, model_width),
        shaped(small_width, high, part),
    ]
    kept = staged_call(
        functools.partial(attention_kernel, group_count, gain_column, chips, local_count),
        [scalars] + token_blocks + [cosine, sine] + given,
        outputs,
        token_blocks + [cosine, sine, dense_shape] + outputs[len(made) :],
        [],
        group_count + 2 + owner_count + len(outputs) + 2 * group_count,
    )
    if chips:
        dense, kept = kept[0], kept[1:]
    saved, (branch, router_local, counts) = dict(zip(KEPT, kept)), kept[len(KEPT) :]
    for relative in range(2, owner_count, 2):
        if forwarded(relative):
            block = after(expert_up[relative ^ 2], branch)
            expert_up[relative] = swap(block, "expert", 2)
    expert_up = [expert_up[relative] for relative in range(0, owner_count, 2)]
    near = [after(piece, branch) for piece in expert_pieces]
    expert_others = [swap(piece, "expert", 1) for piece in near]
    far = [
        swap(expert_pieces[1][:half], "dp", 2),
        swap(expert_pieces[2][half:], "dp", 1),
    ]
    expert_others += [swap(after(piece, branch), "expert", 1) for piece in far]
    branch = scatter_rows(branch)
    hidden = add_blocks(raise_(sequence), after(branch, expert_up[-1], *expert_others))
    small = dense[:, :, OUTPUT_EDGE:].reshape(model_width, -1)
    expert_counts = counts[:, gain_column + 1 : small_used].reshape(-1)[:expert_total]
    expert_counts = expert_counts.astype(jnp.int32)

    hidden_low = lower(hidden)
    expert_both = expert_pieces + far + expert_others
    order = [0] + list(range(2, len(expert_up))) + [1]
    expert_rows, back, slopes, gateds = {0: hidden_low}, {}, {}, {}
    arriving = {}
    for relative in range(2, owner_count, 2):
        if not forwarded(relative):
            arriving[relative] = swap(hidden_low, "expert", relative)
    before = None
    for chip in order:
        if chip:
            others = [arriving[2]] if chip == order[1] else []
            block = after(arriving[2 * chip], before, *others)
            if chip % 2 == 0 and chip + 1 < len(expert_up):
                arriving[2 * chip + 2] = swap(block, "expert", 2)
            expert_rows[chip] = block
        back[chip], slopes[chip], gateds[chip] = expert_call(
            spots, expert_rows[chip], expert_up[chip], router_local, expert_both
        )
        before = slopes[chip]
    back_terms = send_expert([back[chip] for chip in range(len(order))])
    back_terms = [back_terms[chip] for chip in order]
    expert_rows, slopes, gateds = [
        [found[chip] for chip in range(len(order))] for found in (expert_rows, slopes, gateds)
    ]

    def side_grads(after_spots, side):
        return expert_grads(
            after_spots,
            expert_rows,
            expert_up,
            slopes,
            gateds,
            side,
            group_count,
            tuple(range(group_count)),
        )

    other_grads = side_grads(spots, 1)
    own_grads = side_grads(after(spots, other_grads), 0)
    back_terms[1:] = [after(term, own_grads) for term in back_terms[1:]]

    hidden_grad, hidden_grad_low, router_grad = wide_call(
        functools.partial(hidden_back_kernel, len(back_terms)),
        [scalars] + back_terms + [hidden, upstream, small],
        [
            shaped(model_width, high, row_count),
            jax.ShapeDtypeStruct((group_count, row_count, model_width), low),
            shaped(small_width, high, model_width),
        ],
        limit=24,
    )
    hidden_grad_rows = exchange_rows(hidden_grad_low)
    produced = []
    for start in range(0, len(gateds), 4):
        produced += expert_out_call(
            after(spots, hidden_grad_low), expert_both, gateds[start : start + 4]
        )
    moe_terms = send_expert(produced)
    other_grads = swap(after(other_grads, hidden_grad_low), "expert", 1)

    across, along = halving(after(spots, *produced), own_grads, other_grads, row_count)
    across, along = swap(across, "dp", 1), swap(along, "dp", 2)
    layer_out = hidden
    for term in moe_terms:
        layer_out = layer_out + raise_(term)
    layer_out = lower(layer_out)

    scratch = [
        pltpu.VMEM((bucket_rows, HEAD_DIM), low),
        pltpu.VMEM((bucket_rows, small_width), high),
        pltpu.VMEM((bucket_rows, HEAD_DIM), high),
        pltpu.VMEM((bucket_rows, HEAD_DIM), high),
        pltpu.VMEM((bucket_rows, HEAD_DIM), high),
        pltpu.VMEM((bucket_rows, VALUE_WIDTH), low),
        pltpu.VMEM((bucket_rows, QK_EDGE), low),
        pltpu.VMEM((bucket_rows, small_width), low),
        pltpu.VMEM((bucket_rows, model_width), low),
    ]
    made = [dense_shape]
    if chips:
        made = [jax.ShapeDtypeStruct((chips, group_count, part, dense.shape[2]), low)] * 2
    saved.update(
        upstream=hidden_grad_rows, dense=dense, cosine=cosine, sine=sine, router_grad=router_grad
    )
    inputs = [saved[name] for name in BACK]
    terms_shape = shaped(model_width, low)
    *dense_parts, input_terms = staged_call(
        functools.partial(attention_back_kernel, group_count, gain_column, chips),
        [scalars] + inputs + token_blocks,
        made + [terms_shape],
        inputs + [dense_shape, terms_shape, terms_shape],
        scratch,
        len(inputs) + 2 * group_count + 3 * owner_count,
    )

    if not chips:
        dense_grad = dense_parts[0].reshape(group_count, owner_count, part, -1)
        dense_parts = [
            jnp.stack(
                [
                    lax.dynamic_index_in_dim(dense_grad, owner ^ relative, 1, keepdims=False)
                    for relative in range(side, owner_count, 2)
                ]
            )
            for side in range(2)
        ]
    late = after(spots, input_terms)
    first, second = halved(late, own_grads, other_grads, across, along)
    dense_parts[1] = after(dense_parts[1], first, second, *moe_terms)
    dense_parts = join(spots, dense_parts[0], swap(dense_parts[1], "expert", 1))
    first, second = swap(first, "dp", 2), swap(second, "dp", 1)
    input_grad = add_blocks(hidden_grad, scatter_rows(input_terms))
    dense_terms = send_expert(dense_parts)
    dense_terms[1:] = [after(term, input_grad, first, second) for term in dense_terms[1:]]
    dense_sums = wide_call(
        dense_sum_kernel,
        [scalars] + dense_terms,
        [jax.ShapeDtypeStruct(dense_terms[0].shape[1:], low)] * group_count,
    )
    dense_sums = [dense_sums[0]] + [
        swap(dense_sums[relative], "dp", relative) for relative in range(1, group_count)
    ]
    masters = [
        (qk_weight, qk_first, qk_second),
        (value_weight, value_first, value_second),
        (output_weight, output_first, output_second),
        (select_weight, select_first, select_second),
        (router_weight, router_first, router_second),
        (gain_weight[None], gain_first[None], gain_second[None]),
    ]
    masters = [array for group in masters for array in group]
    updated = wide_call(
        dense_update_kernel,
        [scalars] + dense_sums + masters,
        [jax.ShapeDtypeStruct(array.shape, high) for array in masters],
        limit=24,
    )
    updated = list(updated[:15]) + [array[0] for array in updated[15:]]
    expert_results = expert_update(
        [
            [(own_grads, 1), (other_grads, 1), (across, 0), (first, 0)],
            [(own_grads, 1), (other_grads, 1), (along, 0), (second, 0)],
        ],
        expert_weight,
        expert_first,
        expert_second,
    )
    return (layer_out[None], input_grad[None], *updated, *expert_results, expert_counts)


def solution(mesh):
    placed = (
        P("expert", "dp", None),
        P("expert", "dp", None),
        P("expert"),
        P("expert", "dp", None, None),
        P("expert", "dp", None),
        P(("dp", "expert"), None),
        P(("dp", "expert"), None),
        P(("dp", "expert"), None),
        P(("dp", "expert"), None),
        P(("dp", "expert"), None),
        P(("dp", "expert"), None),
        P(("dp", "expert"), None),
        P(("dp", "expert"), None),
        P(("dp", "expert"), None),
        P(("dp", "expert"), None),
        P(("dp", "expert"), None),
        P(("dp", "expert"), None),
        P(("dp", "expert"), None),
        P(("dp", "expert"), None),
        P(("dp", "expert"), None),
        P(("dp", "expert")),
        P(("dp", "expert")),
        P(("dp", "expert")),
        P("expert", "dp", None),
        P("expert", "dp", None),
        P("expert", "dp", None),
    )
    return jax.shard_map(
        local,
        mesh=mesh,
        in_specs=placed,
        out_specs=(
            P("expert", "dp", None),
            P("expert", "dp", None),
            P(("dp", "expert"), None),
            P(("dp", "expert"), None),
            P(("dp", "expert"), None),
            P(("dp", "expert"), None),
            P(("dp", "expert"), None),
            P(("dp", "expert"), None),
            P(("dp", "expert"), None),
            P(("dp", "expert"), None),
            P(("dp", "expert"), None),
            P(("dp", "expert"), None),
            P(("dp", "expert"), None),
            P(("dp", "expert"), None),
            P(("dp", "expert"), None),
            P(("dp", "expert"), None),
            P(("dp", "expert"), None),
            P(("dp", "expert")),
            P(("dp", "expert")),
            P(("dp", "expert")),
            P("expert", "dp", None),
            P("expert", "dp", None),
            P("expert", "dp", None),
            P(),
        ),
        check_vma=False,
    )
```

```python
import functools

import numpy as np
import jax
import jax.numpy as jnp
from jax import lax
from jax.experimental import pallas as pl
from jax.experimental.pallas import tpu as pltpu
from jax.sharding import PartitionSpec as P

HEADS = 4
HEAD_DIM = 128
ATT_EXPERTS = 5
EXPERT_H = 128
TOPK = 16
STEP = 10


norm_eps = 1e-05
beta_first = 0.9
beta_second = 0.95
adam_eps = 1e-08
weight_decay = 0.1
masked_score = -1e30
rope_base = 10000.0
rate_query_key = 0.04
rate_value = 0.03
rate_output = 2.0
rate_select = 0.03
rate_router = 0.015
rate_gain = 1.2
rate_expert = 0.05


def product(former, latter):
    return jnp.dot(former, latter, preferred_element_type=jnp.float32)


def product_rows(former, latter):
    return lax.dot_general(
        former, latter, (((0,), (0,)), ((), ())), preferred_element_type=jnp.float32
    )


def product_last(former, latter):
    return lax.dot_general(
        former, latter, (((1,), (1,)), ((), ())), preferred_element_type=jnp.float32
    )


def rope_tables(rows):
    half = HEAD_DIM // 2
    frequency = np.exp(-np.log(rope_base) * np.arange(half) / half)
    angles = np.arange(rows)[:, None] * frequency[None, :]
    cosine, sine = np.cos(angles), np.sin(angles)
    return (
        jnp.asarray(np.concatenate([cosine, cosine], axis=1), jnp.float32),
        jnp.asarray(np.concatenate([-sine, sine], axis=1), jnp.float32),
    )


def adamw_update(weight, first_moment, second_moment, gradient, rate):
    first_new = beta_first * first_moment + (1.0 - beta_first) * gradient
    second_new = beta_second * second_moment + (1.0 - beta_second) * gradient * gradient
    first_hat = first_new / (1.0 - beta_first**STEP)
    second_hat = second_new / (1.0 - beta_second**STEP)
    weight_new = weight - rate * (
        first_hat / (jnp.sqrt(second_hat) + adam_eps) + weight_decay * weight
    )
    return (weight_new, first_new, second_new)


LIGHT = pl.CostEstimate(flops=1000, bytes_accessed=1000, transcendentals=0)


def swap(values, axis, relative):
    count = lax.axis_size(axis)
    return lax.ppermute(values, axis, [(place, place ^ relative) for place in range(count)])


def lower(values):
    return values.astype(jnp.bfloat16)


def raise_(values):
    return values.astype(jnp.float32)


def after(values, *others):
    return lax.optimization_barrier((values,) + others)[0]


def exchange_rows(copies):
    blocks = lax.all_to_all(copies, "dp", split_axis=0, concat_axis=0, tiled=True)
    return blocks.reshape((-1,) + copies.shape[2:])


def scatter_rows(values):
    count = lax.axis_size("dp")
    blocks = values.reshape((count, values.shape[0] // count) + values.shape[1:])
    return lax.all_to_all(blocks, "dp", split_axis=0, concat_axis=0, tiled=True)


def add_blocks(values, blocks):
    for index in range(blocks.shape[0]):
        values = values + raise_(blocks[index])
    return values


def join_kernel(scalars, evens, odds, *results):
    for chip, result in enumerate(results):
        result[...] = lower(raise_(evens[chip]) + raise_(odds[chip]))


def join(scalars, evens, odds):
    shape = jax.ShapeDtypeStruct(evens.shape[1:], jnp.bfloat16)
    return list(wide_call(join_kernel, [scalars, evens, odds], [shape] * evens.shape[0]))


def forwarded(relative):
    return relative & 2 and relative > 2


def gather_chips(values):
    return [values] + [
        swap(values, "expert", relative) for relative in range(2, lax.axis_size("expert"), 2)
    ]


def send_expert(joined):
    return [joined[0]] + [
        swap(term, "expert", 2 * index) for index, term in enumerate(joined) if index
    ]


def full(shape):
    return pl.BlockSpec(shape, lambda *_: (0,) * len(shape))


def wide_call(kernel, inputs, outputs, limit=56):
    specs = [pl.BlockSpec(memory_space=pltpu.SMEM)] + [full(value.shape) for value in inputs[1:]]
    return pl.pallas_call(
        kernel,
        grid=(1,),
        in_specs=specs,
        out_specs=[full(value.shape) for value in outputs],
        out_shape=outputs,
        compiler_params=pltpu.CompilerParams(vmem_limit_bytes=limit * 2**20),
        cost_estimate=LIGHT,
    )(*inputs)


class Copies:
    def __init__(self, sems):
        self.sems, self.count, self.waiting = sems, 0, {}

    def start(self, name, source, target):
        copy = pltpu.make_async_copy(source, target, self.sems.at[self.count])
        copy.start()
        self.count += 1
        self.waiting.setdefault(name, []).append(copy)

    def wait(self, *names):
        for name in names:
            for copy in self.waiting.pop(name, []):
                copy.wait()


def staged_call(kernel, inputs, outputs, held, scratch, copies):
    somewhere = pl.BlockSpec(memory_space=pl.ANY)
    return pl.pallas_call(
        kernel,
        grid=(1,),
        in_specs=[pl.BlockSpec(memory_space=pltpu.SMEM)] + [somewhere] * (len(inputs) - 1),
        out_specs=[somewhere] * len(outputs),
        out_shape=outputs,
        scratch_shapes=[pltpu.VMEM(value.shape, value.dtype) for value in held]
        + list(scratch)
        + [pltpu.SemaphoreType.DMA((copies,))],
        compiler_params=pltpu.CompilerParams(vmem_limit_bytes=56 * 2**20),
        cost_estimate=LIGHT,
    )(*inputs)


def shift_table(rows, columns, offset, count):
    source = lax.broadcasted_iota(jnp.int32, (rows, columns), 0)
    target = lax.broadcasted_iota(jnp.int32, (rows, columns), 1)
    return lower(jnp.where((source == target + offset) & (target < count), 1.0, 0.0))


def moments(values):
    center = values - jnp.mean(values, axis=-1, keepdims=True)
    inverse = lax.rsqrt(jnp.mean(center * center, axis=-1, keepdims=True) + norm_eps)
    return center * inverse, inverse


def turn(rows, cosine, signed_sine, direction):
    return rows * cosine + direction * pltpu.roll(rows, HEAD_DIM // 2, 1) * signed_sine


def masked_scores(queries, key_rows, seq_len, start):
    scores = product_last(queries, key_rows) * HEAD_DIM ** (-0.5)
    query_place = start + lax.broadcasted_iota(jnp.int32, scores.shape, 0)
    key_place = lax.broadcasted_iota(jnp.int32, scores.shape, 1)
    return jnp.where((key_place <= query_place) & (key_place < seq_len), scores, masked_score)


VALUE_WIDTH = ATT_EXPERTS * HEAD_DIM
QK_EDGE = 2 * HEAD_DIM
VALUE_EDGE = QK_EDGE + VALUE_WIDTH
OUTPUT_EDGE = VALUE_EDGE + VALUE_WIDTH
SELECT_COUNT = 2 * ATT_EXPERTS


KEPT = ("queries", "key_rows", "values", "weighting", "projected", "attended", "mixed", "log_total")


def attention_kernel(blocks, gain_column, chips, local_count, scalars, *refs):
    given = blocks + 2 + (chips + 1 if chips else 1)
    outs = (["dense"] if chips else []) + list(KEPT) + ["branch", "router_local", "counts"]
    count = len(outs)
    sources, targets = refs[:given], dict(zip(outs, refs[given : given + count]))
    tokens, (cosine, sine, dense), refs = (
        refs[given + count : given + count + blocks],
        refs[given + count + blocks : given + count + blocks + 3],
        refs[given + count + blocks + 3 : -1] + refs[-1:],
    )
    *kept, branch, router_local, counts, sems = refs
    (queries, key_rows, values, weighting, projected, attended, mixed, log_total) = kept
    copies = Copies(sems)
    for index in range(blocks):
        copies.start("in", sources[index], tokens[index])
    copies.start("in", sources[blocks], cosine)
    copies.start("in", sources[blocks + 1], sine)
    if chips:
        evens, odds = sources[blocks + 2 : blocks + 2 + chips], sources[blocks + 2 + chips]
        part = odds.shape[2]
        for chip in range(chips):
            for other, rows in ((0, evens[chip]), (1, odds.at[chip])):
                start = (scalars[2] ^ (2 * chip + other)) * part
                copies.start("in", rows, dense.at[:, pl.ds(pl.multiple_of(start, part), part), :])
    else:
        copies.start("in", sources[blocks + 2], dense)
    copies.wait("in")
    if chips:
        copies.start("out", dense, targets["dense"])
    place, seq_len = scalars[0], scalars[1]
    width = dense.shape[0] * dense.shape[1]
    block = tokens[0].shape[0]

    def weight(start, end):
        return dense[:, :, start:end].reshape(width, end - start)

    small_rows = weight(OUTPUT_EDGE, dense.shape[2])
    count = local_count
    source = lax.broadcasted_iota(jnp.int32, (small_rows.shape[1], router_local.shape[1]), 0)
    entry = lax.broadcasted_iota(jnp.int32, source.shape, 1)
    first = SELECT_COUNT + scalars[2] * count + entry
    second = SELECT_COUNT + (scalars[2] ^ 1) * count + entry - count
    table = (source == jnp.where(entry < count, first, second)) & (entry < 2 * count)
    router_local[...] = lower(product(small_rows, lower(jnp.where(table, 1.0, 0.0))))
    part = counts.shape[0]
    total = raise_(small_rows[:part])
    for start in range(part, width, part):
        total += raise_(small_rows[start : start + part])
    counts[...] = total
    copies.start("out", counts, targets["counts"])
    copies.start("out", router_local, targets["router_local"])
    gain = raise_(small_rows).T[gain_column : gain_column + 1, :]
    head_table = shift_table(
        tokens[0].shape[1] - width, dense.shape[2] - OUTPUT_EDGE, place * SELECT_COUNT, SELECT_COUNT
    )
    for index in range(blocks):
        span = pl.ds(pl.multiple_of((place ^ index) * block, block), block)
        rows = tokens[index][:, :width]
        scaled, _ = moments(raise_(rows))
        normed_rows = lower(scaled * gain)
        both = product(normed_rows, weight(0, QK_EDGE))
        queries[span, :] = lower(turn(both[:, :HEAD_DIM], cosine[span, :], sine[span, :], 1.0))
        key_rows[span, :] = lower(turn(both[:, HEAD_DIM:], cosine[span, :], sine[span, :], 1.0))
        chosen = product(tokens[index][:, width:], head_table)
        sigma_rows = jax.nn.sigmoid(product(normed_rows, small_rows))
        weights = sigma_rows * chosen
        weighting[span, :] = weights
        columns = product(rows, weight(QK_EDGE, VALUE_EDGE))
        projected[span, :] = columns
        total = weights[:, 0:1] * columns[:, :HEAD_DIM]
        for expert in range(1, ATT_EXPERTS):
            total += (
                weights[:, expert : expert + 1]
                * columns[:, expert * HEAD_DIM : (expert + 1) * HEAD_DIM]
            )
        values[span, :] = lower(total)
    for name, ref in zip(KEPT[:5], kept):
        copies.start("out", ref, targets[name])
    for start in range(0, blocks * block, block):
        span = pl.ds(start, block)
        scores = masked_scores(queries[span, :], key_rows[...], seq_len, start)
        highest = jnp.max(scores, axis=-1, keepdims=True)
        raised = jnp.exp(scores - highest)
        row_total = jnp.sum(raised, axis=-1, keepdims=True)
        log_total[span, :] = jnp.broadcast_to(highest + jnp.log(row_total), (block, HEAD_DIM))
        rows = product(lower(raised / row_total), values[...])
        attended[span, :] = rows
        weights = weighting[span, :]
        for expert in range(ATT_EXPERTS):
            mixed[span, pl.ds(expert * HEAD_DIM, HEAD_DIM)] = lower(
                weights[:, ATT_EXPERTS + expert : ATT_EXPERTS + expert + 1] * rows
            )
        branch[span, :] = lower(product_last(mixed[span, :], weight(VALUE_EDGE, OUTPUT_EDGE)))
        for name, ref in (("mixed", mixed), ("branch", branch)):
            copies.start("out", ref.at[span, :], targets[name].at[span, :])
    copies.start("out", attended, targets["attended"])
    copies.start("out", log_total, targets["log_total"])
    copies.wait("out")


BACK = ("upstream", "dense", "weighting", "attended", "mixed", "queries", "key_rows", "values") + (
    "log_total",
    "projected",
    "cosine",
    "sine",
    "router_grad",
)


def attention_back_kernel(blocks, gain_column, chips, scalars, *refs):
    count = len(BACK)
    sources, token_blocks, refs = refs[:count], refs[count : count + blocks], refs[count + blocks :]
    results, out_terms, refs = refs[: 2 if chips else 1], refs[2 if chips else 1], refs[3 if chips else 2 :]
    held, (grads, terms, tokens), refs = refs[:count], refs[count : count + 3], refs[count + 3 :]
    (upstream, dense, weighting, attended, mixed, queries, key_rows, values, log_total) = held[:9]
    projected, cosine, sine, router_grad = held[9:]
    (attended_grad, weight_grad, key_grad, value_grad, query_grad) = refs[:5]
    projected_grad, pair_grad, select_grad, normed, sems = refs[5:]
    copies = Copies(sems)
    for name, source, target in zip(BACK, sources, held):
        copies.start(name, source, target)
    block = token_blocks[0].shape[0]
    for index, rows in enumerate(token_blocks):
        span = pl.ds(pl.multiple_of((scalars[0] ^ index) * block, block), block)
        copies.start("tokens", rows.at[:, pl.ds(0, tokens.shape[1])], tokens.at[span, :])

    def weight(start, end):
        return dense[:, :, start:end].reshape(tokens.shape[1], end - start)

    def leave(columns):
        if not chips:
            copies.start("out", grads.at[:, :, columns], results[0].at[:, :, columns])
            return
        part = results[0].shape[2]
        for relative in range(2 * chips):
            start = pl.multiple_of((scalars[2] ^ relative) * part, part)
            target = results[relative % 2].at[relative // 2, :, :, columns]
            copies.start("out", grads.at[:, pl.ds(start, part), columns], target)

    def keep(start, values):
        columns = pl.ds(start, values.shape[1])
        grads[:, :, columns] = values.reshape(grads.shape[:2] + values.shape[1:])

    copies.wait("upstream", "dense", "weighting", "attended")
    seq_len = scalars[1]
    width = tokens.shape[1]
    small = dense.shape[2] - OUTPUT_EDGE
    lane = lax.broadcasted_iota(jnp.int32, (block, small), 1)
    scale = HEAD_DIM ** (-0.5)
    gain = raise_(weight(OUTPUT_EDGE, dense.shape[2])).T[gain_column : gain_column + 1, :]
    for start in range(0, tokens.shape[0], block):
        span = pl.ds(start, block)
        mixed_grad = product(upstream[span, :], weight(VALUE_EDGE, OUTPUT_EDGE))
        weights = weighting[span, :]
        heads = attended[span, :]
        total = jnp.zeros((block, HEAD_DIM), jnp.float32)
        found = jnp.zeros((block, small), jnp.float32)
        for expert in range(ATT_EXPERTS):
            piece = mixed_grad[:, expert * HEAD_DIM : (expert + 1) * HEAD_DIM]
            column = ATT_EXPERTS + expert
            total += weights[:, column : column + 1] * piece
            found = jnp.where(lane == column, jnp.sum(piece * heads, axis=1, keepdims=True), found)
        attended_grad[span, :] = lower(total)
        weight_grad[span, :] = found
    copies.wait("mixed")
    keep(VALUE_EDGE, lower(product_rows(upstream[...], mixed[...])))
    leave(pl.ds(VALUE_EDGE, OUTPUT_EDGE - VALUE_EDGE))
    copies.wait("queries", "key_rows", "values", "log_total")
    for start in range(0, tokens.shape[0], block):
        span = pl.ds(start, block)
        scores = masked_scores(queries[span, :], key_rows[...], seq_len, start)
        probs = jnp.exp(scores - log_total[span, :1])
        prob_grad = product_last(attended_grad[span, :], values[...])
        delta = jnp.sum(probs * prob_grad, axis=-1, keepdims=True)
        score_grad = lower(probs * (prob_grad - delta))
        query_grad[span, :] = product(score_grad, key_rows[...]) * scale
        key_terms = product_rows(score_grad, queries[span, :])
        value_terms = product_rows(lower(probs), attended_grad[span, :])
        if start:
            key_grad[...] += key_terms
            value_grad[...] += value_terms
        else:
            key_grad[...] = key_terms
            value_grad[...] = value_terms
    copies.wait("projected", "cosine", "sine", "router_grad", "tokens")
    gain_grad = jnp.zeros((1, width), jnp.float32)
    for start in range(0, tokens.shape[0], block):
        span = pl.ds(start, block)
        rows = value_grad[span, :]
        weights = weighting[span, :]
        found = weight_grad[span, :]
        for expert in range(ATT_EXPERTS):
            piece = pl.ds(expert * HEAD_DIM, HEAD_DIM)
            projected_grad[span, piece] = lower(weights[:, expert : expert + 1] * rows)
            found = jnp.where(
                lane == expert,
                jnp.sum(rows * projected[span, piece], axis=1, keepdims=True),
                found,
            )
        pair_grad[span, :HEAD_DIM] = lower(
            turn(query_grad[span, :], cosine[span, :], sine[span, :], -1.0)
        )
        pair_grad[span, HEAD_DIM:] = lower(
            turn(key_grad[span, :] * scale, cosine[span, :], sine[span, :], -1.0)
        )
        select_rows = lower(found * weights * (1.0 - weights))
        select_grad[span, :] = select_rows
        normed_grad = product_last(pair_grad[span, :], weight(0, QK_EDGE)) + product_last(
            select_rows, weight(OUTPUT_EDGE, dense.shape[2])
        )
        scaled, inverse = moments(raise_(tokens[span, :]))
        normed[span, :] = lower(scaled * gain)
        gain_grad += jnp.sum(normed_grad * scaled, axis=0, keepdims=True)
        through = normed_grad * gain
        norm_grad = inverse * (
            through
            - jnp.mean(through, axis=-1, keepdims=True)
            - scaled * jnp.mean(through * scaled, axis=-1, keepdims=True)
        )
        terms[span, :] = lower(
            product_last(projected_grad[span, :], weight(QK_EDGE, VALUE_EDGE)) + norm_grad
        )
        copies.start("out", terms.at[span, :], out_terms.at[span, :])
    keep(QK_EDGE, lower(product_rows(tokens[...], projected_grad[...])))
    keep(0, lower(product_rows(normed[...], pair_grad[...])))
    row = lax.broadcasted_iota(jnp.int32, (small, width), 0)
    gain_part = jnp.where(row == gain_column, gain_grad, 0.0).T
    rest = product_rows(normed[...], select_grad[...]) + gain_part + router_grad[...]
    keep(OUTPUT_EDGE, lower(rest))
    leave(pl.ds(0, VALUE_EDGE))
    leave(pl.ds(OUTPUT_EDGE, small))
    copies.wait("out")


def piece_copies(place, pieces, target, columns, sems):
    part, last = pieces[0].shape[0], len(pieces) - 2
    half = part // 2
    copies = []
    for index, piece in enumerate(pieces):
        start = (place ^ min(index, last)) * part + (half if index > last else 0)
        rows = pl.ds(pl.multiple_of(start, half), piece.shape[0])
        source = piece.at[:, columns]
        copies.append(pltpu.make_async_copy(source, target.at[rows, :], sems.at[index]))
    return copies


def expert_kernel(pieces, scalars, rows, up, router, *refs):
    weights = refs[: 2 * pieces]
    back, slope, gated, insides, outsides, sems = refs[2 * pieces :]
    block, width = rows.shape
    hidden = slope.shape[1] // 2
    count = hidden // EXPERT_H
    copies = []
    for side in range(2):
        own = weights[side * pieces : (side + 1) * pieces]
        copies.append(
            piece_copies(scalars[0], own, insides.at[side], pl.ds(0, hidden), sems.at[side, 0])
            + piece_copies(
                scalars[0], own, outsides.at[side], pl.ds(hidden, hidden), sems.at[side, 1]
            )
        )
        for copy in copies[side]:
            copy.start()
    small = up.shape[1] - width
    lanes = router.shape[1]
    offsets = [SELECT_COUNT + (scalars[1] ^ index) * count for index in range(2)]

    def column_of(entry):
        return jnp.where(entry < count, offsets[0] + entry, offsets[1] + entry - count)

    source = lax.broadcasted_iota(jnp.int32, (small, lanes), 0)
    entry = lax.broadcasted_iota(jnp.int32, (small, lanes), 1)
    pick_table = lower(jnp.where((source == column_of(entry)) & (entry < 2 * count), 1.0, 0.0))
    entry = lax.broadcasted_iota(jnp.int32, (lanes, small), 0)
    target = lax.broadcasted_iota(jnp.int32, (lanes, small), 1)
    place_table = lower(jnp.where((target == column_of(entry)) & (entry < 2 * count), 1.0, 0.0))
    lane = lax.broadcasted_iota(jnp.int32, (block, lanes), 1)
    scaled, _ = moments(raise_(rows[...]))
    sigma_gate = jax.nn.sigmoid(product(lower(scaled), router[...]))
    gates = sigma_gate * product(up[:, width:], pick_table)
    found = jnp.zeros((block, lanes), jnp.float32)
    for first in range(0, 2 * count, 2):
        side = first // count
        if first % count == 0:
            for copy in copies[side]:
                copy.wait()
        local = pl.ds(first % count * EXPERT_H, 2 * EXPERT_H)
        inner = product(rows[...], insides[side, :, local])
        terms = product(up[:, :width], outsides[side, :, local])
        sigma = jax.nn.sigmoid(inner)
        silu = inner * sigma
        active = raise_(lower(silu))
        both = terms * active
        tilt = sigma + silu * (1.0 - sigma)
        for k in range(2):
            part = slice(k * EXPERT_H, (k + 1) * EXPERT_H)
            columns = pl.ds((first + k) * EXPERT_H, EXPERT_H)
            gate = gates[:, first + k : first + k + 1]
            gated[:, columns] = lower(gate * active[:, part])
            slope[:, columns] = lower(gate * terms[:, part] * tilt[:, part])
            summed = jnp.sum(both[:, part], axis=1, keepdims=True)
            found = jnp.where(lane == first + k, summed, found)
    back[:, :width] = lower(
        product_last(slope[:, :hidden], insides[0]) + product_last(slope[:, hidden:], insides[1])
    )
    back[:, width:] = lower(product(lower(found * gates * (1.0 - sigma_gate)), place_table))


def expert_call(scalars, rows, up, router, weights):
    block, width = rows.shape
    hidden = weights[0].shape[1] // 2
    pieces = len(weights) // 2
    outputs = [
        jax.ShapeDtypeStruct(up.shape, jnp.bfloat16),
        jax.ShapeDtypeStruct((block, 2 * hidden), jnp.bfloat16),
        jax.ShapeDtypeStruct((block, 2 * hidden), jnp.bfloat16),
    ]
    return pl.pallas_call(
        functools.partial(expert_kernel, pieces),
        grid=(1,),
        in_specs=[pl.BlockSpec(memory_space=pltpu.SMEM)]
        + [full(value.shape) for value in (rows, up, router)]
        + [pl.BlockSpec(memory_space=pl.ANY)] * len(weights),
        out_specs=[full(value.shape) for value in outputs],
        out_shape=outputs,
        scratch_shapes=[
            pltpu.VMEM((2, width, hidden), jnp.bfloat16),
            pltpu.VMEM((2, width, hidden), jnp.bfloat16),
            pltpu.SemaphoreType.DMA((2, 2, pieces)),
        ],
        compiler_params=pltpu.CompilerParams(vmem_limit_bytes=56 * 2**20),
        cost_estimate=LIGHT,
    )(scalars, rows, up, router, *weights)


def expert_grad_kernel(chips, blocks, scalars, *refs):
    rows = refs[:chips]
    ups = refs[chips : 2 * chips]
    slopes = refs[2 * chips : 3 * chips]
    gateds = refs[3 * chips : 4 * chips]
    width = rows[0].shape[1]
    part = width // blocks
    quarter = pl.num_programs(0) // 4

    def total(lefts, rights, target):
        for index in range(blocks):
            columns = pl.ds(pl.multiple_of((scalars[0] ^ index) * part, part), part)
            result = product_rows(lefts[0][:, columns], rights[0][...])
            for left, right in zip(lefts[1:], rights[1:]):
                result += product_rows(left[:, columns], right[...])
            target[pl.ds(index * part, part), :] = lower(result)

    for phase in range(4):

        @pl.when(pl.program_id(0) // quarter == phase)
        def _(phase=phase):
            lefts, rights = ((rows, slopes), (ups, gateds))[phase % 2]
            total(lefts, rights, refs[4 * chips + phase // 2])


def expert_grads(scalars, rows, ups, slopes, gateds, blocks):
    chips = len(slopes)
    block, width = rows[0].shape
    hidden = slopes[0].shape[1] // 2
    tile = hidden // 2
    once = pl.Buffered(buffer_count=1)

    def slope_at(j):
        return 0, jnp.where(j < 4, 2 + jnp.minimum(j, 1), jnp.minimum(j - 4, 1))

    def gated_at(j):
        return 0, jnp.where(j < 4, 2 + jnp.maximum(j - 2, 0), jnp.maximum(j - 6, 0))

    shape = jax.ShapeDtypeStruct((width, 2 * hidden), jnp.bfloat16)
    return pl.pallas_call(
        functools.partial(expert_grad_kernel, chips, blocks),
        grid=(8,),
        in_specs=[pl.BlockSpec(memory_space=pltpu.SMEM)]
        + [pl.BlockSpec(v.shape, lambda j: (0, 0), pipeline_mode=once) for v in rows + ups]
        + [pl.BlockSpec((block, tile), slope_at)] * chips
        + [pl.BlockSpec((block, tile), gated_at)] * chips,
        out_specs=[
            pl.BlockSpec((width, tile), lambda j: (0, jnp.minimum(j, 3))),
            pl.BlockSpec((width, tile), lambda j: (0, jnp.maximum(j - 4, 0))),
        ],
        out_shape=[shape, shape],
        compiler_params=pltpu.CompilerParams(vmem_limit_bytes=56 * 2**20),
        cost_estimate=LIGHT,
    )(scalars, *rows, *ups, *slopes, *gateds)


def expert_out_kernel(pieces, scalars, *refs):
    weights, refs = refs[: 2 * pieces], refs[2 * pieces :]
    count = (len(refs) - 5) // 2
    gateds, results = refs[:count], refs[count : 2 * count]
    outsides, lefts, held, sems, gated_sems = refs[2 * count :]
    hidden = outsides.shape[2]
    block, width = results[0].shape
    tile = min(256, width)
    copies = []
    for side in range(2):
        own = weights[side * pieces : (side + 1) * pieces]
        columns = pl.ds(hidden, hidden)
        started = piece_copies(scalars[0], own, outsides.at[side], columns, sems.at[side])
        for index, gated in enumerate(gateds):
            source = gated.at[:, pl.ds(side * hidden, hidden)]
            target = lefts.at[side, pl.ds(index * block, block), :]
            started.append(pltpu.make_async_copy(source, target, gated_sems.at[side, index]))
        for copy in started:
            copy.start()
        copies.append(started)
    for side in range(2):
        for copy in copies[side]:
            copy.wait()
        for start in range(0, width, tile):
            columns = pl.ds(start, tile)
            total = product_last(lefts[side], outsides[side, columns, :])
            if side == 0:
                held[:, columns] = total
            else:
                total += held[:, columns]
                for index, result in enumerate(results):
                    result[:, columns] = lower(total[index * block : (index + 1) * block])


def expert_out_call(scalars, weights, gateds):
    pieces, count = len(weights) // 2, len(gateds)
    hidden = weights[0].shape[1] // 2
    width = sum(weight.shape[0] for weight in weights[:pieces])
    block = gateds[0].shape[0]
    return pl.pallas_call(
        functools.partial(expert_out_kernel, pieces),
        grid=(1,),
        in_specs=[pl.BlockSpec(memory_space=pltpu.SMEM)]
        + [pl.BlockSpec(memory_space=pl.ANY)] * (len(weights) + count),
        out_specs=[full((block, width))] * count,
        out_shape=[jax.ShapeDtypeStruct((block, width), jnp.bfloat16)] * count,
        scratch_shapes=[
            pltpu.VMEM((2, width, hidden), jnp.bfloat16),
            pltpu.VMEM((2, count * block, hidden), jnp.bfloat16),
            pltpu.VMEM((count * block, width), jnp.float32),
            pltpu.SemaphoreType.DMA((2, pieces)),
            pltpu.SemaphoreType.DMA((2, count)),
        ],
        compiler_params=pltpu.CompilerParams(vmem_limit_bytes=56 * 2**20),
        cost_estimate=LIGHT,
    )(scalars, *weights, *gateds)


def hidden_back_kernel(count, scalars, *refs):
    terms = refs[:count]
    hidden, upstream, small, hidden_grad, hidden_grad_low, router_grad = refs[count:]
    width = hidden.shape[1]
    total = raise_(terms[0][...])
    for term in terms[1:]:
        total += raise_(term[...])
    logit_grad = lower(total[:, width:])
    scaled, inverse = moments(hidden[...])
    router_grad[...] = product_rows(lower(scaled), logit_grad)
    through = product_last(logit_grad, small[...])
    norm_grad = inverse * (
        through
        - jnp.mean(through, axis=-1, keepdims=True)
        - scaled * jnp.mean(through * scaled, axis=-1, keepdims=True)
    )
    result = raise_(upstream[:, :width]) + total[:, :width] + norm_grad
    hidden_grad[...] = result
    for index in range(hidden_grad_low.shape[0]):
        hidden_grad_low[index] = lower(result)


def expert_update_kernel(terms, *refs):
    grads = refs[: 2 * terms]
    weight, first, second, new, first_new, second_new = refs[2 * terms :]
    for half in range(2):
        for expert in range(weight.shape[0]):
            source = pl.ds(expert * EXPERT_H, EXPERT_H)
            columns = pl.ds(half * EXPERT_H, EXPERT_H)
            total = raise_(grads[half * terms][:, source])
            for grad in grads[half * terms + 1 : (half + 1) * terms]:
                total += raise_(grad[:, source])
            results = adamw_update(
                weight[expert, :, columns],
                first[expert, :, columns],
                second[expert, :, columns],
                total,
                rate_expert,
            )
            for target, result in zip((new, first_new, second_new), results):
                target[expert, :, columns] = result


def expert_update(grads, weight, first, second):
    count, rows, columns = weight.shape
    some = 3 if count % 3 == 0 else 1
    steps = count // some
    whole = pl.BlockSpec((some, rows, columns), lambda e: (e, 0, 0))
    shape = jax.ShapeDtypeStruct(weight.shape, jnp.float32)
    specs = [
        pl.BlockSpec(
            (rows, some * EXPERT_H), lambda e, start=half * steps * both: (0, start + e)
        )
        for half in range(2)
        for _, both in grads[half]
    ]
    return pl.pallas_call(
        functools.partial(expert_update_kernel, len(grads[0])),
        grid=(steps,),
        in_specs=specs + [whole] * 3,
        out_specs=[whole] * 3,
        out_shape=[shape] * 3,
        compiler_params=pltpu.CompilerParams(vmem_limit_bytes=56 * 2**20),
        cost_estimate=LIGHT,
    )(*[grad for half in grads for grad, _ in half], weight, first, second)


def halving_kernel(scalars, *refs):
    across, along = refs[8:]
    rows = across.shape[0] // 2
    for index in range(4):
        target, half = (across, along)[index // 2], pl.ds(index % 2 * rows, rows)
        target[half, :] = lower(raise_(refs[2 * index][...]) + raise_(refs[2 * index + 1][...]))


def halving(scalars, own, other, rows):
    columns = own.shape[1] // 2
    specs = []
    for row, column in ((1, 0), (3, 0), (2, 1), (3, 1)):
        specs += [pl.BlockSpec((rows, columns), lambda i, row=row, column=column: (row, column))] * 2
    shape = jax.ShapeDtypeStruct((2 * rows, columns), jnp.bfloat16)
    return pl.pallas_call(
        halving_kernel,
        grid=(1,),
        in_specs=[pl.BlockSpec(memory_space=pltpu.SMEM)] + specs,
        out_specs=[full(shape.shape)] * 2,
        out_shape=[shape] * 2,
        compiler_params=pltpu.CompilerParams(vmem_limit_bytes=56 * 2**20),
        cost_estimate=LIGHT,
    )(scalars, *[own, other] * 4)


def halved_kernel(scalars, own_two, other_two, own_one, other_one, across, along, first, second):
    first[...] = lower(raise_(own_two[...]) + raise_(other_two[...]) + raise_(across[...]))
    second[...] = lower(raise_(own_one[...]) + raise_(other_one[...]) + raise_(along[...]))


def halved(scalars, own, other, across, along):
    rows, columns = across.shape[0] // 2, across.shape[1]

    def block(row, column):
        return pl.BlockSpec((rows, columns), lambda i: (row, column))

    return pl.pallas_call(
        halved_kernel,
        grid=(1,),
        in_specs=[pl.BlockSpec(memory_space=pltpu.SMEM)]
        + [block(2, 0), block(2, 0), block(1, 1), block(1, 1), block(1, 0), block(1, 0)],
        out_specs=[block(0, 0)] * 2,
        out_shape=[jax.ShapeDtypeStruct((rows, columns), jnp.bfloat16)] * 2,
        compiler_params=pltpu.CompilerParams(vmem_limit_bytes=56 * 2**20),
        cost_estimate=LIGHT,
    )(scalars, own, other, own, other, across, along)


def dense_sum_kernel(scalars, *refs):
    count = refs[0].shape[0]
    terms, results = refs[:-count], refs[-count:]
    for index, result in enumerate(results):
        spot = scalars[0] ^ index
        total = raise_(terms[0][spot])
        for term in terms[1:]:
            total += raise_(term[spot])
        result[...] = lower(total)


def dense_update_kernel(scalars, *refs):
    sums, refs = refs[:HEADS], refs[HEADS:]
    inputs = [refs[3 * index : 3 * index + 3] for index in range(6)]
    outputs = [refs[3 * index : 3 * index + 3] for index in range(6, 12)]

    def update(index, gradient, columns, rate):
        results = adamw_update(*[ref[:, columns] for ref in inputs[index]], gradient, rate)
        for target, result in zip(outputs[index], results):
            target[:, columns] = result

    part, small = sums[0].shape[0], sums[0].shape[1] - OUTPUT_EDGE
    shared = jnp.zeros((part, small), jnp.float32)
    chosen = jnp.zeros((part, inputs[3][0].shape[1]), jnp.float32)
    for index, rows in enumerate(sums):
        head = scalars[0] ^ index
        for side in range(2):
            span = pl.ds(pl.multiple_of((side * HEADS + head) * HEAD_DIM, HEAD_DIM), HEAD_DIM)
            source = pl.ds(side * HEAD_DIM, HEAD_DIM)
            update(0, raise_(rows[:, source]), span, rate_query_key)
        span = pl.ds(pl.multiple_of(head * VALUE_WIDTH, HEAD_DIM), VALUE_WIDTH)
        update(1, raise_(rows[:, QK_EDGE:VALUE_EDGE]), span, rate_value)
        update(2, raise_(rows[:, VALUE_EDGE:OUTPUT_EDGE]), span, rate_output)
        last = rows[:, OUTPUT_EDGE:]
        source = lax.broadcasted_iota(jnp.int32, (small, chosen.shape[1]), 0)
        target = lax.broadcasted_iota(jnp.int32, (small, chosen.shape[1]), 1)
        side, entry = lax.div(source, ATT_EXPERTS), lax.rem(source, ATT_EXPERTS)
        table = (target == (side * HEADS + head) * ATT_EXPERTS + entry) & (source < SELECT_COUNT)
        chosen += product(last, lower(jnp.where(table, 1.0, 0.0)))
        shared += raise_(last)
    every = slice(None)
    update(3, chosen, every, rate_select)
    expert_total = inputs[4][0].shape[1]
    update(4, pltpu.roll(shared, small - SELECT_COUNT, 1)[:, :expert_total], every, rate_router)
    gain_column = SELECT_COUNT + expert_total
    diagonal = lax.broadcasted_iota(jnp.int32, (part, part), 0) == lax.broadcasted_iota(
        jnp.int32, (part, part), 1
    )
    gain = jnp.where(diagonal, shared[:, gain_column : gain_column + 1], 0.0)
    update(5, jnp.sum(gain, axis=0, keepdims=True), every, rate_gain)


def expert_rows_kernel(weight, rows):
    count = weight.shape[0]
    for expert in range(count):
        rows[:, pl.ds(expert * EXPERT_H, EXPERT_H)] = lower(weight[expert, :, :EXPERT_H])
        rows[:, pl.ds((count + expert) * EXPERT_H, EXPERT_H)] = lower(weight[expert, :, EXPERT_H:])


def expert_rows_of(weight):
    count, rows, columns = weight.shape
    return pl.pallas_call(
        expert_rows_kernel,
        out_shape=jax.ShapeDtypeStruct((rows, count * columns), jnp.bfloat16),
        compiler_params=pltpu.CompilerParams(vmem_limit_bytes=56 * 2**20),
        cost_estimate=LIGHT,
    )(weight)


def front_kernel(scalars, tokens, picks, cotangent, routes, token_rows, upstream):
    rows, width = tokens.shape
    token_rows[:, :width] = tokens[...]
    row = lax.broadcasted_iota(jnp.int32, (token_rows.shape[1] - width, rows), 0)
    chosen = jnp.zeros(row.shape, jnp.float32)
    for head in range(picks.shape[0]):
        start = head % HEADS * SELECT_COUNT + head // HEADS * ATT_EXPERTS
        for pick in range(picks.shape[1]):
            chosen = jnp.where(row == start + picks[head, pick : pick + 1, :], 1.0, chosen)
    token_rows[:, width:] = lower(chosen.T)
    position = scalars[0] * rows + lax.broadcasted_iota(jnp.int32, (rows, 1), 0)
    upstream[:, :width] = lower(jnp.where(position < scalars[1], raise_(cotangent[...]), 0.0))
    row = lax.broadcasted_iota(jnp.int32, (upstream.shape[1] - width, rows), 0)
    hot = jnp.zeros(row.shape, jnp.float32)
    for index in range(routes.shape[0]):
        hot = jnp.where(row == SELECT_COUNT + routes[index : index + 1, :], 1.0, hot)
    upstream[:, width:] = lower(hot.T)


def payload_kernel(scalars, upstream, qk, value, output, select, router, gain, payload):
    part = qk.shape[0]
    small = payload.shape[2] - OUTPUT_EDGE
    rows, width = upstream.shape[0], upstream.shape[1] - small
    expert_total = router.shape[1]
    position = scalars[0] * rows + lax.broadcasted_iota(jnp.int32, (rows, 1), 0)
    valid = position < scalars[1]
    hot = raise_(upstream[:, width:])
    counts = jnp.sum(jnp.where(valid, hot, 0.0), axis=0, keepdims=True)
    gain_column = SELECT_COUNT + expert_total
    count_columns = -(-expert_total // part)
    row = lax.broadcasted_iota(jnp.int32, (part, small), 0)
    lane = lax.broadcasted_iota(jnp.int32, (part, small), 1)
    shared = product(lower(router[...]), shift_back(expert_total, small, SELECT_COUNT))
    diagonal = lax.broadcasted_iota(jnp.int32, (part, part), 0) == lax.broadcasted_iota(
        jnp.int32, (part, part), 1
    )
    gain_rows = jnp.sum(jnp.where(diagonal, gain[...], 0.0), axis=1, keepdims=True)
    shared = jnp.where(lane == gain_column, gain_rows, shared)
    for column in range(count_columns):
        mine = lane - SELECT_COUNT == row * count_columns + column
        found = jnp.sum(jnp.where(mine, counts, 0.0), axis=1, keepdims=True)
        shared = jnp.where(lane == gain_column + 1 + column, found, shared)
    picked = lower(select[...])
    for head in range(HEADS):
        span = pl.ds(head * HEAD_DIM, HEAD_DIM)
        payload[head, :, :HEAD_DIM] = lower(qk[:, span])
        span = pl.ds((HEADS + head) * HEAD_DIM, HEAD_DIM)
        payload[head, :, HEAD_DIM:QK_EDGE] = lower(qk[:, span])
        span = pl.ds(head * VALUE_WIDTH, VALUE_WIDTH)
        payload[head, :, QK_EDGE:VALUE_EDGE] = lower(value[:, span])
        payload[head, :, VALUE_EDGE:OUTPUT_EDGE] = lower(output[:, span])
        source = lax.broadcasted_iota(jnp.int32, (picked.shape[1], small), 0)
        target = lax.broadcasted_iota(jnp.int32, (picked.shape[1], small), 1)
        side, entry = lax.div(target, ATT_EXPERTS), lax.rem(target, ATT_EXPERTS)
        table = (source == (side * HEADS + head) * ATT_EXPERTS + entry) & (target < SELECT_COUNT)
        chosen = product(picked, lower(jnp.where(table, 1.0, 0.0)))
        payload[head, :, OUTPUT_EDGE:] = lower(shared + chosen)


def shift_back(rows, columns, offset):
    source = lax.broadcasted_iota(jnp.int32, (rows, columns), 0)
    target = lax.broadcasted_iota(jnp.int32, (rows, columns), 1)
    return lower(jnp.where(target == source + offset, 1.0, 0.0))


def local(
    tokens,
    cotangent,
    lengths,
    picks,
    routes,
    qk_weight,
    qk_first,
    qk_second,
    value_weight,
    value_first,
    value_second,
    output_weight,
    output_first,
    output_second,
    select_weight,
    select_first,
    select_second,
    router_weight,
    router_first,
    router_second,
    gain_weight,
    gain_first,
    gain_second,
    expert_weight,
    expert_first,
    expert_second,
):
    row_count = tokens.shape[1]
    model_width = tokens.shape[2]
    group_count = lax.axis_size("dp")
    owner_count = lax.axis_size("expert")
    local_count = expert_weight.shape[0]
    expert_total = local_count * owner_count
    bucket_rows = row_count * group_count
    part = qk_weight.shape[0]
    place = lax.axis_index("dp")
    owner = lax.axis_index("expert")
    seq_len = lengths[0]
    sequence = tokens[0]
    scalars = jnp.stack(
        [place.astype(jnp.int32), seq_len.astype(jnp.int32), owner.astype(jnp.int32)]
    )
    spots = jnp.stack([place.astype(jnp.int32), owner.astype(jnp.int32)])
    low, high = jnp.bfloat16, jnp.float32

    def shaped(columns, kind, rows=bucket_rows):
        return jax.ShapeDtypeStruct((rows, columns), kind)

    gain_column = SELECT_COUNT + expert_total
    count_columns = -(-expert_total // part)
    small_used = gain_column + 1 + count_columns
    small_width = small_used + -small_used % 128
    token_width = model_width + HEADS * SELECT_COUNT + -(HEADS * SELECT_COUNT) % 128

    token_own, upstream = wide_call(
        front_kernel,
        [scalars, sequence, picks[0].transpose(1, 2, 0), cotangent[0], routes[0].T],
        [
            shaped(token_width, low, row_count),
            shaped(model_width + small_width, low, row_count),
        ],
    )
    expert_up = {0: upstream}
    for relative in range(2, owner_count, 2):
        if not forwarded(relative):
            expert_up[relative] = swap(upstream, "expert", relative)
    token_blocks = [token_own] + [
        swap(token_own, "dp", relative) for relative in range(1, group_count)
    ]

    (payload,) = wide_call(
        payload_kernel,
        [
            scalars,
            upstream,
            qk_weight,
            value_weight,
            output_weight,
            select_weight,
            router_weight,
            gain_weight[None],
        ],
        [jax.ShapeDtypeStruct((HEADS, part, OUTPUT_EDGE + small_width), low)],
    )
    mine = lax.all_to_all(payload, "dp", split_axis=0, concat_axis=0, tiled=True)
    mine = after(
        mine, *token_blocks[1:], *[up for relative, up in expert_up.items() if relative]
    )

    half = row_count // 2
    expert_own = after(expert_rows_of(expert_weight), mine)
    expert_pieces = [expert_own, swap(expert_own, "dp", 1), swap(expert_own, "dp", 2)]
    dense_blocks = gather_chips(mine)
    dense_others = swap(
        after(jnp.stack(dense_blocks), *expert_pieces[1:]), "expert", 1
    )

    cosine, sine = rope_tables(bucket_rows)
    if part % 16 == 0:
        chips, made = owner_count // 2, []
        given = dense_blocks + [dense_others]
    else:
        dense = jnp.zeros((group_count, owner_count) + mine.shape[1:], jnp.bfloat16)
        for chip, block in enumerate(dense_blocks):
            for other, rows in enumerate((block, dense_others[chip])):
                spot = owner ^ (2 * chip + other)
                dense = lax.dynamic_update_slice_in_dim(dense, rows[:, None], spot, axis=1)
        dense = dense.reshape(group_count, row_count, -1)
        chips, made, given = 0, [], [dense]
    dense_shape = jax.ShapeDtypeStruct((group_count, row_count, payload.shape[2]), low)
    if chips:
        made = [dense_shape]
    outputs = made + [
        shaped(HEAD_DIM, low),
        shaped(HEAD_DIM, low),
        shaped(HEAD_DIM, low),
        shaped(small_width, high),
        shaped(VALUE_WIDTH, high),
        shaped(HEAD_DIM, high),
        shaped(VALUE_WIDTH, low),
        shaped(HEAD_DIM, high),
        shaped(model_width, low),
        shaped(2 * local_count + -2 * local_count % 128, low, model_width),
        shaped(small_width, high, part),
    ]
    kept = staged_call(
        functools.partial(attention_kernel, group_count, gain_column, chips, local_count),
        [scalars] + token_blocks + [cosine, sine] + given,
        outputs,
        token_blocks + [cosine, sine, dense_shape] + outputs[len(made) :],
        [],
        group_count + 2 + owner_count + len(outputs) + 2 * group_count,
    )
    if chips:
        dense, kept = kept[0], kept[1:]
    saved, (branch, router_local, counts) = dict(zip(KEPT, kept)), kept[len(KEPT) :]
    for relative in range(2, owner_count, 2):
        if forwarded(relative):
            block = after(expert_up[relative ^ 2], branch)
            expert_up[relative] = swap(block, "expert", 2)
    expert_up = [expert_up[relative] for relative in range(0, owner_count, 2)]
    near = [after(piece, branch) for piece in expert_pieces]
    expert_others = [swap(piece, "expert", 1) for piece in near]
    far = [
        swap(expert_pieces[1][:half], "dp", 2),
        swap(expert_pieces[2][half:], "dp", 1),
    ]
    expert_others += [swap(after(piece, branch), "expert", 1) for piece in far]
    branch = scatter_rows(branch)
    hidden = add_blocks(raise_(sequence), after(branch, expert_up[-1], *expert_others))
    small = dense[:, :, OUTPUT_EDGE:].reshape(model_width, -1)
    expert_counts = counts[:, gain_column + 1 : small_used].reshape(-1)[:expert_total]
    expert_counts = expert_counts.astype(jnp.int32)

    hidden_low = lower(hidden)
    expert_both = expert_pieces + far + expert_others
    order = [0] + list(range(2, len(expert_up))) + [1]
    expert_rows, back, slopes, gateds = {0: hidden_low}, {}, {}, {}
    arriving = {}
    for relative in range(2, owner_count, 2):
        if not forwarded(relative):
            arriving[relative] = swap(hidden_low, "expert", relative)
    before = None
    for chip in order:
        if chip:
            others = [arriving[2]] if chip == order[1] else []
            block = after(arriving[2 * chip], before, *others)
            if chip % 2 == 0 and chip + 1 < len(expert_up):
                arriving[2 * chip + 2] = swap(block, "expert", 2)
            expert_rows[chip] = block
        back[chip], slopes[chip], gateds[chip] = expert_call(
            spots, expert_rows[chip], expert_up[chip], router_local, expert_both
        )
        before = slopes[chip]
    back_terms = send_expert([back[chip] for chip in range(len(order))])
    back_terms = [back_terms[chip] for chip in order]
    expert_rows, slopes, gateds = [
        [found[chip] for chip in range(len(order))] for found in (expert_rows, slopes, gateds)
    ]

    other_grads, own_grads = expert_grads(
        spots, expert_rows, expert_up, slopes, gateds, group_count
    )
    back_terms[1:] = [after(term, own_grads) for term in back_terms[1:]]

    hidden_grad, hidden_grad_low, router_grad = wide_call(
        functools.partial(hidden_back_kernel, len(back_terms)),
        [scalars] + back_terms + [hidden, upstream, small],
        [
            shaped(model_width, high, row_count),
            jax.ShapeDtypeStruct((group_count, row_count, model_width), low),
            shaped(small_width, high, model_width),
        ],
        limit=24,
    )
    hidden_grad_rows = exchange_rows(hidden_grad_low)
    produced = []
    for start in range(0, len(gateds), 4):
        produced += expert_out_call(
            after(spots, hidden_grad_low), expert_both, gateds[start : start + 4]
        )
    moe_terms = send_expert(produced)
    other_grads = swap(after(other_grads, hidden_grad_low), "expert", 1)

    across, along = halving(after(spots, *produced), own_grads, other_grads, row_count)
    across, along = swap(across, "dp", 1), swap(along, "dp", 2)
    layer_out = hidden
    for term in moe_terms:
        layer_out = layer_out + raise_(term)
    layer_out = lower(layer_out)

    scratch = [
        pltpu.VMEM((bucket_rows, HEAD_DIM), low),
        pltpu.VMEM((bucket_rows, small_width), high),
        pltpu.VMEM((bucket_rows, HEAD_DIM), high),
        pltpu.VMEM((bucket_rows, HEAD_DIM), high),
        pltpu.VMEM((bucket_rows, HEAD_DIM), high),
        pltpu.VMEM((bucket_rows, VALUE_WIDTH), low),
        pltpu.VMEM((bucket_rows, QK_EDGE), low),
        pltpu.VMEM((bucket_rows, small_width), low),
        pltpu.VMEM((bucket_rows, model_width), low),
    ]
    made = [dense_shape]
    if chips:
        made = [jax.ShapeDtypeStruct((chips, group_count, part, dense.shape[2]), low)] * 2
    saved.update(
        upstream=hidden_grad_rows, dense=dense, cosine=cosine, sine=sine, router_grad=router_grad
    )
    inputs = [saved[name] for name in BACK]
    terms_shape = shaped(model_width, low)
    *dense_parts, input_terms = staged_call(
        functools.partial(attention_back_kernel, group_count, gain_column, chips),
        [scalars] + inputs + token_blocks,
        made + [terms_shape],
        inputs + [dense_shape, terms_shape, terms_shape],
        scratch,
        len(inputs) + 2 * group_count + 3 * owner_count,
    )

    if not chips:
        dense_grad = dense_parts[0].reshape(group_count, owner_count, part, -1)
        dense_parts = [
            jnp.stack(
                [
                    lax.dynamic_index_in_dim(dense_grad, owner ^ relative, 1, keepdims=False)
                    for relative in range(side, owner_count, 2)
                ]
            )
            for side in range(2)
        ]
    late = after(spots, input_terms)
    first, second = halved(late, own_grads, other_grads, across, along)
    dense_parts[1] = after(dense_parts[1], first, second, *moe_terms)
    dense_parts = join(spots, dense_parts[0], swap(dense_parts[1], "expert", 1))
    first, second = swap(first, "dp", 2), swap(second, "dp", 1)
    input_grad = add_blocks(hidden_grad, scatter_rows(input_terms))
    dense_terms = send_expert(dense_parts)
    dense_terms[1:] = [after(term, input_grad, first, second) for term in dense_terms[1:]]
    dense_sums = wide_call(
        dense_sum_kernel,
        [scalars] + dense_terms,
        [jax.ShapeDtypeStruct(dense_terms[0].shape[1:], low)] * group_count,
    )
    dense_sums = [dense_sums[0]] + [
        swap(dense_sums[relative], "dp", relative) for relative in range(1, group_count)
    ]
    masters = [
        (qk_weight, qk_first, qk_second),
        (value_weight, value_first, value_second),
        (output_weight, output_first, output_second),
        (select_weight, select_first, select_second),
        (router_weight, router_first, router_second),
        (gain_weight[None], gain_first[None], gain_second[None]),
    ]
    masters = [array for group in masters for array in group]
    updated = wide_call(
        dense_update_kernel,
        [scalars] + dense_sums + masters,
        [jax.ShapeDtypeStruct(array.shape, high) for array in masters],
        limit=24,
    )
    updated = list(updated[:15]) + [array[0] for array in updated[15:]]
    expert_results = expert_update(
        [
            [(own_grads, 1), (other_grads, 1), (across, 0), (first, 0)],
            [(own_grads, 1), (other_grads, 1), (along, 0), (second, 0)],
        ],
        expert_weight,
        expert_first,
        expert_second,
    )
    return (layer_out[None], input_grad[None], *updated, *expert_results, expert_counts)


def solution(mesh):
    placed = (
        P("expert", "dp", None),
        P("expert", "dp", None),
        P("expert"),
        P("expert", "dp", None, None),
        P("expert", "dp", None),
        P(("dp", "expert"), None),
        P(("dp", "expert"), None),
        P(("dp", "expert"), None),
        P(("dp", "expert"), None),
        P(("dp", "expert"), None),
        P(("dp", "expert"), None),
        P(("dp", "expert"), None),
        P(("dp", "expert"), None),
        P(("dp", "expert"), None),
        P(("dp", "expert"), None),
        P(("dp", "expert"), None),
        P(("dp", "expert"), None),
        P(("dp", "expert"), None),
        P(("dp", "expert"), None),
        P(("dp", "expert"), None),
        P(("dp", "expert")),
        P(("dp", "expert")),
        P(("dp", "expert")),
        P("expert", "dp", None),
        P("expert", "dp", None),
        P("expert", "dp", None),
    )
    return jax.shard_map(
        local,
        mesh=mesh,
        in_specs=placed,
        out_specs=(
            P("expert", "dp", None),
            P("expert", "dp", None),
            P(("dp", "expert"), None),
            P(("dp", "expert"), None),
            P(("dp", "expert"), None),
            P(("dp", "expert"), None),
            P(("dp", "expert"), None),
            P(("dp", "expert"), None),
            P(("dp", "expert"), None),
            P(("dp", "expert"), None),
            P(("dp", "expert"), None),
            P(("dp", "expert"), None),
            P(("dp", "expert"), None),
            P(("dp", "expert"), None),
            P(("dp", "expert"), None),
            P(("dp", "expert"), None),
            P(("dp", "expert"), None),
            P(("dp", "expert")),
            P(("dp", "expert")),
            P(("dp", "expert")),
            P("expert", "dp", None),
            P("expert", "dp", None),
            P("expert", "dp", None),
            P(),
        ),
        check_vma=False,
    )
```

```python
import functools

import numpy as np
import jax
import jax.numpy as jnp
from jax import lax
from jax.experimental import pallas as pl
from jax.experimental.pallas import tpu as pltpu
from jax.sharding import PartitionSpec as P

HEADS = 4
HEAD_DIM = 128
ATT_EXPERTS = 5
EXPERT_H = 128
TOPK = 16
STEP = 10


norm_eps = 1e-05
beta_first = 0.9
beta_second = 0.95
adam_eps = 1e-08
weight_decay = 0.1
masked_score = -1e30
rope_base = 10000.0
rate_query_key = 0.04
rate_value = 0.03
rate_output = 2.0
rate_select = 0.03
rate_router = 0.015
rate_gain = 1.2
rate_expert = 0.05


def product(former, latter):
    return jnp.dot(former, latter, preferred_element_type=jnp.float32)


def product_rows(former, latter):
    return lax.dot_general(
        former, latter, (((0,), (0,)), ((), ())), preferred_element_type=jnp.float32
    )


def product_last(former, latter):
    return lax.dot_general(
        former, latter, (((1,), (1,)), ((), ())), preferred_element_type=jnp.float32
    )


def rope_tables(rows):
    half = HEAD_DIM // 2
    frequency = np.exp(-np.log(rope_base) * np.arange(half) / half)
    angles = np.arange(rows)[:, None] * frequency[None, :]
    cosine, sine = np.cos(angles), np.sin(angles)
    return (
        jnp.asarray(np.concatenate([cosine, cosine], axis=1), jnp.float32),
        jnp.asarray(np.concatenate([-sine, sine], axis=1), jnp.float32),
    )


def adamw_update(weight, first_moment, second_moment, gradient, rate):
    first_new = beta_first * first_moment + (1.0 - beta_first) * gradient
    second_new = beta_second * second_moment + (1.0 - beta_second) * gradient * gradient
    first_hat = first_new / (1.0 - beta_first**STEP)
    second_hat = second_new / (1.0 - beta_second**STEP)
    weight_new = weight - rate * (
        first_hat / (jnp.sqrt(second_hat) + adam_eps) + weight_decay * weight
    )
    return (weight_new, first_new, second_new)


LIGHT = pl.CostEstimate(flops=1000, bytes_accessed=1000, transcendentals=0)


def swap(values, axis, relative):
    count = lax.axis_size(axis)
    return lax.ppermute(values, axis, [(place, place ^ relative) for place in range(count)])


def lower(values):
    return values.astype(jnp.bfloat16)


def raise_(values):
    return values.astype(jnp.float32)


def after(values, *others):
    return lax.optimization_barrier((values,) + others)[0]


def exchange_rows(copies):
    blocks = lax.all_to_all(copies, "dp", split_axis=0, concat_axis=0, tiled=True)
    return blocks.reshape((-1,) + copies.shape[2:])


def scatter_rows(values):
    count = lax.axis_size("dp")
    blocks = values.reshape((count, values.shape[0] // count) + values.shape[1:])
    return lax.all_to_all(blocks, "dp", split_axis=0, concat_axis=0, tiled=True)


def add_blocks(values, blocks):
    for index in range(blocks.shape[0]):
        values = values + raise_(blocks[index])
    return values


def join_kernel(scalars, evens, odds, *results):
    for chip, result in enumerate(results):
        result[...] = lower(raise_(evens[chip]) + raise_(odds[chip]))


def join(scalars, evens, odds):
    shape = jax.ShapeDtypeStruct(evens.shape[1:], jnp.bfloat16)
    return list(wide_call(join_kernel, [scalars, evens, odds], [shape] * evens.shape[0]))


def forwarded(relative):
    return relative & 2 and relative > 2


def gather_chips(values):
    return [values] + [
        swap(values, "expert", relative) for relative in range(2, lax.axis_size("expert"), 2)
    ]


def send_expert(joined):
    return [joined[0]] + [
        swap(term, "expert", 2 * index) for index, term in enumerate(joined) if index
    ]


def full(shape):
    return pl.BlockSpec(shape, lambda *_: (0,) * len(shape))


def wide_call(kernel, inputs, outputs, limit=56):
    specs = [pl.BlockSpec(memory_space=pltpu.SMEM)] + [full(value.shape) for value in inputs[1:]]
    return pl.pallas_call(
        kernel,
        grid=(1,),
        in_specs=specs,
        out_specs=[full(value.shape) for value in outputs],
        out_shape=outputs,
        compiler_params=pltpu.CompilerParams(vmem_limit_bytes=limit * 2**20),
        cost_estimate=LIGHT,
    )(*inputs)


class Copies:
    def __init__(self, sems):
        self.sems, self.count, self.waiting = sems, 0, {}

    def start(self, name, source, target):
        copy = pltpu.make_async_copy(source, target, self.sems.at[self.count])
        copy.start()
        self.count += 1
        self.waiting.setdefault(name, []).append(copy)

    def wait(self, *names):
        for name in names:
            for copy in self.waiting.pop(name, []):
                copy.wait()


def staged_call(kernel, inputs, outputs, held, scratch, copies):
    somewhere = pl.BlockSpec(memory_space=pl.ANY)
    return pl.pallas_call(
        kernel,
        grid=(1,),
        in_specs=[pl.BlockSpec(memory_space=pltpu.SMEM)] + [somewhere] * (len(inputs) - 1),
        out_specs=[somewhere] * len(outputs),
        out_shape=outputs,
        scratch_shapes=[pltpu.VMEM(value.shape, value.dtype) for value in held]
        + list(scratch)
        + [pltpu.SemaphoreType.DMA((copies,))],
        compiler_params=pltpu.CompilerParams(vmem_limit_bytes=56 * 2**20),
        cost_estimate=LIGHT,
    )(*inputs)


def shift_table(rows, columns, offset, count):
    source = lax.broadcasted_iota(jnp.int32, (rows, columns), 0)
    target = lax.broadcasted_iota(jnp.int32, (rows, columns), 1)
    return lower(jnp.where((source == target + offset) & (target < count), 1.0, 0.0))


def moments(values):
    center = values - jnp.mean(values, axis=-1, keepdims=True)
    inverse = lax.rsqrt(jnp.mean(center * center, axis=-1, keepdims=True) + norm_eps)
    return center * inverse, inverse


def turn(rows, cosine, signed_sine, direction):
    return rows * cosine + direction * pltpu.roll(rows, HEAD_DIM // 2, 1) * signed_sine


def masked_scores(queries, key_rows, seq_len, start):
    scores = product_last(queries, key_rows) * HEAD_DIM ** (-0.5)
    query_place = start + lax.broadcasted_iota(jnp.int32, scores.shape, 0)
    key_place = lax.broadcasted_iota(jnp.int32, scores.shape, 1)
    return jnp.where((key_place <= query_place) & (key_place < seq_len), scores, masked_score)


VALUE_WIDTH = ATT_EXPERTS * HEAD_DIM
QK_EDGE = 2 * HEAD_DIM
VALUE_EDGE = QK_EDGE + VALUE_WIDTH
OUTPUT_EDGE = VALUE_EDGE + VALUE_WIDTH
SELECT_COUNT = 2 * ATT_EXPERTS


KEPT = ("queries", "key_rows", "values", "weighting", "projected", "attended", "mixed", "log_total")


def attention_kernel(blocks, gain_column, chips, local_count, scalars, *refs):
    given = blocks + 2 + (chips + 1 if chips else 1)
    outs = (["dense"] if chips else []) + list(KEPT) + ["branch", "router_local", "counts"]
    count = len(outs)
    sources, targets = refs[:given], dict(zip(outs, refs[given : given + count]))
    tokens, (cosine, sine, dense), refs = (
        refs[given + count : given + count + blocks],
        refs[given + count + blocks : given + count + blocks + 3],
        refs[given + count + blocks + 3 : -1] + refs[-1:],
    )
    *kept, branch, router_local, counts, sems = refs
    (queries, key_rows, values, weighting, projected, attended, mixed, log_total) = kept
    copies = Copies(sems)
    for index in range(blocks):
        copies.start("in", sources[index], tokens[index])
    copies.start("in", sources[blocks], cosine)
    copies.start("in", sources[blocks + 1], sine)
    if chips:
        evens, odds = sources[blocks + 2 : blocks + 2 + chips], sources[blocks + 2 + chips]
        part = odds.shape[2]
        for chip in range(chips):
            for other, rows in ((0, evens[chip]), (1, odds.at[chip])):
                start = (scalars[2] ^ (2 * chip + other)) * part
                copies.start("in", rows, dense.at[:, pl.ds(pl.multiple_of(start, part), part), :])
    else:
        copies.start("in", sources[blocks + 2], dense)
    copies.wait("in")
    if chips:
        copies.start("out", dense, targets["dense"])
    place, seq_len = scalars[0], scalars[1]
    width = dense.shape[0] * dense.shape[1]
    block = tokens[0].shape[0]

    def weight(start, end):
        return dense[:, :, start:end].reshape(width, end - start)

    small_rows = weight(OUTPUT_EDGE, dense.shape[2])
    count = local_count
    source = lax.broadcasted_iota(jnp.int32, (small_rows.shape[1], router_local.shape[1]), 0)
    entry = lax.broadcasted_iota(jnp.int32, source.shape, 1)
    first = SELECT_COUNT + scalars[2] * count + entry
    second = SELECT_COUNT + (scalars[2] ^ 1) * count + entry - count
    table = (source == jnp.where(entry < count, first, second)) & (entry < 2 * count)
    router_local[...] = lower(product(small_rows, lower(jnp.where(table, 1.0, 0.0))))
    part = counts.shape[0]
    total = raise_(small_rows[:part])
    for start in range(part, width, part):
        total += raise_(small_rows[start : start + part])
    counts[...] = total
    copies.start("out", counts, targets["counts"])
    copies.start("out", router_local, targets["router_local"])
    gain = raise_(small_rows).T[gain_column : gain_column + 1, :]
    head_table = shift_table(
        tokens[0].shape[1] - width, dense.shape[2] - OUTPUT_EDGE, place * SELECT_COUNT, SELECT_COUNT
    )
    for index in range(blocks):
        span = pl.ds(pl.multiple_of((place ^ index) * block, block), block)
        rows = tokens[index][:, :width]
        scaled, _ = moments(raise_(rows))
        normed_rows = lower(scaled * gain)
        both = product(normed_rows, weight(0, QK_EDGE))
        queries[span, :] = lower(turn(both[:, :HEAD_DIM], cosine[span, :], sine[span, :], 1.0))
        key_rows[span, :] = lower(turn(both[:, HEAD_DIM:], cosine[span, :], sine[span, :], 1.0))
        chosen = product(tokens[index][:, width:], head_table)
        sigma_rows = jax.nn.sigmoid(product(normed_rows, small_rows))
        weights = sigma_rows * chosen
        weighting[span, :] = weights
        columns = product(rows, weight(QK_EDGE, VALUE_EDGE))
        projected[span, :] = columns
        total = weights[:, 0:1] * columns[:, :HEAD_DIM]
        for expert in range(1, ATT_EXPERTS):
            total += (
                weights[:, expert : expert + 1]
                * columns[:, expert * HEAD_DIM : (expert + 1) * HEAD_DIM]
            )
        values[span, :] = lower(total)
    for name, ref in zip(KEPT[:5], kept):
        copies.start("out", ref, targets[name])
    for start in range(0, blocks * block, block):
        span = pl.ds(start, block)
        scores = masked_scores(queries[span, :], key_rows[...], seq_len, start)
        highest = jnp.max(scores, axis=-1, keepdims=True)
        raised = jnp.exp(scores - highest)
        row_total = jnp.sum(raised, axis=-1, keepdims=True)
        log_total[span, :] = jnp.broadcast_to(highest + jnp.log(row_total), (block, HEAD_DIM))
        rows = product(lower(raised / row_total), values[...])
        attended[span, :] = rows
        weights = weighting[span, :]
        for expert in range(ATT_EXPERTS):
            mixed[span, pl.ds(expert * HEAD_DIM, HEAD_DIM)] = lower(
                weights[:, ATT_EXPERTS + expert : ATT_EXPERTS + expert + 1] * rows
            )
        branch[span, :] = lower(product_last(mixed[span, :], weight(VALUE_EDGE, OUTPUT_EDGE)))
        for name, ref in (("mixed", mixed), ("branch", branch)):
            copies.start("out", ref.at[span, :], targets[name].at[span, :])
    copies.start("out", attended, targets["attended"])
    copies.start("out", log_total, targets["log_total"])
    copies.wait("out")


BACK = ("upstream", "dense", "weighting", "attended", "mixed", "queries", "key_rows", "values") + (
    "log_total",
    "projected",
    "cosine",
    "sine",
    "router_grad",
)


def attention_back_kernel(blocks, gain_column, chips, scalars, *refs):
    count = len(BACK)
    sources, token_blocks, refs = refs[:count], refs[count : count + blocks], refs[count + blocks :]
    results, out_terms, refs = refs[: 2 if chips else 1], refs[2 if chips else 1], refs[3 if chips else 2 :]
    held, (grads, terms, tokens), refs = refs[:count], refs[count : count + 3], refs[count + 3 :]
    (upstream, dense, weighting, attended, mixed, queries, key_rows, values, log_total) = held[:9]
    projected, cosine, sine, router_grad = held[9:]
    (attended_grad, weight_grad, key_grad, value_grad, query_grad) = refs[:5]
    projected_grad, pair_grad, select_grad, normed, sems = refs[5:]
    copies = Copies(sems)
    for name, source, target in zip(BACK, sources, held):
        copies.start(name, source, target)
    block = token_blocks[0].shape[0]
    for index, rows in enumerate(token_blocks):
        span = pl.ds(pl.multiple_of((scalars[0] ^ index) * block, block), block)
        copies.start("tokens", rows.at[:, pl.ds(0, tokens.shape[1])], tokens.at[span, :])

    def weight(start, end):
        return dense[:, :, start:end].reshape(tokens.shape[1], end - start)

    def leave(columns):
        if not chips:
            copies.start("out", grads.at[:, :, columns], results[0].at[:, :, columns])
            return
        part = results[0].shape[2]
        for relative in range(2 * chips):
            start = pl.multiple_of((scalars[2] ^ relative) * part, part)
            target = results[relative % 2].at[relative // 2, :, :, columns]
            copies.start("out", grads.at[:, pl.ds(start, part), columns], target)

    def keep(start, values):
        columns = pl.ds(start, values.shape[1])
        grads[:, :, columns] = values.reshape(grads.shape[:2] + values.shape[1:])

    copies.wait("upstream", "dense", "weighting", "attended")
    seq_len = scalars[1]
    width = tokens.shape[1]
    small = dense.shape[2] - OUTPUT_EDGE
    lane = lax.broadcasted_iota(jnp.int32, (block, small), 1)
    scale = HEAD_DIM ** (-0.5)
    gain = raise_(weight(OUTPUT_EDGE, dense.shape[2])).T[gain_column : gain_column + 1, :]
    for start in range(0, tokens.shape[0], block):
        span = pl.ds(start, block)
        mixed_grad = product(upstream[span, :], weight(VALUE_EDGE, OUTPUT_EDGE))
        weights = weighting[span, :]
        heads = attended[span, :]
        total = jnp.zeros((block, HEAD_DIM), jnp.float32)
        found = jnp.zeros((block, small), jnp.float32)
        for expert in range(ATT_EXPERTS):
            piece = mixed_grad[:, expert * HEAD_DIM : (expert + 1) * HEAD_DIM]
            column = ATT_EXPERTS + expert
            total += weights[:, column : column + 1] * piece
            found = jnp.where(lane == column, jnp.sum(piece * heads, axis=1, keepdims=True), found)
        attended_grad[span, :] = lower(total)
        weight_grad[span, :] = found
    copies.wait("mixed")
    keep(VALUE_EDGE, lower(product_rows(upstream[...], mixed[...])))
    leave(pl.ds(VALUE_EDGE, OUTPUT_EDGE - VALUE_EDGE))
    copies.wait("queries", "key_rows", "values", "log_total")
    for start in range(0, tokens.shape[0], block):
        span = pl.ds(start, block)
        scores = masked_scores(queries[span, :], key_rows[...], seq_len, start)
        probs = jnp.exp(scores - log_total[span, :1])
        prob_grad = product_last(attended_grad[span, :], values[...])
        delta = jnp.sum(probs * prob_grad, axis=-1, keepdims=True)
        score_grad = lower(probs * (prob_grad - delta))
        query_grad[span, :] = product(score_grad, key_rows[...]) * scale
        key_terms = product_rows(score_grad, queries[span, :])
        value_terms = product_rows(lower(probs), attended_grad[span, :])
        if start:
            key_grad[...] += key_terms
            value_grad[...] += value_terms
        else:
            key_grad[...] = key_terms
            value_grad[...] = value_terms
    copies.wait("projected", "cosine", "sine", "router_grad", "tokens")
    gain_grad = jnp.zeros((1, width), jnp.float32)
    for start in range(0, tokens.shape[0], block):
        span = pl.ds(start, block)
        rows = value_grad[span, :]
        weights = weighting[span, :]
        found = weight_grad[span, :]
        for expert in range(ATT_EXPERTS):
            piece = pl.ds(expert * HEAD_DIM, HEAD_DIM)
            projected_grad[span, piece] = lower(weights[:, expert : expert + 1] * rows)
            found = jnp.where(
                lane == expert,
                jnp.sum(rows * projected[span, piece], axis=1, keepdims=True),
                found,
            )
        pair_grad[span, :HEAD_DIM] = lower(
            turn(query_grad[span, :], cosine[span, :], sine[span, :], -1.0)
        )
        pair_grad[span, HEAD_DIM:] = lower(
            turn(key_grad[span, :] * scale, cosine[span, :], sine[span, :], -1.0)
        )
        select_rows = lower(found * weights * (1.0 - weights))
        select_grad[span, :] = select_rows
        normed_grad = product_last(pair_grad[span, :], weight(0, QK_EDGE)) + product_last(
            select_rows, weight(OUTPUT_EDGE, dense.shape[2])
        )
        scaled, inverse = moments(raise_(tokens[span, :]))
        normed[span, :] = lower(scaled * gain)
        gain_grad += jnp.sum(normed_grad * scaled, axis=0, keepdims=True)
        through = normed_grad * gain
        norm_grad = inverse * (
            through
            - jnp.mean(through, axis=-1, keepdims=True)
            - scaled * jnp.mean(through * scaled, axis=-1, keepdims=True)
        )
        terms[span, :] = lower(
            product_last(projected_grad[span, :], weight(QK_EDGE, VALUE_EDGE)) + norm_grad
        )
        copies.start("out", terms.at[span, :], out_terms.at[span, :])
    keep(QK_EDGE, lower(product_rows(tokens[...], projected_grad[...])))
    keep(0, lower(product_rows(normed[...], pair_grad[...])))
    row = lax.broadcasted_iota(jnp.int32, (small, width), 0)
    gain_part = jnp.where(row == gain_column, gain_grad, 0.0).T
    rest = product_rows(normed[...], select_grad[...]) + gain_part + router_grad[...]
    keep(OUTPUT_EDGE, lower(rest))
    leave(pl.ds(0, VALUE_EDGE))
    leave(pl.ds(OUTPUT_EDGE, small))
    copies.wait("out")


def piece_copies(place, pieces, target, columns, sems):
    part, last = pieces[0].shape[0], len(pieces) - 2
    half = part // 2
    copies = []
    for index, piece in enumerate(pieces):
        start = (place ^ min(index, last)) * part + (half if index > last else 0)
        rows = pl.ds(pl.multiple_of(start, half), piece.shape[0])
        source = piece.at[:, columns]
        copies.append(pltpu.make_async_copy(source, target.at[rows, :], sems.at[index]))
    return copies


def expert_kernel(pieces, scalars, rows, up, router, *refs):
    weights = refs[: 2 * pieces]
    back, slope, gated, insides, outsides, sems = refs[2 * pieces :]
    block, width = rows.shape
    hidden = slope.shape[1] // 2
    count = hidden // EXPERT_H
    copies = []
    for side in range(2):
        own = weights[side * pieces : (side + 1) * pieces]
        copies.append(
            piece_copies(scalars[0], own, insides.at[side], pl.ds(0, hidden), sems.at[side, 0])
            + piece_copies(
                scalars[0], own, outsides.at[side], pl.ds(hidden, hidden), sems.at[side, 1]
            )
        )
        for copy in copies[side]:
            copy.start()
    small = up.shape[1] - width
    lanes = router.shape[1]
    offsets = [SELECT_COUNT + (scalars[1] ^ index) * count for index in range(2)]

    def column_of(entry):
        return jnp.where(entry < count, offsets[0] + entry, offsets[1] + entry - count)

    source = lax.broadcasted_iota(jnp.int32, (small, lanes), 0)
    entry = lax.broadcasted_iota(jnp.int32, (small, lanes), 1)
    pick_table = lower(jnp.where((source == column_of(entry)) & (entry < 2 * count), 1.0, 0.0))
    entry = lax.broadcasted_iota(jnp.int32, (lanes, small), 0)
    target = lax.broadcasted_iota(jnp.int32, (lanes, small), 1)
    place_table = lower(jnp.where((target == column_of(entry)) & (entry < 2 * count), 1.0, 0.0))
    lane = lax.broadcasted_iota(jnp.int32, (block, lanes), 1)
    scaled, _ = moments(raise_(rows[...]))
    sigma_gate = jax.nn.sigmoid(product(lower(scaled), router[...]))
    gates = sigma_gate * product(up[:, width:], pick_table)
    found = jnp.zeros((block, lanes), jnp.float32)
    for first in range(0, 2 * count, 2):
        side = first // count
        if first % count == 0:
            for copy in copies[side]:
                copy.wait()
        local = pl.ds(first % count * EXPERT_H, 2 * EXPERT_H)
        inner = product(rows[...], insides[side, :, local])
        terms = product(up[:, :width], outsides[side, :, local])
        sigma = jax.nn.sigmoid(inner)
        silu = inner * sigma
        active = raise_(lower(silu))
        both = terms * active
        tilt = sigma + silu * (1.0 - sigma)
        for k in range(2):
            part = slice(k * EXPERT_H, (k + 1) * EXPERT_H)
            columns = pl.ds((first + k) * EXPERT_H, EXPERT_H)
            gate = gates[:, first + k : first + k + 1]
            gated[:, columns] = lower(gate * active[:, part])
            slope[:, columns] = lower(gate * terms[:, part] * tilt[:, part])
            summed = jnp.sum(both[:, part], axis=1, keepdims=True)
            found = jnp.where(lane == first + k, summed, found)
    back[:, :width] = lower(
        product_last(slope[:, :hidden], insides[0]) + product_last(slope[:, hidden:], insides[1])
    )
    back[:, width:] = lower(product(lower(found * gates * (1.0 - sigma_gate)), place_table))


def expert_call(scalars, rows, up, router, weights):
    block, width = rows.shape
    hidden = weights[0].shape[1] // 2
    pieces = len(weights) // 2
    outputs = [
        jax.ShapeDtypeStruct(up.shape, jnp.bfloat16),
        jax.ShapeDtypeStruct((block, 2 * hidden), jnp.bfloat16),
        jax.ShapeDtypeStruct((block, 2 * hidden), jnp.bfloat16),
    ]
    return pl.pallas_call(
        functools.partial(expert_kernel, pieces),
        grid=(1,),
        in_specs=[pl.BlockSpec(memory_space=pltpu.SMEM)]
        + [full(value.shape) for value in (rows, up, router)]
        + [pl.BlockSpec(memory_space=pl.ANY)] * len(weights),
        out_specs=[full(value.shape) for value in outputs],
        out_shape=outputs,
        scratch_shapes=[
            pltpu.VMEM((2, width, hidden), jnp.bfloat16),
            pltpu.VMEM((2, width, hidden), jnp.bfloat16),
            pltpu.SemaphoreType.DMA((2, 2, pieces)),
        ],
        compiler_params=pltpu.CompilerParams(vmem_limit_bytes=56 * 2**20),
        cost_estimate=LIGHT,
    )(scalars, rows, up, router, *weights)


def expert_grad_kernel(chips, blocks, scalars, *refs):
    rows = refs[:chips]
    ups = refs[chips : 2 * chips]
    slopes = refs[2 * chips : 3 * chips]
    gateds = refs[3 * chips : 4 * chips]
    width = rows[0].shape[1]
    part = width // blocks
    quarter = pl.num_programs(0) // 4

    def total(lefts, rights, target):
        for index in range(blocks):
            columns = pl.ds(pl.multiple_of((scalars[0] ^ index) * part, part), part)
            result = product_rows(lefts[0][:, columns], rights[0][...])
            for left, right in zip(lefts[1:], rights[1:]):
                result += product_rows(left[:, columns], right[...])
            target[pl.ds(index * part, part), :] = lower(result)

    for phase in range(4):

        @pl.when(pl.program_id(0) // quarter == phase)
        def _(phase=phase):
            lefts, rights = ((rows, slopes), (ups, gateds))[phase % 2]
            total(lefts, rights, refs[4 * chips + phase // 2])


def expert_grads(scalars, rows, ups, slopes, gateds, blocks):
    chips = len(slopes)
    block, width = rows[0].shape
    hidden = slopes[0].shape[1] // 2
    tile = hidden // 2
    once = pl.Buffered(buffer_count=1)

    def slope_at(j):
        return 0, jnp.where(j < 4, 2 + jnp.minimum(j, 1), jnp.minimum(j - 4, 1))

    def gated_at(j):
        return 0, jnp.where(j < 4, 2 + jnp.maximum(j - 2, 0), jnp.maximum(j - 6, 0))

    shape = jax.ShapeDtypeStruct((width, 2 * hidden), jnp.bfloat16)
    return pl.pallas_call(
        functools.partial(expert_grad_kernel, chips, blocks),
        grid=(8,),
        in_specs=[pl.BlockSpec(memory_space=pltpu.SMEM)]
        + [pl.BlockSpec(v.shape, lambda j: (0, 0), pipeline_mode=once) for v in rows + ups]
        + [pl.BlockSpec((block, tile), slope_at)] * chips
        + [pl.BlockSpec((block, tile), gated_at)] * chips,
        out_specs=[
            pl.BlockSpec((width, tile), lambda j: (0, jnp.minimum(j, 3))),
            pl.BlockSpec((width, tile), lambda j: (0, jnp.maximum(j - 4, 0))),
        ],
        out_shape=[shape, shape],
        compiler_params=pltpu.CompilerParams(vmem_limit_bytes=56 * 2**20),
        cost_estimate=LIGHT,
    )(scalars, *rows, *ups, *slopes, *gateds)


def expert_out_kernel(pieces, scalars, *refs):
    weights, refs = refs[: 2 * pieces], refs[2 * pieces :]
    count = (len(refs) - 5) // 2
    gateds, results = refs[:count], refs[count : 2 * count]
    outsides, lefts, held, sems, gated_sems = refs[2 * count :]
    hidden = outsides.shape[2]
    block, width = results[0].shape
    tile = min(256, width)
    copies = []
    for side in range(2):
        own = weights[side * pieces : (side + 1) * pieces]
        columns = pl.ds(hidden, hidden)
        started = piece_copies(scalars[0], own, outsides.at[side], columns, sems.at[side])
        for index, gated in enumerate(gateds):
            source = gated.at[:, pl.ds(side * hidden, hidden)]
            target = lefts.at[side, pl.ds(index * block, block), :]
            started.append(pltpu.make_async_copy(source, target, gated_sems.at[side, index]))
        for copy in started:
            copy.start()
        copies.append(started)
    for side in range(2):
        for copy in copies[side]:
            copy.wait()
        for start in range(0, width, tile):
            columns = pl.ds(start, tile)
            total = product_last(lefts[side], outsides[side, columns, :])
            if side == 0:
                held[:, columns] = total
            else:
                total += held[:, columns]
                for index, result in enumerate(results):
                    result[:, columns] = lower(total[index * block : (index + 1) * block])


def expert_out_call(scalars, weights, gateds):
    pieces, count = len(weights) // 2, len(gateds)
    hidden = weights[0].shape[1] // 2
    width = sum(weight.shape[0] for weight in weights[:pieces])
    block = gateds[0].shape[0]
    return pl.pallas_call(
        functools.partial(expert_out_kernel, pieces),
        grid=(1,),
        in_specs=[pl.BlockSpec(memory_space=pltpu.SMEM)]
        + [pl.BlockSpec(memory_space=pl.ANY)] * (len(weights) + count),
        out_specs=[full((block, width))] * count,
        out_shape=[jax.ShapeDtypeStruct((block, width), jnp.bfloat16)] * count,
        scratch_shapes=[
            pltpu.VMEM((2, width, hidden), jnp.bfloat16),
            pltpu.VMEM((2, count * block, hidden), jnp.bfloat16),
            pltpu.VMEM((count * block, width), jnp.float32),
            pltpu.SemaphoreType.DMA((2, pieces)),
            pltpu.SemaphoreType.DMA((2, count)),
        ],
        compiler_params=pltpu.CompilerParams(vmem_limit_bytes=56 * 2**20),
        cost_estimate=LIGHT,
    )(scalars, *weights, *gateds)


def hidden_back_kernel(count, scalars, *refs):
    terms = refs[:count]
    hidden, upstream, small, hidden_grad, hidden_grad_low, router_grad = refs[count:]
    width = hidden.shape[1]
    total = raise_(terms[0][...])
    for term in terms[1:]:
        total += raise_(term[...])
    logit_grad = lower(total[:, width:])
    scaled, inverse = moments(hidden[...])
    router_grad[...] = product_rows(lower(scaled), logit_grad)
    through = product_last(logit_grad, small[...])
    norm_grad = inverse * (
        through
        - jnp.mean(through, axis=-1, keepdims=True)
        - scaled * jnp.mean(through * scaled, axis=-1, keepdims=True)
    )
    result = raise_(upstream[:, :width]) + total[:, :width] + norm_grad
    hidden_grad[...] = result
    for index in range(hidden_grad_low.shape[0]):
        hidden_grad_low[index] = lower(result)


def hidden_kernel(scalars, sequence, blocks, hidden, hidden_low):
    total = raise_(sequence[...])
    for index in range(blocks.shape[0]):
        total += raise_(blocks[index])
    hidden[...] = total
    hidden_low[...] = lower(total)


def kept_kernel(scalars, own, other, across, along, kept):
    columns = across.shape[1]
    for half, received in enumerate((across, along)):
        span = pl.ds(half * columns, columns)
        kept[:, span] = raise_(own[:, span]) + raise_(other[:, span]) + raise_(received[...])


def kept_rows(scalars, own, other, across, along):
    rows, columns = across.shape[0] // 2, own.shape[1]
    wide = pl.BlockSpec((rows, columns), lambda i: (0, 0))
    half = pl.BlockSpec((rows, columns // 2), lambda i: (0, 0))
    return pl.pallas_call(
        kept_kernel,
        grid=(1,),
        in_specs=[pl.BlockSpec(memory_space=pltpu.SMEM), wide, wide, half, half],
        out_specs=wide,
        out_shape=jax.ShapeDtypeStruct((rows, columns), jnp.float32),
        compiler_params=pltpu.CompilerParams(vmem_limit_bytes=56 * 2**20),
        cost_estimate=LIGHT,
    )(scalars, own, other, across, along)


def expert_update_kernel(*refs):
    grads, (weight, first, second, new, first_new, second_new) = refs[:4], refs[4:]
    for half in range(2):
        for expert in range(weight.shape[0]):
            source = pl.ds(expert * EXPERT_H, EXPERT_H)
            columns = pl.ds(half * EXPERT_H, EXPERT_H)
            results = adamw_update(
                weight[expert, :, columns],
                first[expert, :, columns],
                second[expert, :, columns],
                grads[2 * half][:, source] + raise_(grads[2 * half + 1][:, source]),
                rate_expert,
            )
            for target, result in zip((new, first_new, second_new), results):
                target[expert, :, columns] = result


def expert_update(kept, last, weight, first, second):
    count, rows, columns = weight.shape
    some = 3 if count % 3 == 0 else 1
    steps = count // some
    width = some * EXPERT_H
    whole = pl.BlockSpec((some, rows, columns), lambda e: (e, 0, 0))
    shape = jax.ShapeDtypeStruct(weight.shape, jnp.float32)
    specs, terms = [], []
    for half in range(2):
        specs.append(pl.BlockSpec((rows, width), lambda e, start=half * steps: (0, start + e)))
        specs.append(pl.BlockSpec((rows, width), lambda e: (0, e)))
        terms += [kept, last[half]]
    return pl.pallas_call(
        expert_update_kernel,
        grid=(steps,),
        in_specs=specs + [whole] * 3,
        out_specs=[whole] * 3,
        out_shape=[shape] * 3,
        compiler_params=pltpu.CompilerParams(vmem_limit_bytes=56 * 2**20),
        cost_estimate=LIGHT,
    )(*terms, weight, first, second)


def halving_kernel(scalars, *refs):
    across, along = refs[8:]
    rows = across.shape[0] // 2
    for index in range(4):
        target, half = (across, along)[index // 2], pl.ds(index % 2 * rows, rows)
        target[half, :] = lower(raise_(refs[2 * index][...]) + raise_(refs[2 * index + 1][...]))


def halving(scalars, own, other, rows):
    columns = own.shape[1] // 2
    specs = []
    for row, column in ((1, 0), (3, 0), (2, 1), (3, 1)):
        specs += [pl.BlockSpec((rows, columns), lambda i, row=row, column=column: (row, column))] * 2
    shape = jax.ShapeDtypeStruct((2 * rows, columns), jnp.bfloat16)
    return pl.pallas_call(
        halving_kernel,
        grid=(1,),
        in_specs=[pl.BlockSpec(memory_space=pltpu.SMEM)] + specs,
        out_specs=[full(shape.shape)] * 2,
        out_shape=[shape] * 2,
        compiler_params=pltpu.CompilerParams(vmem_limit_bytes=56 * 2**20),
        cost_estimate=LIGHT,
    )(scalars, *[own, other] * 4)


def halved_kernel(scalars, own_two, other_two, own_one, other_one, across, along, first, second):
    first[...] = lower(raise_(own_two[...]) + raise_(other_two[...]) + raise_(across[...]))
    second[...] = lower(raise_(own_one[...]) + raise_(other_one[...]) + raise_(along[...]))


def halved(scalars, own, other, across, along):
    rows, columns = across.shape[0] // 2, across.shape[1]

    def block(row, column):
        return pl.BlockSpec((rows, columns), lambda i: (row, column))

    return pl.pallas_call(
        halved_kernel,
        grid=(1,),
        in_specs=[pl.BlockSpec(memory_space=pltpu.SMEM)]
        + [block(2, 0), block(2, 0), block(1, 1), block(1, 1), block(1, 0), block(1, 0)],
        out_specs=[block(0, 0)] * 2,
        out_shape=[jax.ShapeDtypeStruct((rows, columns), jnp.bfloat16)] * 2,
        compiler_params=pltpu.CompilerParams(vmem_limit_bytes=56 * 2**20),
        cost_estimate=LIGHT,
    )(scalars, own, other, own, other, across, along)


def dense_sum_kernel(scalars, *refs):
    count = refs[0].shape[0]
    terms, results = refs[:-count], refs[-count:]
    for index, result in enumerate(results):
        spot = scalars[0] ^ index
        total = raise_(terms[0][spot])
        for term in terms[1:]:
            total += raise_(term[spot])
        result[...] = lower(total)


def dense_update_kernel(scalars, *refs):
    sums, refs = refs[:HEADS], refs[HEADS:]
    inputs = [refs[3 * index : 3 * index + 3] for index in range(6)]
    outputs = [refs[3 * index : 3 * index + 3] for index in range(6, 12)]

    def update(index, gradient, columns, rate):
        results = adamw_update(*[ref[:, columns] for ref in inputs[index]], gradient, rate)
        for target, result in zip(outputs[index], results):
            target[:, columns] = result

    part, small = sums[0].shape[0], sums[0].shape[1] - OUTPUT_EDGE
    shared = jnp.zeros((part, small), jnp.float32)
    chosen = jnp.zeros((part, inputs[3][0].shape[1]), jnp.float32)
    for index, rows in enumerate(sums):
        head = scalars[0] ^ index
        for side in range(2):
            span = pl.ds(pl.multiple_of((side * HEADS + head) * HEAD_DIM, HEAD_DIM), HEAD_DIM)
            source = pl.ds(side * HEAD_DIM, HEAD_DIM)
            update(0, raise_(rows[:, source]), span, rate_query_key)
        span = pl.ds(pl.multiple_of(head * VALUE_WIDTH, HEAD_DIM), VALUE_WIDTH)
        update(1, raise_(rows[:, QK_EDGE:VALUE_EDGE]), span, rate_value)
        update(2, raise_(rows[:, VALUE_EDGE:OUTPUT_EDGE]), span, rate_output)
        last = rows[:, OUTPUT_EDGE:]
        source = lax.broadcasted_iota(jnp.int32, (small, chosen.shape[1]), 0)
        target = lax.broadcasted_iota(jnp.int32, (small, chosen.shape[1]), 1)
        side, entry = lax.div(source, ATT_EXPERTS), lax.rem(source, ATT_EXPERTS)
        table = (target == (side * HEADS + head) * ATT_EXPERTS + entry) & (source < SELECT_COUNT)
        chosen += product(last, lower(jnp.where(table, 1.0, 0.0)))
        shared += raise_(last)
    every = slice(None)
    update(3, chosen, every, rate_select)
    expert_total = inputs[4][0].shape[1]
    update(4, pltpu.roll(shared, small - SELECT_COUNT, 1)[:, :expert_total], every, rate_router)
    gain_column = SELECT_COUNT + expert_total
    diagonal = lax.broadcasted_iota(jnp.int32, (part, part), 0) == lax.broadcasted_iota(
        jnp.int32, (part, part), 1
    )
    gain = jnp.where(diagonal, shared[:, gain_column : gain_column + 1], 0.0)
    update(5, jnp.sum(gain, axis=0, keepdims=True), every, rate_gain)


def expert_rows_kernel(weight, rows):
    count = weight.shape[0]
    for expert in range(count):
        rows[:, pl.ds(expert * EXPERT_H, EXPERT_H)] = lower(weight[expert, :, :EXPERT_H])
        rows[:, pl.ds((count + expert) * EXPERT_H, EXPERT_H)] = lower(weight[expert, :, EXPERT_H:])


def expert_rows_of(weight):
    count, rows, columns = weight.shape
    return pl.pallas_call(
        expert_rows_kernel,
        out_shape=jax.ShapeDtypeStruct((rows, count * columns), jnp.bfloat16),
        compiler_params=pltpu.CompilerParams(vmem_limit_bytes=56 * 2**20),
        cost_estimate=LIGHT,
    )(weight)


def front_kernel(scalars, tokens, picks, cotangent, routes, token_rows, upstream):
    rows, width = tokens.shape
    token_rows[:, :width] = tokens[...]
    row = lax.broadcasted_iota(jnp.int32, (token_rows.shape[1] - width, rows), 0)
    chosen = jnp.zeros(row.shape, jnp.float32)
    for head in range(picks.shape[0]):
        start = head % HEADS * SELECT_COUNT + head // HEADS * ATT_EXPERTS
        for pick in range(picks.shape[1]):
            chosen = jnp.where(row == start + picks[head, pick : pick + 1, :], 1.0, chosen)
    token_rows[:, width:] = lower(chosen.T)
    position = scalars[0] * rows + lax.broadcasted_iota(jnp.int32, (rows, 1), 0)
    upstream[:, :width] = lower(jnp.where(position < scalars[1], raise_(cotangent[...]), 0.0))
    row = lax.broadcasted_iota(jnp.int32, (upstream.shape[1] - width, rows), 0)
    hot = jnp.zeros(row.shape, jnp.float32)
    for index in range(routes.shape[0]):
        hot = jnp.where(row == SELECT_COUNT + routes[index : index + 1, :], 1.0, hot)
    upstream[:, width:] = lower(hot.T)


def payload_kernel(scalars, upstream, qk, value, output, select, router, gain, payload):
    part = qk.shape[0]
    small = payload.shape[2] - OUTPUT_EDGE
    rows, width = upstream.shape[0], upstream.shape[1] - small
    expert_total = router.shape[1]
    position = scalars[0] * rows + lax.broadcasted_iota(jnp.int32, (rows, 1), 0)
    valid = position < scalars[1]
    hot = raise_(upstream[:, width:])
    counts = jnp.sum(jnp.where(valid, hot, 0.0), axis=0, keepdims=True)
    gain_column = SELECT_COUNT + expert_total
    count_columns = -(-expert_total // part)
    row = lax.broadcasted_iota(jnp.int32, (part, small), 0)
    lane = lax.broadcasted_iota(jnp.int32, (part, small), 1)
    shared = product(lower(router[...]), shift_back(expert_total, small, SELECT_COUNT))
    diagonal = lax.broadcasted_iota(jnp.int32, (part, part), 0) == lax.broadcasted_iota(
        jnp.int32, (part, part), 1
    )
    gain_rows = jnp.sum(jnp.where(diagonal, gain[...], 0.0), axis=1, keepdims=True)
    shared = jnp.where(lane == gain_column, gain_rows, shared)
    for column in range(count_columns):
        mine = lane - SELECT_COUNT == row * count_columns + column
        found = jnp.sum(jnp.where(mine, counts, 0.0), axis=1, keepdims=True)
        shared = jnp.where(lane == gain_column + 1 + column, found, shared)
    picked = lower(select[...])
    for head in range(HEADS):
        span = pl.ds(head * HEAD_DIM, HEAD_DIM)
        payload[head, :, :HEAD_DIM] = lower(qk[:, span])
        span = pl.ds((HEADS + head) * HEAD_DIM, HEAD_DIM)
        payload[head, :, HEAD_DIM:QK_EDGE] = lower(qk[:, span])
        span = pl.ds(head * VALUE_WIDTH, VALUE_WIDTH)
        payload[head, :, QK_EDGE:VALUE_EDGE] = lower(value[:, span])
        payload[head, :, VALUE_EDGE:OUTPUT_EDGE] = lower(output[:, span])
        source = lax.broadcasted_iota(jnp.int32, (picked.shape[1], small), 0)
        target = lax.broadcasted_iota(jnp.int32, (picked.shape[1], small), 1)
        side, entry = lax.div(target, ATT_EXPERTS), lax.rem(target, ATT_EXPERTS)
        table = (source == (side * HEADS + head) * ATT_EXPERTS + entry) & (target < SELECT_COUNT)
        chosen = product(picked, lower(jnp.where(table, 1.0, 0.0)))
        payload[head, :, OUTPUT_EDGE:] = lower(shared + chosen)


def shift_back(rows, columns, offset):
    source = lax.broadcasted_iota(jnp.int32, (rows, columns), 0)
    target = lax.broadcasted_iota(jnp.int32, (rows, columns), 1)
    return lower(jnp.where(target == source + offset, 1.0, 0.0))


def local(
    tokens,
    cotangent,
    lengths,
    picks,
    routes,
    qk_weight,
    qk_first,
    qk_second,
    value_weight,
    value_first,
    value_second,
    output_weight,
    output_first,
    output_second,
    select_weight,
    select_first,
    select_second,
    router_weight,
    router_first,
    router_second,
    gain_weight,
    gain_first,
    gain_second,
    expert_weight,
    expert_first,
    expert_second,
):
    row_count = tokens.shape[1]
    model_width = tokens.shape[2]
    group_count = lax.axis_size("dp")
    owner_count = lax.axis_size("expert")
    local_count = expert_weight.shape[0]
    expert_total = local_count * owner_count
    bucket_rows = row_count * group_count
    part = qk_weight.shape[0]
    place = lax.axis_index("dp")
    owner = lax.axis_index("expert")
    seq_len = lengths[0]
    sequence = tokens[0]
    scalars = jnp.stack(
        [place.astype(jnp.int32), seq_len.astype(jnp.int32), owner.astype(jnp.int32)]
    )
    spots = jnp.stack([place.astype(jnp.int32), owner.astype(jnp.int32)])
    low, high = jnp.bfloat16, jnp.float32

    def shaped(columns, kind, rows=bucket_rows):
        return jax.ShapeDtypeStruct((rows, columns), kind)

    gain_column = SELECT_COUNT + expert_total
    count_columns = -(-expert_total // part)
    small_used = gain_column + 1 + count_columns
    small_width = small_used + -small_used % 128
    token_width = model_width + HEADS * SELECT_COUNT + -(HEADS * SELECT_COUNT) % 128

    token_own, upstream = wide_call(
        front_kernel,
        [scalars, sequence, picks[0].transpose(1, 2, 0), cotangent[0], routes[0].T],
        [
            shaped(token_width, low, row_count),
            shaped(model_width + small_width, low, row_count),
        ],
    )
    expert_up = {0: upstream}
    for relative in range(2, owner_count, 2):
        if not forwarded(relative):
            expert_up[relative] = swap(upstream, "expert", relative)
    token_blocks = [token_own] + [
        swap(token_own, "dp", relative) for relative in range(1, group_count)
    ]

    (payload,) = wide_call(
        payload_kernel,
        [
            scalars,
            upstream,
            qk_weight,
            value_weight,
            output_weight,
            select_weight,
            router_weight,
            gain_weight[None],
        ],
        [jax.ShapeDtypeStruct((HEADS, part, OUTPUT_EDGE + small_width), low)],
    )
    mine = lax.all_to_all(payload, "dp", split_axis=0, concat_axis=0, tiled=True)
    mine = after(
        mine, *token_blocks[1:], *[up for relative, up in expert_up.items() if relative]
    )

    half = row_count // 2
    expert_own = after(expert_rows_of(expert_weight), mine)
    expert_pieces = [expert_own, swap(expert_own, "dp", 1), swap(expert_own, "dp", 2)]
    dense_blocks = gather_chips(mine)
    dense_others = swap(
        after(jnp.stack(dense_blocks), *expert_pieces[1:]), "expert", 1
    )

    cosine, sine = rope_tables(bucket_rows)
    if part % 16 == 0:
        chips, made = owner_count // 2, []
        given = dense_blocks + [dense_others]
    else:
        dense = jnp.zeros((group_count, owner_count) + mine.shape[1:], jnp.bfloat16)
        for chip, block in enumerate(dense_blocks):
            for other, rows in enumerate((block, dense_others[chip])):
                spot = owner ^ (2 * chip + other)
                dense = lax.dynamic_update_slice_in_dim(dense, rows[:, None], spot, axis=1)
        dense = dense.reshape(group_count, row_count, -1)
        chips, made, given = 0, [], [dense]
    dense_shape = jax.ShapeDtypeStruct((group_count, row_count, payload.shape[2]), low)
    if chips:
        made = [dense_shape]
    outputs = made + [
        shaped(HEAD_DIM, low),
        shaped(HEAD_DIM, low),
        shaped(HEAD_DIM, low),
        shaped(small_width, high),
        shaped(VALUE_WIDTH, high),
        shaped(HEAD_DIM, high),
        shaped(VALUE_WIDTH, low),
        shaped(HEAD_DIM, high),
        shaped(model_width, low),
        shaped(2 * local_count + -2 * local_count % 128, low, model_width),
        shaped(small_width, high, part),
    ]
    kept = staged_call(
        functools.partial(attention_kernel, group_count, gain_column, chips, local_count),
        [scalars] + token_blocks + [cosine, sine] + given,
        outputs,
        token_blocks + [cosine, sine, dense_shape] + outputs[len(made) :],
        [],
        group_count + 2 + owner_count + len(outputs) + 2 * group_count,
    )
    if chips:
        dense, kept = kept[0], kept[1:]
    saved, (branch, router_local, counts) = dict(zip(KEPT, kept)), kept[len(KEPT) :]
    for relative in range(2, owner_count, 2):
        if forwarded(relative):
            block = after(expert_up[relative ^ 2], branch)
            expert_up[relative] = swap(block, "expert", 2)
    expert_up = [expert_up[relative] for relative in range(0, owner_count, 2)]
    near = [after(piece, branch) for piece in expert_pieces]
    expert_others = [swap(piece, "expert", 1) for piece in near]
    far = [
        swap(expert_pieces[1][:half], "dp", 2),
        swap(expert_pieces[2][half:], "dp", 1),
    ]
    expert_others += [swap(after(piece, branch), "expert", 1) for piece in far]
    branch = scatter_rows(branch)
    hidden, hidden_low = wide_call(
        hidden_kernel,
        [spots, sequence, after(branch, expert_up[-1], *expert_others)],
        [shaped(model_width, high, row_count), shaped(model_width, low, row_count)],
        limit=24,
    )
    small = dense[:, :, OUTPUT_EDGE:].reshape(model_width, -1)
    expert_counts = counts[:, gain_column + 1 : small_used].reshape(-1)[:expert_total]
    expert_counts = expert_counts.astype(jnp.int32)

    expert_both = expert_pieces + far + expert_others
    order = [0] + list(range(2, len(expert_up))) + [1]
    expert_rows, back, slopes, gateds = {0: hidden_low}, {}, {}, {}
    arriving = {}
    for relative in range(2, owner_count, 2):
        if not forwarded(relative):
            arriving[relative] = swap(hidden_low, "expert", relative)
    before = None
    for chip in order:
        if chip:
            others = [arriving[2]] if chip == order[1] else []
            block = after(arriving[2 * chip], before, *others)
            if chip % 2 == 0 and chip + 1 < len(expert_up):
                arriving[2 * chip + 2] = swap(block, "expert", 2)
            expert_rows[chip] = block
        back[chip], slopes[chip], gateds[chip] = expert_call(
            spots, expert_rows[chip], expert_up[chip], router_local, expert_both
        )
        before = slopes[chip]
    back_terms = send_expert([back[chip] for chip in range(len(order))])
    back_terms = [back_terms[chip] for chip in order]
    expert_rows, slopes, gateds = [
        [found[chip] for chip in range(len(order))] for found in (expert_rows, slopes, gateds)
    ]

    other_grads, own_grads = expert_grads(
        spots, expert_rows, expert_up, slopes, gateds, group_count
    )
    back_terms[1:] = [after(term, own_grads) for term in back_terms[1:]]

    hidden_grad, hidden_grad_low, router_grad = wide_call(
        functools.partial(hidden_back_kernel, len(back_terms)),
        [scalars] + back_terms + [hidden, upstream, small],
        [
            shaped(model_width, high, row_count),
            jax.ShapeDtypeStruct((group_count, row_count, model_width), low),
            shaped(small_width, high, model_width),
        ],
        limit=24,
    )
    hidden_grad_rows = exchange_rows(hidden_grad_low)
    produced = []
    for start in range(0, len(gateds), 4):
        produced += expert_out_call(
            after(spots, hidden_grad_low), expert_both, gateds[start : start + 4]
        )
    moe_terms = send_expert(produced)
    other_grads = swap(after(other_grads, hidden_grad_low), "expert", 1)

    across, along = halving(after(spots, *produced), own_grads, other_grads, row_count)
    across, along = swap(across, "dp", 1), swap(along, "dp", 2)
    layer_out = hidden
    for term in moe_terms:
        layer_out = layer_out + raise_(term)
    layer_out = lower(layer_out)

    scratch = [
        pltpu.VMEM((bucket_rows, HEAD_DIM), low),
        pltpu.VMEM((bucket_rows, small_width), high),
        pltpu.VMEM((bucket_rows, HEAD_DIM), high),
        pltpu.VMEM((bucket_rows, HEAD_DIM), high),
        pltpu.VMEM((bucket_rows, HEAD_DIM), high),
        pltpu.VMEM((bucket_rows, VALUE_WIDTH), low),
        pltpu.VMEM((bucket_rows, QK_EDGE), low),
        pltpu.VMEM((bucket_rows, small_width), low),
        pltpu.VMEM((bucket_rows, model_width), low),
    ]
    made = [dense_shape]
    if chips:
        made = [jax.ShapeDtypeStruct((chips, group_count, part, dense.shape[2]), low)] * 2
    saved.update(
        upstream=hidden_grad_rows, dense=dense, cosine=cosine, sine=sine, router_grad=router_grad
    )
    inputs = [saved[name] for name in BACK]
    terms_shape = shaped(model_width, low)
    *dense_parts, input_terms = staged_call(
        functools.partial(attention_back_kernel, group_count, gain_column, chips),
        [scalars] + inputs + token_blocks,
        made + [terms_shape],
        inputs + [dense_shape, terms_shape, terms_shape],
        scratch,
        len(inputs) + 2 * group_count + 3 * owner_count,
    )

    if not chips:
        dense_grad = dense_parts[0].reshape(group_count, owner_count, part, -1)
        dense_parts = [
            jnp.stack(
                [
                    lax.dynamic_index_in_dim(dense_grad, owner ^ relative, 1, keepdims=False)
                    for relative in range(side, owner_count, 2)
                ]
            )
            for side in range(2)
        ]
    late = after(spots, input_terms)
    first, second = halved(late, own_grads, other_grads, across, along)
    dense_parts[1] = after(dense_parts[1], first, second, *moe_terms)
    dense_parts = join(spots, dense_parts[0], swap(dense_parts[1], "expert", 1))
    first, second = swap(first, "dp", 2), swap(second, "dp", 1)
    input_grad = add_blocks(hidden_grad, scatter_rows(input_terms))
    dense_terms = send_expert(dense_parts)
    kept_grads = kept_rows(after(spots, *dense_parts), own_grads, other_grads, across, along)
    dense_terms[1:] = [
        after(term, input_grad, kept_grads, first, second) for term in dense_terms[1:]
    ]
    dense_sums = wide_call(
        dense_sum_kernel,
        [scalars] + dense_terms,
        [jax.ShapeDtypeStruct(dense_terms[0].shape[1:], low)] * group_count,
    )
    dense_sums = [dense_sums[0]] + [
        swap(dense_sums[relative], "dp", relative) for relative in range(1, group_count)
    ]
    masters = [
        (qk_weight, qk_first, qk_second),
        (value_weight, value_first, value_second),
        (output_weight, output_first, output_second),
        (select_weight, select_first, select_second),
        (router_weight, router_first, router_second),
        (gain_weight[None], gain_first[None], gain_second[None]),
    ]
    masters = [array for group in masters for array in group]
    updated = wide_call(
        dense_update_kernel,
        [scalars] + dense_sums + masters,
        [jax.ShapeDtypeStruct(array.shape, high) for array in masters],
        limit=24,
    )
    updated = list(updated[:15]) + [array[0] for array in updated[15:]]
    expert_results = expert_update(
        kept_grads, (first, second), expert_weight, expert_first, expert_second
    )
    return (layer_out[None], input_grad[None], *updated, *expert_results, expert_counts)


def solution(mesh):
    placed = (
        P("expert", "dp", None),
        P("expert", "dp", None),
        P("expert"),
        P("expert", "dp", None, None),
        P("expert", "dp", None),
        P(("dp", "expert"), None),
        P(("dp", "expert"), None),
        P(("dp", "expert"), None),
        P(("dp", "expert"), None),
        P(("dp", "expert"), None),
        P(("dp", "expert"), None),
        P(("dp", "expert"), None),
        P(("dp", "expert"), None),
        P(("dp", "expert"), None),
        P(("dp", "expert"), None),
        P(("dp", "expert"), None),
        P(("dp", "expert"), None),
        P(("dp", "expert"), None),
        P(("dp", "expert"), None),
        P(("dp", "expert"), None),
        P(("dp", "expert")),
        P(("dp", "expert")),
        P(("dp", "expert")),
        P("expert", "dp", None),
        P("expert", "dp", None),
        P("expert", "dp", None),
    )
    return jax.shard_map(
        local,
        mesh=mesh,
        in_specs=placed,
        out_specs=(
            P("expert", "dp", None),
            P("expert", "dp", None),
            P(("dp", "expert"), None),
            P(("dp", "expert"), None),
            P(("dp", "expert"), None),
            P(("dp", "expert"), None),
            P(("dp", "expert"), None),
            P(("dp", "expert"), None),
            P(("dp", "expert"), None),
            P(("dp", "expert"), None),
            P(("dp", "expert"), None),
            P(("dp", "expert"), None),
            P(("dp", "expert"), None),
            P(("dp", "expert"), None),
            P(("dp", "expert"), None),
            P(("dp", "expert"), None),
            P(("dp", "expert"), None),
            P(("dp", "expert")),
            P(("dp", "expert")),
            P(("dp", "expert")),
            P("expert", "dp", None),
            P("expert", "dp", None),
            P("expert", "dp", None),
            P(),
        ),
        check_vma=False,
    )
```

```python
import functools

import numpy as np
import jax
import jax.numpy as jnp
from jax import lax
from jax.experimental import pallas as pl
from jax.experimental.pallas import tpu as pltpu
from jax.sharding import PartitionSpec as P

HEADS = 4
HEAD_DIM = 128
ATT_EXPERTS = 5
EXPERT_H = 128
TOPK = 16
STEP = 10


norm_eps = 1e-05
beta_first = 0.9
beta_second = 0.95
adam_eps = 1e-08
weight_decay = 0.1
masked_score = -1e30
rope_base = 10000.0
rate_query_key = 0.04
rate_value = 0.03
rate_output = 2.0
rate_select = 0.03
rate_router = 0.015
rate_gain = 1.2
rate_expert = 0.05


def product(former, latter):
    return jnp.dot(former, latter, preferred_element_type=jnp.float32)


def product_rows(former, latter):
    return lax.dot_general(
        former, latter, (((0,), (0,)), ((), ())), preferred_element_type=jnp.float32
    )


def product_last(former, latter):
    return lax.dot_general(
        former, latter, (((1,), (1,)), ((), ())), preferred_element_type=jnp.float32
    )


def rope_tables(rows):
    half = HEAD_DIM // 2
    frequency = np.exp(-np.log(rope_base) * np.arange(half) / half)
    angles = np.arange(rows)[:, None] * frequency[None, :]
    cosine, sine = np.cos(angles), np.sin(angles)
    return (
        jnp.asarray(np.concatenate([cosine, cosine], axis=1), jnp.float32),
        jnp.asarray(np.concatenate([-sine, sine], axis=1), jnp.float32),
    )


def adamw_update(weight, first_moment, second_moment, gradient, rate):
    first_new = beta_first * first_moment + (1.0 - beta_first) * gradient
    second_new = beta_second * second_moment + (1.0 - beta_second) * gradient * gradient
    first_hat = first_new / (1.0 - beta_first**STEP)
    second_hat = second_new / (1.0 - beta_second**STEP)
    weight_new = weight - rate * (
        first_hat / (jnp.sqrt(second_hat) + adam_eps) + weight_decay * weight
    )
    return (weight_new, first_new, second_new)


LIGHT = pl.CostEstimate(flops=1000, bytes_accessed=1000, transcendentals=0)


def swap(values, axis, relative):
    count = lax.axis_size(axis)
    return lax.ppermute(values, axis, [(place, place ^ relative) for place in range(count)])


def lower(values):
    return values.astype(jnp.bfloat16)


def raise_(values):
    return values.astype(jnp.float32)


def after(values, *others):
    return lax.optimization_barrier((values,) + others)[0]


def exchange_rows(copies):
    blocks = lax.all_to_all(copies, "dp", split_axis=0, concat_axis=0, tiled=True)
    return blocks.reshape((-1,) + copies.shape[2:])


def scatter_rows(values):
    count = lax.axis_size("dp")
    blocks = values.reshape((count, values.shape[0] // count) + values.shape[1:])
    return lax.all_to_all(blocks, "dp", split_axis=0, concat_axis=0, tiled=True)


def add_blocks(values, blocks):
    for index in range(blocks.shape[0]):
        values = values + raise_(blocks[index])
    return values


def join_kernel(scalars, evens, odds, *results):
    for chip, result in enumerate(results):
        result[...] = lower(raise_(evens[chip]) + raise_(odds[chip]))


def join(scalars, evens, odds):
    shape = jax.ShapeDtypeStruct(evens.shape[1:], jnp.bfloat16)
    return list(wide_call(join_kernel, [scalars, evens, odds], [shape] * evens.shape[0]))


def forwarded(relative):
    return relative & 2 and relative > 2


def gather_chips(values):
    return [values] + [
        swap(values, "expert", relative) for relative in range(2, lax.axis_size("expert"), 2)
    ]


def send_expert(joined):
    return [joined[0]] + [
        swap(term, "expert", 2 * index) for index, term in enumerate(joined) if index
    ]


def full(shape):
    return pl.BlockSpec(shape, lambda *_: (0,) * len(shape))


def wide_call(kernel, inputs, outputs, limit=56):
    specs = [pl.BlockSpec(memory_space=pltpu.SMEM)] + [full(value.shape) for value in inputs[1:]]
    return pl.pallas_call(
        kernel,
        grid=(1,),
        in_specs=specs,
        out_specs=[full(value.shape) for value in outputs],
        out_shape=outputs,
        compiler_params=pltpu.CompilerParams(vmem_limit_bytes=limit * 2**20),
        cost_estimate=LIGHT,
    )(*inputs)


class Copies:
    def __init__(self, sems):
        self.sems, self.count, self.waiting = sems, 0, {}

    def start(self, name, source, target):
        copy = pltpu.make_async_copy(source, target, self.sems.at[self.count])
        copy.start()
        self.count += 1
        self.waiting.setdefault(name, []).append(copy)

    def wait(self, *names):
        for name in names:
            for copy in self.waiting.pop(name, []):
                copy.wait()


def staged_call(kernel, inputs, outputs, held, scratch, copies):
    somewhere = pl.BlockSpec(memory_space=pl.ANY)
    return pl.pallas_call(
        kernel,
        grid=(1,),
        in_specs=[pl.BlockSpec(memory_space=pltpu.SMEM)] + [somewhere] * (len(inputs) - 1),
        out_specs=[somewhere] * len(outputs),
        out_shape=outputs,
        scratch_shapes=[pltpu.VMEM(value.shape, value.dtype) for value in held]
        + list(scratch)
        + [pltpu.SemaphoreType.DMA((copies,))],
        compiler_params=pltpu.CompilerParams(vmem_limit_bytes=56 * 2**20),
        cost_estimate=LIGHT,
    )(*inputs)


def shift_table(rows, columns, offset, count):
    source = lax.broadcasted_iota(jnp.int32, (rows, columns), 0)
    target = lax.broadcasted_iota(jnp.int32, (rows, columns), 1)
    return lower(jnp.where((source == target + offset) & (target < count), 1.0, 0.0))


def moments(values):
    center = values - jnp.mean(values, axis=-1, keepdims=True)
    inverse = lax.rsqrt(jnp.mean(center * center, axis=-1, keepdims=True) + norm_eps)
    return center * inverse, inverse


def turn(rows, cosine, signed_sine, direction):
    return rows * cosine + direction * pltpu.roll(rows, HEAD_DIM // 2, 1) * signed_sine


def masked_scores(queries, key_rows, seq_len, start):
    scores = product_last(queries, key_rows) * HEAD_DIM ** (-0.5)
    query_place = start + lax.broadcasted_iota(jnp.int32, scores.shape, 0)
    key_place = lax.broadcasted_iota(jnp.int32, scores.shape, 1)
    return jnp.where((key_place <= query_place) & (key_place < seq_len), scores, masked_score)


VALUE_WIDTH = ATT_EXPERTS * HEAD_DIM
QK_EDGE = 2 * HEAD_DIM
VALUE_EDGE = QK_EDGE + VALUE_WIDTH
OUTPUT_EDGE = VALUE_EDGE + VALUE_WIDTH
SELECT_COUNT = 2 * ATT_EXPERTS


KEPT = ("queries", "key_rows", "values", "weighting", "projected", "attended", "mixed", "log_total")


def attention_kernel(blocks, gain_column, chips, local_count, scalars, *refs):
    given = blocks + 2 + (chips + 1 if chips else 1)
    outs = (["dense"] if chips else []) + list(KEPT) + ["branch", "router_local", "counts"]
    count = len(outs)
    sources, targets = refs[:given], dict(zip(outs, refs[given : given + count]))
    tokens, (cosine, sine, dense), refs = (
        refs[given + count : given + count + blocks],
        refs[given + count + blocks : given + count + blocks + 3],
        refs[given + count + blocks + 3 : -1] + refs[-1:],
    )
    *kept, branch, router_local, counts, sems = refs
    (queries, key_rows, values, weighting, projected, attended, mixed, log_total) = kept
    copies = Copies(sems)
    for index in range(blocks):
        copies.start("in", sources[index], tokens[index])
    copies.start("in", sources[blocks], cosine)
    copies.start("in", sources[blocks + 1], sine)
    if chips:
        evens, odds = sources[blocks + 2 : blocks + 2 + chips], sources[blocks + 2 + chips]
        part = odds.shape[2]
        for chip in range(chips):
            for other, rows in ((0, evens[chip]), (1, odds.at[chip])):
                start = (scalars[2] ^ (2 * chip + other)) * part
                copies.start("in", rows, dense.at[:, pl.ds(pl.multiple_of(start, part), part), :])
    else:
        copies.start("in", sources[blocks + 2], dense)
    copies.wait("in")
    if chips:
        copies.start("out", dense, targets["dense"])
    place, seq_len = scalars[0], scalars[1]
    width = dense.shape[0] * dense.shape[1]
    block = tokens[0].shape[0]

    def weight(start, end):
        return dense[:, :, start:end].reshape(width, end - start)

    small_rows = weight(OUTPUT_EDGE, dense.shape[2])
    count = local_count
    source = lax.broadcasted_iota(jnp.int32, (small_rows.shape[1], router_local.shape[1]), 0)
    entry = lax.broadcasted_iota(jnp.int32, source.shape, 1)
    first = SELECT_COUNT + scalars[2] * count + entry
    second = SELECT_COUNT + (scalars[2] ^ 1) * count + entry - count
    table = (source == jnp.where(entry < count, first, second)) & (entry < 2 * count)
    router_local[...] = lower(product(small_rows, lower(jnp.where(table, 1.0, 0.0))))
    part = counts.shape[0]
    total = raise_(small_rows[:part])
    for start in range(part, width, part):
        total += raise_(small_rows[start : start + part])
    counts[...] = total
    copies.start("out", counts, targets["counts"])
    copies.start("out", router_local, targets["router_local"])
    gain = raise_(small_rows).T[gain_column : gain_column + 1, :]
    head_table = shift_table(
        tokens[0].shape[1] - width, dense.shape[2] - OUTPUT_EDGE, place * SELECT_COUNT, SELECT_COUNT
    )
    for index in range(blocks):
        span = pl.ds(pl.multiple_of((place ^ index) * block, block), block)
        rows = tokens[index][:, :width]
        scaled, _ = moments(raise_(rows))
        normed_rows = lower(scaled * gain)
        both = product(normed_rows, weight(0, QK_EDGE))
        queries[span, :] = lower(turn(both[:, :HEAD_DIM], cosine[span, :], sine[span, :], 1.0))
        key_rows[span, :] = lower(turn(both[:, HEAD_DIM:], cosine[span, :], sine[span, :], 1.0))
        chosen = product(tokens[index][:, width:], head_table)
        sigma_rows = jax.nn.sigmoid(product(normed_rows, small_rows))
        weights = sigma_rows * chosen
        weighting[span, :] = weights
        columns = product(rows, weight(QK_EDGE, VALUE_EDGE))
        projected[span, :] = columns
        total = weights[:, 0:1] * columns[:, :HEAD_DIM]
        for expert in range(1, ATT_EXPERTS):
            total += (
                weights[:, expert : expert + 1]
                * columns[:, expert * HEAD_DIM : (expert + 1) * HEAD_DIM]
            )
        values[span, :] = lower(total)
    for name, ref in zip(KEPT[:5], kept):
        copies.start("out", ref, targets[name])
    for start in range(0, blocks * block, block):
        span = pl.ds(start, block)
        scores = masked_scores(queries[span, :], key_rows[...], seq_len, start)
        highest = jnp.max(scores, axis=-1, keepdims=True)
        raised = jnp.exp(scores - highest)
        row_total = jnp.sum(raised, axis=-1, keepdims=True)
        log_total[span, :] = jnp.broadcast_to(highest + jnp.log(row_total), (block, HEAD_DIM))
        rows = product(lower(raised / row_total), values[...])
        attended[span, :] = rows
        weights = weighting[span, :]
        for expert in range(ATT_EXPERTS):
            mixed[span, pl.ds(expert * HEAD_DIM, HEAD_DIM)] = lower(
                weights[:, ATT_EXPERTS + expert : ATT_EXPERTS + expert + 1] * rows
            )
        branch[span, :] = lower(product_last(mixed[span, :], weight(VALUE_EDGE, OUTPUT_EDGE)))
        for name, ref in (("mixed", mixed), ("branch", branch)):
            copies.start("out", ref.at[span, :], targets[name].at[span, :])
    copies.start("out", attended, targets["attended"])
    copies.start("out", log_total, targets["log_total"])
    copies.wait("out")


BACK = ("upstream", "dense", "weighting", "attended", "mixed", "queries", "key_rows", "values") + (
    "log_total",
    "projected",
    "cosine",
    "sine",
    "router_grad",
)


def attention_back_kernel(blocks, gain_column, chips, scalars, *refs):
    count = len(BACK)
    sources, token_blocks, refs = refs[:count], refs[count : count + blocks], refs[count + blocks :]
    results, out_terms, refs = refs[: 2 if chips else 1], refs[2 if chips else 1], refs[3 if chips else 2 :]
    held, (grads, terms, tokens), refs = refs[:count], refs[count : count + 3], refs[count + 3 :]
    (upstream, dense, weighting, attended, mixed, queries, key_rows, values, log_total) = held[:9]
    projected, cosine, sine, router_grad = held[9:]
    (attended_grad, weight_grad, key_grad, value_grad, query_grad) = refs[:5]
    projected_grad, pair_grad, select_grad, normed, sems = refs[5:]
    copies = Copies(sems)
    for name, source, target in zip(BACK, sources, held):
        copies.start(name, source, target)
    block = token_blocks[0].shape[0]
    for index, rows in enumerate(token_blocks):
        span = pl.ds(pl.multiple_of((scalars[0] ^ index) * block, block), block)
        copies.start("tokens", rows.at[:, pl.ds(0, tokens.shape[1])], tokens.at[span, :])

    def weight(start, end):
        return dense[:, :, start:end].reshape(tokens.shape[1], end - start)

    def leave(columns):
        if not chips:
            copies.start("out", grads.at[:, :, columns], results[0].at[:, :, columns])
            return
        part = results[0].shape[2]
        for relative in range(2 * chips):
            start = pl.multiple_of((scalars[2] ^ relative) * part, part)
            target = results[relative % 2].at[relative // 2, :, :, columns]
            copies.start("out", grads.at[:, pl.ds(start, part), columns], target)

    def keep(start, values):
        columns = pl.ds(start, values.shape[1])
        grads[:, :, columns] = values.reshape(grads.shape[:2] + values.shape[1:])

    copies.wait("upstream", "dense", "weighting", "attended")
    seq_len = scalars[1]
    width = tokens.shape[1]
    small = dense.shape[2] - OUTPUT_EDGE
    lane = lax.broadcasted_iota(jnp.int32, (block, small), 1)
    scale = HEAD_DIM ** (-0.5)
    gain = raise_(weight(OUTPUT_EDGE, dense.shape[2])).T[gain_column : gain_column + 1, :]
    for start in range(0, tokens.shape[0], block):
        span = pl.ds(start, block)
        mixed_grad = product(upstream[span, :], weight(VALUE_EDGE, OUTPUT_EDGE))
        weights = weighting[span, :]
        heads = attended[span, :]
        total = jnp.zeros((block, HEAD_DIM), jnp.float32)
        found = jnp.zeros((block, small), jnp.float32)
        for expert in range(ATT_EXPERTS):
            piece = mixed_grad[:, expert * HEAD_DIM : (expert + 1) * HEAD_DIM]
            column = ATT_EXPERTS + expert
            total += weights[:, column : column + 1] * piece
            found = jnp.where(lane == column, jnp.sum(piece * heads, axis=1, keepdims=True), found)
        attended_grad[span, :] = lower(total)
        weight_grad[span, :] = found
    copies.wait("mixed")
    keep(VALUE_EDGE, lower(product_rows(upstream[...], mixed[...])))
    leave(pl.ds(VALUE_EDGE, OUTPUT_EDGE - VALUE_EDGE))
    copies.wait("queries", "key_rows", "values", "log_total")
    for start in range(0, tokens.shape[0], block):
        span = pl.ds(start, block)
        scores = masked_scores(queries[span, :], key_rows[...], seq_len, start)
        probs = jnp.exp(scores - log_total[span, :1])
        prob_grad = product_last(attended_grad[span, :], values[...])
        delta = jnp.sum(probs * prob_grad, axis=-1, keepdims=True)
        score_grad = lower(probs * (prob_grad - delta))
        query_grad[span, :] = product(score_grad, key_rows[...]) * scale
        key_terms = product_rows(score_grad, queries[span, :])
        value_terms = product_rows(lower(probs), attended_grad[span, :])
        if start:
            key_grad[...] += key_terms
            value_grad[...] += value_terms
        else:
            key_grad[...] = key_terms
            value_grad[...] = value_terms
    copies.wait("projected", "cosine", "sine", "router_grad", "tokens")
    gain_grad = jnp.zeros((1, width), jnp.float32)
    for start in range(0, tokens.shape[0], block):
        span = pl.ds(start, block)
        rows = value_grad[span, :]
        weights = weighting[span, :]
        found = weight_grad[span, :]
        for expert in range(ATT_EXPERTS):
            piece = pl.ds(expert * HEAD_DIM, HEAD_DIM)
            projected_grad[span, piece] = lower(weights[:, expert : expert + 1] * rows)
            found = jnp.where(
                lane == expert,
                jnp.sum(rows * projected[span, piece], axis=1, keepdims=True),
                found,
            )
        pair_grad[span, :HEAD_DIM] = lower(
            turn(query_grad[span, :], cosine[span, :], sine[span, :], -1.0)
        )
        pair_grad[span, HEAD_DIM:] = lower(
            turn(key_grad[span, :] * scale, cosine[span, :], sine[span, :], -1.0)
        )
        select_rows = lower(found * weights * (1.0 - weights))
        select_grad[span, :] = select_rows
        normed_grad = product_last(pair_grad[span, :], weight(0, QK_EDGE)) + product_last(
            select_rows, weight(OUTPUT_EDGE, dense.shape[2])
        )
        scaled, inverse = moments(raise_(tokens[span, :]))
        normed[span, :] = lower(scaled * gain)
        gain_grad += jnp.sum(normed_grad * scaled, axis=0, keepdims=True)
        through = normed_grad * gain
        norm_grad = inverse * (
            through
            - jnp.mean(through, axis=-1, keepdims=True)
            - scaled * jnp.mean(through * scaled, axis=-1, keepdims=True)
        )
        terms[span, :] = lower(
            product_last(projected_grad[span, :], weight(QK_EDGE, VALUE_EDGE)) + norm_grad
        )
        copies.start("out", terms.at[span, :], out_terms.at[span, :])
    keep(QK_EDGE, lower(product_rows(tokens[...], projected_grad[...])))
    keep(0, lower(product_rows(normed[...], pair_grad[...])))
    row = lax.broadcasted_iota(jnp.int32, (small, width), 0)
    gain_part = jnp.where(row == gain_column, gain_grad, 0.0).T
    rest = product_rows(normed[...], select_grad[...]) + gain_part + router_grad[...]
    keep(OUTPUT_EDGE, lower(rest))
    leave(pl.ds(0, VALUE_EDGE))
    leave(pl.ds(OUTPUT_EDGE, small))
    copies.wait("out")


def piece_copies(place, pieces, target, columns, sems):
    part, last = pieces[0].shape[0], len(pieces) - 2
    half = part // 2
    copies = []
    for index, piece in enumerate(pieces):
        start = (place ^ min(index, last)) * part + (half if index > last else 0)
        rows = pl.ds(pl.multiple_of(start, half), piece.shape[0])
        source = piece.at[:, columns]
        copies.append(pltpu.make_async_copy(source, target.at[rows, :], sems.at[index]))
    return copies


def expert_kernel(pieces, scalars, rows, up, router, *refs):
    weights = refs[: 2 * pieces]
    back, slope, gated, insides, outsides, sems = refs[2 * pieces :]
    block, width = rows.shape
    hidden = slope.shape[1] // 2
    count = hidden // EXPERT_H
    copies = []
    for side in range(2):
        own = weights[side * pieces : (side + 1) * pieces]
        copies.append(
            piece_copies(scalars[0], own, insides.at[side], pl.ds(0, hidden), sems.at[side, 0])
            + piece_copies(
                scalars[0], own, outsides.at[side], pl.ds(hidden, hidden), sems.at[side, 1]
            )
        )
        for copy in copies[side]:
            copy.start()
    small = up.shape[1] - width
    lanes = router.shape[1]
    offsets = [SELECT_COUNT + (scalars[1] ^ index) * count for index in range(2)]

    def column_of(entry):
        return jnp.where(entry < count, offsets[0] + entry, offsets[1] + entry - count)

    source = lax.broadcasted_iota(jnp.int32, (small, lanes), 0)
    entry = lax.broadcasted_iota(jnp.int32, (small, lanes), 1)
    pick_table = lower(jnp.where((source == column_of(entry)) & (entry < 2 * count), 1.0, 0.0))
    entry = lax.broadcasted_iota(jnp.int32, (lanes, small), 0)
    target = lax.broadcasted_iota(jnp.int32, (lanes, small), 1)
    place_table = lower(jnp.where((target == column_of(entry)) & (entry < 2 * count), 1.0, 0.0))
    lane = lax.broadcasted_iota(jnp.int32, (block, lanes), 1)
    scaled, _ = moments(raise_(rows[...]))
    sigma_gate = jax.nn.sigmoid(product(lower(scaled), router[...]))
    gates = sigma_gate * product(up[:, width:], pick_table)
    found = jnp.zeros((block, lanes), jnp.float32)
    for first in range(0, 2 * count, 2):
        side = first // count
        if first % count == 0:
            for copy in copies[side]:
                copy.wait()
        local = pl.ds(first % count * EXPERT_H, 2 * EXPERT_H)
        inner = product(rows[...], insides[side, :, local])
        terms = product(up[:, :width], outsides[side, :, local])
        sigma = jax.nn.sigmoid(inner)
        silu = inner * sigma
        active = raise_(lower(silu))
        both = terms * active
        tilt = sigma + silu * (1.0 - sigma)
        for k in range(2):
            part = slice(k * EXPERT_H, (k + 1) * EXPERT_H)
            columns = pl.ds((first + k) * EXPERT_H, EXPERT_H)
            gate = gates[:, first + k : first + k + 1]
            gated[:, columns] = lower(gate * active[:, part])
            slope[:, columns] = lower(gate * terms[:, part] * tilt[:, part])
            summed = jnp.sum(both[:, part], axis=1, keepdims=True)
            found = jnp.where(lane == first + k, summed, found)
    back[:, :width] = lower(
        product_last(slope[:, :hidden], insides[0]) + product_last(slope[:, hidden:], insides[1])
    )
    back[:, width:] = lower(product(lower(found * gates * (1.0 - sigma_gate)), place_table))


def expert_call(scalars, rows, up, router, weights):
    block, width = rows.shape
    hidden = weights[0].shape[1] // 2
    pieces = len(weights) // 2
    outputs = [
        jax.ShapeDtypeStruct(up.shape, jnp.bfloat16),
        jax.ShapeDtypeStruct((block, 2 * hidden), jnp.bfloat16),
        jax.ShapeDtypeStruct((block, 2 * hidden), jnp.bfloat16),
    ]
    return pl.pallas_call(
        functools.partial(expert_kernel, pieces),
        grid=(1,),
        in_specs=[pl.BlockSpec(memory_space=pltpu.SMEM)]
        + [full(value.shape) for value in (rows, up, router)]
        + [pl.BlockSpec(memory_space=pl.ANY)] * len(weights),
        out_specs=[full(value.shape) for value in outputs],
        out_shape=outputs,
        scratch_shapes=[
            pltpu.VMEM((2, width, hidden), jnp.bfloat16),
            pltpu.VMEM((2, width, hidden), jnp.bfloat16),
            pltpu.SemaphoreType.DMA((2, 2, pieces)),
        ],
        compiler_params=pltpu.CompilerParams(vmem_limit_bytes=56 * 2**20),
        cost_estimate=LIGHT,
    )(scalars, rows, up, router, *weights)


def expert_grad_kernel(chips, blocks, scalars, *refs):
    rows = refs[:chips]
    ups = refs[chips : 2 * chips]
    slopes = refs[2 * chips : 3 * chips]
    gateds = refs[3 * chips : 4 * chips]
    width = rows[0].shape[1]
    part = width // blocks
    quarter = pl.num_programs(0) // 4

    def total(lefts, rights, target):
        for index in range(blocks):
            columns = pl.ds(pl.multiple_of((scalars[0] ^ index) * part, part), part)
            result = product_rows(lefts[0][:, columns], rights[0][...])
            for left, right in zip(lefts[1:], rights[1:]):
                result += product_rows(left[:, columns], right[...])
            target[pl.ds(index * part, part), :] = lower(result)

    for phase in range(4):

        @pl.when(pl.program_id(0) // quarter == phase)
        def _(phase=phase):
            lefts, rights = ((rows, slopes), (ups, gateds))[phase % 2]
            total(lefts, rights, refs[4 * chips + phase // 2])


def expert_grads(scalars, rows, ups, slopes, gateds, blocks):
    chips = len(slopes)
    block, width = rows[0].shape
    hidden = slopes[0].shape[1] // 2
    tile = hidden // 2
    once = pl.Buffered(buffer_count=1)

    def slope_at(j):
        return 0, jnp.where(j < 4, 2 + jnp.minimum(j, 1), jnp.minimum(j - 4, 1))

    def gated_at(j):
        return 0, jnp.where(j < 4, 2 + jnp.maximum(j - 2, 0), jnp.maximum(j - 6, 0))

    shape = jax.ShapeDtypeStruct((width, 2 * hidden), jnp.bfloat16)
    return pl.pallas_call(
        functools.partial(expert_grad_kernel, chips, blocks),
        grid=(8,),
        in_specs=[pl.BlockSpec(memory_space=pltpu.SMEM)]
        + [pl.BlockSpec(v.shape, lambda j: (0, 0), pipeline_mode=once) for v in rows + ups]
        + [pl.BlockSpec((block, tile), slope_at)] * chips
        + [pl.BlockSpec((block, tile), gated_at)] * chips,
        out_specs=[
            pl.BlockSpec((width, tile), lambda j: (0, jnp.minimum(j, 3))),
            pl.BlockSpec((width, tile), lambda j: (0, jnp.maximum(j - 4, 0))),
        ],
        out_shape=[shape, shape],
        compiler_params=pltpu.CompilerParams(vmem_limit_bytes=56 * 2**20),
        cost_estimate=LIGHT,
    )(scalars, *rows, *ups, *slopes, *gateds)


def expert_out_kernel(pieces, scalars, *refs):
    weights, refs = refs[: 2 * pieces], refs[2 * pieces :]
    count = (len(refs) - 5) // 2
    gateds, results = refs[:count], refs[count : 2 * count]
    outsides, lefts, held, sems, gated_sems = refs[2 * count :]
    hidden = outsides.shape[2]
    block, width = results[0].shape
    tile = min(256, width)
    copies = []
    for side in range(2):
        own = weights[side * pieces : (side + 1) * pieces]
        columns = pl.ds(hidden, hidden)
        started = piece_copies(scalars[0], own, outsides.at[side], columns, sems.at[side])
        for index, gated in enumerate(gateds):
            source = gated.at[:, pl.ds(side * hidden, hidden)]
            target = lefts.at[side, pl.ds(index * block, block), :]
            started.append(pltpu.make_async_copy(source, target, gated_sems.at[side, index]))
        for copy in started:
            copy.start()
        copies.append(started)
    for side in range(2):
        for copy in copies[side]:
            copy.wait()
        for start in range(0, width, tile):
            columns = pl.ds(start, tile)
            total = product_last(lefts[side], outsides[side, columns, :])
            if side == 0:
                held[:, columns] = total
            else:
                total += held[:, columns]
                for index, result in enumerate(results):
                    result[:, columns] = lower(total[index * block : (index + 1) * block])


def expert_out_call(scalars, weights, gateds):
    pieces, count = len(weights) // 2, len(gateds)
    hidden = weights[0].shape[1] // 2
    width = sum(weight.shape[0] for weight in weights[:pieces])
    block = gateds[0].shape[0]
    return pl.pallas_call(
        functools.partial(expert_out_kernel, pieces),
        grid=(1,),
        in_specs=[pl.BlockSpec(memory_space=pltpu.SMEM)]
        + [pl.BlockSpec(memory_space=pl.ANY)] * (len(weights) + count),
        out_specs=[full((block, width))] * count,
        out_shape=[jax.ShapeDtypeStruct((block, width), jnp.bfloat16)] * count,
        scratch_shapes=[
            pltpu.VMEM((2, width, hidden), jnp.bfloat16),
            pltpu.VMEM((2, count * block, hidden), jnp.bfloat16),
            pltpu.VMEM((count * block, width), jnp.float32),
            pltpu.SemaphoreType.DMA((2, pieces)),
            pltpu.SemaphoreType.DMA((2, count)),
        ],
        compiler_params=pltpu.CompilerParams(vmem_limit_bytes=56 * 2**20),
        cost_estimate=LIGHT,
    )(scalars, *weights, *gateds)


def hidden_back_kernel(count, scalars, *refs):
    terms = refs[:count]
    hidden, upstream, small, hidden_grad, hidden_grad_low, router_grad = refs[count:]
    width = hidden.shape[1]
    total = raise_(terms[0][...])
    for term in terms[1:]:
        total += raise_(term[...])
    logit_grad = lower(total[:, width:])
    scaled, inverse = moments(hidden[...])
    router_grad[...] = product_rows(lower(scaled), logit_grad)
    through = product_last(logit_grad, small[...])
    norm_grad = inverse * (
        through
        - jnp.mean(through, axis=-1, keepdims=True)
        - scaled * jnp.mean(through * scaled, axis=-1, keepdims=True)
    )
    result = raise_(upstream[:, :width]) + total[:, :width] + norm_grad
    hidden_grad[...] = result
    for index in range(hidden_grad_low.shape[0]):
        hidden_grad_low[index] = lower(result)


def hidden_kernel(scalars, sequence, blocks, hidden, hidden_low):
    total = raise_(sequence[...])
    for index in range(blocks.shape[0]):
        total += raise_(blocks[index])
    hidden[...] = total
    hidden_low[...] = lower(total)


def layer_out_kernel(scalars, hidden, *refs):
    total = hidden[...]
    for term in refs[:-1]:
        total += raise_(term[...])
    refs[-1][...] = lower(total)


def kept_kernel(scalars, own, other, across, along, kept):
    columns = across.shape[1]
    for half, received in enumerate((across, along)):
        span = pl.ds(half * columns, columns)
        kept[:, span] = raise_(own[:, span]) + raise_(other[:, span]) + raise_(received[...])


def kept_rows(scalars, own, other, across, along):
    rows, columns = across.shape[0] // 2, own.shape[1]
    wide = pl.BlockSpec((rows, columns), lambda i: (0, 0))
    half = pl.BlockSpec((rows, columns // 2), lambda i: (0, 0))
    return pl.pallas_call(
        kept_kernel,
        grid=(1,),
        in_specs=[pl.BlockSpec(memory_space=pltpu.SMEM), wide, wide, half, half],
        out_specs=wide,
        out_shape=jax.ShapeDtypeStruct((rows, columns), jnp.float32),
        compiler_params=pltpu.CompilerParams(vmem_limit_bytes=56 * 2**20),
        cost_estimate=LIGHT,
    )(scalars, own, other, across, along)


def expert_update_kernel(*refs):
    grads, (weight, first, second, new, first_new, second_new) = refs[:4], refs[4:]
    for half in range(2):
        for expert in range(weight.shape[0]):
            source = pl.ds(expert * EXPERT_H, EXPERT_H)
            columns = pl.ds(half * EXPERT_H, EXPERT_H)
            results = adamw_update(
                weight[expert, :, columns],
                first[expert, :, columns],
                second[expert, :, columns],
                grads[2 * half][:, source] + raise_(grads[2 * half + 1][:, source]),
                rate_expert,
            )
            for target, result in zip((new, first_new, second_new), results):
                target[expert, :, columns] = result


def expert_update(kept, last, weight, first, second):
    count, rows, columns = weight.shape
    some = 3 if count % 3 == 0 else 1
    steps = count // some
    width = some * EXPERT_H
    whole = pl.BlockSpec((some, rows, columns), lambda e: (e, 0, 0))
    shape = jax.ShapeDtypeStruct(weight.shape, jnp.float32)
    specs, terms = [], []
    for half in range(2):
        specs.append(pl.BlockSpec((rows, width), lambda e, start=half * steps: (0, start + e)))
        specs.append(pl.BlockSpec((rows, width), lambda e: (0, e)))
        terms += [kept, last[half]]
    return pl.pallas_call(
        expert_update_kernel,
        grid=(steps,),
        in_specs=specs + [whole] * 3,
        out_specs=[whole] * 3,
        out_shape=[shape] * 3,
        compiler_params=pltpu.CompilerParams(vmem_limit_bytes=56 * 2**20),
        cost_estimate=LIGHT,
    )(*terms, weight, first, second)


def halving_kernel(scalars, *refs):
    across, along = refs[8:]
    rows = across.shape[0] // 2
    for index in range(4):
        target, half = (across, along)[index // 2], pl.ds(index % 2 * rows, rows)
        target[half, :] = lower(raise_(refs[2 * index][...]) + raise_(refs[2 * index + 1][...]))


def halving(scalars, own, other, rows):
    columns = own.shape[1] // 2
    specs = []
    for row, column in ((1, 0), (3, 0), (2, 1), (3, 1)):
        specs += [pl.BlockSpec((rows, columns), lambda i, row=row, column=column: (row, column))] * 2
    shape = jax.ShapeDtypeStruct((2 * rows, columns), jnp.bfloat16)
    return pl.pallas_call(
        halving_kernel,
        grid=(1,),
        in_specs=[pl.BlockSpec(memory_space=pltpu.SMEM)] + specs,
        out_specs=[full(shape.shape)] * 2,
        out_shape=[shape] * 2,
        compiler_params=pltpu.CompilerParams(vmem_limit_bytes=56 * 2**20),
        cost_estimate=LIGHT,
    )(scalars, *[own, other] * 4)


def halved_kernel(scalars, own_two, other_two, own_one, other_one, across, along, first, second):
    first[...] = lower(raise_(own_two[...]) + raise_(other_two[...]) + raise_(across[...]))
    second[...] = lower(raise_(own_one[...]) + raise_(other_one[...]) + raise_(along[...]))


def halved(scalars, own, other, across, along):
    rows, columns = across.shape[0] // 2, across.shape[1]

    def block(row, column):
        return pl.BlockSpec((rows, columns), lambda i: (row, column))

    return pl.pallas_call(
        halved_kernel,
        grid=(1,),
        in_specs=[pl.BlockSpec(memory_space=pltpu.SMEM)]
        + [block(2, 0), block(2, 0), block(1, 1), block(1, 1), block(1, 0), block(1, 0)],
        out_specs=[block(0, 0)] * 2,
        out_shape=[jax.ShapeDtypeStruct((rows, columns), jnp.bfloat16)] * 2,
        compiler_params=pltpu.CompilerParams(vmem_limit_bytes=56 * 2**20),
        cost_estimate=LIGHT,
    )(scalars, own, other, own, other, across, along)


def dense_sum_kernel(scalars, *refs):
    count = refs[0].shape[0]
    terms, results = refs[:-count], refs[-count:]
    for index, result in enumerate(results):
        spot = scalars[0] ^ index
        total = raise_(terms[0][spot])
        for term in terms[1:]:
            total += raise_(term[spot])
        result[...] = lower(total)


def dense_update_kernel(scalars, *refs):
    sums, refs = refs[:HEADS], refs[HEADS:]
    inputs = [refs[3 * index : 3 * index + 3] for index in range(6)]
    outputs = [refs[3 * index : 3 * index + 3] for index in range(6, 12)]

    def update(index, gradient, columns, rate):
        results = adamw_update(*[ref[:, columns] for ref in inputs[index]], gradient, rate)
        for target, result in zip(outputs[index], results):
            target[:, columns] = result

    part, small = sums[0].shape[0], sums[0].shape[1] - OUTPUT_EDGE
    shared = jnp.zeros((part, small), jnp.float32)
    chosen = jnp.zeros((part, inputs[3][0].shape[1]), jnp.float32)
    for index, rows in enumerate(sums):
        head = scalars[0] ^ index
        for side in range(2):
            span = pl.ds(pl.multiple_of((side * HEADS + head) * HEAD_DIM, HEAD_DIM), HEAD_DIM)
            source = pl.ds(side * HEAD_DIM, HEAD_DIM)
            update(0, raise_(rows[:, source]), span, rate_query_key)
        span = pl.ds(pl.multiple_of(head * VALUE_WIDTH, HEAD_DIM), VALUE_WIDTH)
        update(1, raise_(rows[:, QK_EDGE:VALUE_EDGE]), span, rate_value)
        update(2, raise_(rows[:, VALUE_EDGE:OUTPUT_EDGE]), span, rate_output)
        last = rows[:, OUTPUT_EDGE:]
        source = lax.broadcasted_iota(jnp.int32, (small, chosen.shape[1]), 0)
        target = lax.broadcasted_iota(jnp.int32, (small, chosen.shape[1]), 1)
        side, entry = lax.div(source, ATT_EXPERTS), lax.rem(source, ATT_EXPERTS)
        table = (target == (side * HEADS + head) * ATT_EXPERTS + entry) & (source < SELECT_COUNT)
        chosen += product(last, lower(jnp.where(table, 1.0, 0.0)))
        shared += raise_(last)
    every = slice(None)
    update(3, chosen, every, rate_select)
    expert_total = inputs[4][0].shape[1]
    update(4, pltpu.roll(shared, small - SELECT_COUNT, 1)[:, :expert_total], every, rate_router)
    gain_column = SELECT_COUNT + expert_total
    diagonal = lax.broadcasted_iota(jnp.int32, (part, part), 0) == lax.broadcasted_iota(
        jnp.int32, (part, part), 1
    )
    gain = jnp.where(diagonal, shared[:, gain_column : gain_column + 1], 0.0)
    update(5, jnp.sum(gain, axis=0, keepdims=True), every, rate_gain)


def expert_rows_kernel(weight, rows):
    count = weight.shape[0]
    for expert in range(count):
        rows[:, pl.ds(expert * EXPERT_H, EXPERT_H)] = lower(weight[expert, :, :EXPERT_H])
        rows[:, pl.ds((count + expert) * EXPERT_H, EXPERT_H)] = lower(weight[expert, :, EXPERT_H:])


def expert_rows_of(weight):
    count, rows, columns = weight.shape
    return pl.pallas_call(
        expert_rows_kernel,
        out_shape=jax.ShapeDtypeStruct((rows, count * columns), jnp.bfloat16),
        compiler_params=pltpu.CompilerParams(vmem_limit_bytes=56 * 2**20),
        cost_estimate=LIGHT,
    )(weight)


def front_kernel(scalars, tokens, picks, cotangent, routes, token_rows, upstream):
    rows, width = tokens.shape
    token_rows[:, :width] = tokens[...]
    row = lax.broadcasted_iota(jnp.int32, (token_rows.shape[1] - width, rows), 0)
    chosen = jnp.zeros(row.shape, jnp.float32)
    for head in range(picks.shape[0]):
        start = head % HEADS * SELECT_COUNT + head // HEADS * ATT_EXPERTS
        for pick in range(picks.shape[1]):
            chosen = jnp.where(row == start + picks[head, pick : pick + 1, :], 1.0, chosen)
    token_rows[:, width:] = lower(chosen.T)
    position = scalars[0] * rows + lax.broadcasted_iota(jnp.int32, (rows, 1), 0)
    upstream[:, :width] = lower(jnp.where(position < scalars[1], raise_(cotangent[...]), 0.0))
    row = lax.broadcasted_iota(jnp.int32, (upstream.shape[1] - width, rows), 0)
    hot = jnp.zeros(row.shape, jnp.float32)
    for index in range(routes.shape[0]):
        hot = jnp.where(row == SELECT_COUNT + routes[index : index + 1, :], 1.0, hot)
    upstream[:, width:] = lower(hot.T)


def payload_kernel(scalars, upstream, qk, value, output, select, router, gain, payload):
    part = qk.shape[0]
    small = payload.shape[2] - OUTPUT_EDGE
    rows, width = upstream.shape[0], upstream.shape[1] - small
    expert_total = router.shape[1]
    position = scalars[0] * rows + lax.broadcasted_iota(jnp.int32, (rows, 1), 0)
    valid = position < scalars[1]
    hot = raise_(upstream[:, width:])
    counts = jnp.sum(jnp.where(valid, hot, 0.0), axis=0, keepdims=True)
    gain_column = SELECT_COUNT + expert_total
    count_columns = -(-expert_total // part)
    row = lax.broadcasted_iota(jnp.int32, (part, small), 0)
    lane = lax.broadcasted_iota(jnp.int32, (part, small), 1)
    shared = product(lower(router[...]), shift_back(expert_total, small, SELECT_COUNT))
    diagonal = lax.broadcasted_iota(jnp.int32, (part, part), 0) == lax.broadcasted_iota(
        jnp.int32, (part, part), 1
    )
    gain_rows = jnp.sum(jnp.where(diagonal, gain[...], 0.0), axis=1, keepdims=True)
    shared = jnp.where(lane == gain_column, gain_rows, shared)
    for column in range(count_columns):
        mine = lane - SELECT_COUNT == row * count_columns + column
        found = jnp.sum(jnp.where(mine, counts, 0.0), axis=1, keepdims=True)
        shared = jnp.where(lane == gain_column + 1 + column, found, shared)
    picked = lower(select[...])
    for head in range(HEADS):
        span = pl.ds(head * HEAD_DIM, HEAD_DIM)
        payload[head, :, :HEAD_DIM] = lower(qk[:, span])
        span = pl.ds((HEADS + head) * HEAD_DIM, HEAD_DIM)
        payload[head, :, HEAD_DIM:QK_EDGE] = lower(qk[:, span])
        span = pl.ds(head * VALUE_WIDTH, VALUE_WIDTH)
        payload[head, :, QK_EDGE:VALUE_EDGE] = lower(value[:, span])
        payload[head, :, VALUE_EDGE:OUTPUT_EDGE] = lower(output[:, span])
        source = lax.broadcasted_iota(jnp.int32, (picked.shape[1], small), 0)
        target = lax.broadcasted_iota(jnp.int32, (picked.shape[1], small), 1)
        side, entry = lax.div(target, ATT_EXPERTS), lax.rem(target, ATT_EXPERTS)
        table = (source == (side * HEADS + head) * ATT_EXPERTS + entry) & (target < SELECT_COUNT)
        chosen = product(picked, lower(jnp.where(table, 1.0, 0.0)))
        payload[head, :, OUTPUT_EDGE:] = lower(shared + chosen)


def shift_back(rows, columns, offset):
    source = lax.broadcasted_iota(jnp.int32, (rows, columns), 0)
    target = lax.broadcasted_iota(jnp.int32, (rows, columns), 1)
    return lower(jnp.where(target == source + offset, 1.0, 0.0))


def local(
    tokens,
    cotangent,
    lengths,
    picks,
    routes,
    qk_weight,
    qk_first,
    qk_second,
    value_weight,
    value_first,
    value_second,
    output_weight,
    output_first,
    output_second,
    select_weight,
    select_first,
    select_second,
    router_weight,
    router_first,
    router_second,
    gain_weight,
    gain_first,
    gain_second,
    expert_weight,
    expert_first,
    expert_second,
):
    row_count = tokens.shape[1]
    model_width = tokens.shape[2]
    group_count = lax.axis_size("dp")
    owner_count = lax.axis_size("expert")
    local_count = expert_weight.shape[0]
    expert_total = local_count * owner_count
    bucket_rows = row_count * group_count
    part = qk_weight.shape[0]
    place = lax.axis_index("dp")
    owner = lax.axis_index("expert")
    seq_len = lengths[0]
    sequence = tokens[0]
    scalars = jnp.stack(
        [place.astype(jnp.int32), seq_len.astype(jnp.int32), owner.astype(jnp.int32)]
    )
    spots = jnp.stack([place.astype(jnp.int32), owner.astype(jnp.int32)])
    low, high = jnp.bfloat16, jnp.float32

    def shaped(columns, kind, rows=bucket_rows):
        return jax.ShapeDtypeStruct((rows, columns), kind)

    gain_column = SELECT_COUNT + expert_total
    count_columns = -(-expert_total // part)
    small_used = gain_column + 1 + count_columns
    small_width = small_used + -small_used % 128
    token_width = model_width + HEADS * SELECT_COUNT + -(HEADS * SELECT_COUNT) % 128

    token_own, upstream = wide_call(
        front_kernel,
        [scalars, sequence, picks[0].transpose(1, 2, 0), cotangent[0], routes[0].T],
        [
            shaped(token_width, low, row_count),
            shaped(model_width + small_width, low, row_count),
        ],
    )
    expert_up = {0: upstream}
    for relative in range(2, owner_count, 2):
        if not forwarded(relative):
            expert_up[relative] = swap(upstream, "expert", relative)
    token_blocks = [token_own] + [
        swap(token_own, "dp", relative) for relative in range(1, group_count)
    ]

    (payload,) = wide_call(
        payload_kernel,
        [
            scalars,
            upstream,
            qk_weight,
            value_weight,
            output_weight,
            select_weight,
            router_weight,
            gain_weight[None],
        ],
        [jax.ShapeDtypeStruct((HEADS, part, OUTPUT_EDGE + small_width), low)],
    )
    mine = lax.all_to_all(payload, "dp", split_axis=0, concat_axis=0, tiled=True)
    mine = after(
        mine, *token_blocks[1:], *[up for relative, up in expert_up.items() if relative]
    )

    half = row_count // 2
    expert_own = after(expert_rows_of(expert_weight), mine)
    expert_pieces = [expert_own, swap(expert_own, "dp", 1), swap(expert_own, "dp", 2)]
    dense_blocks = gather_chips(mine)
    dense_others = swap(
        after(jnp.stack(dense_blocks), *expert_pieces[1:]), "expert", 1
    )

    cosine, sine = rope_tables(bucket_rows)
    if part % 16 == 0:
        chips, made = owner_count // 2, []
        given = dense_blocks + [dense_others]
    else:
        dense = jnp.zeros((group_count, owner_count) + mine.shape[1:], jnp.bfloat16)
        for chip, block in enumerate(dense_blocks):
            for other, rows in enumerate((block, dense_others[chip])):
                spot = owner ^ (2 * chip + other)
                dense = lax.dynamic_update_slice_in_dim(dense, rows[:, None], spot, axis=1)
        dense = dense.reshape(group_count, row_count, -1)
        chips, made, given = 0, [], [dense]
    dense_shape = jax.ShapeDtypeStruct((group_count, row_count, payload.shape[2]), low)
    if chips:
        made = [dense_shape]
    outputs = made + [
        shaped(HEAD_DIM, low),
        shaped(HEAD_DIM, low),
        shaped(HEAD_DIM, low),
        shaped(small_width, high),
        shaped(VALUE_WIDTH, high),
        shaped(HEAD_DIM, high),
        shaped(VALUE_WIDTH, low),
        shaped(HEAD_DIM, high),
        shaped(model_width, low),
        shaped(2 * local_count + -2 * local_count % 128, low, model_width),
        shaped(small_width, high, part),
    ]
    kept = staged_call(
        functools.partial(attention_kernel, group_count, gain_column, chips, local_count),
        [scalars] + token_blocks + [cosine, sine] + given,
        outputs,
        token_blocks + [cosine, sine, dense_shape] + outputs[len(made) :],
        [],
        group_count + 2 + owner_count + len(outputs) + 2 * group_count,
    )
    if chips:
        dense, kept = kept[0], kept[1:]
    saved, (branch, router_local, counts) = dict(zip(KEPT, kept)), kept[len(KEPT) :]
    for relative in range(2, owner_count, 2):
        if forwarded(relative):
            block = after(expert_up[relative ^ 2], branch)
            expert_up[relative] = swap(block, "expert", 2)
    expert_up = [expert_up[relative] for relative in range(0, owner_count, 2)]
    near = [after(piece, branch) for piece in expert_pieces]
    expert_others = [swap(piece, "expert", 1) for piece in near]
    far = [
        swap(expert_pieces[1][:half], "dp", 2),
        swap(expert_pieces[2][half:], "dp", 1),
    ]
    expert_others += [swap(after(piece, branch), "expert", 1) for piece in far]
    branch = scatter_rows(branch)
    hidden, hidden_low = wide_call(
        hidden_kernel,
        [spots, sequence, after(branch, expert_up[-1], *expert_others)],
        [shaped(model_width, high, row_count), shaped(model_width, low, row_count)],
        limit=24,
    )
    small = dense[:, :, OUTPUT_EDGE:].reshape(model_width, -1)
    expert_counts = counts[:, gain_column + 1 : small_used].reshape(-1)[:expert_total]
    expert_counts = expert_counts.astype(jnp.int32)

    expert_both = expert_pieces + far + expert_others
    order = [0] + list(range(2, len(expert_up))) + [1]
    expert_rows, back, slopes, gateds = {0: hidden_low}, {}, {}, {}
    arriving = {}
    for relative in range(2, owner_count, 2):
        if not forwarded(relative):
            arriving[relative] = swap(hidden_low, "expert", relative)
    before = None
    for chip in order:
        if chip:
            others = [arriving[2]] if chip == order[1] else []
            block = after(arriving[2 * chip], before, *others)
            if chip % 2 == 0 and chip + 1 < len(expert_up):
                arriving[2 * chip + 2] = swap(block, "expert", 2)
            expert_rows[chip] = block
        back[chip], slopes[chip], gateds[chip] = expert_call(
            spots, expert_rows[chip], expert_up[chip], router_local, expert_both
        )
        before = slopes[chip]
    back_terms = send_expert([back[chip] for chip in range(len(order))])
    back_terms = [back_terms[chip] for chip in order]
    expert_rows, slopes, gateds = [
        [found[chip] for chip in range(len(order))] for found in (expert_rows, slopes, gateds)
    ]

    other_grads, own_grads = expert_grads(
        spots, expert_rows, expert_up, slopes, gateds, group_count
    )
    back_terms[1:] = [after(term, own_grads) for term in back_terms[1:]]

    hidden_grad, hidden_grad_low, router_grad = wide_call(
        functools.partial(hidden_back_kernel, len(back_terms)),
        [scalars] + back_terms + [hidden, upstream, small],
        [
            shaped(model_width, high, row_count),
            jax.ShapeDtypeStruct((group_count, row_count, model_width), low),
            shaped(small_width, high, model_width),
        ],
        limit=24,
    )
    hidden_grad_rows = exchange_rows(hidden_grad_low)
    produced = []
    for start in range(0, len(gateds), 4):
        produced += expert_out_call(
            after(spots, hidden_grad_low), expert_both, gateds[start : start + 4]
        )
    moe_terms = send_expert(produced)
    other_grads = swap(after(other_grads, hidden_grad_low), "expert", 1)

    across, along = halving(after(spots, *produced), own_grads, other_grads, row_count)
    across, along = swap(across, "dp", 1), swap(along, "dp", 2)
    scratch = [
        pltpu.VMEM((bucket_rows, HEAD_DIM), low),
        pltpu.VMEM((bucket_rows, small_width), high),
        pltpu.VMEM((bucket_rows, HEAD_DIM), high),
        pltpu.VMEM((bucket_rows, HEAD_DIM), high),
        pltpu.VMEM((bucket_rows, HEAD_DIM), high),
        pltpu.VMEM((bucket_rows, VALUE_WIDTH), low),
        pltpu.VMEM((bucket_rows, QK_EDGE), low),
        pltpu.VMEM((bucket_rows, small_width), low),
        pltpu.VMEM((bucket_rows, model_width), low),
    ]
    made = [dense_shape]
    if chips:
        made = [jax.ShapeDtypeStruct((chips, group_count, part, dense.shape[2]), low)] * 2
    saved.update(
        upstream=hidden_grad_rows, dense=dense, cosine=cosine, sine=sine, router_grad=router_grad
    )
    inputs = [saved[name] for name in BACK]
    terms_shape = shaped(model_width, low)
    *dense_parts, input_terms = staged_call(
        functools.partial(attention_back_kernel, group_count, gain_column, chips),
        [scalars] + inputs + token_blocks,
        made + [terms_shape],
        inputs + [dense_shape, terms_shape, terms_shape],
        scratch,
        len(inputs) + 2 * group_count + 3 * owner_count,
    )

    if not chips:
        dense_grad = dense_parts[0].reshape(group_count, owner_count, part, -1)
        dense_parts = [
            jnp.stack(
                [
                    lax.dynamic_index_in_dim(dense_grad, owner ^ relative, 1, keepdims=False)
                    for relative in range(side, owner_count, 2)
                ]
            )
            for side in range(2)
        ]
    late = after(spots, input_terms)
    first, second = halved(late, own_grads, other_grads, across, along)
    dense_parts[1] = after(dense_parts[1], first, second, *moe_terms)
    dense_parts = join(spots, dense_parts[0], swap(dense_parts[1], "expert", 1))
    first, second = swap(first, "dp", 2), swap(second, "dp", 1)
    input_grad = add_blocks(hidden_grad, scatter_rows(input_terms))
    dense_terms = send_expert(dense_parts)
    kept_grads = kept_rows(after(spots, *dense_parts), own_grads, other_grads, across, along)
    (layer_out,) = wide_call(
        layer_out_kernel,
        [after(spots, *dense_parts), hidden] + moe_terms,
        [shaped(model_width, low, row_count)],
    )
    dense_terms[1:] = [
        after(term, input_grad, layer_out, kept_grads, first, second) for term in dense_terms[1:]
    ]
    dense_sums = wide_call(
        dense_sum_kernel,
        [scalars] + dense_terms,
        [jax.ShapeDtypeStruct(dense_terms[0].shape[1:], low)] * group_count,
    )
    dense_sums = [dense_sums[0]] + [
        swap(dense_sums[relative], "dp", relative) for relative in range(1, group_count)
    ]
    masters = [
        (qk_weight, qk_first, qk_second),
        (value_weight, value_first, value_second),
        (output_weight, output_first, output_second),
        (select_weight, select_first, select_second),
        (router_weight, router_first, router_second),
        (gain_weight[None], gain_first[None], gain_second[None]),
    ]
    masters = [array for group in masters for array in group]
    updated = wide_call(
        dense_update_kernel,
        [scalars] + dense_sums + masters,
        [jax.ShapeDtypeStruct(array.shape, high) for array in masters],
        limit=24,
    )
    updated = list(updated[:15]) + [array[0] for array in updated[15:]]
    expert_results = expert_update(
        kept_grads, (first, second), expert_weight, expert_first, expert_second
    )
    return (layer_out[None], input_grad[None], *updated, *expert_results, expert_counts)


def solution(mesh):
    placed = (
        P("expert", "dp", None),
        P("expert", "dp", None),
        P("expert"),
        P("expert", "dp", None, None),
        P("expert", "dp", None),
        P(("dp", "expert"), None),
        P(("dp", "expert"), None),
        P(("dp", "expert"), None),
        P(("dp", "expert"), None),
        P(("dp", "expert"), None),
        P(("dp", "expert"), None),
        P(("dp", "expert"), None),
        P(("dp", "expert"), None),
        P(("dp", "expert"), None),
        P(("dp", "expert"), None),
        P(("dp", "expert"), None),
        P(("dp", "expert"), None),
        P(("dp", "expert"), None),
        P(("dp", "expert"), None),
        P(("dp", "expert"), None),
        P(("dp", "expert")),
        P(("dp", "expert")),
        P(("dp", "expert")),
        P("expert", "dp", None),
        P("expert", "dp", None),
        P("expert", "dp", None),
    )
    return jax.shard_map(
        local,
        mesh=mesh,
        in_specs=placed,
        out_specs=(
            P("expert", "dp", None),
            P("expert", "dp", None),
            P(("dp", "expert"), None),
            P(("dp", "expert"), None),
            P(("dp", "expert"), None),
            P(("dp", "expert"), None),
            P(("dp", "expert"), None),
            P(("dp", "expert"), None),
            P(("dp", "expert"), None),
            P(("dp", "expert"), None),
            P(("dp", "expert"), None),
            P(("dp", "expert"), None),
            P(("dp", "expert"), None),
            P(("dp", "expert"), None),
            P(("dp", "expert"), None),
            P(("dp", "expert"), None),
            P(("dp", "expert"), None),
            P(("dp", "expert")),
            P(("dp", "expert")),
            P(("dp", "expert")),
            P("expert", "dp", None),
            P("expert", "dp", None),
            P("expert", "dp", None),
            P(),
        ),
        check_vma=False,
    )
```
